32 devices in a mesh: seq: 8 (over z, x), row: 4 (over y, core).
Axes of the slice: x: 2, y: 2, z: 4, core: 2. Of those that a mesh axis runs over, the one named last changes fastest.
Arguments:
- block_input: bfloat16 [4, 1024, 1024], P('row', 'seq'), may hold values from -6 to 6
- cotangent: bfloat16 [4, 1024, 1024], P('row', 'seq'), may hold values from -6 to 6
- doc_starts: int32 [4, 8], P('row'), may hold values from 0 to 1023, as said below
- qkv_weight: bfloat16 [1024, 3072], P('seq'), may hold values from -0.1875 to 0.1875
- beta_weight: bfloat16 [1024, 8], P('seq'), may hold values from -0.1875 to 0.1875
- conv_weight: bfloat16 [4, 3072], P(None, 'seq'), may hold values from -3 to 3
- norm_gains: bfloat16 [2, 1024], P(None, 'seq'), may hold values from 0.25 to 1.75
- head_gain: bfloat16 [128], P('seq'), may hold values from 0.25 to 1.75
- out_weight: bfloat16 [1024, 1024], P('seq'), may hold values from -0.1875 to 0.1875
- gate_up_weight: bfloat16 [1024, 5632], P('seq'), may hold values from -0.1875 to 0.1875
- down_weight: bfloat16 [2816, 1024], P('seq'), may hold values from -0.109375 to 0.109375
Outputs:
- mixed: bfloat16 [4, 1024, 1024], P('row', 'seq')
- block_input_gradient: bfloat16 [4, 1024, 1024], P('row', 'seq')
- grad_qkv: float32 [1024, 3072], P('seq')
- grad_beta: float32 [1024, 8], P('seq')
- grad_conv: float32 [4, 3072], P(None, 'seq')
- grad_gains: float32 [2, 1024], P(None, 'seq')
- grad_head_gain: float32 [128], P('seq')
- grad_out: float32 [1024, 1024], P('seq')
- grad_gate_up: float32 [1024, 5632], P('seq')
- grad_down: float32 [2816, 1024], P('seq')
The draws below stay inside these ranges and needn't reach their ends.
Inputs may be any that keep to these rules, and one draw needn't show every extreme that they name: `doc_starts`: in each row the starts are non-decreasing, the first is 0 and the last is 1024 - 1 (a document may be empty); one document begins among the row's first 128 tokens and ends among its last 128.
All inputs are finite; a program needn't handle non-finite values.
Results may differ from the reference program's by a relative error of at most 0.023.
Values may be sent and summed in bfloat16 or wider, within the bound.
No kernel may reach another device: no remote copies, remote signals or barrier semaphores. Data moves between devices by JAX's collectives and lax.ppermute only.
A program may use at most 256 MiB of HBM per device.

```python
import jax
import jax.numpy as jnp
from jax import lax

D = 1024
H = 8
DK = 128
FF = 2816
GROUP = 64
CONV = 4
NDOCS = 8
TOK_DEV = 128
LENGTH = 1024
ROWS = 4


def draw_doc_starts(key, part):
    key = jax.random.fold_in(key, 7)
    key_first, key_last, key_count, key_lower, key_upper = jax.random.split(key, 5)
    big_start = jax.random.randint(key_first, (ROWS, 1), 2, TOK_DEV)
    big_end = LENGTH - jax.random.randint(key_last, (ROWS, 1), 1, TOK_DEV)
    before = jax.random.randint(key_count, (ROWS, 1), 1, NDOCS - 1)
    places = jnp.arange(NDOCS, dtype=jnp.int32)[None, :]
    lower_pos = jax.random.randint(key_lower, (ROWS, NDOCS), 1, big_start)
    upper_pos = jax.random.randint(key_upper, (ROWS, NDOCS), big_end, LENGTH)
    upper_pos = jnp.where(places == NDOCS - 1, LENGTH - 1, upper_pos)
    starts = jnp.where(places == 0, 0, jnp.where(places < before, lower_pos, jnp.where(places == before, big_start, upper_pos)))
    return jnp.sort(starts, axis=1).astype(jnp.int32)


def shard_levels(key, dims, cuts, smallest, high):
    def one(axis_at, parts):
        heights = jax.random.uniform(jax.random.fold_in(jax.random.fold_in(key, 6), axis_at), (parts,), jnp.float32, smallest / len(cuts), high / len(cuts))
        return jnp.repeat(jnp.exp(heights), dims[axis_at] // parts).reshape((-1,) + (1,) * (len(dims) - axis_at - 1))

    factor_of = one(*cuts[0])
    for cut in cuts[1:]:
        factor_of = factor_of * one(*cut)
    return factor_of


def normal_values(stream_key, shape, scale, limit, cuts=(), kind=jnp.bfloat16):
    values = scale * jax.random.normal(stream_key, shape, jnp.float32)
    if cuts:
        values = values * shard_levels(stream_key, shape, cuts, -0.22, 0.18)
    return jnp.clip(values, -limit, limit).astype(kind)


def setup_inputs(seed: int = 0) -> dict:
    streams_of = jax.random.split(jax.random.key(seed), 12)
    block_input = normal_values(streams_of[0], (ROWS, LENGTH, D), 1.0, 6.0, ((0, 4), (1, 8)))
    cotangent = normal_values(streams_of[1], (ROWS, LENGTH, D), 1.0, 6.0, ((0, 4), (1, 8)))
    doc_starts = draw_doc_starts(jax.random.fold_in(streams_of[11], 71), 0)
    qkv_weight = normal_values(streams_of[3], (D, 3 * D), D ** -0.5, 0.1875, ((0, 8),))
    beta_weight = normal_values(streams_of[4], (D, H), D ** -0.5, 0.1875, ((0, 8),))
    conv_weight = normal_values(streams_of[5], (CONV, 3 * D), 0.5, 3.0, ((1, 8),))
    norm_gains = jnp.clip(1.0 + 0.15 * jax.random.normal(streams_of[6], (2, D), jnp.float32), 0.25, 1.75).astype(jnp.bfloat16)
    head_gain = jnp.clip(1.0 + 0.15 * jax.random.normal(streams_of[7], (DK,), jnp.float32), 0.25, 1.75).astype(jnp.bfloat16)
    out_weight = normal_values(streams_of[8], (D, D), D ** -0.5, 0.1875, ((0, 8),))
    gate_up_weight = normal_values(streams_of[9], (D, 2 * FF), D ** -0.5, 0.1875, ((0, 8),))
    down_weight = normal_values(streams_of[10], (FF, D), FF ** -0.5, 0.109375, ((0, 8),))
    return {"block_input": block_input, "cotangent": cotangent, "doc_starts": doc_starts, "qkv_weight": qkv_weight, "beta_weight": beta_weight, "conv_weight": conv_weight, "norm_gains": norm_gains, "head_gain": head_gain, "out_weight": out_weight, "gate_up_weight": gate_up_weight, "down_weight": down_weight}


EPS_NORM = 1e-06
EPS_HEAD = 1e-05
EPS_UNIT = 1e-06
HIGH = lax.Precision.HIGHEST

@jax.custom_vjp
def low(v):
    return lax.optimization_barrier(v.astype(jnp.bfloat16)).astype(jnp.float32)

@jax.custom_vjp
def low_back(v):
    return v

def low_keep(v):
    return (low(v), None)

def low_pass(kept, grad):
    return (grad,)

def back_keep(v):
    return (v, None)

def back_low(kept, grad):
    return (low(grad),)
low.defvjp(low_keep, low_pass)
low_back.defvjp(back_keep, back_low)

def dotf(first_op, second_op):
    return jnp.matmul(first_op, second_op, precision=HIGH)

def unit_inverse(lower):
    identity = jnp.eye(lower.shape[-1], dtype=lower.dtype)
    power = lower
    result = identity - lower
    for step_index in range(lower.shape[-1].bit_length() - 2):
        power = dotf(power, power)
        result = dotf(result, identity + power)
    return result

def doc_index(positions, starts):
    return lax.optimization_barrier(jnp.sum((starts[None, :] <= positions[:, None]).astype(jnp.int32), axis=1)) - 1

def group_step(state, inputs):
    scaled_q, keys, values, rates, block_doc, prev_doc = inputs
    count = block_doc.shape[0]
    places = jnp.arange(count)
    same = block_doc[:, None] == block_doc[None, :]
    strict = (places[:, None] > places[None, :]) & same
    incl = (places[:, None] >= places[None, :]) & same
    keep = (block_doc == prev_doc).astype(jnp.float32)
    tail = (block_doc == block_doc[-1]).astype(jnp.float32)
    whole = keep[-1]
    scaled = keys * rates[..., None]
    lower = jnp.einsum('hid,hjd->hij', scaled, keys, precision=HIGH) * strict
    inverse = unit_inverse(lower)
    w_mat = dotf(inverse, scaled)
    base = dotf(inverse, values * rates[..., None])
    pseudo = base - keep[None, :, None] * dotf(w_mat, state)
    scores = jnp.einsum('hid,hjd->hij', scaled_q, keys, precision=HIGH) * incl
    output = keep[None, :, None] * dotf(scaled_q, state) + dotf(scores, pseudo)
    new_state = whole * state + jnp.einsum('hcd,hce->hde', keys * tail[None, :, None], pseudo, precision=HIGH)
    return (new_state, output)

def layer(token_rows, w_qkv, w_beta, w_conv, gains, head_g, w_out, w_gu, w_down, doc, prev_docs):
    seq_len = token_rows.shape[0]
    width = token_rows.shape[1]
    first_inverse_norm = lax.rsqrt(lax.optimization_barrier(jnp.mean(token_rows * token_rows, -1, keepdims=True)) + EPS_NORM)
    first_activation = low(token_rows * first_inverse_norm * gains[0])
    proj = low_back(low(dotf(first_activation, w_qkv)))
    rates_tok = jax.nn.sigmoid(low_back(dotf(first_activation, w_beta)))
    rim = w_conv.shape[0] - 1
    padded = jnp.concatenate([jnp.zeros((rim, proj.shape[1]), proj.dtype), proj], 0)
    pad_doc = jnp.concatenate([jnp.full((rim,), -1, jnp.int32), doc])
    pre = jnp.zeros_like(proj)
    for tap in range(rim + 1):
        window = padded[rim - tap:rim - tap + seq_len]
        match = (pad_doc[rim - tap:rim - tap + seq_len] == doc).astype(jnp.float32)[:, None]
        pre = pre + w_conv[tap] * window * match
    act = jax.nn.silu(pre)
    q_raw = act[:, :width].reshape(seq_len, H, DK)
    k_raw = act[:, width:2 * width].reshape(seq_len, H, DK)
    v_raw = act[:, 2 * width:].reshape(seq_len, H, DK)
    q_unit = q_raw * lax.rsqrt(lax.optimization_barrier(jnp.sum(q_raw * q_raw, -1, keepdims=True)) + EPS_UNIT)
    k_unit = k_raw * lax.rsqrt(lax.optimization_barrier(jnp.sum(k_raw * k_raw, -1, keepdims=True)) + EPS_UNIT)
    queries = low(q_unit)
    keys = low(k_unit)
    values = low(v_raw)

    def to_groups(arr):
        return arr.reshape(seq_len // GROUP, GROUP, H, DK).transpose(0, 2, 1, 3)
    rates = rates_tok.reshape(seq_len // GROUP, GROUP, H).transpose(0, 2, 1)
    docs = doc.reshape(-1, GROUP)
    state0 = jnp.zeros((H, DK, DK), jnp.float32)
    final_state, outputs = lax.scan(jax.checkpoint(group_step), state0, (to_groups(queries) * DK ** (-0.5), to_groups(keys), to_groups(values), rates, docs, prev_docs))
    mixed_o = outputs.transpose(0, 2, 1, 3).reshape(seq_len, H, DK)
    head_inv = lax.rsqrt(lax.optimization_barrier(jnp.mean(mixed_o * mixed_o, -1, keepdims=True)) + EPS_HEAD)
    act_two = low((mixed_o * head_inv * head_g).reshape(seq_len, width))
    resid = token_rows + low_back(dotf(act_two, w_out))
    inv_two = lax.rsqrt(lax.optimization_barrier(jnp.mean(resid * resid, -1, keepdims=True)) + EPS_NORM)
    act_three = low(resid * inv_two * gains[1])
    gate_up = low_back(dotf(act_three, w_gu))
    hidden_units = w_gu.shape[1] // 2
    act_four = low(jax.nn.silu(gate_up[:, :hidden_units]) * gate_up[:, hidden_units:])
    return resid + low_back(dotf(act_four, w_down))

def reference(block_input, cotangent, doc_starts, qkv_weight, beta_weight, conv_weight, norm_gains, head_gain, out_weight, gate_up_weight, down_weight):
    weights = tuple((weight.astype(jnp.float32) for weight in (qkv_weight, beta_weight, conv_weight, norm_gains, head_gain, out_weight, gate_up_weight, down_weight)))
    positions = jnp.arange(LENGTH, dtype=jnp.int32)
    prev_positions = jnp.arange(0, LENGTH, GROUP, dtype=jnp.int32) - 1

    def row_step(totals, inputs):
        row_input, row_cot, starts = inputs
        doc = doc_index(positions, starts)
        prev_docs = doc_index(prev_positions, starts)

        def forward(token_rows, *params):
            return layer(token_rows, *params, doc, prev_docs)
        result, pullback = jax.vjp(forward, row_input.astype(jnp.float32), *weights)
        grads = pullback(row_cot.astype(jnp.float32))
        totals = tuple((total + grad for total, grad in zip(totals, grads[1:])))
        return (totals, (result.astype(jnp.bfloat16), grads[0].astype(jnp.bfloat16)))
    initial = tuple((jnp.zeros_like(weight) for weight in weights))
    totals, (mixed, block_input_gradient) = lax.scan(row_step, initial, (block_input, cotangent, doc_starts))
    return (mixed, block_input_gradient, totals[0], totals[1], totals[2], totals[3], totals[4], totals[5], totals[6], totals[7])
```

```python
import functools

import jax
import jax.numpy as jnp
from jax import lax
from jax.experimental import pallas as pl
from jax.experimental.pallas import tpu as pltpu
from jax.sharding import PartitionSpec as P

H = 8
DK = 128
GROUP = 64


EPS_NORM = 1e-06
EPS_HEAD = 1e-05
EPS_UNIT = 1e-06
HIGH = lax.Precision.HIGHEST


def shifted(block, axis, distance):
    devices = range(lax.axis_size(axis))
    route = [(i - distance, i) for i in devices if i - distance in devices]
    return lax.ppermute(block, axis, route)


def dotf(first_op, second_op):
    return jnp.matmul(first_op, second_op, precision=HIGH)


def swap_last(matrix):
    return jnp.swapaxes(matrix, -1, -2)


def tok_dot(first_op, second_op):
    return lax.dot_general(
        first_op, second_op, (((0,), (0,)), ((), ())), preferred_element_type=jnp.float32
    )


def back_dot(first_op, second_op):
    return lax.dot_general(
        first_op, second_op, (((1,), (1,)), ((), ())), preferred_element_type=jnp.float32
    )


def unit_inverse(lower):
    identity = jnp.eye(lower.shape[-1], dtype=lower.dtype)
    power = lower
    result = identity - lower
    for step_index in range(lower.shape[-1].bit_length() - 2):
        power = dotf(power, power)
        result = dotf(result, identity + power)
    return result


def doc_index(positions, starts):
    return jnp.sum((starts[None, :] <= positions[:, None]).astype(jnp.int32), axis=1) - 1


def root_mean_square_backward(grad_in, normed, inverse):
    return inverse * (grad_in - normed * jnp.mean(grad_in * normed, -1, keepdims=True))


def silu_back(grad_in, pre):
    sig = jax.nn.sigmoid(pre)
    return grad_in * sig * (1.0 + pre * (1.0 - sig))


def on_device(
    block_input,
    cotangent,
    doc_starts,
    qkv_weight,
    beta_weight,
    conv_weight,
    norm_gains,
    head_gain,
    out_weight,
    gate_up_weight,
    down_weight,
):
    token_rows = block_input[0].astype(jnp.float32)
    cot_low = cotangent[0]
    seq_len = token_rows.shape[0]
    width = token_rows.shape[1]
    n_groups = seq_len // GROUP
    scale = DK ** (-0.5)
    w_qkv, w_beta, w_conv, w_gains, w_head, w_out, w_gu, w_down = (
        lax.all_gather(qkv_weight, "seq", axis=0, tiled=True),
        lax.all_gather(beta_weight, "seq", axis=0, tiled=True),
        lax.all_gather(conv_weight, "seq", axis=1, tiled=True),
        lax.all_gather(norm_gains, "seq", axis=1, tiled=True),
        lax.all_gather(head_gain, "seq", axis=0, tiled=True),
        lax.all_gather(out_weight, "seq", axis=0, tiled=True),
        lax.all_gather(gate_up_weight, "seq", axis=0, tiled=True),
        lax.all_gather(down_weight, "seq", axis=0, tiled=True),
    )
    conv_f = w_conv.astype(jnp.float32)
    float_gains = w_gains.astype(jnp.float32)
    head_f = w_head.astype(jnp.float32)
    seq_count = lax.axis_size("seq")
    seq_place = lax.axis_index("seq")
    starts = doc_starts[0]
    positions = seq_place * seq_len + jnp.arange(seq_len, dtype=jnp.int32)
    doc = doc_index(positions, starts)
    rim = conv_f.shape[0] - 1
    rim_doc = doc_index(seq_place * seq_len - rim + jnp.arange(rim, dtype=jnp.int32), starts)
    first_inverse_norm = lax.rsqrt(jnp.mean(token_rows * token_rows, -1, keepdims=True) + EPS_NORM)
    normalized_input = token_rows * first_inverse_norm
    first_activation = (normalized_input * float_gains[0]).astype(jnp.bfloat16)
    proj = jnp.dot(first_activation, w_qkv, preferred_element_type=jnp.float32).astype(jnp.bfloat16)
    rates_tok = jax.nn.sigmoid(
        jnp.dot(first_activation, w_beta, preferred_element_type=jnp.float32)
    )
    rim_vals = shifted(proj[seq_len - rim :], "seq", 1)
    extended = jnp.concatenate([rim_vals, proj], 0).astype(jnp.float32)
    ext_doc = jnp.concatenate([rim_doc, doc])
    matches = [
        (ext_doc[rim - tap : rim - tap + seq_len] == doc).astype(jnp.float32)[:, None]
        for tap in range(rim + 1)
    ]
    pre = jnp.zeros((seq_len, extended.shape[1]), jnp.float32)
    for tap in range(rim + 1):
        pre = pre + conv_f[tap] * extended[rim - tap : rim - tap + seq_len] * matches[tap]
    act = jax.nn.silu(pre)
    q_raw = act[:, :width].reshape(seq_len, H, DK)
    k_raw = act[:, width : 2 * width].reshape(seq_len, H, DK)
    v_raw = act[:, 2 * width :].reshape(seq_len, H, DK)
    q_inv = lax.rsqrt(jnp.sum(q_raw * q_raw, -1, keepdims=True) + EPS_UNIT)
    k_inv = lax.rsqrt(jnp.sum(k_raw * k_raw, -1, keepdims=True) + EPS_UNIT)
    q_unit = q_raw * q_inv
    k_unit = k_raw * k_inv

    def to_groups(arr):
        return (
            arr.astype(jnp.bfloat16)
            .astype(jnp.float32)
            .reshape(n_groups, GROUP, H, DK)
            .transpose(0, 2, 1, 3)
        )

    scaled_q = to_groups(q_unit) * scale
    keys = to_groups(k_unit)
    values = to_groups(v_raw)
    rates = rates_tok.reshape(n_groups, GROUP, H).transpose(0, 2, 1)
    block_doc = doc.reshape(n_groups, GROUP)
    prev_doc = doc_index(
        seq_place * seq_len + jnp.arange(n_groups, dtype=jnp.int32) * GROUP - 1, starts
    )
    places = jnp.arange(GROUP)
    same = block_doc[:, :, None] == block_doc[:, None, :]
    strict = ((places[:, None] > places[None, :])[None] & same)[:, None].astype(jnp.float32)
    incl = ((places[:, None] >= places[None, :])[None] & same)[:, None].astype(jnp.float32)
    keep = (block_doc == prev_doc[:, None]).astype(jnp.float32)[:, None, :, None]
    tail = (block_doc == block_doc[:, -1:]).astype(jnp.float32)[:, None, :, None]
    whole = keep[:, 0, -1, 0]
    scaled = keys * rates[..., None]
    lower = jnp.einsum("nhid,nhjd->nhij", scaled, keys, precision=HIGH) * strict
    inverse = unit_inverse(lower)
    w_mat = dotf(inverse, scaled)
    base = dotf(inverse, values * rates[..., None])
    eye_heads = jnp.broadcast_to(jnp.eye(DK, dtype=jnp.float32), (H, DK, DK))
    zero_heads = jnp.zeros((H, DK, DK), jnp.float32)

    def chain_step(maps, inputs):
        c_keys, c_w, c_base, c_keep, c_tail, c_whole = inputs
        mixed_maps = dotf(c_w[None], maps)
        reduce_part = jnp.einsum(
            "hcd,shce->shde", c_keys * (c_tail * c_keep), mixed_maps, precision=HIGH
        )
        maps = c_whole * maps - reduce_part
        shift_add = jnp.einsum("hcd,hce->hde", c_keys * c_tail, c_base, precision=HIGH)
        return (jnp.stack([maps[0], maps[1] + shift_add]), None)

    block_maps, unused = lax.scan(
        chain_step, jnp.stack([eye_heads, zero_heads]), (keys, w_mat, base, keep, tail, whole)
    )
    every_map, every_shift = (
        lax.all_gather(block_maps[0][None].astype(jnp.bfloat16), "seq", axis=0, tiled=True).astype(
            jnp.float32
        ),
        lax.all_gather(block_maps[1][None].astype(jnp.bfloat16), "seq", axis=0, tiled=True).astype(
            jnp.float32
        ),
    )

    def apply_map(position, state):
        return jnp.where(
            position < seq_place, dotf(every_map[position], state) + every_shift[position], state
        )

    state_in = lax.fori_loop(0, seq_count, apply_map, zero_heads)

    def out_step(state, inputs):
        c_q, c_keys, c_w, c_base, c_keep, c_tail, c_whole, c_incl = inputs
        pseudo = c_base - c_keep * dotf(c_w, state)
        scores = jnp.einsum("hid,hjd->hij", c_q, c_keys, precision=HIGH) * c_incl
        output = c_keep * dotf(c_q, state) + dotf(scores, pseudo)
        new_state = c_whole * state + jnp.einsum(
            "hcd,hce->hde", c_keys * c_tail, pseudo, precision=HIGH
        )
        return (new_state, (output, state))

    last_state, (outputs, block_states) = lax.scan(
        out_step, state_in, (scaled_q, keys, w_mat, base, keep, tail, whole, incl)
    )
    mixed_o = outputs.transpose(0, 2, 1, 3).reshape(seq_len, H, DK)
    head_inv = lax.rsqrt(jnp.mean(mixed_o * mixed_o, -1, keepdims=True) + EPS_HEAD)
    ohat = mixed_o * head_inv
    act_two = (ohat * head_f).reshape(seq_len, width).astype(jnp.bfloat16)
    resid = token_rows + jnp.dot(act_two, w_out, preferred_element_type=jnp.float32)
    inv_two = lax.rsqrt(jnp.mean(resid * resid, -1, keepdims=True) + EPS_NORM)
    rhat = resid * inv_two
    act_three = (rhat * float_gains[1]).astype(jnp.bfloat16)
    gate_up = jnp.dot(act_three, w_gu, preferred_element_type=jnp.float32)
    hidden_units = gate_up.shape[1] // 2
    gate = gate_up[:, :hidden_units]
    up_part = gate_up[:, hidden_units:]
    act_four = (jax.nn.silu(gate) * up_part).astype(jnp.bfloat16)
    mixed = (resid + jnp.dot(act_four, w_down, preferred_element_type=jnp.float32)).astype(
        jnp.bfloat16
    )
    grad_down = tok_dot(act_four, cot_low)
    d_act_four = back_dot(cot_low, w_down)
    d_gate = silu_back(d_act_four * up_part, gate)
    d_up = d_act_four * jax.nn.silu(gate)
    d_gate_up = jnp.concatenate([d_gate, d_up], 1).astype(jnp.bfloat16)
    grad_gate_up = tok_dot(act_three, d_gate_up)
    d_act_three = back_dot(d_gate_up, w_gu)
    grad_gain_two = jnp.sum(d_act_three * rhat, 0)
    residual_gradient = cot_low.astype(jnp.float32) + root_mean_square_backward(
        d_act_three * float_gains[1], rhat, inv_two
    )
    d_resid_low = residual_gradient.astype(jnp.bfloat16)
    grad_out = tok_dot(act_two, d_resid_low)
    d_act_two = back_dot(d_resid_low, w_out).reshape(seq_len, H, DK)
    grad_head = jnp.sum(d_act_two * ohat, (0, 1))
    d_mixed_o = root_mean_square_backward(d_act_two * head_f, ohat, head_inv)
    d_out_groups = d_mixed_o.reshape(n_groups, GROUP, H, DK).transpose(0, 2, 1, 3)

    def state_grad(grad_state, inputs):
        c_q, c_keys, c_scaled, c_inverse, c_keep, c_tail, c_whole, c_incl, c_dout = inputs
        scores = jnp.einsum("hid,hjd->hij", c_q, c_keys, precision=HIGH) * c_incl
        d_pseudo = jnp.einsum("hij,hid->hjd", scores, c_dout, precision=HIGH) + c_tail * dotf(
            c_keys, grad_state
        )
        d_res = jnp.einsum("hij,hid->hjd", c_inverse, d_pseudo, precision=HIGH)
        prior = (
            jnp.einsum("hcd,hce->hde", c_q * c_keep, c_dout, precision=HIGH) + c_whole * grad_state
        )
        return (prior - jnp.einsum("hcd,hce->hde", c_scaled * c_keep, d_res, precision=HIGH), None)

    local_grad, unused = lax.scan(
        state_grad,
        zero_heads,
        (scaled_q, keys, scaled, inverse, keep, tail, whole, incl, d_out_groups),
        reverse=True,
    )
    back_maps = swap_last(block_maps[0])
    every_back, every_grad = (
        lax.all_gather(back_maps[None].astype(jnp.bfloat16), "seq", axis=0, tiled=True).astype(
            jnp.float32
        ),
        lax.all_gather(local_grad[None].astype(jnp.bfloat16), "seq", axis=0, tiled=True).astype(
            jnp.float32
        ),
    )

    def apply_back(step_index, grad_state):
        position = seq_count - 1 - step_index
        return jnp.where(
            position > seq_place,
            dotf(every_back[position], grad_state) + every_grad[position],
            grad_state,
        )

    grad_state_out = lax.fori_loop(0, seq_count, apply_back, zero_heads)

    def full_back(grad_state, inputs):
        (
            c_q,
            c_keys,
            c_values,
            c_rates,
            c_scaled,
            c_inverse,
            c_w,
            c_base,
            c_keep,
            c_tail,
            c_whole,
            c_strict,
            c_incl,
            c_dout,
            c_state,
        ) = inputs
        pseudo = c_base - c_keep * dotf(c_w, c_state)
        scores = jnp.einsum("hid,hjd->hij", c_q, c_keys, precision=HIGH) * c_incl
        d_pseudo = jnp.einsum("hij,hid->hjd", scores, c_dout, precision=HIGH) + c_tail * dotf(
            c_keys, grad_state
        )
        d_res = jnp.einsum("hij,hid->hjd", c_inverse, d_pseudo, precision=HIGH)
        prior = (
            jnp.einsum("hcd,hce->hde", c_q * c_keep, c_dout, precision=HIGH) + c_whole * grad_state
        )
        prior = prior - jnp.einsum("hcd,hce->hde", c_scaled * c_keep, d_res, precision=HIGH)
        d_scores = jnp.einsum("hid,hjd->hij", c_dout, pseudo, precision=HIGH) * c_incl
        d_query = c_keep * dotf(c_dout, swap_last(c_state)) + dotf(d_scores, c_keys)
        d_keys = jnp.einsum("hij,hid->hjd", d_scores, c_q, precision=HIGH) + c_tail * dotf(
            pseudo, swap_last(grad_state)
        )
        d_lower = -jnp.einsum("hid,hjd->hij", d_res, pseudo, precision=HIGH) * c_strict
        d_scaled = -c_keep * dotf(d_res, swap_last(c_state)) + dotf(d_lower, c_keys)
        d_keys = (
            d_keys
            + jnp.einsum("hij,hid->hjd", d_lower, c_scaled, precision=HIGH)
            + c_rates[..., None] * d_scaled
        )
        d_values = c_rates[..., None] * d_res
        d_rates = jnp.sum(d_res * c_values, -1) + jnp.sum(d_scaled * c_keys, -1)
        return (prior, (d_query * scale, d_keys, d_values, d_rates))

    first_grad, (d_q_groups, d_k_groups, d_v_groups, d_rate_groups) = lax.scan(
        full_back,
        grad_state_out,
        (
            scaled_q,
            keys,
            values,
            rates,
            scaled,
            inverse,
            w_mat,
            base,
            keep,
            tail,
            whole,
            strict,
            incl,
            d_out_groups,
            block_states,
        ),
        reverse=True,
    )

    def from_groups(arr):
        return arr.transpose(0, 2, 1, 3).reshape(seq_len, H, DK)

    d_q_unit = from_groups(d_q_groups)
    d_k_unit = from_groups(d_k_groups)
    d_q_raw = q_inv * (d_q_unit - q_unit * jnp.sum(d_q_unit * q_unit, -1, keepdims=True))
    d_k_raw = k_inv * (d_k_unit - k_unit * jnp.sum(d_k_unit * k_unit, -1, keepdims=True))
    d_act = jnp.concatenate(
        [
            d_q_raw.reshape(seq_len, width),
            d_k_raw.reshape(seq_len, width),
            from_groups(d_v_groups).reshape(seq_len, width),
        ],
        1,
    )
    d_pre = silu_back(d_act, pre)
    d_extended = jnp.zeros((seq_len + rim, d_pre.shape[1]), jnp.float32)
    conv_grads = []
    for tap in range(rim + 1):
        masked = d_pre * matches[tap]
        d_extended = d_extended + jnp.pad(conv_f[tap] * masked, ((rim - tap, tap), (0, 0)))
        conv_grads.append(jnp.sum(masked * extended[rim - tap : rim - tap + seq_len], 0))
    grad_conv = jnp.stack(conv_grads)
    rim_back = shifted(d_extended[:rim].astype(jnp.bfloat16), "seq", -1).astype(jnp.float32)
    d_proj = (d_extended[rim:] + jnp.pad(rim_back, ((seq_len - rim, 0), (0, 0)))).astype(
        jnp.bfloat16
    )
    d_rates_tok = d_rate_groups.transpose(0, 2, 1).reshape(seq_len, H)
    d_logits = (d_rates_tok * rates_tok * (1.0 - rates_tok)).astype(jnp.bfloat16)
    grad_qkv = tok_dot(first_activation, d_proj)
    grad_beta = tok_dot(first_activation, d_logits)
    first_activation_gradient = back_dot(d_proj, w_qkv) + back_dot(d_logits, w_beta)
    first_gain_gradient = jnp.sum(first_activation_gradient * normalized_input, 0)
    block_input_gradient = (
        residual_gradient
        + root_mean_square_backward(
            first_activation_gradient * float_gains[0], normalized_input, first_inverse_norm
        )
    ).astype(jnp.bfloat16)
    grad_gains = jnp.stack([first_gain_gradient, grad_gain_two])
    red_qkv, red_beta, red_conv, red_gains, red_head, red_out, red_gu, red_down = (
        lax.psum_scatter(
            grad_qkv.astype(jnp.bfloat16), "seq", scatter_dimension=0, tiled=True
        ).astype(jnp.float32),
        lax.psum_scatter(
            grad_beta.astype(jnp.bfloat16), "seq", scatter_dimension=0, tiled=True
        ).astype(jnp.float32),
        lax.psum_scatter(
            grad_conv.astype(jnp.bfloat16), "seq", scatter_dimension=1, tiled=True
        ).astype(jnp.float32),
        lax.psum_scatter(
            grad_gains.astype(jnp.bfloat16), "seq", scatter_dimension=1, tiled=True
        ).astype(jnp.float32),
        lax.psum_scatter(
            grad_head.astype(jnp.bfloat16), "seq", scatter_dimension=0, tiled=True
        ).astype(jnp.float32),
        lax.psum_scatter(
            grad_out.astype(jnp.bfloat16), "seq", scatter_dimension=0, tiled=True
        ).astype(jnp.float32),
        lax.psum_scatter(
            grad_gate_up.astype(jnp.bfloat16), "seq", scatter_dimension=0, tiled=True
        ).astype(jnp.float32),
        lax.psum_scatter(
            grad_down.astype(jnp.bfloat16), "seq", scatter_dimension=0, tiled=True
        ).astype(jnp.float32),
    )
    red_qkv, red_beta, red_conv, red_gains, red_head, red_out, red_gu, red_down = (
        lax.psum(red_qkv.astype(jnp.bfloat16), "row").astype(jnp.float32),
        lax.psum(red_beta.astype(jnp.bfloat16), "row").astype(jnp.float32),
        lax.psum(red_conv.astype(jnp.bfloat16), "row").astype(jnp.float32),
        lax.psum(red_gains.astype(jnp.bfloat16), "row").astype(jnp.float32),
        lax.psum(red_head.astype(jnp.bfloat16), "row").astype(jnp.float32),
        lax.psum(red_out.astype(jnp.bfloat16), "row").astype(jnp.float32),
        lax.psum(red_gu.astype(jnp.bfloat16), "row").astype(jnp.float32),
        lax.psum(red_down.astype(jnp.bfloat16), "row").astype(jnp.float32),
    )
    return (
        mixed[None],
        block_input_gradient[None],
        red_qkv,
        red_beta,
        red_conv,
        red_gains,
        red_head,
        red_out,
        red_gu,
        red_down,
    )


BF = jnp.bfloat16
F32 = jnp.float32
RIM = 8
NN = (((1,), (0,)), ((), ()))
NT = (((1,), (1,)), ((), ()))
TN = (((0,), (0,)), ((), ()))


def dot_low(a, b, dims=NN):
    return lax.dot_general(a, b, dims, preferred_element_type=F32)


def parts_of(a):
    if a.dtype == BF:
        return (a,)
    high = a.astype(BF)
    return high, (a - high.astype(F32)).astype(BF)


def mm(a, b, dims=NN):
    a_parts, b_parts = parts_of(a), parts_of(b)
    total = dot_low(a_parts[0], b_parts[0], dims)
    if len(b_parts) > 1:
        total = total + dot_low(a_parts[0], b_parts[1], dims)
    if len(a_parts) > 1:
        total = total + dot_low(a_parts[1], b_parts[0], dims)
    return total


def mm1(a, b, dims=NN):
    return dot_low(a.astype(BF), b.astype(BF), dims)


def begin_of(pos, starts_ref):
    begin = jnp.zeros_like(pos)
    for i in range(starts_ref.shape[0]):
        begin = jnp.maximum(begin, jnp.where(pos >= starts_ref[i], starts_ref[i], 0))
    return begin


def begin_at(pos, starts_ref):
    begin = jnp.int32(0)
    for i in range(starts_ref.shape[0]):
        begin = jnp.maximum(begin, jnp.where(starts_ref[i] <= pos, starts_ref[i], 0))
    return begin


def chunk_marks(n, size, starts_ref):
    first = n * size
    col = begin_of(first + lax.broadcasted_iota(jnp.int32, (size, 1), 0), starts_ref)
    last = begin_at(first + size - 1, starts_ref)
    keep = (col < first).astype(F32)
    tail = (col == last).astype(F32)
    whole = (last < first).astype(F32)
    return col, keep, tail, whole


def chunk_masks(n, size, col, starts_ref):
    across = begin_of(n * size + lax.broadcasted_iota(jnp.int32, (1, size), 1), starts_ref)
    here = lax.broadcasted_iota(jnp.int32, (size, size), 0)
    there = lax.broadcasted_iota(jnp.int32, (size, size), 1)
    same = col == across
    return here, there, same & (here > there), same & (here >= there)


def conv_chunk(n, size, pad, conv, col):
    depth = n * size + lax.broadcasted_iota(jnp.int32, (size, 1), 0) - col
    pre = conv[0:1, :] * pad[pl.ds(RIM + n * size, size), :]
    for tap in range(1, conv.shape[0]):
        match = (depth >= tap).astype(F32)
        pre = pre + conv[tap : tap + 1, :] * pad[pl.ds(RIM - tap + n * size, size), :] * match
    return pre


def front_kernel(taps, place_ref, starts_ref, *refs):
    n_seq = refs[-1].shape[0]
    x_refs = refs[:n_seq]
    (
        got_ref,
        act1_ref,
        proj_ref,
        rates_ref,
        o_ref,
        act2_ref,
        inv_ref,
        w_ref,
        att_ref,
        p_ref,
        u_ref,
        s_ref,
        conv_ref,
        gains_ref,
        beta_ref,
        head_ref,
        pad,
        lower,
        tmp,
        q_scr,
        k_scr,
        v_scr,
        add,
    ) = refs[n_seq:]
    place = place_ref[0]
    size = x_refs[0].shape[0]
    dk = o_ref.shape[1]
    half = n_seq // 2
    z, side = place // 2, lax.rem(place, 2)
    gains = jnp.concatenate([got_ref[s, size + 4 : size + 6, 0:dk] for s in range(n_seq)], 1).astype(F32)
    gains_ref[...] = jnp.zeros_like(gains_ref)
    gains_ref[0:2, :] = gains
    beta = jnp.concatenate([got_ref[s, size + 8 : size + 16, 0:dk] for s in range(n_seq)], 1)
    beta_ref[...] = beta
    head_gain = got_ref[0, size + 6 : size + 7, 0:dk].astype(F32)
    for s in range(1, n_seq):
        head_gain = head_gain + got_ref[s, size + 6 : size + 7, 0:dk].astype(F32)
    head_ref[...] = jnp.broadcast_to(head_gain, head_ref.shape)
    conv_parts = []
    for part in range(3):
        block = part * n_seq + place
        shard = block // 3
        offset = pl.multiple_of((block - shard * 3) * dk, dk)
        conv_parts.append(got_ref[shard, size : size + 8, pl.ds(offset, dk)])
    conv = jnp.concatenate(conv_parts, 1).astype(F32)
    conv_ref[...] = conv
    conv = conv[0:taps]
    weight = got_ref[:, 0:size, :].reshape(n_seq * size, 3 * dk)
    lanes = lax.broadcasted_iota(jnp.int32, (size, 8), 1)
    pad[0:RIM, :] = jnp.zeros((RIM, 3 * dk), F32)
    for k in range(half):
        for j in range(2):
            chunk = lax.rem(z - k + half, half) * 2 + (side if j == 0 else 1 - side)
            at = pl.multiple_of(chunk * size, size)
            rows = x_refs[2 * k + j][...].astype(F32)
            inv = lax.rsqrt(jnp.mean(rows * rows, -1, keepdims=True) + EPS_NORM)
            act = ((rows * inv) * gains[0:1]).astype(BF)
            act1_ref[pl.ds(at, size), :] = act
            proj = dot_low(act, weight).astype(BF)
            proj_ref[pl.ds(at, size), :] = proj
            pad[pl.ds(pl.multiple_of(RIM + at, 8), size), :] = proj.astype(F32)
            logits = dot_low(act, beta, NT)
            rate = jax.nn.sigmoid(jnp.sum(jnp.where(lanes == place, logits, 0.0), 1, keepdims=True))
            rates_ref[pl.ds(at, size), :] = jnp.broadcast_to(rate, (size, dk))
    marks = []
    for n in range(n_seq):
        at = n * size
        col, keep, tail, whole = chunk_marks(n, size, starts_ref)
        marks.append((keep, tail, whole))
        pre = conv_chunk(n, size, pad, conv, col)
        act = pre * jax.nn.sigmoid(pre)
        q_raw, k_raw, v_raw = act[:, :dk], act[:, dk : 2 * dk], act[:, 2 * dk :]
        q = (q_raw * lax.rsqrt(jnp.sum(q_raw * q_raw, -1, keepdims=True) + EPS_UNIT)).astype(BF)
        key = (k_raw * lax.rsqrt(jnp.sum(k_raw * k_raw, -1, keepdims=True) + EPS_UNIT)).astype(BF)
        q_scr[pl.ds(at, size), :] = q
        k_scr[pl.ds(at, size), :] = key
        v_scr[pl.ds(at, size), :] = v_raw.astype(BF)
        here, there, strict, incl = chunk_masks(n, size, col, starts_ref)
        rate = rates_ref[pl.ds(at, size), :]
        low = jnp.where(strict, dot_low(key, key, NT) * rate, 0.0)
        att_ref[n] = jnp.where(incl, dot_low(q, key, NT) * (dk**-0.5), 0.0)
        lower[n] = low
        eye = (here == there).astype(F32)
        inv_ref[n] = eye - jnp.where((here // 2) == (there // 2), low, 0.0)
    span = 2
    while span < size:
        here = lax.broadcasted_iota(jnp.int32, (size, size), 0)
        there = lax.broadcasted_iota(jnp.int32, (size, size), 1)
        cross = ((here // (2 * span)) == (there // (2 * span))) & ((here // span) != (there // span))
        for n in range(n_seq):
            tmp[n] = mm(inv_ref[n], jnp.where(cross, lower[n], 0.0))
        for n in range(n_seq):
            inv_ref[n] = inv_ref[n] - mm(tmp[n], inv_ref[n])
        span *= 2
    for n in range(n_seq):
        keep, tail, whole = marks[n]
        rows = pl.ds(n * size, size)
        rate = rates_ref[rows, :]
        key = k_scr[rows, :]
        inv = inv_ref[n]
        w = mm(inv, rate * key.astype(F32))
        base = mm(inv, rate * v_scr[rows, :].astype(F32))
        w_ref[n] = w
        u_ref[n] = base
        p_ref[n] = mm(key, (tail * keep) * w, TN)
        add[n] = mm(key, tail * base, TN)
    state = jnp.zeros((dk, dk), F32)
    for n in range(n_seq):
        s_ref[n] = state
        if n + 1 < n_seq:
            state = marks[n][2] * state - mm(p_ref[n], state) + add[n]
    for n in range(n_seq):
        keep, tail, whole = marks[n]
        rows = pl.ds(n * size, size)
        state = s_ref[n]
        u = u_ref[n] - keep * mm(w_ref[n], state)
        u_ref[n] = u
        out = (keep * (dk**-0.5)) * mm(q_scr[rows, :], state) + mm(att_ref[n], u)
        o_ref[rows, :] = out
        inv = lax.rsqrt(jnp.mean(out * out, -1, keepdims=True) + EPS_HEAD)
        act2_ref[n] = ((out * inv) * head_gain).astype(BF)


def back_kernel(taps, starts_ref, *refs):
    (
        dact_ref,
        o_ref,
        head_ref,
        conv_ref,
        proj_ref,
        rates_ref,
        inv_ref,
        w_ref,
        att_ref,
        p_ref,
        u_ref,
        s_ref,
        dproj_ref,
        dlog_ref,
        gconv_ref,
        ghead_ref,
        pad,
        pre_scr,
        dpre,
        do_scr,
        g_scr,
        add,
        x_scr,
        q_scr,
        k_scr,
    ) = refs
    n_seq, size, dk = dact_ref.shape
    scale = dk**-0.5
    head_gain = head_ref[0:1, :]
    conv = conv_ref[0:taps, :]
    total = n_seq * size
    pad[0:RIM, :] = jnp.zeros((RIM, 3 * dk), F32)
    pad[pl.ds(RIM, total), :] = proj_ref[...].astype(F32)
    dpre[pl.ds(total, RIM), :] = jnp.zeros((RIM, 3 * dk), F32)
    marks = []
    ghead = jnp.zeros((1, dk), F32)
    for n in range(n_seq):
        rows = pl.ds(n * size, size)
        col, keep, tail, whole = chunk_marks(n, size, starts_ref)
        marks.append((col, keep, tail, whole))
        pre = conv_chunk(n, size, pad, conv, col)
        pre_scr[rows, :] = pre
        act = pre * jax.nn.sigmoid(pre)
        q_raw, k_raw = act[:, :dk], act[:, dk : 2 * dk]
        q = (q_raw * lax.rsqrt(jnp.sum(q_raw * q_raw, -1, keepdims=True) + EPS_UNIT)).astype(BF)
        key = (k_raw * lax.rsqrt(jnp.sum(k_raw * k_raw, -1, keepdims=True) + EPS_UNIT)).astype(BF)
        q_scr[rows, :] = q
        k_scr[rows, :] = key
        out = o_ref[rows, :]
        inv = lax.rsqrt(jnp.mean(out * out, -1, keepdims=True) + EPS_HEAD)
        ohat = out * inv
        d_act2 = dact_ref[n].astype(F32)
        ghead = ghead + jnp.sum(d_act2 * ohat, 0, keepdims=True)
        lean = d_act2 * head_gain
        d_out = inv * (lean - ohat * jnp.mean(lean * ohat, -1, keepdims=True))
        do_scr[rows, :] = d_out
        g_scr[rows, :] = mm(att_ref[n], d_out, TN)
    ghead_ref[...] = jnp.broadcast_to(ghead, ghead_ref.shape)
    for n in range(n_seq):
        rows = pl.ds(n * size, size)
        col, keep, tail, whole = marks[n]
        add[n] = mm(q_scr[rows, :], (scale * keep) * do_scr[rows, :], TN) - mm(w_ref[n], keep * g_scr[rows, :], TN)
    grad = jnp.zeros((dk, dk), F32)
    for n in range(n_seq - 1, -1, -1):
        x_scr[n] = grad
        if n > 0:
            grad = marks[n][3] * grad - mm(p_ref[n], grad, TN) + add[n]
    gconv = [jnp.zeros((1, 3 * dk), F32) for _ in range(taps)]
    for n in range(n_seq - 1, -1, -1):
        rows = pl.ds(n * size, size)
        col, keep, tail, whole = marks[n]
        here, there, strict, incl = chunk_masks(n, size, col, starts_ref)
        rate = rates_ref[rows, :]
        key, q = k_scr[rows, :], q_scr[rows, :]
        key_f, q_f = key.astype(F32), q.astype(F32)
        pre = pre_scr[rows, :]
        sig = jax.nn.sigmoid(pre)
        act = pre * sig
        value = act[:, 2 * dk :].astype(BF).astype(F32)
        grad, state, u = x_scr[n], s_ref[n], u_ref[n]
        d_out = do_scr[rows, :]
        d_u = g_scr[rows, :] + tail * mm(key, grad)
        d_r = mm(inv_ref[n], d_u, TN)
        d_att = jnp.where(incl, mm(d_out, u, NT), 0.0)
        d_low = jnp.where(strict, -mm(d_r, u, NT), 0.0)
        d_q = keep * mm(d_out, state, NT) + mm(d_att, key)
        d_kb = mm(d_low, key) - keep * mm(d_r, state, NT)
        d_k = (
            scale * mm(d_att, q, TN)
            + mm(d_low, rate * key_f, TN)
            + tail * mm(u, grad, NT)
            + rate * d_kb
        )
        d_v = rate * d_r
        d_rate = jnp.sum(d_r * value + d_kb * key_f, -1, keepdims=True)
        d_q = d_q * scale
        q_raw, k_raw = act[:, :dk], act[:, dk : 2 * dk]
        q_inv = lax.rsqrt(jnp.sum(q_raw * q_raw, -1, keepdims=True) + EPS_UNIT)
        k_inv = lax.rsqrt(jnp.sum(k_raw * k_raw, -1, keepdims=True) + EPS_UNIT)
        q_unit, k_unit = q_raw * q_inv, k_raw * k_inv
        d_q = q_inv * (d_q - q_unit * jnp.sum(d_q * q_unit, -1, keepdims=True))
        d_k = k_inv * (d_k - k_unit * jnp.sum(d_k * k_unit, -1, keepdims=True))
        d_act = jnp.concatenate([d_q, d_k, d_v], 1)
        d_pre = d_act * sig * (1.0 + pre * (1.0 - sig))
        dpre[rows, :] = d_pre
        pos = n * size + lax.broadcasted_iota(jnp.int32, (size, 1), 0)
        d_proj = conv[0:1, :] * d_pre
        gconv[0] = gconv[0] + jnp.sum(d_pre * pad[pl.ds(RIM + n * size, size), :], 0, keepdims=True)
        for tap in range(1, taps):
            later = pos + tap
            match = ((begin_of(later, starts_ref) <= pos) & (later < total)).astype(F32)
            d_proj = d_proj + conv[tap : tap + 1, :] * dpre[pl.ds(n * size + tap, size), :] * match
            reach = (pos - col >= tap).astype(F32)
            gconv[tap] = gconv[tap] + jnp.sum(
                d_pre * reach * pad[pl.ds(RIM - tap + n * size, size), :], 0, keepdims=True
            )
        dproj_ref[n, 0:size, :] = d_proj.astype(BF)
        one_rate = rate[:, 0:1]
        d_logit = d_rate * one_rate * (1.0 - one_rate)
        spread = jnp.broadcast_to(d_logit, (size, dk)).T
        row_form = jnp.concatenate([spread[0:16], jnp.zeros((16, 2 * dk), F32)], 1).astype(BF)
        dproj_ref[n, pl.ds(size, 16), :] = row_form
        dlog_ref[pl.ds(n, 1), :] = spread[0:1]
    gconv_ref[...] = jnp.zeros_like(gconv_ref)
    for tap in range(taps):
        gconv_ref[tap : tap + 1, :] = gconv[tap]


def mid_kernel(act2_ref, weight_ref, x_ref, gains_ref, resid_ref, act3_ref):
    heads = act2_ref.shape[0]
    act2 = jnp.concatenate([act2_ref[h] for h in range(heads)], 1)
    resid = x_ref[...].astype(F32) + dot_low(act2, weight_ref[...])
    resid_ref[...] = resid
    inv = lax.rsqrt(jnp.mean(resid * resid, -1, keepdims=True) + EPS_NORM)
    act3_ref[...] = ((resid * inv) * gains_ref[1:2, :]).astype(BF)


def feed_kernel(act3_ref, cot_ref, gu_ref, down_ref, part_ref, act4_ref, dgu_ref, down):
    hidden, wide = down_ref.shape[0], down.shape[0]
    down[0:hidden, :] = down_ref[...]
    if wide > hidden:
        down[hidden:wide, :] = jnp.zeros((wide - hidden, down.shape[1]), BF)
    gate_up = dot_low(act3_ref[...], gu_ref[...])
    gate, up = gate_up[:, :wide], gate_up[:, wide:]
    sig = jax.nn.sigmoid(gate)
    silu = gate * sig
    act4_ref[...] = (silu * up).astype(BF)
    d_act4 = dot_low(cot_ref[...], down[...], NT)
    d_gate = d_act4 * up * sig * (1.0 + gate * (1.0 - sig))
    d_gu = jnp.concatenate([d_gate, d_act4 * silu], 1).astype(BF)
    dgu_ref[...] = d_gu
    part_ref[...] = dot_low(d_gu, gu_ref[...], NT).astype(BF)


def turn_kernel(heads, dact3_ref, resid_ref, cot_ref, gains_ref, weight_ref, dresid_ref, low_ref, dact2_ref):
    resid = resid_ref[...]
    inv = lax.rsqrt(jnp.mean(resid * resid, -1, keepdims=True) + EPS_NORM)
    rhat = resid * inv
    lean = dact3_ref[...] * gains_ref[1:2, :]
    d_resid = cot_ref[...].astype(F32) + inv * (lean - rhat * jnp.mean(lean * rhat, -1, keepdims=True))
    dresid_ref[...] = d_resid
    low = d_resid.astype(BF)
    low_ref[...] = low
    d_act2 = dot_low(low, weight_ref[...], NT).astype(BF)
    dk = d_act2.shape[1] // heads
    for h in range(heads):
        dact2_ref[h] = d_act2[:, h * dk : (h + 1) * dk]


def last_kernel(got_ref, weight_ref, beta_ref, x_ref, gains_ref, dresid_ref, out_ref):
    heads = got_ref.shape[0]
    size = x_ref.shape[0]
    dk = got_ref.shape[2] // 3
    d_proj = jnp.concatenate(
        [got_ref[h, 0:size, part * dk : (part + 1) * dk] for part in range(3) for h in range(heads)], 1
    )
    d_logits = jnp.concatenate([got_ref[h, size : size + 1, 0:dk] for h in range(heads)], 0)
    d_act1 = dot_low(d_proj, weight_ref[...], NT) + dot_low(d_logits, beta_ref[0:heads, :], TN)
    rows = x_ref[...].astype(F32)
    inv = lax.rsqrt(jnp.mean(rows * rows, -1, keepdims=True) + EPS_NORM)
    xhat = rows * inv
    lean = d_act1 * gains_ref[0:1, :]
    out = dresid_ref[...] + inv * (lean - xhat * jnp.mean(lean * xhat, -1, keepdims=True))
    out_ref[...] = out.astype(BF)


def local_call(kernel, outs, args, scratch=(), smem=0, flops=0, name=None):
    space = [pl.BlockSpec(memory_space=pltpu.SMEM)] * smem
    space += [pl.BlockSpec(memory_space=pltpu.VMEM)] * (len(args) - smem)
    moved = sum(a.size * a.dtype.itemsize for a in args) + sum(o.size * o.dtype.itemsize for o in outs)
    return pl.pallas_call(
        kernel,
        out_shape=tuple(outs),
        in_specs=space,
        out_specs=tuple(pl.BlockSpec(memory_space=pltpu.VMEM) for _ in outs),
        scratch_shapes=list(scratch),
        compiler_params=pltpu.CompilerParams(vmem_limit_bytes=56 * 2**20),
        cost_estimate=pl.CostEstimate(flops=flops, bytes_accessed=moved, transcendentals=0),
        name=name,
    )(*args)


def head_plan(
    block_input,
    cotangent,
    doc_starts,
    qkv_weight,
    beta_weight,
    conv_weight,
    norm_gains,
    head_gain,
    out_weight,
    gate_up_weight,
    down_weight,
):
    x, cot = block_input[0], cotangent[0]
    starts = doc_starts[0]
    size, width = x.shape
    n_seq, n_row = lax.axis_size("seq"), lax.axis_size("row")
    place, row = lax.axis_index("seq"), lax.axis_index("row")
    half = n_seq // 2
    z, side = place // 2, place % 2
    total = n_seq * size
    taps = conv_weight.shape[0]
    hidden = down_weight.shape[0]
    wide = -(-hidden // 128) * 128
    shape = jax.ShapeDtypeStruct

    def flip(v):
        return lax.ppermute(v, "seq", [(s, s ^ 1) for s in range(n_seq)])

    def roll(v, k):
        return lax.ppermute(v, "seq", [(s, (s // 2 + k) % half * 2 + s % 2) for s in range(n_seq)])

    def core(v):
        return lax.ppermute(v, "row", [(r, r ^ 1) for r in range(n_row)])

    def across(v):
        return lax.ppermute(v, "row", [(r, r ^ 2) for r in range(n_row)])

    pairs = [
        (s * n_row + r, (r * 2 + s // n_row) * n_row + s % n_row)
        for s in range(n_seq)
        for r in range(n_row)
    ]

    def spread(v):
        return lax.ppermute(v, ("seq", "row"), pairs)

    def collect(v):
        return lax.ppermute(v, ("seq", "row"), [(b, a) for a, b in pairs])

    def group_gather(v):
        y, s = across(v), flip(v)
        four = jnp.stack([v, y, s, flip(y)])
        return jnp.concatenate([four, core(four)], 0).reshape(8 * v.shape[0], v.shape[1])

    def group_sum(parts):
        mine = parts[0:4].astype(F32) + core(parts[4:8]).astype(F32)
        low = mine.astype(BF)
        first = mine[1] + flip(low[3]).astype(F32)
        second = mine[0] + flip(low[2]).astype(F32)
        return second + across(first.astype(BF)).astype(F32)

    def row_pieces(v):
        return [lax.dynamic_index_in_dim(v, row ^ m, v.ndim - 3, False) for m in range(n_row)]

    def row_sum(pieces):
        got = core(jnp.stack([pieces[1], pieces[3]])).astype(F32)
        first = pieces[0].astype(F32) + got[0]
        second = pieces[2].astype(F32) + got[1]
        return first + across(second.astype(BF)).astype(F32)

    def row_gather(v):
        pair = jnp.stack([v, core(v)])
        four = jnp.concatenate([pair, across(pair)], 0)
        return [lax.dynamic_index_in_dim(four, row ^ m, 0, False) for m in range(n_row)]

    near = flip(x)
    pieces = [x, near]
    for k in range(1, half):
        far = roll(x, k)
        pieces += [far, flip(far)]
    by_head = qkv_weight.reshape(size, 3, n_seq, width // n_seq).transpose(2, 0, 1, 3)
    by_head = by_head.reshape(n_seq, size, 3 * width // n_seq)
    cols = by_head.shape[2]
    lane = jnp.arange(128)
    per = head_gain.shape[0]
    head_row = jnp.where(lane // per == place, jnp.tile(head_gain, 128 // per), jnp.zeros((), BF))

    def wide_rows(v):
        return jnp.pad(v, ((0, 0), (0, cols - v.shape[1])))

    small = jnp.concatenate(
        [
            conv_weight,
            wide_rows(norm_gains),
            wide_rows(head_row[None]),
            jnp.zeros((1, cols), BF),
            wide_rows(beta_weight.T),
        ],
        0,
    )
    payload = jnp.concatenate([by_head, jnp.broadcast_to(small[None], (n_seq,) + small.shape)], 1)
    got = lax.all_to_all(payload, "seq", 0, 0)

    def columns(block):
        gate = lax.dynamic_slice_in_dim(gate_up_weight, block * hidden, hidden, 1)
        up = lax.dynamic_slice_in_dim(gate_up_weight, (n_seq + block) * hidden, hidden, 1)
        gap = jnp.zeros((size, wide - hidden), BF)
        return jnp.concatenate([gate, gap, up, gap], 1)

    own_cols = columns(side * n_row + row)
    other_cols = flip(columns((1 - side) * n_row + row))
    pair_cols = jnp.where(
        side == 0, jnp.stack([own_cols, other_cols]), jnp.stack([other_cols, own_cols])
    ).reshape(2 * size, 2 * wide)
    w_gu = jnp.zeros((half, 2 * size, 2 * wide), BF)
    w_gu = lax.dynamic_update_index_in_dim(w_gu, pair_cols, z, 0)
    for k in range(1, half):
        w_gu = lax.dynamic_update_index_in_dim(w_gu, roll(pair_cols, k), (z - k) % half, 0)
    w_gu = w_gu.reshape(total, 2 * wide)
    w_down = spread(down_weight)
    cot_all = group_gather(cot)
    w_out = lax.all_gather(out_weight, "seq", axis=0, tiled=True)
    w_qkv = lax.all_gather(qkv_weight, "seq", axis=0, tiled=True)

    dk = width // n_seq
    square = shape((n_seq, size, dk), F32)
    (
        act1,
        proj,
        rates,
        outs,
        act2,
        inverse,
        w_mat,
        att,
        p_mat,
        u_mat,
        states,
        conv,
        gains,
        beta,
        head,
    ) = local_call(
        functools.partial(front_kernel, taps),
        [
            shape((total, width), BF),
            shape((total, 3 * dk), BF),
            shape((total, dk), F32),
            shape((total, dk), F32),
            shape((n_seq, size, dk), BF),
            square,
            square,
            square,
            square,
            square,
            square,
            shape((8, 3 * dk), F32),
            shape((8, width), F32),
            shape((8, width), BF),
            shape((8, dk), F32),
        ],
        [place.reshape(1), starts, *pieces, got],
        scratch=[
            pltpu.VMEM((RIM + total, 3 * dk), F32),
            pltpu.VMEM((n_seq, size, size), F32),
            pltpu.VMEM((n_seq, size, size), F32),
            pltpu.VMEM((total, dk), BF),
            pltpu.VMEM((total, dk), BF),
            pltpu.VMEM((total, dk), BF),
            pltpu.VMEM((n_seq, dk, dk), F32),
        ],
        smem=2,
        flops=2 * 10**10,
        name="front",
    )
    act2 = lax.all_to_all(act2, "seq", 0, 0)
    resid, act3 = local_call(
        mid_kernel,
        [shape((size, width), F32), shape((size, width), BF)],
        [act2, w_out, x, gains],
        flops=2 * size * width * width,
        name="mid",
    )
    act3_all = group_gather(act3)
    block = total // 4
    wide_block = pl.BlockSpec((block, width), lambda i: (i, 0))
    d_parts, act4, d_gu = pl.pallas_call(
        feed_kernel,
        grid=(4,),
        out_shape=(
            shape((total, width), BF),
            shape((total, wide), BF),
            shape((total, 2 * wide), BF),
        ),
        in_specs=[
            wide_block,
            wide_block,
            pl.BlockSpec((width, 2 * wide), lambda i: (0, 0)),
            pl.BlockSpec((hidden, width), lambda i: (0, 0)),
        ],
        out_specs=(
            wide_block,
            pl.BlockSpec((block, wide), lambda i: (i, 0)),
            pl.BlockSpec((block, 2 * wide), lambda i: (i, 0)),
        ),
        scratch_shapes=[pltpu.VMEM((wide, width), BF)],
        compiler_params=pltpu.CompilerParams(vmem_limit_bytes=56 * 2**20),
        cost_estimate=pl.CostEstimate(
            flops=10 * total * width * wide, bytes_accessed=14 * 2**20, transcendentals=0
        ),
        name="feed",
    )(act3_all, cot_all, w_gu, w_down)
    d_act3 = group_sum(d_parts.reshape(8, size, width))
    mixed_parts = jnp.dot(act4[:, :hidden], w_down, preferred_element_type=F32).astype(BF)
    mixed = (resid + group_sum(mixed_parts.reshape(8, size, width))).astype(BF)
    grad_down = tok_dot(act4, cot_all)[:hidden].astype(BF)
    grad_gu = tok_dot(act3_all, d_gu).astype(BF)
    d_resid, d_low, d_act2 = local_call(
        functools.partial(turn_kernel, n_seq),
        [shape((size, width), F32), shape((size, width), BF), shape((n_seq, size, dk), BF)],
        [d_act3, resid, cot, gains, w_out],
        flops=2 * size * width * width,
        name="turn",
    )
    d_act2 = lax.all_to_all(d_act2, "seq", 0, 0)
    d_proj, d_log, g_conv, g_head = local_call(
        functools.partial(back_kernel, taps),
        [
            shape((n_seq, size + 16, 3 * dk), BF),
            shape((n_seq, size), F32),
            shape((8, 3 * dk), F32),
            shape((8, dk), F32),
        ],
        [starts, d_act2, outs, head, conv, proj, rates, inverse, w_mat, att, p_mat, u_mat, states],
        scratch=[
            pltpu.VMEM((RIM + total, 3 * dk), F32),
            pltpu.VMEM((total, 3 * dk), F32),
            pltpu.VMEM((RIM + total, 3 * dk), F32),
            pltpu.VMEM((total, dk), F32),
            pltpu.VMEM((total, dk), F32),
            pltpu.VMEM((n_seq, dk, dk), F32),
            pltpu.VMEM((n_seq, dk, dk), F32),
            pltpu.VMEM((total, dk), BF),
            pltpu.VMEM((total, dk), BF),
        ],
        smem=1,
        flops=2 * 10**10,
        name="back",
    )
    back = lax.all_to_all(d_proj, "seq", 0, 0)
    (input_gradient,) = local_call(
        last_kernel,
        [shape((size, width), BF)],
        [back, w_qkv, beta, x, gains, d_resid],
        flops=6 * size * width * width,
        name="last",
    )

    own = side
    blocks = grad_gu.reshape(half, 2 * size, 2 * wide)
    gu_sum = lax.dynamic_index_in_dim(blocks, z, 0, False).astype(F32)
    for k in range(1, half):
        gu_sum = gu_sum + roll(
            lax.dynamic_index_in_dim(blocks, (z + k) % half, 0, False), k
        ).astype(F32)
    gu_sum = gu_sum.astype(BF).reshape(2, size, 2 * wide)
    gu_mine = lax.dynamic_index_in_dim(gu_sum, side, 0, False)
    gu_other = flip(lax.dynamic_index_in_dim(gu_sum, 1 - side, 0, False))
    gu_two = jnp.where(side == 0, jnp.stack([gu_mine, gu_other]), jnp.stack([gu_other, gu_mine]))
    gu_rows = row_gather(gu_two)
    gu_blocks = [gu_rows[b % n_row][b // n_row] for b in range(n_seq)]
    red_gu = jnp.concatenate(
        [b[:, :hidden] for b in gu_blocks] + [b[:, wide : wide + hidden] for b in gu_blocks], 1
    ).astype(F32)
    down_here = collect(grad_down).reshape(n_row, hidden // n_row, width)
    red_down = jnp.concatenate(row_gather(row_sum(row_pieces(down_here)).astype(BF)), 0).astype(F32)

    def seq_row_sum(full):
        cols = full.shape[1]
        cut = full.reshape(n_seq, n_row, size // n_row, cols)
        mine = row_sum(row_pieces(cut)).astype(BF)
        return lax.all_to_all(mine, "seq", 0, 0)

    act2_rows = act2.transpose(1, 0, 2).reshape(size, width)
    grad_out = tok_dot(act2_rows, d_low).astype(BF)
    out_piece = seq_row_sum(grad_out).astype(F32).sum(0).astype(BF)
    red_out = jnp.concatenate(row_gather(out_piece), 0).astype(F32)
    grad_qkv = tok_dot(act1, d_proj[:, :size].reshape(total, 3 * dk)).astype(BF)
    qkv_piece = seq_row_sum(grad_qkv)
    qkv_piece = qkv_piece.reshape(n_seq, size // n_row, 3, dk).transpose(1, 2, 0, 3)
    qkv_piece = qkv_piece.reshape(size // n_row, 3 * width)
    red_qkv = jnp.concatenate(row_gather(qkv_piece), 0).astype(F32)
    g_beta = jnp.dot(
        d_log.astype(BF).reshape(1, total), act1, preferred_element_type=F32
    ).reshape(n_seq, 1, size)
    g_conv_rows = g_conv[:taps].reshape(taps * 3, dk)
    small_out = jnp.concatenate(
        [
            g_beta,
            jnp.broadcast_to(g_conv_rows[None], (n_seq, taps * 3, dk)),
            jnp.broadcast_to(g_head[None, 0:1], (n_seq, 1, dk)),
            jnp.zeros((n_seq, 2, dk), F32),
        ],
        1,
    )
    small_in = lax.all_to_all(small_out, "seq", 0, 0)
    small_in = small_in + core(small_in)
    small_in = small_in + across(small_in)
    red_beta = small_in[:, 0, :].T
    conv_in = small_in[:, 1 : 1 + taps * 3].reshape(n_seq, taps, 3, dk)
    conv_in = conv_in.transpose(1, 2, 0, 3).reshape(taps, 3 * width)
    red_conv = lax.dynamic_slice_in_dim(conv_in, place * 3 * dk, 3 * dk, 1)
    red_head = lax.dynamic_slice_in_dim(small_in[:, 1 + taps * 3].sum(0), place * per, per, 0)
    own_gains = norm_gains.astype(F32)
    first_gain = (
        jnp.sum(qkv_weight.astype(F32) * red_qkv, 1) + jnp.sum(beta_weight.astype(F32) * red_beta, 1)
    ) / own_gains[0]
    second_gain = jnp.sum(gate_up_weight.astype(F32) * red_gu, 1) / own_gains[1]
    red_gains = jnp.stack([first_gain, second_gain])
    return (
        mixed[None],
        input_gradient[None],
        red_qkv,
        red_beta,
        red_conv,
        red_gains,
        red_head,
        red_out,
        red_gu,
        red_down,
    )


def plan(block_input, *rest):
    seq, row = lax.axis_size("seq"), lax.axis_size("row")
    if seq == H and row * 2 == H and block_input.shape[1] == DK:
        return head_plan(block_input, *rest)
    return on_device(block_input, *rest)


def solution(mesh):
    in_specs = (
        P("row", "seq", None),
        P("row", "seq", None),
        P("row", None),
        P("seq", None),
        P("seq", None),
        P(None, "seq"),
        P(None, "seq"),
        P("seq"),
        P("seq", None),
        P("seq", None),
        P("seq", None),
    )
    out_specs = (
        P("row", "seq", None),
        P("row", "seq", None),
        P("seq", None),
        P("seq", None),
        P(None, "seq"),
        P(None, "seq"),
        P("seq"),
        P("seq", None),
        P("seq", None),
        P("seq", None),
    )
    return jax.shard_map(
        plan, mesh=mesh, in_specs=in_specs, out_specs=out_specs, check_vma=False
    )
```

```python
import functools

import jax
import jax.numpy as jnp
from jax import lax
from jax.experimental import pallas as pl
from jax.experimental.pallas import tpu as pltpu
from jax.sharding import PartitionSpec as P

H = 8
DK = 128
GROUP = 64


EPS_NORM = 1e-06
EPS_HEAD = 1e-05
EPS_UNIT = 1e-06
HIGH = lax.Precision.HIGHEST


def shifted(block, axis, distance):
    devices = range(lax.axis_size(axis))
    route = [(i - distance, i) for i in devices if i - distance in devices]
    return lax.ppermute(block, axis, route)


def dotf(first_op, second_op):
    return jnp.matmul(first_op, second_op, precision=HIGH)


def swap_last(matrix):
    return jnp.swapaxes(matrix, -1, -2)


def tok_dot(first_op, second_op):
    return lax.dot_general(
        first_op, second_op, (((0,), (0,)), ((), ())), preferred_element_type=jnp.float32
    )


def back_dot(first_op, second_op):
    return lax.dot_general(
        first_op, second_op, (((1,), (1,)), ((), ())), preferred_element_type=jnp.float32
    )


def unit_inverse(lower):
    identity = jnp.eye(lower.shape[-1], dtype=lower.dtype)
    power = lower
    result = identity - lower
    for step_index in range(lower.shape[-1].bit_length() - 2):
        power = dotf(power, power)
        result = dotf(result, identity + power)
    return result


def doc_index(positions, starts):
    return jnp.sum((starts[None, :] <= positions[:, None]).astype(jnp.int32), axis=1) - 1


def root_mean_square_backward(grad_in, normed, inverse):
    return inverse * (grad_in - normed * jnp.mean(grad_in * normed, -1, keepdims=True))


def silu_back(grad_in, pre):
    sig = jax.nn.sigmoid(pre)
    return grad_in * sig * (1.0 + pre * (1.0 - sig))


def on_device(
    block_input,
    cotangent,
    doc_starts,
    qkv_weight,
    beta_weight,
    conv_weight,
    norm_gains,
    head_gain,
    out_weight,
    gate_up_weight,
    down_weight,
):
    token_rows = block_input[0].astype(jnp.float32)
    cot_low = cotangent[0]
    seq_len = token_rows.shape[0]
    width = token_rows.shape[1]
    n_groups = seq_len // GROUP
    scale = DK ** (-0.5)
    w_qkv, w_beta, w_conv, w_gains, w_head, w_out, w_gu, w_down = (
        lax.all_gather(qkv_weight, "seq", axis=0, tiled=True),
        lax.all_gather(beta_weight, "seq", axis=0, tiled=True),
        lax.all_gather(conv_weight, "seq", axis=1, tiled=True),
        lax.all_gather(norm_gains, "seq", axis=1, tiled=True),
        lax.all_gather(head_gain, "seq", axis=0, tiled=True),
        lax.all_gather(out_weight, "seq", axis=0, tiled=True),
        lax.all_gather(gate_up_weight, "seq", axis=0, tiled=True),
        lax.all_gather(down_weight, "seq", axis=0, tiled=True),
    )
    conv_f = w_conv.astype(jnp.float32)
    float_gains = w_gains.astype(jnp.float32)
    head_f = w_head.astype(jnp.float32)
    seq_count = lax.axis_size("seq")
    seq_place = lax.axis_index("seq")
    starts = doc_starts[0]
    positions = seq_place * seq_len + jnp.arange(seq_len, dtype=jnp.int32)
    doc = doc_index(positions, starts)
    rim = conv_f.shape[0] - 1
    rim_doc = doc_index(seq_place * seq_len - rim + jnp.arange(rim, dtype=jnp.int32), starts)
    first_inverse_norm = lax.rsqrt(jnp.mean(token_rows * token_rows, -1, keepdims=True) + EPS_NORM)
    normalized_input = token_rows * first_inverse_norm
    first_activation = (normalized_input * float_gains[0]).astype(jnp.bfloat16)
    proj = jnp.dot(first_activation, w_qkv, preferred_element_type=jnp.float32).astype(jnp.bfloat16)
    rates_tok = jax.nn.sigmoid(
        jnp.dot(first_activation, w_beta, preferred_element_type=jnp.float32)
    )
    rim_vals = shifted(proj[seq_len - rim :], "seq", 1)
    extended = jnp.concatenate([rim_vals, proj], 0).astype(jnp.float32)
    ext_doc = jnp.concatenate([rim_doc, doc])
    matches = [
        (ext_doc[rim - tap : rim - tap + seq_len] == doc).astype(jnp.float32)[:, None]
        for tap in range(rim + 1)
    ]
    pre = jnp.zeros((seq_len, extended.shape[1]), jnp.float32)
    for tap in range(rim + 1):
        pre = pre + conv_f[tap] * extended[rim - tap : rim - tap + seq_len] * matches[tap]
    act = jax.nn.silu(pre)
    q_raw = act[:, :width].reshape(seq_len, H, DK)
    k_raw = act[:, width : 2 * width].reshape(seq_len, H, DK)
    v_raw = act[:, 2 * width :].reshape(seq_len, H, DK)
    q_inv = lax.rsqrt(jnp.sum(q_raw * q_raw, -1, keepdims=True) + EPS_UNIT)
    k_inv = lax.rsqrt(jnp.sum(k_raw * k_raw, -1, keepdims=True) + EPS_UNIT)
    q_unit = q_raw * q_inv
    k_unit = k_raw * k_inv

    def to_groups(arr):
        return (
            arr.astype(jnp.bfloat16)
            .astype(jnp.float32)
            .reshape(n_groups, GROUP, H, DK)
            .transpose(0, 2, 1, 3)
        )

    scaled_q = to_groups(q_unit) * scale
    keys = to_groups(k_unit)
    values = to_groups(v_raw)
    rates = rates_tok.reshape(n_groups, GROUP, H).transpose(0, 2, 1)
    block_doc = doc.reshape(n_groups, GROUP)
    prev_doc = doc_index(
        seq_place * seq_len + jnp.arange(n_groups, dtype=jnp.int32) * GROUP - 1, starts
    )
    places = jnp.arange(GROUP)
    same = block_doc[:, :, None] == block_doc[:, None, :]
    strict = ((places[:, None] > places[None, :])[None] & same)[:, None].astype(jnp.float32)
    incl = ((places[:, None] >= places[None, :])[None] & same)[:, None].astype(jnp.float32)
    keep = (block_doc == prev_doc[:, None]).astype(jnp.float32)[:, None, :, None]
    tail = (block_doc == block_doc[:, -1:]).astype(jnp.float32)[:, None, :, None]
    whole = keep[:, 0, -1, 0]
    scaled = keys * rates[..., None]
    lower = jnp.einsum("nhid,nhjd->nhij", scaled, keys, precision=HIGH) * strict
    inverse = unit_inverse(lower)
    w_mat = dotf(inverse, scaled)
    base = dotf(inverse, values * rates[..., None])
    eye_heads = jnp.broadcast_to(jnp.eye(DK, dtype=jnp.float32), (H, DK, DK))
    zero_heads = jnp.zeros((H, DK, DK), jnp.float32)

    def chain_step(maps, inputs):
        c_keys, c_w, c_base, c_keep, c_tail, c_whole = inputs
        mixed_maps = dotf(c_w[None], maps)
        reduce_part = jnp.einsum(
            "hcd,shce->shde", c_keys * (c_tail * c_keep), mixed_maps, precision=HIGH
        )
        maps = c_whole * maps - reduce_part
        shift_add = jnp.einsum("hcd,hce->hde", c_keys * c_tail, c_base, precision=HIGH)
        return (jnp.stack([maps[0], maps[1] + shift_add]), None)

    block_maps, unused = lax.scan(
        chain_step, jnp.stack([eye_heads, zero_heads]), (keys, w_mat, base, keep, tail, whole)
    )
    every_map, every_shift = (
        lax.all_gather(block_maps[0][None].astype(jnp.bfloat16), "seq", axis=0, tiled=True).astype(
            jnp.float32
        ),
        lax.all_gather(block_maps[1][None].astype(jnp.bfloat16), "seq", axis=0, tiled=True).astype(
            jnp.float32
        ),
    )

    def apply_map(position, state):
        return jnp.where(
            position < seq_place, dotf(every_map[position], state) + every_shift[position], state
        )

    state_in = lax.fori_loop(0, seq_count, apply_map, zero_heads)

    def out_step(state, inputs):
        c_q, c_keys, c_w, c_base, c_keep, c_tail, c_whole, c_incl = inputs
        pseudo = c_base - c_keep * dotf(c_w, state)
        scores = jnp.einsum("hid,hjd->hij", c_q, c_keys, precision=HIGH) * c_incl
        output = c_keep * dotf(c_q, state) + dotf(scores, pseudo)
        new_state = c_whole * state + jnp.einsum(
            "hcd,hce->hde", c_keys * c_tail, pseudo, precision=HIGH
        )
        return (new_state, (output, state))

    last_state, (outputs, block_states) = lax.scan(
        out_step, state_in, (scaled_q, keys, w_mat, base, keep, tail, whole, incl)
    )
    mixed_o = outputs.transpose(0, 2, 1, 3).reshape(seq_len, H, DK)
    head_inv = lax.rsqrt(jnp.mean(mixed_o * mixed_o, -1, keepdims=True) + EPS_HEAD)
    ohat = mixed_o * head_inv
    act_two = (ohat * head_f).reshape(seq_len, width).astype(jnp.bfloat16)
    resid = token_rows + jnp.dot(act_two, w_out, preferred_element_type=jnp.float32)
    inv_two = lax.rsqrt(jnp.mean(resid * resid, -1, keepdims=True) + EPS_NORM)
    rhat = resid * inv_two
    act_three = (rhat * float_gains[1]).astype(jnp.bfloat16)
    gate_up = jnp.dot(act_three, w_gu, preferred_element_type=jnp.float32)
    hidden_units = gate_up.shape[1] // 2
    gate = gate_up[:, :hidden_units]
    up_part = gate_up[:, hidden_units:]
    act_four = (jax.nn.silu(gate) * up_part).astype(jnp.bfloat16)
    mixed = (resid + jnp.dot(act_four, w_down, preferred_element_type=jnp.float32)).astype(
        jnp.bfloat16
    )
    grad_down = tok_dot(act_four, cot_low)
    d_act_four = back_dot(cot_low, w_down)
    d_gate = silu_back(d_act_four * up_part, gate)
    d_up = d_act_four * jax.nn.silu(gate)
    d_gate_up = jnp.concatenate([d_gate, d_up], 1).astype(jnp.bfloat16)
    grad_gate_up = tok_dot(act_three, d_gate_up)
    d_act_three = back_dot(d_gate_up, w_gu)
    grad_gain_two = jnp.sum(d_act_three * rhat, 0)
    residual_gradient = cot_low.astype(jnp.float32) + root_mean_square_backward(
        d_act_three * float_gains[1], rhat, inv_two
    )
    d_resid_low = residual_gradient.astype(jnp.bfloat16)
    grad_out = tok_dot(act_two, d_resid_low)
    d_act_two = back_dot(d_resid_low, w_out).reshape(seq_len, H, DK)
    grad_head = jnp.sum(d_act_two * ohat, (0, 1))
    d_mixed_o = root_mean_square_backward(d_act_two * head_f, ohat, head_inv)
    d_out_groups = d_mixed_o.reshape(n_groups, GROUP, H, DK).transpose(0, 2, 1, 3)

    def state_grad(grad_state, inputs):
        c_q, c_keys, c_scaled, c_inverse, c_keep, c_tail, c_whole, c_incl, c_dout = inputs
        scores = jnp.einsum("hid,hjd->hij", c_q, c_keys, precision=HIGH) * c_incl
        d_pseudo = jnp.einsum("hij,hid->hjd", scores, c_dout, precision=HIGH) + c_tail * dotf(
            c_keys, grad_state
        )
        d_res = jnp.einsum("hij,hid->hjd", c_inverse, d_pseudo, precision=HIGH)
        prior = (
            jnp.einsum("hcd,hce->hde", c_q * c_keep, c_dout, precision=HIGH) + c_whole * grad_state
        )
        return (prior - jnp.einsum("hcd,hce->hde", c_scaled * c_keep, d_res, precision=HIGH), None)

    local_grad, unused = lax.scan(
        state_grad,
        zero_heads,
        (scaled_q, keys, scaled, inverse, keep, tail, whole, incl, d_out_groups),
        reverse=True,
    )
    back_maps = swap_last(block_maps[0])
    every_back, every_grad = (
        lax.all_gather(back_maps[None].astype(jnp.bfloat16), "seq", axis=0, tiled=True).astype(
            jnp.float32
        ),
        lax.all_gather(local_grad[None].astype(jnp.bfloat16), "seq", axis=0, tiled=True).astype(
            jnp.float32
        ),
    )

    def apply_back(step_index, grad_state):
        position = seq_count - 1 - step_index
        return jnp.where(
            position > seq_place,
            dotf(every_back[position], grad_state) + every_grad[position],
            grad_state,
        )

    grad_state_out = lax.fori_loop(0, seq_count, apply_back, zero_heads)

    def full_back(grad_state, inputs):
        (
            c_q,
            c_keys,
            c_values,
            c_rates,
            c_scaled,
            c_inverse,
            c_w,
            c_base,
            c_keep,
            c_tail,
            c_whole,
            c_strict,
            c_incl,
            c_dout,
            c_state,
        ) = inputs
        pseudo = c_base - c_keep * dotf(c_w, c_state)
        scores = jnp.einsum("hid,hjd->hij", c_q, c_keys, precision=HIGH) * c_incl
        d_pseudo = jnp.einsum("hij,hid->hjd", scores, c_dout, precision=HIGH) + c_tail * dotf(
            c_keys, grad_state
        )
        d_res = jnp.einsum("hij,hid->hjd", c_inverse, d_pseudo, precision=HIGH)
        prior = (
            jnp.einsum("hcd,hce->hde", c_q * c_keep, c_dout, precision=HIGH) + c_whole * grad_state
        )
        prior = prior - jnp.einsum("hcd,hce->hde", c_scaled * c_keep, d_res, precision=HIGH)
        d_scores = jnp.einsum("hid,hjd->hij", c_dout, pseudo, precision=HIGH) * c_incl
        d_query = c_keep * dotf(c_dout, swap_last(c_state)) + dotf(d_scores, c_keys)
        d_keys = jnp.einsum("hij,hid->hjd", d_scores, c_q, precision=HIGH) + c_tail * dotf(
            pseudo, swap_last(grad_state)
        )
        d_lower = -jnp.einsum("hid,hjd->hij", d_res, pseudo, precision=HIGH) * c_strict
        d_scaled = -c_keep * dotf(d_res, swap_last(c_state)) + dotf(d_lower, c_keys)
        d_keys = (
            d_keys
            + jnp.einsum("hij,hid->hjd", d_lower, c_scaled, precision=HIGH)
            + c_rates[..., None] * d_scaled
        )
        d_values = c_rates[..., None] * d_res
        d_rates = jnp.sum(d_res * c_values, -1) + jnp.sum(d_scaled * c_keys, -1)
        return (prior, (d_query * scale, d_keys, d_values, d_rates))

    first_grad, (d_q_groups, d_k_groups, d_v_groups, d_rate_groups) = lax.scan(
        full_back,
        grad_state_out,
        (
            scaled_q,
            keys,
            values,
            rates,
            scaled,
            inverse,
            w_mat,
            base,
            keep,
            tail,
            whole,
            strict,
            incl,
            d_out_groups,
            block_states,
        ),
        reverse=True,
    )

    def from_groups(arr):
        return arr.transpose(0, 2, 1, 3).reshape(seq_len, H, DK)

    d_q_unit = from_groups(d_q_groups)
    d_k_unit = from_groups(d_k_groups)
    d_q_raw = q_inv * (d_q_unit - q_unit * jnp.sum(d_q_unit * q_unit, -1, keepdims=True))
    d_k_raw = k_inv * (d_k_unit - k_unit * jnp.sum(d_k_unit * k_unit, -1, keepdims=True))
    d_act = jnp.concatenate(
        [
            d_q_raw.reshape(seq_len, width),
            d_k_raw.reshape(seq_len, width),
            from_groups(d_v_groups).reshape(seq_len, width),
        ],
        1,
    )
    d_pre = silu_back(d_act, pre)
    d_extended = jnp.zeros((seq_len + rim, d_pre.shape[1]), jnp.float32)
    conv_grads = []
    for tap in range(rim + 1):
        masked = d_pre * matches[tap]
        d_extended = d_extended + jnp.pad(conv_f[tap] * masked, ((rim - tap, tap), (0, 0)))
        conv_grads.append(jnp.sum(masked * extended[rim - tap : rim - tap + seq_len], 0))
    grad_conv = jnp.stack(conv_grads)
    rim_back = shifted(d_extended[:rim].astype(jnp.bfloat16), "seq", -1).astype(jnp.float32)
    d_proj = (d_extended[rim:] + jnp.pad(rim_back, ((seq_len - rim, 0), (0, 0)))).astype(
        jnp.bfloat16
    )
    d_rates_tok = d_rate_groups.transpose(0, 2, 1).reshape(seq_len, H)
    d_logits = (d_rates_tok * rates_tok * (1.0 - rates_tok)).astype(jnp.bfloat16)
    grad_qkv = tok_dot(first_activation, d_proj)
    grad_beta = tok_dot(first_activation, d_logits)
    first_activation_gradient = back_dot(d_proj, w_qkv) + back_dot(d_logits, w_beta)
    first_gain_gradient = jnp.sum(first_activation_gradient * normalized_input, 0)
    block_input_gradient = (
        residual_gradient
        + root_mean_square_backward(
            first_activation_gradient * float_gains[0], normalized_input, first_inverse_norm
        )
    ).astype(jnp.bfloat16)
    grad_gains = jnp.stack([first_gain_gradient, grad_gain_two])
    red_qkv, red_beta, red_conv, red_gains, red_head, red_out, red_gu, red_down = (
        lax.psum_scatter(
            grad_qkv.astype(jnp.bfloat16), "seq", scatter_dimension=0, tiled=True
        ).astype(jnp.float32),
        lax.psum_scatter(
            grad_beta.astype(jnp.bfloat16), "seq", scatter_dimension=0, tiled=True
        ).astype(jnp.float32),
        lax.psum_scatter(
            grad_conv.astype(jnp.bfloat16), "seq", scatter_dimension=1, tiled=True
        ).astype(jnp.float32),
        lax.psum_scatter(
            grad_gains.astype(jnp.bfloat16), "seq", scatter_dimension=1, tiled=True
        ).astype(jnp.float32),
        lax.psum_scatter(
            grad_head.astype(jnp.bfloat16), "seq", scatter_dimension=0, tiled=True
        ).astype(jnp.float32),
        lax.psum_scatter(
            grad_out.astype(jnp.bfloat16), "seq", scatter_dimension=0, tiled=True
        ).astype(jnp.float32),
        lax.psum_scatter(
            grad_gate_up.astype(jnp.bfloat16), "seq", scatter_dimension=0, tiled=True
        ).astype(jnp.float32),
        lax.psum_scatter(
            grad_down.astype(jnp.bfloat16), "seq", scatter_dimension=0, tiled=True
        ).astype(jnp.float32),
    )
    red_qkv, red_beta, red_conv, red_gains, red_head, red_out, red_gu, red_down = (
        lax.psum(red_qkv.astype(jnp.bfloat16), "row").astype(jnp.float32),
        lax.psum(red_beta.astype(jnp.bfloat16), "row").astype(jnp.float32),
        lax.psum(red_conv.astype(jnp.bfloat16), "row").astype(jnp.float32),
        lax.psum(red_gains.astype(jnp.bfloat16), "row").astype(jnp.float32),
        lax.psum(red_head.astype(jnp.bfloat16), "row").astype(jnp.float32),
        lax.psum(red_out.astype(jnp.bfloat16), "row").astype(jnp.float32),
        lax.psum(red_gu.astype(jnp.bfloat16), "row").astype(jnp.float32),
        lax.psum(red_down.astype(jnp.bfloat16), "row").astype(jnp.float32),
    )
    return (
        mixed[None],
        block_input_gradient[None],
        red_qkv,
        red_beta,
        red_conv,
        red_gains,
        red_head,
        red_out,
        red_gu,
        red_down,
    )


BF = jnp.bfloat16
F32 = jnp.float32
RIM = 8
NN = (((1,), (0,)), ((), ()))
NT = (((1,), (1,)), ((), ()))
TN = (((0,), (0,)), ((), ()))


def dot_low(a, b, dims=NN):
    return lax.dot_general(a, b, dims, preferred_element_type=F32)


def parts_of(a):
    if a.dtype == BF:
        return (a,)
    high = a.astype(BF)
    return high, (a - high.astype(F32)).astype(BF)


def mm(a, b, dims=NN):
    a_parts, b_parts = parts_of(a), parts_of(b)
    total = dot_low(a_parts[0], b_parts[0], dims)
    if len(b_parts) > 1:
        total = total + dot_low(a_parts[0], b_parts[1], dims)
    if len(a_parts) > 1:
        total = total + dot_low(a_parts[1], b_parts[0], dims)
    return total


def mm1(a, b, dims=NN):
    return dot_low(a.astype(BF), b.astype(BF), dims)


def begin_of(pos, starts_ref):
    begin = jnp.zeros_like(pos)
    for i in range(starts_ref.shape[0]):
        begin = jnp.maximum(begin, jnp.where(pos >= starts_ref[i], starts_ref[i], 0))
    return begin


def begin_at(pos, starts_ref):
    begin = jnp.int32(0)
    for i in range(starts_ref.shape[0]):
        begin = jnp.maximum(begin, jnp.where(starts_ref[i] <= pos, starts_ref[i], 0))
    return begin


def chunk_marks(n, size, starts_ref):
    first = n * size
    col = begin_of(first + lax.broadcasted_iota(jnp.int32, (size, 1), 0), starts_ref)
    last = begin_at(first + size - 1, starts_ref)
    keep = (col < first).astype(F32)
    tail = (col == last).astype(F32)
    whole = (last < first).astype(F32)
    return col, keep, tail, whole


def chunk_masks(n, size, col, starts_ref):
    across = begin_of(n * size + lax.broadcasted_iota(jnp.int32, (1, size), 1), starts_ref)
    here = lax.broadcasted_iota(jnp.int32, (size, size), 0)
    there = lax.broadcasted_iota(jnp.int32, (size, size), 1)
    same = col == across
    return here, there, same & (here > there), same & (here >= there)


def conv_chunk(n, size, pad, conv, col):
    depth = n * size + lax.broadcasted_iota(jnp.int32, (size, 1), 0) - col
    pre = conv[0:1, :] * pad[pl.ds(RIM + n * size, size), :]
    for tap in range(1, conv.shape[0]):
        match = (depth >= tap).astype(F32)
        pre = pre + conv[tap : tap + 1, :] * pad[pl.ds(RIM - tap + n * size, size), :] * match
    return pre


def front_kernel(taps, place_ref, starts_ref, *refs):
    n_seq = refs[-1].shape[0]
    n_row = n_seq // 2
    x_refs = refs[:n_seq]
    got_ref, got_y_ref, got_cores_ref = refs[n_seq : n_seq + 3]
    got_refs = (got_ref, got_cores_ref.at[0], got_y_ref, got_cores_ref.at[1])
    (
        weight_ref,
        act1_ref,
        proj_ref,
        rates_ref,
        o_ref,
        act2_ref,
        inv_ref,
        w_ref,
        att_ref,
        p_ref,
        u_ref,
        s_ref,
        conv_ref,
        gains_ref,
        beta_ref,
        head_ref,
        pad,
        lower,
        tmp,
        q_scr,
        k_scr,
        v_scr,
        add,
    ) = refs[n_seq + 3 :]
    place, row = place_ref[0], place_ref[1]
    size = s_ref.shape[1]
    part_rows = size // n_row
    dk = o_ref.shape[1]
    half = n_seq // 2
    z, side = place // 2, lax.rem(place, 2)
    base = 3 * part_rows
    gains = jnp.concatenate([got_ref[s, base + 4 : base + 6, :] for s in range(n_seq)], 1).astype(F32)
    gains_ref[...] = jnp.zeros_like(gains_ref)
    gains_ref[0:2, :] = gains
    beta = jnp.concatenate([got_ref[s, base + 8 : base + 16, :] for s in range(n_seq)], 1)
    beta_ref[...] = beta
    head_gain = got_ref[0, base + 6 : base + 7, :].astype(F32)
    for s in range(1, n_seq):
        head_gain = head_gain + got_ref[s, base + 6 : base + 7, :].astype(F32)
    head_ref[...] = jnp.broadcast_to(head_gain, head_ref.shape)
    conv_parts = []
    for part in range(3):
        block = part * n_seq + place
        shard = block // 3
        offset = pl.multiple_of(base + (block - shard * 3) * 16, 16)
        conv_parts.append(got_ref[shard, pl.ds(offset, 16), :][0:8])
    conv = jnp.concatenate(conv_parts, 1).astype(F32)
    conv_ref[...] = conv
    conv = conv[0:taps]
    for m, ref in enumerate(got_refs):
        for s in range(n_seq):
            at = pl.multiple_of(s * size + (row ^ m) * part_rows, part_rows)
            for kind in range(3):
                block = ref[s, kind * part_rows : (kind + 1) * part_rows, :]
                weight_ref[pl.ds(at, part_rows), kind * dk : (kind + 1) * dk] = block
    weight = weight_ref[...]
    lanes = lax.broadcasted_iota(jnp.int32, (size, 8), 1)
    pad[0:RIM, :] = jnp.zeros((RIM, 3 * dk), F32)
    for k in range(half):
        for j in range(2):
            chunk = lax.rem(z - k + half, half) * 2 + (side if j == 0 else 1 - side)
            at = pl.multiple_of(chunk * size, size)
            rows = x_refs[2 * k + j][0:size, :].astype(F32)
            inv = lax.rsqrt(jnp.mean(rows * rows, -1, keepdims=True) + EPS_NORM)
            act = ((rows * inv) * gains[0:1]).astype(BF)
            act1_ref[pl.ds(at, size), :] = act
            proj = dot_low(act, weight).astype(BF)
            proj_ref[pl.ds(at, size), :] = proj
            pad[pl.ds(pl.multiple_of(RIM + at, 8), size), :] = proj.astype(F32)
            logits = dot_low(act, beta, NT)
            rate = jax.nn.sigmoid(jnp.sum(jnp.where(lanes == place, logits, 0.0), 1, keepdims=True))
            rates_ref[pl.ds(at, size), :] = jnp.broadcast_to(rate, (size, dk))
    marks = []
    for n in range(n_seq):
        at = n * size
        col, keep, tail, whole = chunk_marks(n, size, starts_ref)
        marks.append((keep, tail, whole))
        pre = conv_chunk(n, size, pad, conv, col)
        act = pre * jax.nn.sigmoid(pre)
        q_raw, k_raw, v_raw = act[:, :dk], act[:, dk : 2 * dk], act[:, 2 * dk :]
        q = (q_raw * lax.rsqrt(jnp.sum(q_raw * q_raw, -1, keepdims=True) + EPS_UNIT)).astype(BF)
        key = (k_raw * lax.rsqrt(jnp.sum(k_raw * k_raw, -1, keepdims=True) + EPS_UNIT)).astype(BF)
        q_scr[pl.ds(at, size), :] = q
        k_scr[pl.ds(at, size), :] = key
        v_scr[pl.ds(at, size), :] = v_raw.astype(BF)
        here, there, strict, incl = chunk_masks(n, size, col, starts_ref)
        rate = rates_ref[pl.ds(at, size), :]
        low = jnp.where(strict, dot_low(key, key, NT) * rate, 0.0)
        att_ref[n] = jnp.where(incl, dot_low(q, key, NT) * (dk**-0.5), 0.0)
        lower[n] = low
        eye = (here == there).astype(F32)
        inv_ref[n] = eye - jnp.where((here // 2) == (there // 2), low, 0.0)
    span = 2
    while span < size:
        here = lax.broadcasted_iota(jnp.int32, (size, size), 0)
        there = lax.broadcasted_iota(jnp.int32, (size, size), 1)
        cross = ((here // (2 * span)) == (there // (2 * span))) & ((here // span) != (there // span))
        for n in range(n_seq):
            tmp[n] = mm(inv_ref[n], jnp.where(cross, lower[n], 0.0))
        for n in range(n_seq):
            inv_ref[n] = inv_ref[n] - mm(tmp[n], inv_ref[n])
        span *= 2
    for n in range(n_seq):
        keep, tail, whole = marks[n]
        rows = pl.ds(n * size, size)
        rate = rates_ref[rows, :]
        key = k_scr[rows, :]
        inv = inv_ref[n]
        w = mm(inv, rate * key.astype(F32))
        base = mm(inv, rate * v_scr[rows, :].astype(F32))
        w_ref[n] = w
        u_ref[n] = base
        p_ref[n] = mm(key, (tail * keep) * w, TN)
        add[n] = mm(key, tail * base, TN)
    state = jnp.zeros((dk, dk), F32)
    for n in range(n_seq):
        s_ref[n] = state
        if n + 1 < n_seq:
            state = marks[n][2] * state - mm(p_ref[n], state) + add[n]
    for n in range(n_seq):
        keep, tail, whole = marks[n]
        rows = pl.ds(n * size, size)
        state = s_ref[n]
        u = u_ref[n] - keep * mm(w_ref[n], state)
        u_ref[n] = u
        out = (keep * (dk**-0.5)) * mm(q_scr[rows, :], state) + mm(att_ref[n], u)
        o_ref[rows, :] = out
        inv = lax.rsqrt(jnp.mean(out * out, -1, keepdims=True) + EPS_HEAD)
        act2_ref[n] = ((out * inv) * head_gain).astype(BF)


def back_kernel(taps, place_ref, starts_ref, *refs):
    (
        dact_ref,
        o_ref,
        head_ref,
        conv_ref,
        proj_ref,
        rates_ref,
        inv_ref,
        w_ref,
        att_ref,
        p_ref,
        u_ref,
        s_ref,
        weight_ref,
        beta_ref,
        dproj_ref,
        *part_refs,
        dlog_ref,
        gconv_ref,
        ghead_ref,
        part_ref,
        pad,
        pre_scr,
        dpre,
        do_scr,
        g_scr,
        add,
        x_scr,
        q_scr,
        k_scr,
    ) = refs
    n_seq, size, dk = dact_ref.shape
    scale = dk**-0.5
    place = place_ref[0]
    half = n_seq // 2
    z, side = place // 2, lax.rem(place, 2)
    beta_all = beta_ref[...].astype(F32)
    beta_lane = lax.broadcasted_iota(jnp.int32, beta_all.shape, 0) == place
    beta_row = jnp.sum(jnp.where(beta_lane, beta_all, 0.0), 0, keepdims=True)
    head_gain = head_ref[0:1, :]
    conv = conv_ref[0:taps, :]
    total = n_seq * size
    pad[0:RIM, :] = jnp.zeros((RIM, 3 * dk), F32)
    pad[pl.ds(RIM, total), :] = proj_ref[...].astype(F32)
    dpre[pl.ds(total, RIM), :] = jnp.zeros((RIM, 3 * dk), F32)
    marks = []
    ghead = jnp.zeros((1, dk), F32)
    for n in range(n_seq):
        rows = pl.ds(n * size, size)
        col, keep, tail, whole = chunk_marks(n, size, starts_ref)
        marks.append((col, keep, tail, whole))
        pre = conv_chunk(n, size, pad, conv, col)
        pre_scr[rows, :] = pre
        act = pre * jax.nn.sigmoid(pre)
        q_raw, k_raw = act[:, :dk], act[:, dk : 2 * dk]
        q = (q_raw * lax.rsqrt(jnp.sum(q_raw * q_raw, -1, keepdims=True) + EPS_UNIT)).astype(BF)
        key = (k_raw * lax.rsqrt(jnp.sum(k_raw * k_raw, -1, keepdims=True) + EPS_UNIT)).astype(BF)
        q_scr[rows, :] = q
        k_scr[rows, :] = key
        out = o_ref[rows, :]
        inv = lax.rsqrt(jnp.mean(out * out, -1, keepdims=True) + EPS_HEAD)
        ohat = out * inv
        d_act2 = dact_ref[n].astype(F32)
        ghead = ghead + jnp.sum(d_act2 * ohat, 0, keepdims=True)
        lean = d_act2 * head_gain
        d_out = inv * (lean - ohat * jnp.mean(lean * ohat, -1, keepdims=True))
        do_scr[rows, :] = d_out
        g_scr[rows, :] = mm(att_ref[n], d_out, TN)
    ghead_ref[...] = jnp.broadcast_to(ghead, ghead_ref.shape)
    for n in range(n_seq):
        rows = pl.ds(n * size, size)
        col, keep, tail, whole = marks[n]
        add[n] = mm(q_scr[rows, :], (scale * keep) * do_scr[rows, :], TN) - mm(w_ref[n], keep * g_scr[rows, :], TN)
    grad = jnp.zeros((dk, dk), F32)
    for n in range(n_seq - 1, -1, -1):
        x_scr[n] = grad
        if n > 0:
            grad = marks[n][3] * grad - mm(p_ref[n], grad, TN) + add[n]
    gconv = [jnp.zeros((1, 3 * dk), F32) for _ in range(taps)]
    for n in range(n_seq - 1, -1, -1):
        rows = pl.ds(n * size, size)
        col, keep, tail, whole = marks[n]
        here, there, strict, incl = chunk_masks(n, size, col, starts_ref)
        rate = rates_ref[rows, :]
        key, q = k_scr[rows, :], q_scr[rows, :]
        key_f, q_f = key.astype(F32), q.astype(F32)
        pre = pre_scr[rows, :]
        sig = jax.nn.sigmoid(pre)
        act = pre * sig
        value = act[:, 2 * dk :].astype(BF).astype(F32)
        grad, state, u = x_scr[n], s_ref[n], u_ref[n]
        d_out = do_scr[rows, :]
        d_u = g_scr[rows, :] + tail * mm(key, grad)
        d_r = mm(inv_ref[n], d_u, TN)
        d_att = jnp.where(incl, mm(d_out, u, NT), 0.0)
        d_low = jnp.where(strict, -mm(d_r, u, NT), 0.0)
        d_q = keep * mm(d_out, state, NT) + mm(d_att, key)
        d_kb = mm(d_low, key) - keep * mm(d_r, state, NT)
        d_k = (
            scale * mm(d_att, q, TN)
            + mm(d_low, rate * key_f, TN)
            + tail * mm(u, grad, NT)
            + rate * d_kb
        )
        d_v = rate * d_r
        d_rate = jnp.sum(d_r * value + d_kb * key_f, -1, keepdims=True)
        d_q = d_q * scale
        q_raw, k_raw = act[:, :dk], act[:, dk : 2 * dk]
        q_inv = lax.rsqrt(jnp.sum(q_raw * q_raw, -1, keepdims=True) + EPS_UNIT)
        k_inv = lax.rsqrt(jnp.sum(k_raw * k_raw, -1, keepdims=True) + EPS_UNIT)
        q_unit, k_unit = q_raw * q_inv, k_raw * k_inv
        d_q = q_inv * (d_q - q_unit * jnp.sum(d_q * q_unit, -1, keepdims=True))
        d_k = k_inv * (d_k - k_unit * jnp.sum(d_k * k_unit, -1, keepdims=True))
        d_act = jnp.concatenate([d_q, d_k, d_v], 1)
        d_pre = d_act * sig * (1.0 + pre * (1.0 - sig))
        dpre[rows, :] = d_pre
        pos = n * size + lax.broadcasted_iota(jnp.int32, (size, 1), 0)
        d_proj = conv[0:1, :] * d_pre
        gconv[0] = gconv[0] + jnp.sum(d_pre * pad[pl.ds(RIM + n * size, size), :], 0, keepdims=True)
        for tap in range(1, taps):
            later = pos + tap
            match = ((begin_of(later, starts_ref) <= pos) & (later < total)).astype(F32)
            d_proj = d_proj + conv[tap : tap + 1, :] * dpre[pl.ds(n * size + tap, size), :] * match
            reach = (pos - col >= tap).astype(F32)
            gconv[tap] = gconv[tap] + jnp.sum(
                d_pre * reach * pad[pl.ds(RIM - tap + n * size, size), :], 0, keepdims=True
            )
        d_proj = d_proj.astype(BF)
        dproj_ref[rows, :] = d_proj
        one_rate = rate[:, 0:1]
        d_logit = (d_rate * one_rate * (1.0 - one_rate)).astype(BF).astype(F32)
        d_act1 = dot_low(d_proj, weight_ref[...], NT) + d_logit * beta_row
        slot = lax.rem(n // 2 - z + half, half) * 2 + ((n % 2) ^ side)
        part_ref[slot] = d_act1.astype(BF)
        dlog_ref[pl.ds(n, 1), :] = jnp.broadcast_to(d_logit, (size, dk)).T[0:1]
    for slot in range(n_seq):
        part_refs[slot][...] = part_ref[slot]
    gconv_ref[...] = jnp.zeros_like(gconv_ref)
    for tap in range(taps):
        gconv_ref[tap : tap + 1, :] = gconv[tap]


def lead_kernel(place_ref, qkv_ref, conv_ref, gains_ref, head_ref, beta_ref, out_ref, rows):
    place, row = place_ref[0], place_ref[1]
    heads, dk = out_ref.shape[0], out_ref.shape[2]
    part = dk // 4
    from_row = pl.ds(pl.multiple_of(row * part, part), part)
    per = head_ref.shape[1]
    down = lax.broadcasted_iota(jnp.int32, (dk, dk), 0)
    along = lax.broadcasted_iota(jnp.int32, (dk, dk), 1)
    spot = (along == down + place * per)[0:per].astype(BF)
    rows[...] = jnp.zeros_like(rows)
    taps = conv_ref.shape[0]
    for kind in range(3):
        rows[kind * 16 : kind * 16 + taps, :] = conv_ref[:, kind * dk : (kind + 1) * dk].astype(F32)
    rows[4:6, :] = gains_ref[...].astype(F32)
    rows[6:7, :] = dot_low(jnp.broadcast_to(head_ref[...], (16, per)), spot)[0:1]
    rows[8:16, :] = beta_ref[...].astype(F32)
    small = rows[...].astype(BF)
    for h in range(heads):
        for kind in range(3):
            block = qkv_ref[from_row, pl.ds((kind * heads + h) * dk, dk)]
            out_ref[h, kind * part : (kind + 1) * part, :] = block
        out_ref[h, 3 * part : 3 * part + 48, :] = small


def pack_kernel(place_ref, own_ref, other_ref, down_ref, out_ref):
    side = lax.rem(place_ref[0], 2)
    size, lanes = own_ref.shape[0], out_ref.shape[1]
    slot = 96
    for j in range(own_ref.shape[1] // lanes):
        cols = pl.ds(j * lanes, lanes)
        at = pl.multiple_of(j * 2 * size + side * size, size)
        out_ref[pl.ds(at, size), :] = own_ref[:, cols]
        at = pl.multiple_of(j * 2 * size + (1 - side) * size, size)
        out_ref[pl.ds(at, size), :] = other_ref[:, cols]
    base = 2 * size * own_ref.shape[1] // lanes
    part = down_ref.shape[0]
    for j in range(down_ref.shape[1] // lanes):
        block = down_ref[:, j * lanes : (j + 1) * lanes]
        block = jnp.concatenate([block, jnp.zeros((slot - part, lanes), BF)], 0)
        out_ref[pl.ds(base + j * slot, slot), :] = block


def mid_kernel(place_ref, act2_ref, own_ref, y_ref, cores_ref, x_ref, gains_ref, resid_ref, act3_ref, weight_ref):
    place, row = place_ref[0], place_ref[1]
    z, side = place // 2, lax.rem(place, 2)
    heads, size, dk = act2_ref.shape
    part = dk // 4
    for m in range(4):
        ref = (own_ref, cores_ref.at[0], y_ref, cores_ref.at[1])[m]
        for s in range(heads):
            shard = lax.rem(z - s // 2 + 4, 4) * 2 + (side ^ (s % 2))
            at = pl.multiple_of((shard * 4 + (row ^ m)) * part, part)
            weight_ref[pl.ds(at, part), :] = ref[s]
    act2 = jnp.concatenate([act2_ref[h] for h in range(heads)], 1)
    resid = x_ref[...].astype(F32) + dot_low(act2, weight_ref[...])
    resid_ref[...] = resid
    inv = lax.rsqrt(jnp.mean(resid * resid, -1, keepdims=True) + EPS_NORM)
    act3_ref[...] = ((resid * inv) * gains_ref[1:2, :]).astype(BF)


GROUP_BITS = (0, 2, 4, 6, 1, 3, 5, 7)


def store_part(bits, block, own_ref, next_ref):
    @pl.when((bits & 1) == 0)
    def _():
        own_ref[bits >> 1] = block

    @pl.when((bits & 1) == 1)
    def _():
        next_ref[bits >> 1] = block


def mixed_kernel(place_ref, act4_ref, down_ref, own_ref, next_ref):
    me = lax.rem(place_ref[0], 2) * 4 + place_ref[1]
    size = own_ref.shape[1]
    for i in range(4):
        parts = dot_low(act4_ref[pl.ds(i * 2 * size, 2 * size), :], down_ref[...]).astype(BF)
        for half in range(2):
            store_part(me ^ (2 * i + half), parts[half * size : (half + 1) * size], own_ref, next_ref)


def feed_kernel(hidden, place_ref, *refs):
    act3_refs, core_ref, cot_refs, cot_core_ref, packs_ref = refs[0:4], refs[4], refs[5:9], refs[9], refs[10]
    own_ref, next_ref, act4_ref, dgu_ref, act3_ref, cot_ref, down_ref, gu, down32 = refs[11:]
    place, row = place_ref[0], place_ref[1]
    me = lax.rem(place, 2) * 4 + row
    size, width = act3_refs[0].shape
    wide = act4_ref.shape[1]
    lanes = packs_ref.shape[2]
    slot, part = 96, hidden // 4
    gu_rows = gu.shape[0] // 4
    n_cols = gu.shape[1] // lanes
    down32[hidden:wide, :] = jnp.zeros((wide - hidden, width), F32)

    for src in range(4):
        rows = pl.ds(src * gu_rows, gu_rows)
        for j in range(n_cols):
            gu[rows, j * lanes : (j + 1) * lanes] = packs_ref[src, j * gu_rows : (j + 1) * gu_rows, :]
        for j in range(width // lanes):
            block = packs_ref[src, pl.ds(n_cols * gu_rows + j * slot, slot), :].astype(F32)
            down32[src * part : (src + 1) * part, j * lanes : (j + 1) * lanes] = block[0:part]
    down_ref[...] = down32[...].astype(BF)
    for i, bits in enumerate(GROUP_BITS):
        at = pl.multiple_of((me ^ bits) * size, size)
        act3_ref[pl.ds(at, size), :] = act3_refs[i][...] if i < 4 else core_ref[i - 4]
        cot_ref[pl.ds(at, size), :] = cot_refs[i][...] if i < 4 else cot_core_ref[i - 4]
    for i in range(4):
        rows = pl.ds(i * 2 * size, 2 * size)
        act3 = act3_ref[rows, :]
        cot = cot_ref[rows, :]
        gate_up = dot_low(act3, gu[...])
        gate, up = gate_up[:, :wide], gate_up[:, wide:]
        sig = jax.nn.sigmoid(gate)
        silu = gate * sig
        act4_ref[rows, :] = (silu * up).astype(BF)
        d_act4 = dot_low(cot, down_ref[...], NT)
        d_gate = d_act4 * up * sig * (1.0 + gate * (1.0 - sig))
        d_gu = jnp.concatenate([d_gate, d_act4 * silu], 1).astype(BF)
        dgu_ref[rows, :] = d_gu
        parts = dot_low(d_gu, gu[...], NT).astype(BF)
        for half in range(2):
            store_part(me ^ (2 * i + half), parts[half * size : (half + 1) * size], own_ref, next_ref)


def grads_kernel(hidden, act3_ref, cot_ref, act4_ref, dgu_ref, out_ref, down32):
    lanes = out_ref.shape[2]
    slot, part = 96, hidden // 4
    gu_rows = act3_ref.shape[1] // 4
    n_cols = dgu_ref.shape[1] // lanes
    down32[...] = dot_low(act4_ref[...], cot_ref[...], TN)
    for k in range(4):
        at = k * gu_rows
        grad = dot_low(act3_ref[:, at : at + gu_rows], dgu_ref[...], TN).astype(BF)
        for j in range(n_cols):
            out_ref[k, j * gu_rows : (j + 1) * gu_rows, :] = grad[:, j * lanes : (j + 1) * lanes]
        rows = pl.ds(k * part, part)
        for j in range(cot_ref.shape[1] // lanes):
            block = down32[rows, j * lanes : (j + 1) * lanes]
            block = jnp.concatenate([block, jnp.zeros((slot - part, lanes), F32)], 0)
            out_ref[k, pl.ds(n_cols * gu_rows + j * slot, slot), :] = block.astype(BF)


def out_grad_kernel(place_ref, act2_ref, low_ref, same_ref, other_ref, full):
    row = place_ref[1]
    heads, _, dk = act2_ref.shape
    part = dk // 4
    for h in range(heads):
        full[h * dk : (h + 1) * dk, :] = dot_low(act2_ref[h], low_ref[...], TN)
    for m in range(4):
        ref = same_ref if m % 2 == 0 else other_ref
        for h in range(heads):
            at = pl.multiple_of(h * dk + (row ^ m) * part, part)
            ref[m // 2, h] = full[pl.ds(at, part), :].astype(BF)


def qkv_grad_kernel(place_ref, act1_ref, dproj_ref, dlog_ref, gconv_ref, ghead_ref, same_ref, other_ref, full, rows):
    row = place_ref[1]
    shards, total, cols = same_ref.shape[1:]
    dk = cols // 3
    part = total - 16
    for h in range(shards):
        lanes = pl.ds(h * dk, dk)
        full[h * dk : (h + 1) * dk, :] = dot_low(act1_ref[:, lanes], dproj_ref[...], TN)
    g_beta = None
    dlog = dlog_ref[...].astype(BF)
    for n in range(dlog.shape[0]):
        one = jnp.broadcast_to(dlog[n : n + 1], (16, dk))
        term = dot_low(one, act1_ref[n * dk : (n + 1) * dk, :])[0:1]
        g_beta = term if g_beta is None else g_beta + term
    rows[...] = jnp.zeros_like(rows)
    for s in range(shards):
        rows[s, 0:4, :] = gconv_ref[0:4, :]
        rows[s, 4:5, 0:dk] = g_beta[:, s * dk : (s + 1) * dk]
        rows[s, 4:5, dk : 2 * dk] = ghead_ref[0:1, :]
    for m in range(4):
        ref = same_ref if m % 2 == 0 else other_ref
        for s in range(shards):
            at = pl.multiple_of(s * dk + (row ^ m) * part, part)
            ref[m // 2, s, 0:part, :] = full[pl.ds(at, part), :].astype(BF)
            ref[m // 2, s, pl.ds(part, 16), :] = rows[s].astype(BF)


def turn_kernel(heads, own_ref, core_ref, x_ref, y_ref, resid_ref, cot_ref, gains_ref, weight_ref, dresid_ref, low_ref, dact2_ref):
    resid = resid_ref[...]
    inv = lax.rsqrt(jnp.mean(resid * resid, -1, keepdims=True) + EPS_NORM)
    rhat = resid * inv
    d_act3 = own_ref[0].astype(F32) + core_ref[0].astype(F32) + x_ref[...].astype(F32) + y_ref[...].astype(F32)
    lean = d_act3 * gains_ref[1:2, :]
    d_resid = cot_ref[...].astype(F32) + inv * (lean - rhat * jnp.mean(lean * rhat, -1, keepdims=True))
    dresid_ref[...] = d_resid
    low = d_resid.astype(BF)
    low_ref[...] = low
    d_act2 = dot_low(low, weight_ref[...], NT).astype(BF)
    dk = d_act2.shape[1] // heads
    for h in range(heads):
        dact2_ref[h] = d_act2[:, h * dk : (h + 1) * dk]


def last_kernel(own_ref, near_ref, far1_ref, far2_ref, far3_ref, x_ref, gains_ref, dresid_ref, out_ref):
    d_act1 = own_ref[...].astype(F32) + near_ref[...].astype(F32)
    for ref in (far1_ref, far2_ref, far3_ref):
        d_act1 = d_act1 + ref[...].astype(F32)
    rows = x_ref[...].astype(F32)
    inv = lax.rsqrt(jnp.mean(rows * rows, -1, keepdims=True) + EPS_NORM)
    xhat = rows * inv
    lean = d_act1 * gains_ref[0:1, :]
    out = dresid_ref[...] + inv * (lean - xhat * jnp.mean(lean * xhat, -1, keepdims=True))
    out_ref[...] = out.astype(BF)


def row_sums(v):
    total = jnp.sum(v, 1, keepdims=True)
    return jnp.broadcast_to(total, (v.shape[0], 128)).T[0:1]


def lay_feed_kernel(place_ref, *refs):
    own_ref, y_ref, cores_ref = refs[0:3]
    packs = (own_ref, cores_ref.at[0], y_ref, cores_ref.at[1])
    weight_ref, gain_ref, gu_out, down_out, gain_out, held = refs[3:]
    side, row = lax.rem(place_ref[0], 2), place_ref[1]
    size, hidden = gain_out.shape[1], down_out.shape[0]
    lanes, slot, part = packs[0].shape[1], 96, hidden // 4
    wide = held.shape[3] // 2
    n_cols = held.shape[3] // lanes
    for m in range(4):
        for own in range(2):
            block = side if own == 0 else 1 - side
            for j in range(n_cols):
                rows = pl.ds((own * n_cols + j) * size, size)
                held[row ^ m, block, :, j * lanes : (j + 1) * lanes] = packs[m][rows, :]
        at = pl.multiple_of((row ^ m) * part, 8)
        for j in range(down_out.shape[1] // lanes):
            block = packs[m][pl.ds(2 * n_cols * size + j * slot, slot), :].astype(F32)
            down_out[pl.ds(at, part), j * lanes : (j + 1) * lanes] = block[0:part]
    total = None
    for kind in range(2):
        for block in range(8):
            piece = held[block % 4, block // 4, :, kind * wide : kind * wide + hidden].astype(F32)
            cols = pl.ds((kind * 8 + block) * hidden, hidden)
            gu_out[:, cols] = piece
            term = piece * weight_ref[:, cols].astype(F32)
            total = term if total is None else total + term
    gain_out[...] = row_sums(total) / gain_ref[1:2, :].astype(F32)


def lay_mix_kernel(place_ref, *refs):
    qkv_refs = (refs[0], refs[2].at[0], refs[1], refs[2].at[1])
    out_refs = (refs[3], refs[5].at[0], refs[4], refs[5].at[1])
    weight_ref, beta_ref, gain_ref, second_ref, qkv_out, out_out, gain_out, conv_out, beta_out, head_out = refs[6:]
    place, row = place_ref[0], place_ref[1]
    heads, total, cols = qkv_refs[0].shape
    dk = cols // 3
    part = total - 16
    for m in range(4):
        rows = pl.ds(pl.multiple_of((row ^ m) * part, 8), part)
        out_out[rows, :] = out_refs[m][...].astype(F32)
        for h in range(heads):
            for kind in range(3):
                lanes = pl.ds((kind * heads + h) * dk, dk)
                block = qkv_refs[m][h, 0:part, kind * dk : (kind + 1) * dk]
                qkv_out[rows, lanes] = block.astype(F32)
    sums = jnp.sum(qkv_out[...] * weight_ref[...].astype(F32), 1, keepdims=True)
    ref = qkv_refs[0]
    small = [ref[h, pl.ds(part, 16), :].astype(F32) for h in range(heads)]
    beta_rows = jnp.concatenate([v[4:5, 0:dk] for v in small], 0)
    beta_out[...] = beta_rows
    head = small[0][4:5, dk : 2 * dk]
    for v in small[1:]:
        head = head + v[4:5, dk : 2 * dk]
    head_out[...] = head
    for i in range(3):
        block = place * 3 + i
        kind = block // heads
        source = block - kind * heads
        lanes = pl.ds(pl.multiple_of(kind * dk, dk), dk)
        conv_out[:, i * dk : (i + 1) * dk] = ref[source, pl.ds(part, 16), lanes].astype(F32)[0 : conv_out.shape[0]]
    weight_rows = beta_ref[...].astype(F32)
    gain = jnp.broadcast_to(sums, (sums.shape[0], 128)).T[0:1]
    gain = gain + jnp.sum(beta_rows * weight_rows, 0, keepdims=True)
    gain_out[0:1, :] = gain / gain_ref[0:1, :].astype(F32)
    gain_out[1:2, :] = second_ref[...]


def local_call(kernel, outs, args, scratch=(), smem=0, us=1, name=None):
    space = [pl.BlockSpec(memory_space=pltpu.SMEM)] * smem
    space += [pl.BlockSpec(memory_space=pltpu.VMEM)] * (len(args) - smem)
    return pl.pallas_call(
        kernel,
        out_shape=tuple(outs),
        in_specs=space,
        out_specs=tuple(pl.BlockSpec(memory_space=pltpu.VMEM) for _ in outs),
        scratch_shapes=list(scratch),
        compiler_params=pltpu.CompilerParams(vmem_limit_bytes=56 * 2**20),
        cost_estimate=pl.CostEstimate(flops=us * 10**9, bytes_accessed=1024, transcendentals=0),
        name=name,
    )(*args)


def head_plan(
    block_input,
    cotangent,
    doc_starts,
    qkv_weight,
    beta_weight,
    conv_weight,
    norm_gains,
    head_gain,
    out_weight,
    gate_up_weight,
    down_weight,
):
    x, cot = block_input[0], cotangent[0]
    starts = doc_starts[0]
    size, width = x.shape
    n_seq, n_row = lax.axis_size("seq"), lax.axis_size("row")
    place, row = lax.axis_index("seq"), lax.axis_index("row")
    half = n_seq // 2
    z, side = place // 2, place % 2
    total = n_seq * size
    where_at = jnp.stack([place, row])
    taps = conv_weight.shape[0]
    hidden = down_weight.shape[0]
    wide = -(-hidden // 128) * 128
    shape = jax.ShapeDtypeStruct

    def flip(v):
        return lax.ppermute(v, "seq", [(s, s ^ 1) for s in range(n_seq)])

    def roll(v, k):
        return lax.ppermute(v, "seq", [(s, (s // 2 + k) % half * 2 + s % 2) for s in range(n_seq)])

    def core(v):
        return lax.ppermute(v, "row", [(r, r ^ 1) for r in range(n_row)])

    def across(v):
        return lax.ppermute(v, "row", [(r, r ^ 2) for r in range(n_row)])

    pairs = [
        (s * n_row + r, (r * 2 + s // n_row) * n_row + s % n_row)
        for s in range(n_seq)
        for r in range(n_row)
    ]

    def spread(v):
        return lax.ppermute(v, ("seq", "row"), pairs)

    def collect(v):
        return lax.ppermute(v, ("seq", "row"), [(b, a) for a, b in pairs])

    def group_gather(v):
        y, s = across(v), flip(v)
        four = [v, y, s, flip(y)]
        return [*four, core(jnp.stack(four))]

    def group_ends(own, got):
        both = [own[i].astype(F32) + got[i].astype(F32) for i in range(4)]
        y_next = flip(both[3].astype(BF))
        x_next = flip(both[2].astype(BF))
        return x_next, across((both[1] + y_next.astype(F32)).astype(BF))

    def row_sum(same, other):
        mine = same.astype(F32) + core(other).astype(F32)
        return mine[0], mine[1].astype(BF)

    def row_relative(v):
        y = across(v)
        return [v, core(v), y, core(y)]

    def stage(*values):
        return lax.optimization_barrier(values)

    def line(v, step, t):
        ends = range(t - 1, half - 1) if step > 0 else range(1, half - t + 1)
        return lax.ppermute(
            v, "seq", [(2 * a + j, 2 * (a + step) + j) for a in ends for j in range(2)]
        )

    part_rows = size // n_row
    dk = width // n_seq
    lead_rows = 3 * part_rows + 48
    (payload,) = local_call(
        lead_kernel,
        [shape((n_seq, lead_rows, dk), BF)],
        [
            where_at,
            qkv_weight,
            conv_weight,
            norm_gains,
            head_gain.reshape(1, -1),
            beta_weight.T,
        ],
        scratch=[pltpu.VMEM((48, dk), F32)],
        smem=1,
        us=2,
        name="lead",
    )
    def columns(block):
        gate = lax.dynamic_slice_in_dim(gate_up_weight, block * hidden, hidden, 1)
        up = lax.dynamic_slice_in_dim(gate_up_weight, (n_seq + block) * hidden, hidden, 1)
        gap = jnp.zeros((size, wide - hidden), BF)
        return jnp.concatenate([gate, gap, up, gap], 1)

    hidden_part = hidden // n_row
    other_cols = flip(columns((1 - side) * n_row + row))
    down_cut = spread(lax.dynamic_slice_in_dim(down_weight, row * hidden_part, hidden_part, 0))
    pack_rows = 6 * size + 4 * 96
    got = lax.all_to_all(payload, "seq", 0, 0)
    out_part = lax.dynamic_slice_in_dim(out_weight, row * part_rows, part_rows, 0)
    x_out, got, other_cols, down_cut = stage(jnp.concatenate([x, out_part], 0), got, other_cols, down_cut)
    far = {k: roll(x_out, k) for k in (1, 3, 2)}
    pieces = [x_out, flip(x_out)]
    for k in range(1, half):
        pieces += [far[k], flip(far[k])]
    got_y = across(got)
    got_cores = core(jnp.stack([got, got_y]))
    (pack,) = local_call(
        pack_kernel,
        [shape((pack_rows, 256), BF)],
        [where_at, columns(side * n_row + row), other_cols, down_cut],
        smem=1,
        us=2,
        name="pack",
    )
    pack = stage(pack, *far.values())[0]
    groups_z = [[2 * a + j for a in range(half)] for j in range(2)]
    packs = lax.all_gather(pack, "seq", axis_index_groups=groups_z)
    staged = stage(*pieces, got, got_y, got_cores, cot)
    pieces, (got, got_y, got_cores, cot) = staged[:8], staged[8:]
    out_part = jnp.stack([v[size:] for v in pieces])
    cot_y, cot_x, out_y = across(cot), flip(cot), across(out_part)

    square = shape((n_seq, size, dk), F32)
    (
        w_head,
        act1,
        proj,
        rates,
        outs,
        act2,
        inverse,
        w_mat,
        att,
        p_mat,
        u_mat,
        states,
        conv,
        gains,
        beta,
        head,
    ) = local_call(
        functools.partial(front_kernel, taps),
        [
            shape((width, 3 * dk), BF),
            shape((total, width), BF),
            shape((total, 3 * dk), BF),
            shape((total, dk), F32),
            shape((total, dk), F32),
            shape((n_seq, size, dk), BF),
            square,
            square,
            square,
            square,
            square,
            square,
            shape((8, 3 * dk), F32),
            shape((8, width), F32),
            shape((8, width), BF),
            shape((8, dk), F32),
        ],
        [where_at, starts, *pieces, got, got_y, got_cores],
        scratch=[
            pltpu.VMEM((RIM + total, 3 * dk), F32),
            pltpu.VMEM((n_seq, size, size), F32),
            pltpu.VMEM((n_seq, size, size), F32),
            pltpu.VMEM((total, dk), BF),
            pltpu.VMEM((total, dk), BF),
            pltpu.VMEM((total, dk), BF),
            pltpu.VMEM((n_seq, dk, dk), F32),
        ],
        smem=2,
        us=14,
        name="front",
    )
    act2, cot_y, cot_x, out_y = stage(act2, cot_y, cot_x, out_y)
    act2 = lax.all_to_all(act2, "seq", 0, 0)
    out_cores = core(jnp.stack([out_part, out_y]))
    cot_four = [cot, cot_y, cot_x, flip(cot_y)]
    act2, cot_four[3], out_cores = stage(act2, cot_four[3], out_cores)
    cot_all = [*cot_four, core(jnp.stack(cot_four))]
    resid, act3, w_out = local_call(
        mid_kernel,
        [shape((size, width), F32), shape((size, width), BF), shape((width, width), BF)],
        [where_at, act2, out_part, out_y, out_cores, x, gains],
        smem=1,
        us=4,
        name="mid",
    )
    four = shape((4, size, width), BF)
    d_own, d_next, act4, d_gu, act3_all, cot_all, w_down = local_call(
        functools.partial(feed_kernel, hidden),
        [
            four,
            four,
            shape((total, wide), BF),
            shape((total, 2 * wide), BF),
            shape((total, width), BF),
            shape((total, width), BF),
            shape((wide, width), BF),
        ],
        [where_at, *group_gather(act3), *cot_all, packs],
        scratch=[pltpu.VMEM((width, 2 * wide), BF), pltpu.VMEM((wide, width), F32)],
        smem=1,
        us=13,
        name="feed",
    )
    d_got = core(d_next)
    (grads,) = local_call(
        functools.partial(grads_kernel, hidden),
        [shape((half, pack_rows, 256), BF)],
        [act3_all, cot_all, act4, d_gu],
        scratch=[pltpu.VMEM((wide, width), F32)],
        us=7,
        name="grads",
    )
    grads = lax.psum_scatter(grads, "seq", scatter_dimension=0, axis_index_groups=groups_z)
    d_x, d_y = group_ends(d_own, d_got)
    mixed_own, mixed_next = local_call(
        mixed_kernel, [four, four], [where_at, act4, w_down], smem=1, us=5, name="mixed"
    )
    d_x, d_y, mixed_own, mixed_next = stage(d_x, d_y, mixed_own, mixed_next)
    d_resid, d_low, d_act2 = local_call(
        functools.partial(turn_kernel, n_seq),
        [shape((size, width), F32), shape((size, width), BF), shape((n_seq, size, dk), BF)],
        [d_own, d_got, d_x, d_y, resid, cot, gains, w_out],
        us=5,
        name="turn",
    )
    d_act2 = lax.all_to_all(d_act2, "seq", 0, 0)
    out_shape = shape((2, n_seq, part_rows, width), BF)
    out_same, out_other = local_call(
        out_grad_kernel,
        [out_shape, out_shape],
        [where_at, act2, d_low],
        scratch=[pltpu.VMEM((width, width), F32)],
        smem=1,
        us=3,
        name="out_grad",
    )
    out_mine, out_next = row_sum(out_same, out_other)
    mixed_got = core(mixed_next)
    d_act2, out_next, out_mine, mixed_got, grads = stage(d_act2, out_next, out_mine, mixed_got, grads)
    gu_sum = grads[: 6 * size].reshape(3, 2, size, 256)
    gu_mine = lax.dynamic_index_in_dim(gu_sum, side, 1, False).reshape(3 * size, 256)
    gu_other = lax.dynamic_index_in_dim(gu_sum, 1 - side, 1, False).reshape(3 * size, 256)
    gu_other, down_sum = flip(gu_other), collect(grads[6 * size :])
    out_y = across(out_next)
    mixed_both = [mixed_own[i].astype(F32) + mixed_got[i].astype(F32) for i in range(4)]
    mixed_x = flip(jnp.stack([mixed_both[2], mixed_both[3]]).astype(BF))
    d_proj, *d_parts, d_log, g_conv, g_head = local_call(
        functools.partial(back_kernel, taps),
        [
            shape((total, 3 * dk), BF),
            *[shape((size, width), BF)] * n_seq,
            shape((n_seq, size), F32),
            shape((8, 3 * dk), F32),
            shape((8, dk), F32),
        ],
        [
            where_at,
            starts,
            d_act2,
            outs,
            head,
            conv,
            proj,
            rates,
            inverse,
            w_mat,
            att,
            p_mat,
            u_mat,
            states,
            w_head,
            beta,
        ],
        scratch=[
            pltpu.VMEM((n_seq, size, width), BF),
            pltpu.VMEM((RIM + total, 3 * dk), F32),
            pltpu.VMEM((total, 3 * dk), F32),
            pltpu.VMEM((RIM + total, 3 * dk), F32),
            pltpu.VMEM((total, dk), F32),
            pltpu.VMEM((total, dk), F32),
            pltpu.VMEM((n_seq, dk, dk), F32),
            pltpu.VMEM((n_seq, dk, dk), F32),
            pltpu.VMEM((total, dk), BF),
            pltpu.VMEM((total, dk), BF),
        ],
        smem=2,
        us=21,
        name="back",
    )
    d_proj, d_log, g_conv, g_head, out_y, mixed_x, gu_other, down_sum, *d_parts = stage(
        d_proj, d_log, g_conv, g_head, out_y, mixed_x, gu_other, down_sum, *d_parts
    )
    near_parts = {k: flip(d_parts[2 * k + 1]) for k in (2, 1, 3, 0)}
    feed_part = jnp.concatenate([gu_mine, gu_other, down_sum], 0)
    near_parts[2], d_proj, out_y, mixed_x, feed_part = stage(near_parts[2], d_proj, out_y, mixed_x, feed_part)
    out_piece = lax.all_to_all((out_mine + out_y.astype(F32)).astype(BF), "seq", 0, 0)
    cut_shape = shape((2, n_seq, part_rows + 16, 3 * dk), BF)
    qkv_same, qkv_other = local_call(
        qkv_grad_kernel,
        [cut_shape, cut_shape],
        [where_at, act1, d_proj, d_log, g_conv, g_head],
        scratch=[pltpu.VMEM((width, 3 * dk), F32), pltpu.VMEM((n_seq, 16, 3 * dk), F32)],
        smem=1,
        us=5,
        name="qkv_grad",
    )
    qkv_mine, qkv_next = row_sum(qkv_same, qkv_other)
    feed_y = across(feed_part)
    mixed_y = across((mixed_both[1] + mixed_x[1].astype(F32)).astype(BF))
    (
        near_parts[0],
        near_parts[1],
        near_parts[2],
        near_parts[3],
        qkv_mine,
        qkv_next,
        feed_part,
        feed_y,
        mixed_y,
        out_piece,
        *d_parts,
    ) = stage(
        near_parts[0],
        near_parts[1],
        near_parts[2],
        near_parts[3],
        qkv_mine,
        qkv_next,
        feed_part,
        feed_y,
        mixed_y,
        out_piece,
        *d_parts,
    )
    far_parts = {
        k: roll((d_parts[2 * k].astype(F32) + near_parts[k].astype(F32)).astype(BF), k) for k in (2, 1, 3)
    }
    qkv_y = across(qkv_next)
    qkv_piece = lax.all_to_all((qkv_mine + qkv_y.astype(F32)).astype(BF), "seq", 0, 0)
    out_piece = out_piece.astype(F32).sum(0).astype(BF)
    out_y = across(out_piece)
    feed_cores = core(jnp.stack([feed_part, feed_y]))
    mixed = (resid + mixed_both[0] + mixed_x[0].astype(F32) + mixed_y.astype(F32)).astype(BF)
    far_parts[1], far_parts[2], far_parts[3], qkv_piece, out_y, feed_cores, mixed = stage(
        far_parts[1], far_parts[2], far_parts[3], qkv_piece, out_y, feed_cores, mixed
    )
    (input_gradient,) = local_call(
        last_kernel,
        [shape((size, width), BF)],
        [d_parts[0], near_parts[0], *far_parts.values(), x, gains, d_resid],
        us=3,
        name="last",
    )
    qkv_y = across(qkv_piece)
    qkv_cores = core(jnp.stack([qkv_piece, qkv_y]))
    out_cores = core(jnp.stack([out_piece, out_y]))

    red_gu, red_down, second_gain = local_call(
        lay_feed_kernel,
        [
            shape((size, 2 * n_seq * hidden), F32),
            shape((hidden, width), F32),
            shape((1, size), F32),
        ],
        [where_at, feed_part, feed_y, feed_cores, gate_up_weight, norm_gains],
        scratch=[pltpu.VMEM((n_row, 2, size, 2 * wide), BF)],
        smem=1,
        us=5,
        name="lay_feed",
    )
    red_qkv, red_out, red_gains, red_conv, red_beta, red_head = local_call(
        lay_mix_kernel,
        [
            shape((size, 3 * width), F32),
            shape((size, width), F32),
            shape((2, size), F32),
            shape((taps, 3 * dk), F32),
            shape((n_seq, dk), F32),
            shape((1, dk), F32),
        ],
        [where_at, qkv_piece, qkv_y, qkv_cores, out_piece, out_y, out_cores, qkv_weight, beta_weight.T, norm_gains, second_gain],
        smem=1,
        us=3,
        name="lay_mix",
    )
    red_beta = red_beta.T
    per = head_gain.shape[0]
    red_head = lax.dynamic_slice_in_dim(red_head[0], place * per, per, 0)
    return (
        mixed[None],
        input_gradient[None],
        red_qkv,
        red_beta,
        red_conv,
        red_gains,
        red_head,
        red_out,
        red_gu,
        red_down,
    )


def plan(block_input, *rest):
    seq, row = lax.axis_size("seq"), lax.axis_size("row")
    if seq == H and row * 2 == H and block_input.shape[1] == DK:
        return head_plan(block_input, *rest)
    return on_device(block_input, *rest)


def solution(mesh):
    in_specs = (
        P("row", "seq", None),
        P("row", "seq", None),
        P("row", None),
        P("seq", None),
        P("seq", None),
        P(None, "seq"),
        P(None, "seq"),
        P("seq"),
        P("seq", None),
        P("seq", None),
        P("seq", None),
    )
    out_specs = (
        P("row", "seq", None),
        P("row", "seq", None),
        P("seq", None),
        P("seq", None),
        P(None, "seq"),
        P(None, "seq"),
        P("seq"),
        P("seq", None),
        P("seq", None),
        P("seq", None),
    )
    return jax.shard_map(
        plan, mesh=mesh, in_specs=in_specs, out_specs=out_specs, check_vma=False
    )
```

```python
import functools

import jax
import jax.numpy as jnp
from jax import lax
from jax.experimental import pallas as pl
from jax.experimental.pallas import tpu as pltpu
from jax.sharding import PartitionSpec as P

H = 8
DK = 128
GROUP = 64


EPS_NORM = 1e-06
EPS_HEAD = 1e-05
EPS_UNIT = 1e-06
HIGH = lax.Precision.HIGHEST


def shifted(block, axis, distance):
    devices = range(lax.axis_size(axis))
    route = [(i - distance, i) for i in devices if i - distance in devices]
    return lax.ppermute(block, axis, route)


def dotf(first_op, second_op):
    return jnp.matmul(first_op, second_op, precision=HIGH)


def swap_last(matrix):
    return jnp.swapaxes(matrix, -1, -2)


def tok_dot(first_op, second_op):
    return lax.dot_general(
        first_op, second_op, (((0,), (0,)), ((), ())), preferred_element_type=jnp.float32
    )


def back_dot(first_op, second_op):
    return lax.dot_general(
        first_op, second_op, (((1,), (1,)), ((), ())), preferred_element_type=jnp.float32
    )


def unit_inverse(lower):
    identity = jnp.eye(lower.shape[-1], dtype=lower.dtype)
    power = lower
    result = identity - lower
    for step_index in range(lower.shape[-1].bit_length() - 2):
        power = dotf(power, power)
        result = dotf(result, identity + power)
    return result


def doc_index(positions, starts):
    return jnp.sum((starts[None, :] <= positions[:, None]).astype(jnp.int32), axis=1) - 1


def root_mean_square_backward(grad_in, normed, inverse):
    return inverse * (grad_in - normed * jnp.mean(grad_in * normed, -1, keepdims=True))


def silu_back(grad_in, pre):
    sig = jax.nn.sigmoid(pre)
    return grad_in * sig * (1.0 + pre * (1.0 - sig))


def on_device(
    block_input,
    cotangent,
    doc_starts,
    qkv_weight,
    beta_weight,
    conv_weight,
    norm_gains,
    head_gain,
    out_weight,
    gate_up_weight,
    down_weight,
):
    token_rows = block_input[0].astype(jnp.float32)
    cot_low = cotangent[0]
    seq_len = token_rows.shape[0]
    width = token_rows.shape[1]
    n_groups = seq_len // GROUP
    scale = DK ** (-0.5)
    w_qkv, w_beta, w_conv, w_gains, w_head, w_out, w_gu, w_down = (
        lax.all_gather(qkv_weight, "seq", axis=0, tiled=True),
        lax.all_gather(beta_weight, "seq", axis=0, tiled=True),
        lax.all_gather(conv_weight, "seq", axis=1, tiled=True),
        lax.all_gather(norm_gains, "seq", axis=1, tiled=True),
        lax.all_gather(head_gain, "seq", axis=0, tiled=True),
        lax.all_gather(out_weight, "seq", axis=0, tiled=True),
        lax.all_gather(gate_up_weight, "seq", axis=0, tiled=True),
        lax.all_gather(down_weight, "seq", axis=0, tiled=True),
    )
    conv_f = w_conv.astype(jnp.float32)
    float_gains = w_gains.astype(jnp.float32)
    head_f = w_head.astype(jnp.float32)
    seq_count = lax.axis_size("seq")
    seq_place = lax.axis_index("seq")
    starts = doc_starts[0]
    positions = seq_place * seq_len + jnp.arange(seq_len, dtype=jnp.int32)
    doc = doc_index(positions, starts)
    rim = conv_f.shape[0] - 1
    rim_doc = doc_index(seq_place * seq_len - rim + jnp.arange(rim, dtype=jnp.int32), starts)
    first_inverse_norm = lax.rsqrt(jnp.mean(token_rows * token_rows, -1, keepdims=True) + EPS_NORM)
    normalized_input = token_rows * first_inverse_norm
    first_activation = (normalized_input * float_gains[0]).astype(jnp.bfloat16)
    proj = jnp.dot(first_activation, w_qkv, preferred_element_type=jnp.float32).astype(jnp.bfloat16)
    rates_tok = jax.nn.sigmoid(
        jnp.dot(first_activation, w_beta, preferred_element_type=jnp.float32)
    )
    rim_vals = shifted(proj[seq_len - rim :], "seq", 1)
    extended = jnp.concatenate([rim_vals, proj], 0).astype(jnp.float32)
    ext_doc = jnp.concatenate([rim_doc, doc])
    matches = [
        (ext_doc[rim - tap : rim - tap + seq_len] == doc).astype(jnp.float32)[:, None]
        for tap in range(rim + 1)
    ]
    pre = jnp.zeros((seq_len, extended.shape[1]), jnp.float32)
    for tap in range(rim + 1):
        pre = pre + conv_f[tap] * extended[rim - tap : rim - tap + seq_len] * matches[tap]
    act = jax.nn.silu(pre)
    q_raw = act[:, :width].reshape(seq_len, H, DK)
    k_raw = act[:, width : 2 * width].reshape(seq_len, H, DK)
    v_raw = act[:, 2 * width :].reshape(seq_len, H, DK)
    q_inv = lax.rsqrt(jnp.sum(q_raw * q_raw, -1, keepdims=True) + EPS_UNIT)
    k_inv = lax.rsqrt(jnp.sum(k_raw * k_raw, -1, keepdims=True) + EPS_UNIT)
    q_unit = q_raw * q_inv
    k_unit = k_raw * k_inv

    def to_groups(arr):
        return (
            arr.astype(jnp.bfloat16)
            .astype(jnp.float32)
            .reshape(n_groups, GROUP, H, DK)
            .transpose(0, 2, 1, 3)
        )

    scaled_q = to_groups(q_unit) * scale
    keys = to_groups(k_unit)
    values = to_groups(v_raw)
    rates = rates_tok.reshape(n_groups, GROUP, H).transpose(0, 2, 1)
    block_doc = doc.reshape(n_groups, GROUP)
    prev_doc = doc_index(
        seq_place * seq_len + jnp.arange(n_groups, dtype=jnp.int32) * GROUP - 1, starts
    )
    places = jnp.arange(GROUP)
    same = block_doc[:, :, None] == block_doc[:, None, :]
    strict = ((places[:, None] > places[None, :])[None] & same)[:, None].astype(jnp.float32)
    incl = ((places[:, None] >= places[None, :])[None] & same)[:, None].astype(jnp.float32)
    keep = (block_doc == prev_doc[:, None]).astype(jnp.float32)[:, None, :, None]
    tail = (block_doc == block_doc[:, -1:]).astype(jnp.float32)[:, None, :, None]
    whole = keep[:, 0, -1, 0]
    scaled = keys * rates[..., None]
    lower = jnp.einsum("nhid,nhjd->nhij", scaled, keys, precision=HIGH) * strict
    inverse = unit_inverse(lower)
    w_mat = dotf(inverse, scaled)
    base = dotf(inverse, values * rates[..., None])
    eye_heads = jnp.broadcast_to(jnp.eye(DK, dtype=jnp.float32), (H, DK, DK))
    zero_heads = jnp.zeros((H, DK, DK), jnp.float32)

    def chain_step(maps, inputs):
        c_keys, c_w, c_base, c_keep, c_tail, c_whole = inputs
        mixed_maps = dotf(c_w[None], maps)
        reduce_part = jnp.einsum(
            "hcd,shce->shde", c_keys * (c_tail * c_keep), mixed_maps, precision=HIGH
        )
        maps = c_whole * maps - reduce_part
        shift_add = jnp.einsum("hcd,hce->hde", c_keys * c_tail, c_base, precision=HIGH)
        return (jnp.stack([maps[0], maps[1] + shift_add]), None)

    block_maps, unused = lax.scan(
        chain_step, jnp.stack([eye_heads, zero_heads]), (keys, w_mat, base, keep, tail, whole)
    )
    every_map, every_shift = (
        lax.all_gather(block_maps[0][None].astype(jnp.bfloat16), "seq", axis=0, tiled=True).astype(
            jnp.float32
        ),
        lax.all_gather(block_maps[1][None].astype(jnp.bfloat16), "seq", axis=0, tiled=True).astype(
            jnp.float32
        ),
    )

    def apply_map(position, state):
        return jnp.where(
            position < seq_place, dotf(every_map[position], state) + every_shift[position], state
        )

    state_in = lax.fori_loop(0, seq_count, apply_map, zero_heads)

    def out_step(state, inputs):
        c_q, c_keys, c_w, c_base, c_keep, c_tail, c_whole, c_incl = inputs
        pseudo = c_base - c_keep * dotf(c_w, state)
        scores = jnp.einsum("hid,hjd->hij", c_q, c_keys, precision=HIGH) * c_incl
        output = c_keep * dotf(c_q, state) + dotf(scores, pseudo)
        new_state = c_whole * state + jnp.einsum(
            "hcd,hce->hde", c_keys * c_tail, pseudo, precision=HIGH
        )
        return (new_state, (output, state))

    last_state, (outputs, block_states) = lax.scan(
        out_step, state_in, (scaled_q, keys, w_mat, base, keep, tail, whole, incl)
    )
    mixed_o = outputs.transpose(0, 2, 1, 3).reshape(seq_len, H, DK)
    head_inv = lax.rsqrt(jnp.mean(mixed_o * mixed_o, -1, keepdims=True) + EPS_HEAD)
    ohat = mixed_o * head_inv
    act_two = (ohat * head_f).reshape(seq_len, width).astype(jnp.bfloat16)
    resid = token_rows + jnp.dot(act_two, w_out, preferred_element_type=jnp.float32)
    inv_two = lax.rsqrt(jnp.mean(resid * resid, -1, keepdims=True) + EPS_NORM)
    rhat = resid * inv_two
    act_three = (rhat * float_gains[1]).astype(jnp.bfloat16)
    gate_up = jnp.dot(act_three, w_gu, preferred_element_type=jnp.float32)
    hidden_units = gate_up.shape[1] // 2
    gate = gate_up[:, :hidden_units]
    up_part = gate_up[:, hidden_units:]
    act_four = (jax.nn.silu(gate) * up_part).astype(jnp.bfloat16)
    mixed = (resid + jnp.dot(act_four, w_down, preferred_element_type=jnp.float32)).astype(
        jnp.bfloat16
    )
    grad_down = tok_dot(act_four, cot_low)
    d_act_four = back_dot(cot_low, w_down)
    d_gate = silu_back(d_act_four * up_part, gate)
    d_up = d_act_four * jax.nn.silu(gate)
    d_gate_up = jnp.concatenate([d_gate, d_up], 1).astype(jnp.bfloat16)
    grad_gate_up = tok_dot(act_three, d_gate_up)
    d_act_three = back_dot(d_gate_up, w_gu)
    grad_gain_two = jnp.sum(d_act_three * rhat, 0)
    residual_gradient = cot_low.astype(jnp.float32) + root_mean_square_backward(
        d_act_three * float_gains[1], rhat, inv_two
    )
    d_resid_low = residual_gradient.astype(jnp.bfloat16)
    grad_out = tok_dot(act_two, d_resid_low)
    d_act_two = back_dot(d_resid_low, w_out).reshape(seq_len, H, DK)
    grad_head = jnp.sum(d_act_two * ohat, (0, 1))
    d_mixed_o = root_mean_square_backward(d_act_two * head_f, ohat, head_inv)
    d_out_groups = d_mixed_o.reshape(n_groups, GROUP, H, DK).transpose(0, 2, 1, 3)

    def state_grad(grad_state, inputs):
        c_q, c_keys, c_scaled, c_inverse, c_keep, c_tail, c_whole, c_incl, c_dout = inputs
        scores = jnp.einsum("hid,hjd->hij", c_q, c_keys, precision=HIGH) * c_incl
        d_pseudo = jnp.einsum("hij,hid->hjd", scores, c_dout, precision=HIGH) + c_tail * dotf(
            c_keys, grad_state
        )
        d_res = jnp.einsum("hij,hid->hjd", c_inverse, d_pseudo, precision=HIGH)
        prior = (
            jnp.einsum("hcd,hce->hde", c_q * c_keep, c_dout, precision=HIGH) + c_whole * grad_state
        )
        return (prior - jnp.einsum("hcd,hce->hde", c_scaled * c_keep, d_res, precision=HIGH), None)

    local_grad, unused = lax.scan(
        state_grad,
        zero_heads,
        (scaled_q, keys, scaled, inverse, keep, tail, whole, incl, d_out_groups),
        reverse=True,
    )
    back_maps = swap_last(block_maps[0])
    every_back, every_grad = (
        lax.all_gather(back_maps[None].astype(jnp.bfloat16), "seq", axis=0, tiled=True).astype(
            jnp.float32
        ),
        lax.all_gather(local_grad[None].astype(jnp.bfloat16), "seq", axis=0, tiled=True).astype(
            jnp.float32
        ),
    )

    def apply_back(step_index, grad_state):
        position = seq_count - 1 - step_index
        return jnp.where(
            position > seq_place,
            dotf(every_back[position], grad_state) + every_grad[position],
            grad_state,
        )

    grad_state_out = lax.fori_loop(0, seq_count, apply_back, zero_heads)

    def full_back(grad_state, inputs):
        (
            c_q,
            c_keys,
            c_values,
            c_rates,
            c_scaled,
            c_inverse,
            c_w,
            c_base,
            c_keep,
            c_tail,
            c_whole,
            c_strict,
            c_incl,
            c_dout,
            c_state,
        ) = inputs
        pseudo = c_base - c_keep * dotf(c_w, c_state)
        scores = jnp.einsum("hid,hjd->hij", c_q, c_keys, precision=HIGH) * c_incl
        d_pseudo = jnp.einsum("hij,hid->hjd", scores, c_dout, precision=HIGH) + c_tail * dotf(
            c_keys, grad_state
        )
        d_res = jnp.einsum("hij,hid->hjd", c_inverse, d_pseudo, precision=HIGH)
        prior = (
            jnp.einsum("hcd,hce->hde", c_q * c_keep, c_dout, precision=HIGH) + c_whole * grad_state
        )
        prior = prior - jnp.einsum("hcd,hce->hde", c_scaled * c_keep, d_res, precision=HIGH)
        d_scores = jnp.einsum("hid,hjd->hij", c_dout, pseudo, precision=HIGH) * c_incl
        d_query = c_keep * dotf(c_dout, swap_last(c_state)) + dotf(d_scores, c_keys)
        d_keys = jnp.einsum("hij,hid->hjd", d_scores, c_q, precision=HIGH) + c_tail * dotf(
            pseudo, swap_last(grad_state)
        )
        d_lower = -jnp.einsum("hid,hjd->hij", d_res, pseudo, precision=HIGH) * c_strict
        d_scaled = -c_keep * dotf(d_res, swap_last(c_state)) + dotf(d_lower, c_keys)
        d_keys = (
            d_keys
            + jnp.einsum("hij,hid->hjd", d_lower, c_scaled, precision=HIGH)
            + c_rates[..., None] * d_scaled
        )
        d_values = c_rates[..., None] * d_res
        d_rates = jnp.sum(d_res * c_values, -1) + jnp.sum(d_scaled * c_keys, -1)
        return (prior, (d_query * scale, d_keys, d_values, d_rates))

    first_grad, (d_q_groups, d_k_groups, d_v_groups, d_rate_groups) = lax.scan(
        full_back,
        grad_state_out,
        (
            scaled_q,
            keys,
            values,
            rates,
            scaled,
            inverse,
            w_mat,
            base,
            keep,
            tail,
            whole,
            strict,
            incl,
            d_out_groups,
            block_states,
        ),
        reverse=True,
    )

    def from_groups(arr):
        return arr.transpose(0, 2, 1, 3).reshape(seq_len, H, DK)

    d_q_unit = from_groups(d_q_groups)
    d_k_unit = from_groups(d_k_groups)
    d_q_raw = q_inv * (d_q_unit - q_unit * jnp.sum(d_q_unit * q_unit, -1, keepdims=True))
    d_k_raw = k_inv * (d_k_unit - k_unit * jnp.sum(d_k_unit * k_unit, -1, keepdims=True))
    d_act = jnp.concatenate(
        [
            d_q_raw.reshape(seq_len, width),
            d_k_raw.reshape(seq_len, width),
            from_groups(d_v_groups).reshape(seq_len, width),
        ],
        1,
    )
    d_pre = silu_back(d_act, pre)
    d_extended = jnp.zeros((seq_len + rim, d_pre.shape[1]), jnp.float32)
    conv_grads = []
    for tap in range(rim + 1):
        masked = d_pre * matches[tap]
        d_extended = d_extended + jnp.pad(conv_f[tap] * masked, ((rim - tap, tap), (0, 0)))
        conv_grads.append(jnp.sum(masked * extended[rim - tap : rim - tap + seq_len], 0))
    grad_conv = jnp.stack(conv_grads)
    rim_back = shifted(d_extended[:rim].astype(jnp.bfloat16), "seq", -1).astype(jnp.float32)
    d_proj = (d_extended[rim:] + jnp.pad(rim_back, ((seq_len - rim, 0), (0, 0)))).astype(
        jnp.bfloat16
    )
    d_rates_tok = d_rate_groups.transpose(0, 2, 1).reshape(seq_len, H)
    d_logits = (d_rates_tok * rates_tok * (1.0 - rates_tok)).astype(jnp.bfloat16)
    grad_qkv = tok_dot(first_activation, d_proj)
    grad_beta = tok_dot(first_activation, d_logits)
    first_activation_gradient = back_dot(d_proj, w_qkv) + back_dot(d_logits, w_beta)
    first_gain_gradient = jnp.sum(first_activation_gradient * normalized_input, 0)
    block_input_gradient = (
        residual_gradient
        + root_mean_square_backward(
            first_activation_gradient * float_gains[0], normalized_input, first_inverse_norm
        )
    ).astype(jnp.bfloat16)
    grad_gains = jnp.stack([first_gain_gradient, grad_gain_two])
    red_qkv, red_beta, red_conv, red_gains, red_head, red_out, red_gu, red_down = (
        lax.psum_scatter(
            grad_qkv.astype(jnp.bfloat16), "seq", scatter_dimension=0, tiled=True
        ).astype(jnp.float32),
        lax.psum_scatter(
            grad_beta.astype(jnp.bfloat16), "seq", scatter_dimension=0, tiled=True
        ).astype(jnp.float32),
        lax.psum_scatter(
            grad_conv.astype(jnp.bfloat16), "seq", scatter_dimension=1, tiled=True
        ).astype(jnp.float32),
        lax.psum_scatter(
            grad_gains.astype(jnp.bfloat16), "seq", scatter_dimension=1, tiled=True
        ).astype(jnp.float32),
        lax.psum_scatter(
            grad_head.astype(jnp.bfloat16), "seq", scatter_dimension=0, tiled=True
        ).astype(jnp.float32),
        lax.psum_scatter(
            grad_out.astype(jnp.bfloat16), "seq", scatter_dimension=0, tiled=True
        ).astype(jnp.float32),
        lax.psum_scatter(
            grad_gate_up.astype(jnp.bfloat16), "seq", scatter_dimension=0, tiled=True
        ).astype(jnp.float32),
        lax.psum_scatter(
            grad_down.astype(jnp.bfloat16), "seq", scatter_dimension=0, tiled=True
        ).astype(jnp.float32),
    )
    red_qkv, red_beta, red_conv, red_gains, red_head, red_out, red_gu, red_down = (
        lax.psum(red_qkv.astype(jnp.bfloat16), "row").astype(jnp.float32),
        lax.psum(red_beta.astype(jnp.bfloat16), "row").astype(jnp.float32),
        lax.psum(red_conv.astype(jnp.bfloat16), "row").astype(jnp.float32),
        lax.psum(red_gains.astype(jnp.bfloat16), "row").astype(jnp.float32),
        lax.psum(red_head.astype(jnp.bfloat16), "row").astype(jnp.float32),
        lax.psum(red_out.astype(jnp.bfloat16), "row").astype(jnp.float32),
        lax.psum(red_gu.astype(jnp.bfloat16), "row").astype(jnp.float32),
        lax.psum(red_down.astype(jnp.bfloat16), "row").astype(jnp.float32),
    )
    return (
        mixed[None],
        block_input_gradient[None],
        red_qkv,
        red_beta,
        red_conv,
        red_gains,
        red_head,
        red_out,
        red_gu,
        red_down,
    )


BF = jnp.bfloat16
F32 = jnp.float32
RIM = 8
NN = (((1,), (0,)), ((), ()))
NT = (((1,), (1,)), ((), ()))
TN = (((0,), (0,)), ((), ()))


def dot_low(a, b, dims=NN):
    return lax.dot_general(a, b, dims, preferred_element_type=F32)


def parts_of(a):
    if a.dtype == BF:
        return (a,)
    high = a.astype(BF)
    return high, (a - high.astype(F32)).astype(BF)


def mm(a, b, dims=NN):
    a_parts, b_parts = parts_of(a), parts_of(b)
    total = dot_low(a_parts[0], b_parts[0], dims)
    if len(b_parts) > 1:
        total = total + dot_low(a_parts[0], b_parts[1], dims)
    if len(a_parts) > 1:
        total = total + dot_low(a_parts[1], b_parts[0], dims)
    return total


def mm1(a, b, dims=NN):
    return dot_low(a.astype(BF), b.astype(BF), dims)


def begin_of(pos, starts_ref):
    begin = jnp.zeros_like(pos)
    for i in range(starts_ref.shape[0]):
        begin = jnp.maximum(begin, jnp.where(pos >= starts_ref[i], starts_ref[i], 0))
    return begin


def begin_at(pos, starts_ref):
    begin = jnp.int32(0)
    for i in range(starts_ref.shape[0]):
        begin = jnp.maximum(begin, jnp.where(starts_ref[i] <= pos, starts_ref[i], 0))
    return begin


def mark_table(chunks, size, taps, starts_ref):
    pos = lax.broadcasted_iota(jnp.int32, (chunks, size), 0) * size
    pos = pos + lax.broadcasted_iota(jnp.int32, (chunks, size), 1)
    rows = begin_of(pos, starts_ref)
    later = [
        ((begin_of(pos + tap, starts_ref) <= pos) & (pos + tap < chunks * size)).astype(F32)
        for tap in range(1, taps)
    ]
    down = lax.broadcasted_iota(jnp.int32, (size, size), 0)
    eye = (down == lax.broadcasted_iota(jnp.int32, (size, size), 1)).astype(BF)
    rows = rows.astype(F32)
    return rows, mm(eye, rows, NT), [mm(eye, v, NT) for v in later]


def chunk_marks(n, size, table, starts_ref):
    first = n * size
    col = table[1][:, n : n + 1]
    last = begin_at(first + size - 1, starts_ref)
    keep = (col < float(first)).astype(F32)
    tail = (col == last.astype(F32)).astype(F32)
    whole = (last < first).astype(F32)
    return col, keep, tail, whole


def chunk_masks(n, size, col, table):
    here = lax.broadcasted_iota(jnp.int32, (size, size), 0)
    there = lax.broadcasted_iota(jnp.int32, (size, size), 1)
    same = col == table[0][n : n + 1]
    return here, there, same & (here > there), same & (here >= there)


def conv_chunk(n, size, pad, conv, col):
    depth = (n * size + lax.broadcasted_iota(jnp.int32, (size, 1), 0)).astype(F32) - col
    pre = conv[0:1, :] * pad[pl.ds(RIM + n * size, size), :]
    for tap in range(1, conv.shape[0]):
        match = (depth >= float(tap)).astype(F32)
        pre = pre + conv[tap : tap + 1, :] * pad[pl.ds(RIM - tap + n * size, size), :] * match
    return pre


def front_kernel(taps, place_ref, starts_ref, *refs):
    n_seq = refs[-1].shape[0]
    n_row = n_seq // 2
    x_ref, got_ref, got_y_ref, got_cores_ref = refs[:4]
    got_refs = (got_ref, got_cores_ref.at[0], got_y_ref, got_cores_ref.at[1])
    (
        weight_ref,
        act1_ref,
        proj_ref,
        rates_ref,
        o_ref,
        act2_ref,
        inv_ref,
        w_ref,
        att_ref,
        p_ref,
        u_ref,
        s_ref,
        conv_ref,
        gains_ref,
        beta_ref,
        head_ref,
        pad,
        lower,
        tmp,
        q_scr,
        k_scr,
        v_scr,
        add,
    ) = refs[4:]
    place, row = place_ref[0], place_ref[1]
    size = s_ref.shape[1]
    part_rows = size // n_row
    dk = o_ref.shape[1]
    base = 3 * part_rows
    gains = jnp.concatenate([got_ref[s, base + 4 : base + 6, :] for s in range(n_seq)], 1).astype(F32)
    gains_ref[...] = jnp.zeros_like(gains_ref)
    gains_ref[0:2, :] = gains
    beta = jnp.concatenate([got_ref[s, base + 8 : base + 16, :] for s in range(n_seq)], 1)
    beta_ref[...] = beta
    head_gain = got_ref[0, base + 6 : base + 7, :].astype(F32)
    for s in range(1, n_seq):
        head_gain = head_gain + got_ref[s, base + 6 : base + 7, :].astype(F32)
    head_ref[...] = jnp.broadcast_to(head_gain, head_ref.shape)
    conv_parts = []
    for part in range(3):
        block = part * n_seq + place
        shard = block // 3
        offset = pl.multiple_of(base + (block - shard * 3) * 16, 16)
        conv_parts.append(got_ref[shard, pl.ds(offset, 16), :][0:8])
    conv = jnp.concatenate(conv_parts, 1).astype(F32)
    conv_ref[...] = conv
    conv = conv[0:taps]
    for m, ref in enumerate(got_refs):
        for s in range(n_seq):
            at = pl.multiple_of(s * size + (row ^ m) * part_rows, part_rows)
            for kind in range(3):
                block = ref[s, kind * part_rows : (kind + 1) * part_rows, :]
                weight_ref[pl.ds(at, part_rows), kind * dk : (kind + 1) * dk] = block
    weight = weight_ref[...]
    lanes = lax.broadcasted_iota(jnp.int32, (2 * size, 8), 1)
    pad[0:RIM, :] = jnp.zeros((RIM, 3 * dk), F32)
    for n in range(0, n_seq, 2):
        rows_at = pl.ds(n * size, 2 * size)
        rows = x_ref[rows_at, :].astype(F32)
        inv = lax.rsqrt(jnp.mean(rows * rows, -1, keepdims=True) + EPS_NORM)
        act = ((rows * inv) * gains[0:1]).astype(BF)
        act1_ref[rows_at, :] = act
        proj = dot_low(act, weight).astype(BF)
        proj_ref[rows_at, :] = proj
        pad[pl.ds(RIM + n * size, 2 * size), :] = proj.astype(F32)
        logits = dot_low(act, beta, NT)
        rate = jax.nn.sigmoid(jnp.sum(jnp.where(lanes == place, logits, 0.0), 1, keepdims=True))
        rates_ref[rows_at, :] = jnp.broadcast_to(rate, (2 * size, dk))
    table = mark_table(n_seq, size, taps, starts_ref)
    marks = []
    for n in range(n_seq):
        at = n * size
        col, keep, tail, whole = chunk_marks(n, size, table, starts_ref)
        marks.append((keep, tail, whole))
        pre = conv_chunk(n, size, pad, conv, col)
        act = pre * jax.nn.sigmoid(pre)
        q_raw, k_raw, v_raw = act[:, :dk], act[:, dk : 2 * dk], act[:, 2 * dk :]
        q = (q_raw * lax.rsqrt(jnp.sum(q_raw * q_raw, -1, keepdims=True) + EPS_UNIT)).astype(BF)
        key = (k_raw * lax.rsqrt(jnp.sum(k_raw * k_raw, -1, keepdims=True) + EPS_UNIT)).astype(BF)
        q_scr[pl.ds(at, size), :] = q
        k_scr[pl.ds(at, size), :] = key
        v_scr[pl.ds(at, size), :] = v_raw.astype(BF)
        here, there, strict, incl = chunk_masks(n, size, col, table)
        rate = rates_ref[pl.ds(at, size), :]
        low = jnp.where(strict, dot_low(key, key, NT) * rate, 0.0)
        att_ref[n] = jnp.where(incl, dot_low(q, key, NT) * (dk**-0.5), 0.0)
        lower[n] = low
        eye = (here == there).astype(F32)
        inv_ref[n] = eye - jnp.where((here // 2) == (there // 2), low, 0.0)
    span = 2
    while span < size:
        here = lax.broadcasted_iota(jnp.int32, (size, size), 0)
        there = lax.broadcasted_iota(jnp.int32, (size, size), 1)
        cross = ((here // (2 * span)) == (there // (2 * span))) & ((here // span) != (there // span))
        for n in range(n_seq):
            tmp[n] = mm(inv_ref[n], jnp.where(cross, lower[n], 0.0))
        for n in range(n_seq):
            inv_ref[n] = inv_ref[n] - mm(tmp[n], inv_ref[n])
        span *= 2
    for n in range(n_seq):
        keep, tail, whole = marks[n]
        rows = pl.ds(n * size, size)
        rate = rates_ref[rows, :]
        key = k_scr[rows, :]
        inv = inv_ref[n]
        w = mm(inv, rate * key.astype(F32))
        base = mm(inv, rate * v_scr[rows, :].astype(F32))
        w_ref[n] = w
        u_ref[n] = base
        p_ref[n] = mm(key, (tail * keep) * w, TN)
        add[n] = mm(key, tail * base, TN)
    state = jnp.zeros((dk, dk), F32)
    for n in range(n_seq):
        s_ref[n] = state
        if n + 1 < n_seq:
            state = marks[n][2] * state - mm(p_ref[n], state) + add[n]
    for n in range(n_seq):
        keep, tail, whole = marks[n]
        rows = pl.ds(n * size, size)
        state = s_ref[n]
        u = u_ref[n] - keep * mm(w_ref[n], state)
        u_ref[n] = u
        out = (keep * (dk**-0.5)) * mm(q_scr[rows, :], state) + mm(att_ref[n], u)
        o_ref[rows, :] = out
        inv = lax.rsqrt(jnp.mean(out * out, -1, keepdims=True) + EPS_HEAD)
        act2_ref[n] = ((out * inv) * head_gain).astype(BF)


def back_kernel(taps, place_ref, starts_ref, *refs):
    (
        dact_ref,
        o_ref,
        head_ref,
        conv_ref,
        proj_ref,
        rates_ref,
        inv_ref,
        w_ref,
        att_ref,
        p_ref,
        u_ref,
        s_ref,
        weight_ref,
        beta_ref,
        dproj_ref,
        part_ref,
        dlog_ref,
        gconv_ref,
        ghead_ref,
        logit_scr,
        pad,
        pre_scr,
        dpre,
        do_scr,
        g_scr,
        add,
        x_scr,
        q_scr,
        k_scr,
    ) = refs
    n_seq, size, dk = dact_ref.shape
    scale = dk**-0.5
    place = place_ref[0]
    beta_all = beta_ref[...].astype(F32)
    beta_lane = lax.broadcasted_iota(jnp.int32, beta_all.shape, 0) == place
    beta_row = jnp.sum(jnp.where(beta_lane, beta_all, 0.0), 0, keepdims=True)
    head_gain = head_ref[0:1, :]
    conv = conv_ref[0:taps, :]
    total = n_seq * size
    pad[0:RIM, :] = jnp.zeros((RIM, 3 * dk), F32)
    pad[pl.ds(RIM, total), :] = proj_ref[...].astype(F32)
    dpre[pl.ds(total, RIM), :] = jnp.zeros((RIM, 3 * dk), F32)
    table = mark_table(n_seq, size, taps, starts_ref)
    marks = []
    ghead = jnp.zeros((1, dk), F32)
    for n in range(n_seq):
        rows = pl.ds(n * size, size)
        col, keep, tail, whole = chunk_marks(n, size, table, starts_ref)
        marks.append((col, keep, tail, whole))
        pre = conv_chunk(n, size, pad, conv, col)
        pre_scr[rows, :] = pre
        act = pre * jax.nn.sigmoid(pre)
        q_raw, k_raw = act[:, :dk], act[:, dk : 2 * dk]
        q = (q_raw * lax.rsqrt(jnp.sum(q_raw * q_raw, -1, keepdims=True) + EPS_UNIT)).astype(BF)
        key = (k_raw * lax.rsqrt(jnp.sum(k_raw * k_raw, -1, keepdims=True) + EPS_UNIT)).astype(BF)
        q_scr[rows, :] = q
        k_scr[rows, :] = key
        out = o_ref[rows, :]
        inv = lax.rsqrt(jnp.mean(out * out, -1, keepdims=True) + EPS_HEAD)
        ohat = out * inv
        d_act2 = dact_ref[n].astype(F32)
        ghead = ghead + jnp.sum(d_act2 * ohat, 0, keepdims=True)
        lean = d_act2 * head_gain
        d_out = inv * (lean - ohat * jnp.mean(lean * ohat, -1, keepdims=True))
        do_scr[rows, :] = d_out
        g_scr[rows, :] = mm(att_ref[n], d_out, TN)
    ghead_ref[...] = jnp.broadcast_to(ghead, ghead_ref.shape)
    for n in range(n_seq):
        rows = pl.ds(n * size, size)
        col, keep, tail, whole = marks[n]
        add[n] = mm(q_scr[rows, :], (scale * keep) * do_scr[rows, :], TN) - mm(w_ref[n], keep * g_scr[rows, :], TN)
    grad = jnp.zeros((dk, dk), F32)
    for n in range(n_seq - 1, -1, -1):
        x_scr[n] = grad
        if n > 0:
            grad = marks[n][3] * grad - mm(p_ref[n], grad, TN) + add[n]
    gconv = [jnp.zeros((1, 3 * dk), F32) for _ in range(taps)]
    for n in range(n_seq - 1, -1, -1):
        rows = pl.ds(n * size, size)
        col, keep, tail, whole = marks[n]
        here, there, strict, incl = chunk_masks(n, size, col, table)
        rate = rates_ref[rows, :]
        key, q = k_scr[rows, :], q_scr[rows, :]
        key_f, q_f = key.astype(F32), q.astype(F32)
        pre = pre_scr[rows, :]
        sig = jax.nn.sigmoid(pre)
        act = pre * sig
        value = act[:, 2 * dk :].astype(BF).astype(F32)
        grad, state, u = x_scr[n], s_ref[n], u_ref[n]
        d_out = do_scr[rows, :]
        d_u = g_scr[rows, :] + tail * mm(key, grad)
        d_r = mm(inv_ref[n], d_u, TN)
        d_att = jnp.where(incl, mm(d_out, u, NT), 0.0)
        d_low = jnp.where(strict, -mm(d_r, u, NT), 0.0)
        d_q = keep * mm(d_out, state, NT) + mm(d_att, key)
        d_kb = mm(d_low, key) - keep * mm(d_r, state, NT)
        d_k = (
            scale * mm(d_att, q, TN)
            + mm(d_low, rate * key_f, TN)
            + tail * mm(u, grad, NT)
            + rate * d_kb
        )
        d_v = rate * d_r
        d_rate = jnp.sum(d_r * value + d_kb * key_f, -1, keepdims=True)
        d_q = d_q * scale
        q_raw, k_raw = act[:, :dk], act[:, dk : 2 * dk]
        q_inv = lax.rsqrt(jnp.sum(q_raw * q_raw, -1, keepdims=True) + EPS_UNIT)
        k_inv = lax.rsqrt(jnp.sum(k_raw * k_raw, -1, keepdims=True) + EPS_UNIT)
        q_unit, k_unit = q_raw * q_inv, k_raw * k_inv
        d_q = q_inv * (d_q - q_unit * jnp.sum(d_q * q_unit, -1, keepdims=True))
        d_k = k_inv * (d_k - k_unit * jnp.sum(d_k * k_unit, -1, keepdims=True))
        d_act = jnp.concatenate([d_q, d_k, d_v], 1)
        d_pre = d_act * sig * (1.0 + pre * (1.0 - sig))
        dpre[rows, :] = d_pre
        depth = (n * size + lax.broadcasted_iota(jnp.int32, (size, 1), 0)).astype(F32) - col
        d_proj = conv[0:1, :] * d_pre
        gconv[0] = gconv[0] + jnp.sum(d_pre * pad[pl.ds(RIM + n * size, size), :], 0, keepdims=True)
        for tap in range(1, taps):
            match = table[2][tap - 1][:, n : n + 1]
            d_proj = d_proj + conv[tap : tap + 1, :] * dpre[pl.ds(n * size + tap, size), :] * match
            reach = (depth >= float(tap)).astype(F32)
            gconv[tap] = gconv[tap] + jnp.sum(
                d_pre * reach * pad[pl.ds(RIM - tap + n * size, size), :], 0, keepdims=True
            )
        d_proj = d_proj.astype(BF)
        dproj_ref[rows, :] = d_proj
        one_rate = rate[:, 0:1]
        d_logit = (d_rate * one_rate * (1.0 - one_rate)).astype(BF).astype(F32)
        logit_scr[rows, :] = jnp.broadcast_to(d_logit, (size, dk))
        dlog_ref[pl.ds(n, 1), :] = jnp.broadcast_to(d_logit, (size, dk)).T[0:1]
    for n in range(0, n_seq, 2):
        rows = pl.ds(n * size, 2 * size)
        d_act1 = dot_low(dproj_ref[rows, :], weight_ref[...], NT) + logit_scr[rows, 0:1] * beta_row
        part_ref[rows, :] = d_act1.astype(BF)
    gconv_ref[...] = jnp.zeros_like(gconv_ref)
    for tap in range(taps):
        gconv_ref[tap : tap + 1, :] = gconv[tap]


def lead_kernel(place_ref, qkv_ref, conv_ref, gains_ref, head_ref, beta_ref, out_ref, rows):
    place, row = place_ref[0], place_ref[1]
    heads, dk = out_ref.shape[0], out_ref.shape[2]
    part = dk // 4
    from_row = pl.ds(pl.multiple_of(row * part, part), part)
    per = head_ref.shape[1]
    down = lax.broadcasted_iota(jnp.int32, (dk, dk), 0)
    along = lax.broadcasted_iota(jnp.int32, (dk, dk), 1)
    spot = (along == down + place * per)[0:per].astype(BF)
    rows[...] = jnp.zeros_like(rows)
    taps = conv_ref.shape[0]
    for kind in range(3):
        rows[kind * 16 : kind * 16 + taps, :] = conv_ref[:, kind * dk : (kind + 1) * dk].astype(F32)
    rows[4:6, :] = gains_ref[...].astype(F32)
    rows[6:7, :] = dot_low(jnp.broadcast_to(head_ref[...], (16, per)), spot)[0:1]
    rows[8:16, :] = beta_ref[...].astype(F32)
    small = rows[...].astype(BF)
    for h in range(heads):
        for kind in range(3):
            block = qkv_ref[from_row, pl.ds((kind * heads + h) * dk, dk)]
            out_ref[h, kind * part : (kind + 1) * part, :] = block
        out_ref[h, 3 * part : 3 * part + 48, :] = small


def pack_kernel(own_ref, other_ref, down_ref, out_ref):
    size, lanes = own_ref.shape[0], out_ref.shape[1]
    n_cols = own_ref.shape[1] // lanes
    slot, part = 96, down_ref.shape[0]
    for i, ref in enumerate((own_ref, other_ref)):
        for j in range(n_cols):
            out_ref[(i * n_cols + j) * size : (i * n_cols + j + 1) * size, :] = ref[:, j * lanes : (j + 1) * lanes]
    base = 2 * n_cols * size
    for j in range(down_ref.shape[1] // lanes):
        block = down_ref[:, j * lanes : (j + 1) * lanes]
        block = jnp.concatenate([block, jnp.zeros((slot - part, lanes), BF)], 0)
        out_ref[pl.ds(base + j * slot, slot), :] = block


def mid_kernel(place_ref, act2_ref, own_ref, y_ref, cores_ref, x_ref, gains_ref, resid_ref, act3_ref, weight_ref):
    row = place_ref[1]
    heads, size, dk = act2_ref.shape
    part = dk // 4
    for m in range(4):
        ref = (own_ref, cores_ref.at[0], y_ref, cores_ref.at[1])[m]
        for s in range(heads):
            at = pl.multiple_of((s * 4 + (row ^ m)) * part, part)
            weight_ref[pl.ds(at, part), :] = ref[s]
    act2 = jnp.concatenate([act2_ref[h] for h in range(heads)], 1)
    resid = x_ref[...].astype(F32) + dot_low(act2, weight_ref[...])
    resid_ref[...] = resid
    inv = lax.rsqrt(jnp.mean(resid * resid, -1, keepdims=True) + EPS_NORM)
    act3_ref[...] = ((resid * inv) * gains_ref[1:2, :]).astype(BF)


GROUP_BITS = (0, 2, 4, 6, 1, 3, 5, 7)


def store_part(bits, block, own_ref, next_ref):
    @pl.when((bits & 1) == 0)
    def _():
        own_ref[bits >> 1] = block

    @pl.when((bits & 1) == 1)
    def _():
        next_ref[bits >> 1] = block


def mixed_kernel(place_ref, act4_ref, down_ref, own_ref, next_ref):
    me = lax.rem(place_ref[0], 2) * 4 + place_ref[1]
    size = own_ref.shape[1]
    for i in range(4):
        parts = dot_low(act4_ref[pl.ds(i * 2 * size, 2 * size), :], down_ref[...]).astype(BF)
        for half in range(2):
            store_part(me ^ (2 * i + half), parts[half * size : (half + 1) * size], own_ref, next_ref)


def feed_kernel(hidden, place_ref, *refs):
    act3_refs, core_ref, cot_refs, cot_core_ref, packs_ref = refs[0:4], refs[4], refs[5:9], refs[9], refs[10]
    own_ref, next_ref, act4_ref, dgu_ref, act3_ref, cot_ref, down_ref, gu, down32 = refs[11:]
    place, row = place_ref[0], place_ref[1]
    side = lax.rem(place, 2)
    me = side * 4 + row
    size, width = act3_refs[0].shape
    wide = act4_ref.shape[1]
    lanes = packs_ref.shape[2]
    slot, part = 96, hidden // 4
    gu_rows = gu.shape[0] // 4
    n_cols = gu.shape[1] // lanes
    down32[hidden:wide, :] = jnp.zeros((wide - hidden, width), F32)

    for src in range(4):
        for i in range(2):
            shard = src * 2 + (side if i == 0 else 1 - side)
            rows = pl.ds(pl.multiple_of(shard * size, size), size)
            for j in range(n_cols):
                from_rows = pl.ds((i * n_cols + j) * size, size)
                gu[rows, j * lanes : (j + 1) * lanes] = packs_ref[src, from_rows, :]
        for j in range(width // lanes):
            block = packs_ref[src, pl.ds(n_cols * gu_rows + j * slot, slot), :].astype(F32)
            down32[src * part : (src + 1) * part, j * lanes : (j + 1) * lanes] = block[0:part]
    down_ref[...] = down32[...].astype(BF)
    for i, bits in enumerate(GROUP_BITS):
        at = pl.multiple_of((me ^ bits) * size, size)
        act3_ref[pl.ds(at, size), :] = act3_refs[i][...] if i < 4 else core_ref[i - 4]
        cot_ref[pl.ds(at, size), :] = cot_refs[i][...] if i < 4 else cot_core_ref[i - 4]
    for i in range(4):
        rows = pl.ds(i * 2 * size, 2 * size)
        act3 = act3_ref[rows, :]
        cot = cot_ref[rows, :]
        gate_up = dot_low(act3, gu[...])
        gate, up = gate_up[:, :wide], gate_up[:, wide:]
        sig = jax.nn.sigmoid(gate)
        silu = gate * sig
        act4_ref[rows, :] = (silu * up).astype(BF)
        d_act4 = dot_low(cot, down_ref[...], NT)
        d_gate = d_act4 * up * sig * (1.0 + gate * (1.0 - sig))
        d_gu = jnp.concatenate([d_gate, d_act4 * silu], 1).astype(BF)
        dgu_ref[rows, :] = d_gu
        parts = dot_low(d_gu, gu[...], NT).astype(BF)
        for half in range(2):
            store_part(me ^ (2 * i + half), parts[half * size : (half + 1) * size], own_ref, next_ref)


def grads_kernel(hidden, place_ref, act3_ref, cot_ref, act4_ref, dgu_ref, out_ref, down32):
    side = lax.rem(place_ref[0], 2)
    lanes = out_ref.shape[2]
    slot, part = 96, hidden // 4
    gu_rows = act3_ref.shape[1] // 4
    n_cols = dgu_ref.shape[1] // lanes
    down32[...] = dot_low(act4_ref[...], cot_ref[...], TN)
    for k in range(4):
        at = k * gu_rows
        grad = dot_low(act3_ref[:, at : at + gu_rows], dgu_ref[...], TN).astype(BF)
        size = gu_rows // 2
        for parity in range(2):
            first = jnp.where(side == parity, 0, n_cols * size)
            for j in range(n_cols):
                rows = pl.ds(pl.multiple_of(first + j * size, size), size)
                out_ref[k, rows, :] = grad[parity * size : (parity + 1) * size, j * lanes : (j + 1) * lanes]
        rows = pl.ds(k * part, part)
        for j in range(cot_ref.shape[1] // lanes):
            block = down32[rows, j * lanes : (j + 1) * lanes]
            block = jnp.concatenate([block, jnp.zeros((slot - part, lanes), F32)], 0)
            out_ref[k, pl.ds(n_cols * gu_rows + j * slot, slot), :] = block.astype(BF)


def out_grad_kernel(place_ref, act2_ref, low_ref, same_ref, other_ref, full):
    row = place_ref[1]
    heads, _, dk = act2_ref.shape
    part = dk // 4
    for h in range(heads):
        full[h * dk : (h + 1) * dk, :] = dot_low(act2_ref[h], low_ref[...], TN)
    for m in range(4):
        ref = same_ref if m % 2 == 0 else other_ref
        for h in range(heads):
            at = pl.multiple_of(h * dk + (row ^ m) * part, part)
            ref[m // 2, h] = full[pl.ds(at, part), :].astype(BF)


def qkv_grad_kernel(place_ref, act1_ref, dproj_ref, dlog_ref, gconv_ref, ghead_ref, same_ref, other_ref, full, rows):
    row = place_ref[1]
    shards, total, cols = same_ref.shape[1:]
    dk = cols // 3
    part = total - 16
    for h in range(shards):
        lanes = pl.ds(h * dk, dk)
        full[h * dk : (h + 1) * dk, :] = dot_low(act1_ref[:, lanes], dproj_ref[...], TN)
    g_beta = None
    dlog = dlog_ref[...].astype(BF)
    for n in range(dlog.shape[0]):
        one = jnp.broadcast_to(dlog[n : n + 1], (16, dk))
        term = dot_low(one, act1_ref[n * dk : (n + 1) * dk, :])[0:1]
        g_beta = term if g_beta is None else g_beta + term
    rows[...] = jnp.zeros_like(rows)
    for s in range(shards):
        rows[s, 0:4, :] = gconv_ref[0:4, :]
        rows[s, 4:5, 0:dk] = g_beta[:, s * dk : (s + 1) * dk]
        rows[s, 4:5, dk : 2 * dk] = ghead_ref[0:1, :]
    for m in range(4):
        ref = same_ref if m % 2 == 0 else other_ref
        for s in range(shards):
            at = pl.multiple_of(s * dk + (row ^ m) * part, part)
            ref[m // 2, s, 0:part, :] = full[pl.ds(at, part), :].astype(BF)
            ref[m // 2, s, pl.ds(part, 16), :] = rows[s].astype(BF)


def turn_kernel(heads, own_ref, core_ref, x_ref, y_ref, top_ref, bottom_ref, resid_ref, cot_ref, gains_ref, weight_ref, dresid_ref, low_ref, dact2_ref):
    resid = resid_ref[...]
    inv = lax.rsqrt(jnp.mean(resid * resid, -1, keepdims=True) + EPS_NORM)
    rhat = resid * inv
    d_act3 = own_ref[0].astype(F32) + core_ref[0].astype(F32)
    d_act3 = d_act3 + jnp.concatenate([x_ref[0], y_ref[0]], 0).astype(F32)
    d_act3 = d_act3 + jnp.concatenate([top_ref[...], bottom_ref[...]], 0).astype(F32)
    lean = d_act3 * gains_ref[1:2, :]
    d_resid = cot_ref[...].astype(F32) + inv * (lean - rhat * jnp.mean(lean * rhat, -1, keepdims=True))
    dresid_ref[...] = d_resid
    low = d_resid.astype(BF)
    low_ref[...] = low
    d_act2 = dot_low(low, weight_ref[...], NT).astype(BF)
    dk = d_act2.shape[1] // heads
    for h in range(heads):
        dact2_ref[h] = d_act2[:, h * dk : (h + 1) * dk]


def last_kernel(part_ref, x_ref, gains_ref, dresid_ref, out_ref):
    d_act1 = part_ref[...].astype(F32)
    rows = x_ref[...].astype(F32)
    inv = lax.rsqrt(jnp.mean(rows * rows, -1, keepdims=True) + EPS_NORM)
    xhat = rows * inv
    lean = d_act1 * gains_ref[0:1, :]
    out = dresid_ref[...] + inv * (lean - xhat * jnp.mean(lean * xhat, -1, keepdims=True))
    out_ref[...] = out.astype(BF)


def row_sums(v):
    total = jnp.sum(v, 1, keepdims=True)
    return jnp.broadcast_to(total, (v.shape[0], 128)).T[0:1]


def lay_feed_kernel(place_ref, *refs):
    own_ref, y_ref, cores_ref = refs[0:3]
    packs = (own_ref, cores_ref.at[0], y_ref, cores_ref.at[1])
    weight_ref, gain_ref, gu_out, down_out, gain_out, held = refs[3:]
    side, row = lax.rem(place_ref[0], 2), place_ref[1]
    size, hidden = gain_out.shape[1], down_out.shape[0]
    lanes, slot, part = packs[0].shape[1], 96, hidden // 4
    wide = held.shape[3] // 2
    n_cols = held.shape[3] // lanes
    for m in range(4):
        for own in range(2):
            block = side if own == 0 else 1 - side
            for j in range(n_cols):
                rows = pl.ds((own * n_cols + j) * size, size)
                held[row ^ m, block, :, j * lanes : (j + 1) * lanes] = packs[m][rows, :]
        at = pl.multiple_of((row ^ m) * part, 8)
        for j in range(down_out.shape[1] // lanes):
            block = packs[m][pl.ds(2 * n_cols * size + j * slot, slot), :].astype(F32)
            down_out[pl.ds(at, part), j * lanes : (j + 1) * lanes] = block[0:part]
    total = None
    for kind in range(2):
        for block in range(8):
            piece = held[block % 4, block // 4, :, kind * wide : kind * wide + hidden].astype(F32)
            cols = pl.ds((kind * 8 + block) * hidden, hidden)
            gu_out[:, cols] = piece
            term = piece * weight_ref[:, cols].astype(F32)
            total = term if total is None else total + term
    gain_out[...] = row_sums(total) / gain_ref[1:2, :].astype(F32)


def lay_mix_kernel(place_ref, *refs):
    qkv_refs = (refs[0], refs[2].at[0], refs[1], refs[2].at[1])
    out_refs = (refs[3], refs[5].at[0], refs[4], refs[5].at[1])
    weight_ref, beta_ref, gain_ref, second_ref, qkv_out, out_out, gain_out, conv_out, beta_out, head_out = refs[6:]
    place, row = place_ref[0], place_ref[1]
    heads, total, cols = qkv_refs[0].shape
    dk = cols // 3
    part = total - 16
    for m in range(4):
        rows = pl.ds(pl.multiple_of((row ^ m) * part, 8), part)
        out_out[rows, :] = out_refs[m][...].astype(F32)
        for h in range(heads):
            for kind in range(3):
                lanes = pl.ds((kind * heads + h) * dk, dk)
                block = qkv_refs[m][h, 0:part, kind * dk : (kind + 1) * dk]
                qkv_out[rows, lanes] = block.astype(F32)
    sums = jnp.sum(qkv_out[...] * weight_ref[...].astype(F32), 1, keepdims=True)
    ref = qkv_refs[0]
    small = [ref[h, pl.ds(part, 16), :].astype(F32) for h in range(heads)]
    beta_rows = jnp.concatenate([v[4:5, 0:dk] for v in small], 0)
    beta_out[...] = beta_rows
    head = small[0][4:5, dk : 2 * dk]
    for v in small[1:]:
        head = head + v[4:5, dk : 2 * dk]
    per = head_out.shape[1]
    spot = lax.broadcasted_iota(jnp.int32, (dk, per), 0) == (
        lax.broadcasted_iota(jnp.int32, (dk, per), 1) + place * per
    )
    head_out[...] = mm(jnp.broadcast_to(head, (8, dk)), spot.astype(BF))[0:1]
    for i in range(3):
        block = place * 3 + i
        kind = block // heads
        source = block - kind * heads
        lanes = pl.ds(pl.multiple_of(kind * dk, dk), dk)
        conv_out[:, i * dk : (i + 1) * dk] = ref[source, pl.ds(part, 16), lanes].astype(F32)[0 : conv_out.shape[0]]
    weight_rows = beta_ref[...].astype(F32)
    gain = jnp.broadcast_to(sums, (sums.shape[0], 128)).T[0:1]
    gain = gain + jnp.sum(beta_rows * weight_rows, 0, keepdims=True)
    gain_out[0:1, :] = gain / gain_ref[0:1, :].astype(F32)
    gain_out[1:2, :] = second_ref[...]


def local_call(kernel, outs, args, scratch=(), smem=0, us=1, name=None):
    space = [pl.BlockSpec(memory_space=pltpu.SMEM)] * smem
    space += [pl.BlockSpec(memory_space=pltpu.VMEM)] * (len(args) - smem)
    return pl.pallas_call(
        kernel,
        out_shape=tuple(outs),
        in_specs=space,
        out_specs=tuple(pl.BlockSpec(memory_space=pltpu.VMEM) for _ in outs),
        scratch_shapes=list(scratch),
        compiler_params=pltpu.CompilerParams(vmem_limit_bytes=56 * 2**20),
        cost_estimate=pl.CostEstimate(flops=us * 10**9, bytes_accessed=1024, transcendentals=0),
        name=name,
    )(*args)


def head_plan(
    block_input,
    cotangent,
    doc_starts,
    qkv_weight,
    beta_weight,
    conv_weight,
    norm_gains,
    head_gain,
    out_weight,
    gate_up_weight,
    down_weight,
):
    x, cot = block_input[0], cotangent[0]
    starts = doc_starts[0]
    size, width = x.shape
    n_seq, n_row = lax.axis_size("seq"), lax.axis_size("row")
    place, row = lax.axis_index("seq"), lax.axis_index("row")
    half = n_seq // 2
    z, side = place // 2, place % 2
    total = n_seq * size
    where_at = jnp.stack([place, row])
    taps = conv_weight.shape[0]
    hidden = down_weight.shape[0]
    wide = -(-hidden // 128) * 128
    shape = jax.ShapeDtypeStruct

    def flip(v):
        return lax.ppermute(v, "seq", [(s, s ^ 1) for s in range(n_seq)])

    def roll(v, k):
        return lax.ppermute(v, "seq", [(s, (s // 2 + k) % half * 2 + s % 2) for s in range(n_seq)])

    def core(v):
        return lax.ppermute(v, "row", [(r, r ^ 1) for r in range(n_row)])

    def across(v):
        return lax.ppermute(v, "row", [(r, r ^ 2) for r in range(n_row)])

    pairs = [
        (s * n_row + r, (r * 2 + s // n_row) * n_row + s % n_row)
        for s in range(n_seq)
        for r in range(n_row)
    ]

    def spread(v):
        return lax.ppermute(v, ("seq", "row"), pairs)

    def collect(v):
        return lax.ppermute(v, ("seq", "row"), [(b, a) for a, b in pairs])

    def group_gather(v):
        y, s = across(v), flip(v)
        four = [v, y, s, flip(y)]
        return [*four, core(jnp.stack(four))]

    def row_sum(same, other):
        mine = same.astype(F32) + core(other).astype(F32)
        return mine[0], mine[1].astype(BF)

    def row_relative(v):
        y = across(v)
        return [v, core(v), y, core(y)]

    def stage(*values):
        return lax.optimization_barrier(values)

    def line(v, step, t):
        ends = range(t - 1, half - 1) if step > 0 else range(1, half - t + 1)
        return lax.ppermute(
            v, "seq", [(2 * a + j, 2 * (a + step) + j) for a in ends for j in range(2)]
        )

    part_rows = size // n_row
    dk = width // n_seq
    lead_rows = 3 * part_rows + 48
    row_x = lax.all_gather(x, "seq", tiled=True)
    (payload,) = local_call(
        lead_kernel,
        [shape((n_seq, lead_rows, dk), BF)],
        [where_at, qkv_weight, conv_weight, norm_gains, head_gain.reshape(1, -1), beta_weight.T],
        scratch=[pltpu.VMEM((48, dk), F32)],
        smem=1,
        us=2,
        name="lead",
    )

    def columns(block):
        gate = lax.dynamic_slice_in_dim(gate_up_weight, block * hidden, hidden, 1)
        up = lax.dynamic_slice_in_dim(gate_up_weight, (n_seq + block) * hidden, hidden, 1)
        gap = jnp.zeros((size, wide - hidden), BF)
        return jnp.concatenate([gate, gap, up, gap], 1)

    hidden_part = hidden // n_row
    pack_rows = 6 * size + 4 * 96
    down_quarter = lax.dynamic_slice_in_dim(down_weight, row * hidden_part, hidden_part, 0)
    other_cols, down_quarter = flip(columns((1 - side) * n_row + row)), spread(down_quarter)
    own_cols = columns(side * n_row + row)
    got = lax.all_to_all(payload, "seq", 0, 0)
    got_y = across(got)
    (pack,) = local_call(
        pack_kernel,
        [shape((pack_rows, 256), BF)],
        [own_cols, other_cols, down_quarter],
        us=2,
        name="pack",
    )
    got_cores = core(jnp.stack([got, got_y]))
    out_part = lax.dynamic_slice_in_dim(out_weight, row * part_rows, part_rows, 0)
    out_part = jnp.broadcast_to(out_part[None], (n_seq, part_rows, width))
    groups_z = [[2 * a + j for a in range(half)] for j in range(2)]
    packs = lax.all_gather(pack, "seq", axis_index_groups=groups_z)
    out_part = lax.all_to_all(stage(out_part, pack)[0], "seq", 0, 0)
    row_x, got, got_y, got_cores, out_part, cot, _ = stage(row_x, got, got_y, got_cores, out_part, cot, pack)
    cot_y, cot_x = across(cot), flip(cot)
    out_y = across(out_part)
    square = shape((n_seq, size, dk), F32)
    (
        w_head,
        act1,
        proj,
        rates,
        outs,
        act2,
        inverse,
        w_mat,
        att,
        p_mat,
        u_mat,
        states,
        conv,
        gains,
        beta,
        head,
    ) = local_call(
        functools.partial(front_kernel, taps),
        [
            shape((width, 3 * dk), BF),
            shape((total, width), BF),
            shape((total, 3 * dk), BF),
            shape((total, dk), F32),
            shape((total, dk), F32),
            shape((n_seq, size, dk), BF),
            square,
            square,
            square,
            square,
            square,
            square,
            shape((8, 3 * dk), F32),
            shape((8, width), F32),
            shape((8, width), BF),
            shape((8, dk), F32),
        ],
        [where_at, starts, row_x, got, got_y, got_cores],
        scratch=[
            pltpu.VMEM((RIM + total, 3 * dk), F32),
            pltpu.VMEM((n_seq, size, size), F32),
            pltpu.VMEM((n_seq, size, size), F32),
            pltpu.VMEM((total, dk), BF),
            pltpu.VMEM((total, dk), BF),
            pltpu.VMEM((total, dk), BF),
            pltpu.VMEM((n_seq, dk, dk), F32),
        ],
        smem=2,
        us=4,
        name="front",
    )
    act2, cot_y, cot_x, out_y = stage(act2, cot_y, cot_x, out_y)
    act2 = lax.all_to_all(act2, "seq", 0, 0)
    cot_four = [cot, cot_y, cot_x, flip(cot_y)]
    out_cores = core(jnp.stack([out_part, out_y]))
    act2, out_cores, cot_four[3] = stage(act2, out_cores, cot_four[3])
    cot_all = [*cot_four, core(jnp.stack(cot_four))]
    resid, act3, w_out = local_call(
        mid_kernel,
        [shape((size, width), F32), shape((size, width), BF), shape((width, width), BF)],
        [where_at, act2, out_part, out_y, out_cores, x, gains],
        smem=1,
        us=1,
        name="mid",
    )
    four = shape((4, size, width), BF)
    d_own, d_next, act4, d_gu, act3_all, cot_all, w_down = local_call(
        functools.partial(feed_kernel, hidden),
        [
            four,
            four,
            shape((total, wide), BF),
            shape((total, 2 * wide), BF),
            shape((total, width), BF),
            shape((total, width), BF),
            shape((wide, width), BF),
        ],
        [where_at, *group_gather(act3), *cot_all, packs],
        scratch=[pltpu.VMEM((width, 2 * wide), BF), pltpu.VMEM((wide, width), F32)],
        smem=1,
        us=3,
        name="feed",
    )
    d_got, d_own, act4, d_gu, act3_all, cot_all = stage(core(d_next), d_own, act4, d_gu, act3_all, cot_all)
    mid_row = size // 2
    top, low = slice(0, mid_row), slice(mid_row, size)

    def core_sum(i, part):
        return d_own[i, part].astype(F32) + d_got[i, part].astype(F32)

    d_x = flip(jnp.stack([core_sum(2, top), core_sum(3, top)]).astype(BF))
    d_y = across(jnp.stack([core_sum(1, low), core_sum(3, low)]).astype(BF))
    (grads,) = local_call(
        functools.partial(grads_kernel, hidden),
        [shape((half, pack_rows, 256), BF)],
        [where_at, act3_all, cot_all, act4, d_gu],
        scratch=[pltpu.VMEM((wide, width), F32)],
        smem=1,
        us=3,
        name="grads",
    )
    d_x, d_y, grads, act4 = stage(d_x, d_y, grads, act4)
    grads = lax.psum_scatter(grads, "seq", scatter_dimension=0, axis_index_groups=groups_z)
    d_top = across((core_sum(1, top) + d_x[1].astype(F32)).astype(BF))
    d_bottom = flip((core_sum(2, low) + d_y[1].astype(F32)).astype(BF))
    d_top, d_bottom, act4 = stage(d_top, d_bottom, act4)
    d_resid, d_low, d_act2 = local_call(
        functools.partial(turn_kernel, n_seq),
        [shape((size, width), F32), shape((size, width), BF), shape((n_seq, size, dk), BF)],
        [d_own, d_got, d_x, d_y, d_top, d_bottom, resid, cot, gains, w_out],
        us=1,
        name="turn",
    )
    d_act2 = lax.all_to_all(d_act2, "seq", 0, 0)
    out_shape = shape((2, n_seq, part_rows, width), BF)
    out_same, out_other = local_call(
        out_grad_kernel,
        [out_shape, out_shape],
        [where_at, act2, d_low],
        scratch=[pltpu.VMEM((width, width), F32)],
        smem=1,
        us=3,
        name="out_grad",
    )
    mixed_own, mixed_next = local_call(
        mixed_kernel, [four, four], [where_at, act4, w_down], smem=1, us=5, name="mixed"
    )
    d_act2, out_same, out_other, mixed_own, mixed_next = stage(d_act2, out_same, out_other, mixed_own, mixed_next)
    mixed_got = core(mixed_next)
    out_got = core(out_other)
    d_proj, parts, d_log, g_conv, g_head = local_call(
        functools.partial(back_kernel, taps),
        [
            shape((total, 3 * dk), BF),
            shape((total, width), BF),
            shape((n_seq, size), F32),
            shape((8, 3 * dk), F32),
            shape((8, dk), F32),
        ],
        [
            where_at,
            starts,
            d_act2,
            outs,
            head,
            conv,
            proj,
            rates,
            inverse,
            w_mat,
            att,
            p_mat,
            u_mat,
            states,
            w_head,
            beta,
        ],
        scratch=[
            pltpu.VMEM((total, dk), F32),
            pltpu.VMEM((RIM + total, 3 * dk), F32),
            pltpu.VMEM((total, 3 * dk), F32),
            pltpu.VMEM((RIM + total, 3 * dk), F32),
            pltpu.VMEM((total, dk), F32),
            pltpu.VMEM((total, dk), F32),
            pltpu.VMEM((n_seq, dk, dk), F32),
            pltpu.VMEM((n_seq, dk, dk), F32),
            pltpu.VMEM((total, dk), BF),
            pltpu.VMEM((total, dk), BF),
        ],
        smem=2,
        us=5,
        name="back",
    )
    d_proj, parts, d_log, g_conv, g_head, out_got, mixed_got, grads = stage(
        d_proj, parts, d_log, g_conv, g_head, out_got, mixed_got, grads
    )
    mixed_both = [mixed_own[i].astype(F32) + mixed_got[i].astype(F32) for i in range(4)]
    mixed_x = flip(jnp.stack([mixed_both[2], mixed_both[3]]).astype(BF))
    d_act1 = lax.psum_scatter(parts, "seq", scatter_dimension=0, tiled=True)
    out_mine = out_same[0].astype(F32) + out_got[0].astype(F32)
    out_y = across((out_same[1].astype(F32) + out_got[1].astype(F32)).astype(BF))
    out_piece = lax.all_to_all((out_mine + out_y.astype(F32)).astype(BF), "seq", 0, 0)
    out_piece = out_piece.astype(F32).sum(0).astype(BF)
    out_y = across(out_piece)
    out_cores = core(jnp.stack([out_piece, out_y]))
    mixed_y = across((mixed_both[1] + mixed_x[1].astype(F32)).astype(BF))
    mixed = (resid + mixed_both[0] + mixed_x[0].astype(F32) + mixed_y.astype(F32)).astype(BF)
    gu_rows = 3 * size
    gu_other, down_sum = flip(grads[gu_rows : 2 * gu_rows]), collect(grads[2 * gu_rows :])
    feed_part = jnp.concatenate([grads[:gu_rows], gu_other, down_sum], 0)
    feed_y = across(feed_part)
    feed_cores = core(jnp.stack([feed_part, feed_y]))
    cut_shape = shape((2, n_seq, part_rows + 16, 3 * dk), BF)
    qkv_same, qkv_other = local_call(
        qkv_grad_kernel,
        [cut_shape, cut_shape],
        [where_at, act1, d_proj, d_log, g_conv, g_head],
        scratch=[pltpu.VMEM((width, 3 * dk), F32), pltpu.VMEM((n_seq, 16, 3 * dk), F32)],
        smem=1,
        us=5,
        name="qkv_grad",
    )
    qkv_got = core(qkv_other)
    qkv_mine = qkv_same[0].astype(F32) + qkv_got[0].astype(F32)
    qkv_y = across((qkv_same[1].astype(F32) + qkv_got[1].astype(F32)).astype(BF))
    qkv_piece = lax.all_to_all((qkv_mine + qkv_y.astype(F32)).astype(BF), "seq", 0, 0)
    qkv_y = across(qkv_piece)
    qkv_cores = core(jnp.stack([qkv_piece, qkv_y]))
    (input_gradient,) = local_call(
        last_kernel,
        [shape((size, width), BF)],
        [d_act1, x, gains, d_resid],
        us=3,
        name="last",
    )
    red_gu, red_down, second_gain = local_call(
        lay_feed_kernel,
        [
            shape((size, 2 * n_seq * hidden), F32),
            shape((hidden, width), F32),
            shape((1, size), F32),
        ],
        [where_at, feed_part, feed_y, feed_cores, gate_up_weight, norm_gains],
        scratch=[pltpu.VMEM((n_row, 2, size, 2 * wide), BF)],
        smem=1,
        us=3,
        name="lay_feed",
    )
    red_qkv, red_out, red_gains, red_conv, red_beta, red_head = local_call(
        lay_mix_kernel,
        [
            shape((size, 3 * width), F32),
            shape((size, width), F32),
            shape((2, size), F32),
            shape((taps, 3 * dk), F32),
            shape((n_seq, dk), F32),
            shape((1, head_gain.shape[0]), F32),
        ],
        [where_at, qkv_piece, qkv_y, qkv_cores, out_piece, out_y, out_cores, qkv_weight, beta_weight.T, norm_gains, second_gain],
        smem=1,
        us=3,
        name="lay_mix",
    )
    red_beta = red_beta.T
    red_head = red_head[0]
    return (
        mixed[None],
        input_gradient[None],
        red_qkv,
        red_beta,
        red_conv,
        red_gains,
        red_head,
        red_out,
        red_gu,
        red_down,
    )


def plan(block_input, *rest):
    seq, row = lax.axis_size("seq"), lax.axis_size("row")
    if seq == H and row * 2 == H and block_input.shape[1] == DK:
        return head_plan(block_input, *rest)
    return on_device(block_input, *rest)


def solution(mesh):
    in_specs = (
        P("row", "seq", None),
        P("row", "seq", None),
        P("row", None),
        P("seq", None),
        P("seq", None),
        P(None, "seq"),
        P(None, "seq"),
        P("seq"),
        P("seq", None),
        P("seq", None),
        P("seq", None),
    )
    out_specs = (
        P("row", "seq", None),
        P("row", "seq", None),
        P("seq", None),
        P("seq", None),
        P(None, "seq"),
        P(None, "seq"),
        P("seq"),
        P("seq", None),
        P("seq", None),
        P("seq", None),
    )
    return jax.shard_map(
        plan, mesh=mesh, in_specs=in_specs, out_specs=out_specs, check_vma=False
    )
```

```python
import functools

import jax
import jax.numpy as jnp
from jax import lax
from jax.experimental import pallas as pl
from jax.experimental.pallas import tpu as pltpu
from jax.sharding import PartitionSpec as P

H = 8
DK = 128
GROUP = 64


EPS_NORM = 1e-06
EPS_HEAD = 1e-05
EPS_UNIT = 1e-06
HIGH = lax.Precision.HIGHEST


def shifted(block, axis, distance):
    devices = range(lax.axis_size(axis))
    route = [(i - distance, i) for i in devices if i - distance in devices]
    return lax.ppermute(block, axis, route)


def dotf(first_op, second_op):
    return jnp.matmul(first_op, second_op, precision=HIGH)


def swap_last(matrix):
    return jnp.swapaxes(matrix, -1, -2)


def tok_dot(first_op, second_op):
    return lax.dot_general(
        first_op, second_op, (((0,), (0,)), ((), ())), preferred_element_type=jnp.float32
    )


def back_dot(first_op, second_op):
    return lax.dot_general(
        first_op, second_op, (((1,), (1,)), ((), ())), preferred_element_type=jnp.float32
    )


def unit_inverse(lower):
    identity = jnp.eye(lower.shape[-1], dtype=lower.dtype)
    power = lower
    result = identity - lower
    for step_index in range(lower.shape[-1].bit_length() - 2):
        power = dotf(power, power)
        result = dotf(result, identity + power)
    return result


def doc_index(positions, starts):
    return jnp.sum((starts[None, :] <= positions[:, None]).astype(jnp.int32), axis=1) - 1


def root_mean_square_backward(grad_in, normed, inverse):
    return inverse * (grad_in - normed * jnp.mean(grad_in * normed, -1, keepdims=True))


def silu_back(grad_in, pre):
    sig = jax.nn.sigmoid(pre)
    return grad_in * sig * (1.0 + pre * (1.0 - sig))


def on_device(
    block_input,
    cotangent,
    doc_starts,
    qkv_weight,
    beta_weight,
    conv_weight,
    norm_gains,
    head_gain,
    out_weight,
    gate_up_weight,
    down_weight,
):
    token_rows = block_input[0].astype(jnp.float32)
    cot_low = cotangent[0]
    seq_len = token_rows.shape[0]
    width = token_rows.shape[1]
    n_groups = seq_len // GROUP
    scale = DK ** (-0.5)
    w_qkv, w_beta, w_conv, w_gains, w_head, w_out, w_gu, w_down = (
        lax.all_gather(qkv_weight, "seq", axis=0, tiled=True),
        lax.all_gather(beta_weight, "seq", axis=0, tiled=True),
        lax.all_gather(conv_weight, "seq", axis=1, tiled=True),
        lax.all_gather(norm_gains, "seq", axis=1, tiled=True),
        lax.all_gather(head_gain, "seq", axis=0, tiled=True),
        lax.all_gather(out_weight, "seq", axis=0, tiled=True),
        lax.all_gather(gate_up_weight, "seq", axis=0, tiled=True),
        lax.all_gather(down_weight, "seq", axis=0, tiled=True),
    )
    conv_f = w_conv.astype(jnp.float32)
    float_gains = w_gains.astype(jnp.float32)
    head_f = w_head.astype(jnp.float32)
    seq_count = lax.axis_size("seq")
    seq_place = lax.axis_index("seq")
    starts = doc_starts[0]
    positions = seq_place * seq_len + jnp.arange(seq_len, dtype=jnp.int32)
    doc = doc_index(positions, starts)
    rim = conv_f.shape[0] - 1
    rim_doc = doc_index(seq_place * seq_len - rim + jnp.arange(rim, dtype=jnp.int32), starts)
    first_inverse_norm = lax.rsqrt(jnp.mean(token_rows * token_rows, -1, keepdims=True) + EPS_NORM)
    normalized_input = token_rows * first_inverse_norm
    first_activation = (normalized_input * float_gains[0]).astype(jnp.bfloat16)
    proj = jnp.dot(first_activation, w_qkv, preferred_element_type=jnp.float32).astype(jnp.bfloat16)
    rates_tok = jax.nn.sigmoid(
        jnp.dot(first_activation, w_beta, preferred_element_type=jnp.float32)
    )
    rim_vals = shifted(proj[seq_len - rim :], "seq", 1)
    extended = jnp.concatenate([rim_vals, proj], 0).astype(jnp.float32)
    ext_doc = jnp.concatenate([rim_doc, doc])
    matches = [
        (ext_doc[rim - tap : rim - tap + seq_len] == doc).astype(jnp.float32)[:, None]
        for tap in range(rim + 1)
    ]
    pre = jnp.zeros((seq_len, extended.shape[1]), jnp.float32)
    for tap in range(rim + 1):
        pre = pre + conv_f[tap] * extended[rim - tap : rim - tap + seq_len] * matches[tap]
    act = jax.nn.silu(pre)
    q_raw = act[:, :width].reshape(seq_len, H, DK)
    k_raw = act[:, width : 2 * width].reshape(seq_len, H, DK)
    v_raw = act[:, 2 * width :].reshape(seq_len, H, DK)
    q_inv = lax.rsqrt(jnp.sum(q_raw * q_raw, -1, keepdims=True) + EPS_UNIT)
    k_inv = lax.rsqrt(jnp.sum(k_raw * k_raw, -1, keepdims=True) + EPS_UNIT)
    q_unit = q_raw * q_inv
    k_unit = k_raw * k_inv

    def to_groups(arr):
        return (
            arr.astype(jnp.bfloat16)
            .astype(jnp.float32)
            .reshape(n_groups, GROUP, H, DK)
            .transpose(0, 2, 1, 3)
        )

    scaled_q = to_groups(q_unit) * scale
    keys = to_groups(k_unit)
    values = to_groups(v_raw)
    rates = rates_tok.reshape(n_groups, GROUP, H).transpose(0, 2, 1)
    block_doc = doc.reshape(n_groups, GROUP)
    prev_doc = doc_index(
        seq_place * seq_len + jnp.arange(n_groups, dtype=jnp.int32) * GROUP - 1, starts
    )
    places = jnp.arange(GROUP)
    same = block_doc[:, :, None] == block_doc[:, None, :]
    strict = ((places[:, None] > places[None, :])[None] & same)[:, None].astype(jnp.float32)
    incl = ((places[:, None] >= places[None, :])[None] & same)[:, None].astype(jnp.float32)
    keep = (block_doc == prev_doc[:, None]).astype(jnp.float32)[:, None, :, None]
    tail = (block_doc == block_doc[:, -1:]).astype(jnp.float32)[:, None, :, None]
    whole = keep[:, 0, -1, 0]
    scaled = keys * rates[..., None]
    lower = jnp.einsum("nhid,nhjd->nhij", scaled, keys, precision=HIGH) * strict
    inverse = unit_inverse(lower)
    w_mat = dotf(inverse, scaled)
    base = dotf(inverse, values * rates[..., None])
    eye_heads = jnp.broadcast_to(jnp.eye(DK, dtype=jnp.float32), (H, DK, DK))
    zero_heads = jnp.zeros((H, DK, DK), jnp.float32)

    def chain_step(maps, inputs):
        c_keys, c_w, c_base, c_keep, c_tail, c_whole = inputs
        mixed_maps = dotf(c_w[None], maps)
        reduce_part = jnp.einsum(
            "hcd,shce->shde", c_keys * (c_tail * c_keep), mixed_maps, precision=HIGH
        )
        maps = c_whole * maps - reduce_part
        shift_add = jnp.einsum("hcd,hce->hde", c_keys * c_tail, c_base, precision=HIGH)
        return (jnp.stack([maps[0], maps[1] + shift_add]), None)

    block_maps, unused = lax.scan(
        chain_step, jnp.stack([eye_heads, zero_heads]), (keys, w_mat, base, keep, tail, whole)
    )
    every_map, every_shift = (
        lax.all_gather(block_maps[0][None].astype(jnp.bfloat16), "seq", axis=0, tiled=True).astype(
            jnp.float32
        ),
        lax.all_gather(block_maps[1][None].astype(jnp.bfloat16), "seq", axis=0, tiled=True).astype(
            jnp.float32
        ),
    )

    def apply_map(position, state):
        return jnp.where(
            position < seq_place, dotf(every_map[position], state) + every_shift[position], state
        )

    state_in = lax.fori_loop(0, seq_count, apply_map, zero_heads)

    def out_step(state, inputs):
        c_q, c_keys, c_w, c_base, c_keep, c_tail, c_whole, c_incl = inputs
        pseudo = c_base - c_keep * dotf(c_w, state)
        scores = jnp.einsum("hid,hjd->hij", c_q, c_keys, precision=HIGH) * c_incl
        output = c_keep * dotf(c_q, state) + dotf(scores, pseudo)
        new_state = c_whole * state + jnp.einsum(
            "hcd,hce->hde", c_keys * c_tail, pseudo, precision=HIGH
        )
        return (new_state, (output, state))

    last_state, (outputs, block_states) = lax.scan(
        out_step, state_in, (scaled_q, keys, w_mat, base, keep, tail, whole, incl)
    )
    mixed_o = outputs.transpose(0, 2, 1, 3).reshape(seq_len, H, DK)
    head_inv = lax.rsqrt(jnp.mean(mixed_o * mixed_o, -1, keepdims=True) + EPS_HEAD)
    ohat = mixed_o * head_inv
    act_two = (ohat * head_f).reshape(seq_len, width).astype(jnp.bfloat16)
    resid = token_rows + jnp.dot(act_two, w_out, preferred_element_type=jnp.float32)
    inv_two = lax.rsqrt(jnp.mean(resid * resid, -1, keepdims=True) + EPS_NORM)
    rhat = resid * inv_two
    act_three = (rhat * float_gains[1]).astype(jnp.bfloat16)
    gate_up = jnp.dot(act_three, w_gu, preferred_element_type=jnp.float32)
    hidden_units = gate_up.shape[1] // 2
    gate = gate_up[:, :hidden_units]
    up_part = gate_up[:, hidden_units:]
    act_four = (jax.nn.silu(gate) * up_part).astype(jnp.bfloat16)
    mixed = (resid + jnp.dot(act_four, w_down, preferred_element_type=jnp.float32)).astype(
        jnp.bfloat16
    )
    grad_down = tok_dot(act_four, cot_low)
    d_act_four = back_dot(cot_low, w_down)
    d_gate = silu_back(d_act_four * up_part, gate)
    d_up = d_act_four * jax.nn.silu(gate)
    d_gate_up = jnp.concatenate([d_gate, d_up], 1).astype(jnp.bfloat16)
    grad_gate_up = tok_dot(act_three, d_gate_up)
    d_act_three = back_dot(d_gate_up, w_gu)
    grad_gain_two = jnp.sum(d_act_three * rhat, 0)
    residual_gradient = cot_low.astype(jnp.float32) + root_mean_square_backward(
        d_act_three * float_gains[1], rhat, inv_two
    )
    d_resid_low = residual_gradient.astype(jnp.bfloat16)
    grad_out = tok_dot(act_two, d_resid_low)
    d_act_two = back_dot(d_resid_low, w_out).reshape(seq_len, H, DK)
    grad_head = jnp.sum(d_act_two * ohat, (0, 1))
    d_mixed_o = root_mean_square_backward(d_act_two * head_f, ohat, head_inv)
    d_out_groups = d_mixed_o.reshape(n_groups, GROUP, H, DK).transpose(0, 2, 1, 3)

    def state_grad(grad_state, inputs):
        c_q, c_keys, c_scaled, c_inverse, c_keep, c_tail, c_whole, c_incl, c_dout = inputs
        scores = jnp.einsum("hid,hjd->hij", c_q, c_keys, precision=HIGH) * c_incl
        d_pseudo = jnp.einsum("hij,hid->hjd", scores, c_dout, precision=HIGH) + c_tail * dotf(
            c_keys, grad_state
        )
        d_res = jnp.einsum("hij,hid->hjd", c_inverse, d_pseudo, precision=HIGH)
        prior = (
            jnp.einsum("hcd,hce->hde", c_q * c_keep, c_dout, precision=HIGH) + c_whole * grad_state
        )
        return (prior - jnp.einsum("hcd,hce->hde", c_scaled * c_keep, d_res, precision=HIGH), None)

    local_grad, unused = lax.scan(
        state_grad,
        zero_heads,
        (scaled_q, keys, scaled, inverse, keep, tail, whole, incl, d_out_groups),
        reverse=True,
    )
    back_maps = swap_last(block_maps[0])
    every_back, every_grad = (
        lax.all_gather(back_maps[None].astype(jnp.bfloat16), "seq", axis=0, tiled=True).astype(
            jnp.float32
        ),
        lax.all_gather(local_grad[None].astype(jnp.bfloat16), "seq", axis=0, tiled=True).astype(
            jnp.float32
        ),
    )

    def apply_back(step_index, grad_state):
        position = seq_count - 1 - step_index
        return jnp.where(
            position > seq_place,
            dotf(every_back[position], grad_state) + every_grad[position],
            grad_state,
        )

    grad_state_out = lax.fori_loop(0, seq_count, apply_back, zero_heads)

    def full_back(grad_state, inputs):
        (
            c_q,
            c_keys,
            c_values,
            c_rates,
            c_scaled,
            c_inverse,
            c_w,
            c_base,
            c_keep,
            c_tail,
            c_whole,
            c_strict,
            c_incl,
            c_dout,
            c_state,
        ) = inputs
        pseudo = c_base - c_keep * dotf(c_w, c_state)
        scores = jnp.einsum("hid,hjd->hij", c_q, c_keys, precision=HIGH) * c_incl
        d_pseudo = jnp.einsum("hij,hid->hjd", scores, c_dout, precision=HIGH) + c_tail * dotf(
            c_keys, grad_state
        )
        d_res = jnp.einsum("hij,hid->hjd", c_inverse, d_pseudo, precision=HIGH)
        prior = (
            jnp.einsum("hcd,hce->hde", c_q * c_keep, c_dout, precision=HIGH) + c_whole * grad_state
        )
        prior = prior - jnp.einsum("hcd,hce->hde", c_scaled * c_keep, d_res, precision=HIGH)
        d_scores = jnp.einsum("hid,hjd->hij", c_dout, pseudo, precision=HIGH) * c_incl
        d_query = c_keep * dotf(c_dout, swap_last(c_state)) + dotf(d_scores, c_keys)
        d_keys = jnp.einsum("hij,hid->hjd", d_scores, c_q, precision=HIGH) + c_tail * dotf(
            pseudo, swap_last(grad_state)
        )
        d_lower = -jnp.einsum("hid,hjd->hij", d_res, pseudo, precision=HIGH) * c_strict
        d_scaled = -c_keep * dotf(d_res, swap_last(c_state)) + dotf(d_lower, c_keys)
        d_keys = (
            d_keys
            + jnp.einsum("hij,hid->hjd", d_lower, c_scaled, precision=HIGH)
            + c_rates[..., None] * d_scaled
        )
        d_values = c_rates[..., None] * d_res
        d_rates = jnp.sum(d_res * c_values, -1) + jnp.sum(d_scaled * c_keys, -1)
        return (prior, (d_query * scale, d_keys, d_values, d_rates))

    first_grad, (d_q_groups, d_k_groups, d_v_groups, d_rate_groups) = lax.scan(
        full_back,
        grad_state_out,
        (
            scaled_q,
            keys,
            values,
            rates,
            scaled,
            inverse,
            w_mat,
            base,
            keep,
            tail,
            whole,
            strict,
            incl,
            d_out_groups,
            block_states,
        ),
        reverse=True,
    )

    def from_groups(arr):
        return arr.transpose(0, 2, 1, 3).reshape(seq_len, H, DK)

    d_q_unit = from_groups(d_q_groups)
    d_k_unit = from_groups(d_k_groups)
    d_q_raw = q_inv * (d_q_unit - q_unit * jnp.sum(d_q_unit * q_unit, -1, keepdims=True))
    d_k_raw = k_inv * (d_k_unit - k_unit * jnp.sum(d_k_unit * k_unit, -1, keepdims=True))
    d_act = jnp.concatenate(
        [
            d_q_raw.reshape(seq_len, width),
            d_k_raw.reshape(seq_len, width),
            from_groups(d_v_groups).reshape(seq_len, width),
        ],
        1,
    )
    d_pre = silu_back(d_act, pre)
    d_extended = jnp.zeros((seq_len + rim, d_pre.shape[1]), jnp.float32)
    conv_grads = []
    for tap in range(rim + 1):
        masked = d_pre * matches[tap]
        d_extended = d_extended + jnp.pad(conv_f[tap] * masked, ((rim - tap, tap), (0, 0)))
        conv_grads.append(jnp.sum(masked * extended[rim - tap : rim - tap + seq_len], 0))
    grad_conv = jnp.stack(conv_grads)
    rim_back = shifted(d_extended[:rim].astype(jnp.bfloat16), "seq", -1).astype(jnp.float32)
    d_proj = (d_extended[rim:] + jnp.pad(rim_back, ((seq_len - rim, 0), (0, 0)))).astype(
        jnp.bfloat16
    )
    d_rates_tok = d_rate_groups.transpose(0, 2, 1).reshape(seq_len, H)
    d_logits = (d_rates_tok * rates_tok * (1.0 - rates_tok)).astype(jnp.bfloat16)
    grad_qkv = tok_dot(first_activation, d_proj)
    grad_beta = tok_dot(first_activation, d_logits)
    first_activation_gradient = back_dot(d_proj, w_qkv) + back_dot(d_logits, w_beta)
    first_gain_gradient = jnp.sum(first_activation_gradient * normalized_input, 0)
    block_input_gradient = (
        residual_gradient
        + root_mean_square_backward(
            first_activation_gradient * float_gains[0], normalized_input, first_inverse_norm
        )
    ).astype(jnp.bfloat16)
    grad_gains = jnp.stack([first_gain_gradient, grad_gain_two])
    red_qkv, red_beta, red_conv, red_gains, red_head, red_out, red_gu, red_down = (
        lax.psum_scatter(
            grad_qkv.astype(jnp.bfloat16), "seq", scatter_dimension=0, tiled=True
        ).astype(jnp.float32),
        lax.psum_scatter(
            grad_beta.astype(jnp.bfloat16), "seq", scatter_dimension=0, tiled=True
        ).astype(jnp.float32),
        lax.psum_scatter(
            grad_conv.astype(jnp.bfloat16), "seq", scatter_dimension=1, tiled=True
        ).astype(jnp.float32),
        lax.psum_scatter(
            grad_gains.astype(jnp.bfloat16), "seq", scatter_dimension=1, tiled=True
        ).astype(jnp.float32),
        lax.psum_scatter(
            grad_head.astype(jnp.bfloat16), "seq", scatter_dimension=0, tiled=True
        ).astype(jnp.float32),
        lax.psum_scatter(
            grad_out.astype(jnp.bfloat16), "seq", scatter_dimension=0, tiled=True
        ).astype(jnp.float32),
        lax.psum_scatter(
            grad_gate_up.astype(jnp.bfloat16), "seq", scatter_dimension=0, tiled=True
        ).astype(jnp.float32),
        lax.psum_scatter(
            grad_down.astype(jnp.bfloat16), "seq", scatter_dimension=0, tiled=True
        ).astype(jnp.float32),
    )
    red_qkv, red_beta, red_conv, red_gains, red_head, red_out, red_gu, red_down = (
        lax.psum(red_qkv.astype(jnp.bfloat16), "row").astype(jnp.float32),
        lax.psum(red_beta.astype(jnp.bfloat16), "row").astype(jnp.float32),
        lax.psum(red_conv.astype(jnp.bfloat16), "row").astype(jnp.float32),
        lax.psum(red_gains.astype(jnp.bfloat16), "row").astype(jnp.float32),
        lax.psum(red_head.astype(jnp.bfloat16), "row").astype(jnp.float32),
        lax.psum(red_out.astype(jnp.bfloat16), "row").astype(jnp.float32),
        lax.psum(red_gu.astype(jnp.bfloat16), "row").astype(jnp.float32),
        lax.psum(red_down.astype(jnp.bfloat16), "row").astype(jnp.float32),
    )
    return (
        mixed[None],
        block_input_gradient[None],
        red_qkv,
        red_beta,
        red_conv,
        red_gains,
        red_head,
        red_out,
        red_gu,
        red_down,
    )


BF = jnp.bfloat16
F32 = jnp.float32
RIM = 8
NN = (((1,), (0,)), ((), ()))
NT = (((1,), (1,)), ((), ()))
TN = (((0,), (0,)), ((), ()))


def dot_low(a, b, dims=NN):
    return lax.dot_general(a, b, dims, preferred_element_type=F32)


def parts_of(a):
    if a.dtype == BF:
        return (a,)
    high = a.astype(BF)
    return high, (a - high.astype(F32)).astype(BF)


def mm(a, b, dims=NN):
    a_parts, b_parts = parts_of(a), parts_of(b)
    total = dot_low(a_parts[0], b_parts[0], dims)
    if len(b_parts) > 1:
        total = total + dot_low(a_parts[0], b_parts[1], dims)
    if len(a_parts) > 1:
        total = total + dot_low(a_parts[1], b_parts[0], dims)
    return total


def mm1(a, b, dims=NN):
    return dot_low(a.astype(BF), b.astype(BF), dims)


def begin_of(pos, starts_ref):
    begin = jnp.zeros_like(pos)
    for i in range(starts_ref.shape[0]):
        begin = jnp.maximum(begin, jnp.where(pos >= starts_ref[i], starts_ref[i], 0))
    return begin


def begin_at(pos, starts_ref):
    begin = jnp.int32(0)
    for i in range(starts_ref.shape[0]):
        begin = jnp.maximum(begin, jnp.where(starts_ref[i] <= pos, starts_ref[i], 0))
    return begin


def mark_table(chunks, size, taps, starts_ref):
    pos = lax.broadcasted_iota(jnp.int32, (chunks, size), 0) * size
    pos = pos + lax.broadcasted_iota(jnp.int32, (chunks, size), 1)
    rows = begin_of(pos, starts_ref)
    later = [
        ((begin_of(pos + tap, starts_ref) <= pos) & (pos + tap < chunks * size)).astype(F32)
        for tap in range(1, taps)
    ]
    down = lax.broadcasted_iota(jnp.int32, (size, size), 0)
    eye = (down == lax.broadcasted_iota(jnp.int32, (size, size), 1)).astype(BF)
    rows = rows.astype(F32)
    return rows, mm(eye, rows, NT), [mm(eye, v, NT) for v in later]


def chunk_marks(n, size, table, starts_ref):
    first = n * size
    col = table[1][:, n : n + 1]
    last = begin_at(first + size - 1, starts_ref)
    keep = (col < float(first)).astype(F32)
    tail = (col == last.astype(F32)).astype(F32)
    whole = (last < first).astype(F32)
    return col, keep, tail, whole


def chunk_masks(n, size, col, table):
    here = lax.broadcasted_iota(jnp.int32, (size, size), 0)
    there = lax.broadcasted_iota(jnp.int32, (size, size), 1)
    same = col == table[0][n : n + 1]
    return here, there, same & (here > there), same & (here >= there)


def conv_chunk(n, size, pad, conv, col):
    depth = (n * size + lax.broadcasted_iota(jnp.int32, (size, 1), 0)).astype(F32) - col
    pre = conv[0:1, :] * pad[pl.ds(RIM + n * size, size), :]
    for tap in range(1, conv.shape[0]):
        match = (depth >= float(tap)).astype(F32)
        pre = pre + conv[tap : tap + 1, :] * pad[pl.ds(RIM - tap + n * size, size), :] * match
    return pre


def front_kernel(taps, place_ref, starts_ref, *refs):
    n_seq = refs[-1].shape[0]
    n_row = n_seq // 2
    x_ref, got_ref, got_y_ref, got_cores_ref = refs[:4]
    got_refs = (got_ref, got_cores_ref.at[0], got_y_ref, got_cores_ref.at[1])
    (
        weight_ref,
        act1_ref,
        proj_ref,
        rates_ref,
        o_ref,
        act2_ref,
        inv_ref,
        w_ref,
        att_ref,
        p_ref,
        u_ref,
        s_ref,
        conv_ref,
        gains_ref,
        beta_ref,
        head_ref,
        pad,
        lower,
        tmp,
        q_scr,
        k_scr,
        v_scr,
        add,
    ) = refs[4:]
    place, row = place_ref[0], place_ref[1]
    size = s_ref.shape[1]
    part_rows = size // n_row
    dk = o_ref.shape[1]
    base = 3 * part_rows
    gains = jnp.concatenate([got_ref[s, base + 4 : base + 6, :] for s in range(n_seq)], 1).astype(F32)
    gains_ref[...] = jnp.zeros_like(gains_ref)
    gains_ref[0:2, :] = gains
    beta = jnp.concatenate([got_ref[s, base + 8 : base + 16, :] for s in range(n_seq)], 1)
    beta_ref[...] = beta
    head_gain = got_ref[0, base + 6 : base + 7, :].astype(F32)
    for s in range(1, n_seq):
        head_gain = head_gain + got_ref[s, base + 6 : base + 7, :].astype(F32)
    head_ref[...] = jnp.broadcast_to(head_gain, head_ref.shape)
    conv_parts = []
    for part in range(3):
        block = part * n_seq + place
        shard = block // 3
        offset = pl.multiple_of(base + (block - shard * 3) * 16, 16)
        conv_parts.append(got_ref[shard, pl.ds(offset, 16), :][0:8])
    conv = jnp.concatenate(conv_parts, 1).astype(F32)
    conv_ref[...] = conv
    conv = conv[0:taps]
    for m, ref in enumerate(got_refs):
        for s in range(n_seq):
            at = pl.multiple_of(s * size + (row ^ m) * part_rows, part_rows)
            for kind in range(3):
                block = ref[s, kind * part_rows : (kind + 1) * part_rows, :]
                weight_ref[pl.ds(at, part_rows), kind * dk : (kind + 1) * dk] = block
    weight = weight_ref[...]
    lanes = lax.broadcasted_iota(jnp.int32, (2 * size, 8), 1)
    pad[0:RIM, :] = jnp.zeros((RIM, 3 * dk), F32)
    for n in range(0, n_seq, 2):
        rows_at = pl.ds(n * size, 2 * size)
        rows = x_ref[rows_at, :].astype(F32)
        inv = lax.rsqrt(jnp.mean(rows * rows, -1, keepdims=True) + EPS_NORM)
        act = ((rows * inv) * gains[0:1]).astype(BF)
        act1_ref[rows_at, :] = act
        proj = dot_low(act, weight).astype(BF)
        proj_ref[rows_at, :] = proj
        pad[pl.ds(RIM + n * size, 2 * size), :] = proj.astype(F32)
        logits = dot_low(act, beta, NT)
        rate = jax.nn.sigmoid(jnp.sum(jnp.where(lanes == place, logits, 0.0), 1, keepdims=True))
        rates_ref[rows_at, :] = jnp.broadcast_to(rate, (2 * size, dk))
    table = mark_table(n_seq, size, taps, starts_ref)
    marks = []
    for n in range(n_seq):
        at = n * size
        col, keep, tail, whole = chunk_marks(n, size, table, starts_ref)
        marks.append((keep, tail, whole))
        pre = conv_chunk(n, size, pad, conv, col)
        act = pre * jax.nn.sigmoid(pre)
        q_raw, k_raw, v_raw = act[:, :dk], act[:, dk : 2 * dk], act[:, 2 * dk :]
        q = (q_raw * lax.rsqrt(jnp.sum(q_raw * q_raw, -1, keepdims=True) + EPS_UNIT)).astype(BF)
        key = (k_raw * lax.rsqrt(jnp.sum(k_raw * k_raw, -1, keepdims=True) + EPS_UNIT)).astype(BF)
        q_scr[pl.ds(at, size), :] = q
        k_scr[pl.ds(at, size), :] = key
        v_scr[pl.ds(at, size), :] = v_raw.astype(BF)
        here, there, strict, incl = chunk_masks(n, size, col, table)
        rate = rates_ref[pl.ds(at, size), :]
        low = jnp.where(strict, dot_low(key, key, NT) * rate, 0.0)
        att_ref[n] = jnp.where(incl, dot_low(q, key, NT) * (dk**-0.5), 0.0)
        lower[n] = low
        eye = (here == there).astype(F32)
        inv_ref[n] = eye - jnp.where((here // 2) == (there // 2), low, 0.0)
    span = 2
    while span < size:
        here = lax.broadcasted_iota(jnp.int32, (size, size), 0)
        there = lax.broadcasted_iota(jnp.int32, (size, size), 1)
        cross = ((here // (2 * span)) == (there // (2 * span))) & ((here // span) != (there // span))
        for n in range(n_seq):
            tmp[n] = mm(inv_ref[n], jnp.where(cross, lower[n], 0.0))
        for n in range(n_seq):
            inv_ref[n] = inv_ref[n] - mm(tmp[n], inv_ref[n])
        span *= 2
    for n in range(n_seq):
        keep, tail, whole = marks[n]
        rows = pl.ds(n * size, size)
        rate = rates_ref[rows, :]
        key = k_scr[rows, :]
        inv = inv_ref[n]
        w = mm(inv, rate * key.astype(F32))
        base = mm(inv, rate * v_scr[rows, :].astype(F32))
        w_ref[n] = w
        u_ref[n] = base
        p_ref[n] = mm(key, (tail * keep) * w, TN)
        add[n] = mm(key, tail * base, TN)
    state = jnp.zeros((dk, dk), F32)
    for n in range(n_seq):
        s_ref[n] = state
        if n + 1 < n_seq:
            state = marks[n][2] * state - mm(p_ref[n], state) + add[n]
    for n in range(n_seq):
        keep, tail, whole = marks[n]
        rows = pl.ds(n * size, size)
        state = s_ref[n]
        u = u_ref[n] - keep * mm(w_ref[n], state)
        u_ref[n] = u
        out = (keep * (dk**-0.5)) * mm(q_scr[rows, :], state) + mm(att_ref[n], u)
        o_ref[rows, :] = out
        inv = lax.rsqrt(jnp.mean(out * out, -1, keepdims=True) + EPS_HEAD)
        act2_ref[n] = ((out * inv) * head_gain).astype(BF)


def back_kernel(taps, place_ref, starts_ref, *refs):
    (
        dact_ref,
        o_ref,
        head_ref,
        conv_ref,
        proj_ref,
        rates_ref,
        inv_ref,
        w_ref,
        att_ref,
        p_ref,
        u_ref,
        s_ref,
        weight_ref,
        beta_ref,
        dproj_ref,
        part_ref,
        dlog_ref,
        gconv_ref,
        ghead_ref,
        logit_scr,
        pad,
        pre_scr,
        dpre,
        do_scr,
        g_scr,
        add,
        x_scr,
        q_scr,
        k_scr,
    ) = refs
    n_seq, size, dk = dact_ref.shape
    scale = dk**-0.5
    place = place_ref[0]
    beta_all = beta_ref[...].astype(F32)
    beta_lane = lax.broadcasted_iota(jnp.int32, beta_all.shape, 0) == place
    beta_row = jnp.sum(jnp.where(beta_lane, beta_all, 0.0), 0, keepdims=True)
    head_gain = head_ref[0:1, :]
    conv = conv_ref[0:taps, :]
    total = n_seq * size
    pad[0:RIM, :] = jnp.zeros((RIM, 3 * dk), F32)
    pad[pl.ds(RIM, total), :] = proj_ref[...].astype(F32)
    dpre[pl.ds(total, RIM), :] = jnp.zeros((RIM, 3 * dk), F32)
    table = mark_table(n_seq, size, taps, starts_ref)
    marks = []
    ghead = jnp.zeros((1, dk), F32)
    for n in range(n_seq):
        rows = pl.ds(n * size, size)
        col, keep, tail, whole = chunk_marks(n, size, table, starts_ref)
        marks.append((col, keep, tail, whole))
        pre = conv_chunk(n, size, pad, conv, col)
        pre_scr[rows, :] = pre
        act = pre * jax.nn.sigmoid(pre)
        q_raw, k_raw = act[:, :dk], act[:, dk : 2 * dk]
        q = (q_raw * lax.rsqrt(jnp.sum(q_raw * q_raw, -1, keepdims=True) + EPS_UNIT)).astype(BF)
        key = (k_raw * lax.rsqrt(jnp.sum(k_raw * k_raw, -1, keepdims=True) + EPS_UNIT)).astype(BF)
        q_scr[rows, :] = q
        k_scr[rows, :] = key
        out = o_ref[rows, :]
        inv = lax.rsqrt(jnp.mean(out * out, -1, keepdims=True) + EPS_HEAD)
        ohat = out * inv
        d_act2 = dact_ref[n].astype(F32)
        ghead = ghead + jnp.sum(d_act2 * ohat, 0, keepdims=True)
        lean = d_act2 * head_gain
        d_out = inv * (lean - ohat * jnp.mean(lean * ohat, -1, keepdims=True))
        do_scr[rows, :] = d_out
        g_scr[rows, :] = mm(att_ref[n], d_out, TN)
    ghead_ref[...] = jnp.broadcast_to(ghead, ghead_ref.shape)
    for n in range(n_seq):
        rows = pl.ds(n * size, size)
        col, keep, tail, whole = marks[n]
        add[n] = mm(q_scr[rows, :], (scale * keep) * do_scr[rows, :], TN) - mm(w_ref[n], keep * g_scr[rows, :], TN)
    grad = jnp.zeros((dk, dk), F32)
    for n in range(n_seq - 1, -1, -1):
        x_scr[n] = grad
        if n > 0:
            grad = marks[n][3] * grad - mm(p_ref[n], grad, TN) + add[n]
    gconv = [jnp.zeros((1, 3 * dk), F32) for _ in range(taps)]
    for n in range(n_seq - 1, -1, -1):
        rows = pl.ds(n * size, size)
        col, keep, tail, whole = marks[n]
        here, there, strict, incl = chunk_masks(n, size, col, table)
        rate = rates_ref[rows, :]
        key, q = k_scr[rows, :], q_scr[rows, :]
        key_f, q_f = key.astype(F32), q.astype(F32)
        pre = pre_scr[rows, :]
        sig = jax.nn.sigmoid(pre)
        act = pre * sig
        value = act[:, 2 * dk :].astype(BF).astype(F32)
        grad, state, u = x_scr[n], s_ref[n], u_ref[n]
        d_out = do_scr[rows, :]
        d_u = g_scr[rows, :] + tail * mm(key, grad)
        d_r = mm(inv_ref[n], d_u, TN)
        d_att = jnp.where(incl, mm(d_out, u, NT), 0.0)
        d_low = jnp.where(strict, -mm(d_r, u, NT), 0.0)
        d_q = keep * mm(d_out, state, NT) + mm(d_att, key)
        d_kb = mm(d_low, key) - keep * mm(d_r, state, NT)
        d_k = (
            scale * mm(d_att, q, TN)
            + mm(d_low, rate * key_f, TN)
            + tail * mm(u, grad, NT)
            + rate * d_kb
        )
        d_v = rate * d_r
        d_rate = jnp.sum(d_r * value + d_kb * key_f, -1, keepdims=True)
        d_q = d_q * scale
        q_raw, k_raw = act[:, :dk], act[:, dk : 2 * dk]
        q_inv = lax.rsqrt(jnp.sum(q_raw * q_raw, -1, keepdims=True) + EPS_UNIT)
        k_inv = lax.rsqrt(jnp.sum(k_raw * k_raw, -1, keepdims=True) + EPS_UNIT)
        q_unit, k_unit = q_raw * q_inv, k_raw * k_inv
        d_q = q_inv * (d_q - q_unit * jnp.sum(d_q * q_unit, -1, keepdims=True))
        d_k = k_inv * (d_k - k_unit * jnp.sum(d_k * k_unit, -1, keepdims=True))
        d_act = jnp.concatenate([d_q, d_k, d_v], 1)
        d_pre = d_act * sig * (1.0 + pre * (1.0 - sig))
        dpre[rows, :] = d_pre
        depth = (n * size + lax.broadcasted_iota(jnp.int32, (size, 1), 0)).astype(F32) - col
        d_proj = conv[0:1, :] * d_pre
        gconv[0] = gconv[0] + jnp.sum(d_pre * pad[pl.ds(RIM + n * size, size), :], 0, keepdims=True)
        for tap in range(1, taps):
            match = table[2][tap - 1][:, n : n + 1]
            d_proj = d_proj + conv[tap : tap + 1, :] * dpre[pl.ds(n * size + tap, size), :] * match
            reach = (depth >= float(tap)).astype(F32)
            gconv[tap] = gconv[tap] + jnp.sum(
                d_pre * reach * pad[pl.ds(RIM - tap + n * size, size), :], 0, keepdims=True
            )
        d_proj = d_proj.astype(BF)
        dproj_ref[rows, :] = d_proj
        one_rate = rate[:, 0:1]
        d_logit = (d_rate * one_rate * (1.0 - one_rate)).astype(BF).astype(F32)
        logit_scr[rows, :] = jnp.broadcast_to(d_logit, (size, dk))
        dlog_ref[pl.ds(n, 1), :] = jnp.broadcast_to(d_logit, (size, dk)).T[0:1]
    for n in range(0, n_seq, 2):
        rows = pl.ds(n * size, 2 * size)
        d_act1 = dot_low(dproj_ref[rows, :], weight_ref[...], NT) + logit_scr[rows, 0:1] * beta_row
        part_ref[rows, :] = d_act1.astype(BF)
    gconv_ref[...] = jnp.zeros_like(gconv_ref)
    for tap in range(taps):
        gconv_ref[tap : tap + 1, :] = gconv[tap]


def lead_kernel(place_ref, qkv_ref, conv_ref, gains_ref, head_ref, beta_ref, out_ref, rows):
    place, row = place_ref[0], place_ref[1]
    heads, dk = out_ref.shape[0], out_ref.shape[2]
    part = dk // 4
    from_row = pl.ds(pl.multiple_of(row * part, part), part)
    per = head_ref.shape[1]
    down = lax.broadcasted_iota(jnp.int32, (dk, dk), 0)
    along = lax.broadcasted_iota(jnp.int32, (dk, dk), 1)
    spot = (along == down + place * per)[0:per].astype(BF)
    rows[...] = jnp.zeros_like(rows)
    taps = conv_ref.shape[0]
    for kind in range(3):
        rows[kind * 16 : kind * 16 + taps, :] = conv_ref[:, kind * dk : (kind + 1) * dk].astype(F32)
    rows[4:6, :] = gains_ref[...].astype(F32)
    rows[6:7, :] = dot_low(jnp.broadcast_to(head_ref[...], (16, per)), spot)[0:1]
    rows[8:16, :] = beta_ref[...].astype(F32)
    small = rows[...].astype(BF)
    for h in range(heads):
        for kind in range(3):
            block = qkv_ref[from_row, pl.ds((kind * heads + h) * dk, dk)]
            out_ref[h, kind * part : (kind + 1) * part, :] = block
        out_ref[h, 3 * part : 3 * part + 48, :] = small


SLOT = 96


def columns_kernel(place_ref, gu_ref, down_ref, own_ref, other_ref, rows_ref, wide_own, wide_other):
    side, row = lax.rem(place_ref[0], 2), place_ref[1]
    size, lanes = gu_ref.shape[0], own_ref.shape[1]
    hidden = down_ref.shape[0]
    part, wide = hidden // 4, wide_own.shape[1] // 2
    for ref in (wide_own, wide_other):
        for kind in range(2):
            ref[:, kind * wide + wide - 128 : (kind + 1) * wide] = jnp.zeros((size, 128), F32)

    def take(x, r):
        for ref, block in ((wide_own, x), (wide_other, 1 - x)):
            for kind in range(2):
                for z in range(4):
                    at = (kind * 8 + z * 2 + block) * hidden + r * part
                    to = kind * wide + z * part
                    ref[:, to : to + part] = gu_ref[:, at : at + part].astype(F32)
        for j in range(down_ref.shape[1] // lanes):
            block = down_ref[r * part : (r + 1) * part, j * lanes : (j + 1) * lanes].astype(F32)
            block = jnp.concatenate([block, jnp.zeros((SLOT - part, lanes), F32)], 0)
            rows_ref[j * SLOT : (j + 1) * SLOT, :] = block.astype(BF)

    for x in range(2):
        for r in range(4):
            pl.when((side == x) & (row == r))(functools.partial(take, x, r))
    for ref, out in ((wide_own, own_ref), (wide_other, other_ref)):
        for j in range(2 * wide // lanes):
            out[j * size : (j + 1) * size, :] = ref[:, j * lanes : (j + 1) * lanes].astype(BF)


def mid_kernel(place_ref, act2_ref, own_ref, y_ref, cores_ref, x_ref, gains_ref, resid_ref, act3_ref, weight_ref):
    row = place_ref[1]
    heads, size, dk = act2_ref.shape
    part = dk // 4
    for m in range(4):
        ref = (own_ref, cores_ref.at[0], y_ref, cores_ref.at[1])[m]
        for s in range(heads):
            at = pl.multiple_of((s * 4 + (row ^ m)) * part, part)
            weight_ref[pl.ds(at, part), :] = ref[s]
    act2 = jnp.concatenate([act2_ref[h] for h in range(heads)], 1)
    resid = x_ref[...].astype(F32) + dot_low(act2, weight_ref[...])
    resid_ref[...] = resid
    inv = lax.rsqrt(jnp.mean(resid * resid, -1, keepdims=True) + EPS_NORM)
    act3_ref[...] = ((resid * inv) * gains_ref[1:2, :]).astype(BF)


GROUP_BITS = (0, 2, 4, 6, 1, 3, 5, 7)


def store_part(bits, block, own_ref, next_ref):
    @pl.when((bits & 1) == 0)
    def _():
        own_ref[bits >> 1] = block

    @pl.when((bits & 1) == 1)
    def _():
        next_ref[bits >> 1] = block


def mixed_kernel(place_ref, act4_ref, down_ref, own_ref, next_ref):
    me = lax.rem(place_ref[0], 2) * 4 + place_ref[1]
    size = own_ref.shape[1]
    for i in range(4):
        parts = dot_low(act4_ref[pl.ds(i * 2 * size, 2 * size), :], down_ref[...]).astype(BF)
        for half in range(2):
            store_part(me ^ (2 * i + half), parts[half * size : (half + 1) * size], own_ref, next_ref)


def feed_kernel(hidden, place_ref, *refs):
    act3_refs, core_ref, cot_refs, cot_core_ref, packs_ref = refs[0:4], refs[4], refs[5:9], refs[9], refs[10]
    own_ref, next_ref, act4_ref, dgu_ref, act3_ref, cot_ref, down_ref, gu, down32 = refs[11:]
    place, row = place_ref[0], place_ref[1]
    side = lax.rem(place, 2)
    me = side * 4 + row
    size, width = act3_refs[0].shape
    wide = act4_ref.shape[1]
    lanes = packs_ref.shape[2]
    slot, part = 96, hidden // 4
    gu_rows = gu.shape[0] // 4
    n_cols = gu.shape[1] // lanes
    down32[hidden:wide, :] = jnp.zeros((wide - hidden, width), F32)

    for src in range(4):
        for i in range(2):
            shard = src * 2 + (side if i == 0 else 1 - side)
            rows = pl.ds(pl.multiple_of(shard * size, size), size)
            for j in range(n_cols):
                from_rows = pl.ds((i * n_cols + j) * size, size)
                gu[rows, j * lanes : (j + 1) * lanes] = packs_ref[src, from_rows, :]
        for j in range(width // lanes):
            block = packs_ref[src, pl.ds(n_cols * gu_rows + j * slot, slot), :].astype(F32)
            down32[src * part : (src + 1) * part, j * lanes : (j + 1) * lanes] = block[0:part]
    down_ref[...] = down32[...].astype(BF)
    for i, bits in enumerate(GROUP_BITS):
        at = pl.multiple_of((me ^ bits) * size, size)
        act3_ref[pl.ds(at, size), :] = act3_refs[i][...] if i < 4 else core_ref[i - 4]
        cot_ref[pl.ds(at, size), :] = cot_refs[i][...] if i < 4 else cot_core_ref[i - 4]
    for i in range(4):
        rows = pl.ds(i * 2 * size, 2 * size)
        act3 = act3_ref[rows, :]
        cot = cot_ref[rows, :]
        gate_up = dot_low(act3, gu[...])
        gate, up = gate_up[:, :wide], gate_up[:, wide:]
        sig = jax.nn.sigmoid(gate)
        silu = gate * sig
        act4_ref[rows, :] = (silu * up).astype(BF)
        d_act4 = dot_low(cot, down_ref[...], NT)
        d_gate = d_act4 * up * sig * (1.0 + gate * (1.0 - sig))
        d_gu = jnp.concatenate([d_gate, d_act4 * silu], 1).astype(BF)
        dgu_ref[rows, :] = d_gu
        parts = dot_low(d_gu, gu[...], NT).astype(BF)
        for half in range(2):
            store_part(me ^ (2 * i + half), parts[half * size : (half + 1) * size], own_ref, next_ref)


def grads_kernel(hidden, place_ref, act3_ref, cot_ref, act4_ref, dgu_ref, out_ref, down32):
    side = lax.rem(place_ref[0], 2)
    lanes = out_ref.shape[2]
    slot, part = 96, hidden // 4
    gu_rows = act3_ref.shape[1] // 4
    n_cols = dgu_ref.shape[1] // lanes
    down32[...] = dot_low(act4_ref[...], cot_ref[...], TN)
    for k in range(4):
        at = k * gu_rows
        grad = dot_low(act3_ref[:, at : at + gu_rows], dgu_ref[...], TN).astype(BF)
        size = gu_rows // 2
        for parity in range(2):
            first = jnp.where(side == parity, 0, n_cols * size)
            for j in range(n_cols):
                rows = pl.ds(pl.multiple_of(first + j * size, size), size)
                out_ref[k, rows, :] = grad[parity * size : (parity + 1) * size, j * lanes : (j + 1) * lanes]
        rows = pl.ds(k * part, part)
        for j in range(cot_ref.shape[1] // lanes):
            block = down32[rows, j * lanes : (j + 1) * lanes]
            block = jnp.concatenate([block, jnp.zeros((slot - part, lanes), F32)], 0)
            out_ref[k, pl.ds(n_cols * gu_rows + j * slot, slot), :] = block.astype(BF)


def out_grad_kernel(place_ref, act2_ref, low_ref, same_ref, other_ref, full):
    row = place_ref[1]
    heads, _, dk = act2_ref.shape
    part = dk // 4
    for h in range(heads):
        full[h * dk : (h + 1) * dk, :] = dot_low(act2_ref[h], low_ref[...], TN)
    for m in range(4):
        ref = same_ref if m % 2 == 0 else other_ref
        for h in range(heads):
            at = pl.multiple_of(h * dk + (row ^ m) * part, part)
            ref[m // 2, h] = full[pl.ds(at, part), :].astype(BF)


def qkv_grad_kernel(place_ref, act1_ref, dproj_ref, dlog_ref, gconv_ref, ghead_ref, same_ref, other_ref, full, rows):
    row = place_ref[1]
    shards, total, cols = same_ref.shape[1:]
    dk = cols // 3
    part = total - 16
    for h in range(shards):
        lanes = pl.ds(h * dk, dk)
        full[h * dk : (h + 1) * dk, :] = dot_low(act1_ref[:, lanes], dproj_ref[...], TN)
    g_beta = None
    dlog = dlog_ref[...].astype(BF)
    for n in range(dlog.shape[0]):
        one = jnp.broadcast_to(dlog[n : n + 1], (16, dk))
        term = dot_low(one, act1_ref[n * dk : (n + 1) * dk, :])[0:1]
        g_beta = term if g_beta is None else g_beta + term
    rows[...] = jnp.zeros_like(rows)
    for s in range(shards):
        rows[s, 0:4, :] = gconv_ref[0:4, :]
        rows[s, 4:5, 0:dk] = g_beta[:, s * dk : (s + 1) * dk]
        rows[s, 4:5, dk : 2 * dk] = ghead_ref[0:1, :]
    for m in range(4):
        ref = same_ref if m % 2 == 0 else other_ref
        for s in range(shards):
            at = pl.multiple_of(s * dk + (row ^ m) * part, part)
            ref[m // 2, s, 0:part, :] = full[pl.ds(at, part), :].astype(BF)
            ref[m // 2, s, pl.ds(part, 16), :] = rows[s].astype(BF)


def turn_kernel(heads, own_ref, core_ref, x_ref, y_ref, top_ref, bottom_ref, resid_ref, cot_ref, gains_ref, weight_ref, dresid_ref, low_ref, dact2_ref):
    resid = resid_ref[...]
    inv = lax.rsqrt(jnp.mean(resid * resid, -1, keepdims=True) + EPS_NORM)
    rhat = resid * inv
    d_act3 = own_ref[0].astype(F32) + core_ref[0].astype(F32)
    d_act3 = d_act3 + jnp.concatenate([x_ref[0], y_ref[0]], 0).astype(F32)
    d_act3 = d_act3 + jnp.concatenate([top_ref[...], bottom_ref[...]], 0).astype(F32)
    lean = d_act3 * gains_ref[1:2, :]
    d_resid = cot_ref[...].astype(F32) + inv * (lean - rhat * jnp.mean(lean * rhat, -1, keepdims=True))
    dresid_ref[...] = d_resid
    low = d_resid.astype(BF)
    low_ref[...] = low
    d_act2 = dot_low(low, weight_ref[...], NT).astype(BF)
    dk = d_act2.shape[1] // heads
    for h in range(heads):
        dact2_ref[h] = d_act2[:, h * dk : (h + 1) * dk]


def last_kernel(part_ref, x_ref, gains_ref, dresid_ref, out_ref):
    d_act1 = part_ref[...].astype(F32)
    rows = x_ref[...].astype(F32)
    inv = lax.rsqrt(jnp.mean(rows * rows, -1, keepdims=True) + EPS_NORM)
    xhat = rows * inv
    lean = d_act1 * gains_ref[0:1, :]
    out = dresid_ref[...] + inv * (lean - xhat * jnp.mean(lean * xhat, -1, keepdims=True))
    out_ref[...] = out.astype(BF)


def row_sums(v):
    total = jnp.sum(v, 1, keepdims=True)
    return jnp.broadcast_to(total, (v.shape[0], 128)).T[0:1]


def lay_feed_kernel(place_ref, *refs):
    own_ref, y_ref, cores_ref = refs[0:3]
    packs = (own_ref, cores_ref.at[0], y_ref, cores_ref.at[1])
    weight_ref, gain_ref, gu_out, down_out, gain_out, held = refs[3:]
    side, row = lax.rem(place_ref[0], 2), place_ref[1]
    size, hidden = gain_out.shape[1], down_out.shape[0]
    lanes, slot, part = packs[0].shape[1], 96, hidden // 4
    wide = held.shape[3] // 2
    n_cols = held.shape[3] // lanes
    for m in range(4):
        for own in range(2):
            block = side if own == 0 else 1 - side
            for j in range(n_cols):
                rows = pl.ds((own * n_cols + j) * size, size)
                held[row ^ m, block, :, j * lanes : (j + 1) * lanes] = packs[m][rows, :]
        at = pl.multiple_of((row ^ m) * part, 8)
        for j in range(down_out.shape[1] // lanes):
            block = packs[m][pl.ds(2 * n_cols * size + j * slot, slot), :].astype(F32)
            down_out[pl.ds(at, part), j * lanes : (j + 1) * lanes] = block[0:part]
    total = None
    for kind in range(2):
        for m in range(4):
            for x in range(2):
                for z in range(4):
                    at = kind * wide + z * part
                    piece = held[m, x, :, at : at + part].astype(F32)
                    to = (kind * 8 + z * 2 + x) * hidden + m * part
                    gu_out[:, to : to + part] = piece
                    term = piece * weight_ref[:, to : to + part].astype(F32)
                    total = term if total is None else total + term
    gain_out[...] = row_sums(total) / gain_ref[1:2, :].astype(F32)


def lay_mix_kernel(place_ref, *refs):
    qkv_refs = (refs[0], refs[2].at[0], refs[1], refs[2].at[1])
    out_refs = (refs[3], refs[5].at[0], refs[4], refs[5].at[1])
    weight_ref, beta_ref, gain_ref, second_ref, qkv_out, out_out, gain_out, conv_out, beta_out, head_out = refs[6:]
    place, row = place_ref[0], place_ref[1]
    heads, total, cols = qkv_refs[0].shape
    dk = cols // 3
    part = total - 16
    for m in range(4):
        rows = pl.ds(pl.multiple_of((row ^ m) * part, 8), part)
        out_out[rows, :] = out_refs[m][...].astype(F32)
        for h in range(heads):
            for kind in range(3):
                lanes = pl.ds((kind * heads + h) * dk, dk)
                block = qkv_refs[m][h, 0:part, kind * dk : (kind + 1) * dk]
                qkv_out[rows, lanes] = block.astype(F32)
    sums = jnp.sum(qkv_out[...] * weight_ref[...].astype(F32), 1, keepdims=True)
    ref = qkv_refs[0]
    small = [ref[h, pl.ds(part, 16), :].astype(F32) for h in range(heads)]
    beta_rows = jnp.concatenate([v[4:5, 0:dk] for v in small], 0)
    beta_out[...] = beta_rows
    head = small[0][4:5, dk : 2 * dk]
    for v in small[1:]:
        head = head + v[4:5, dk : 2 * dk]
    per = head_out.shape[1]
    spot = lax.broadcasted_iota(jnp.int32, (dk, per), 0) == (
        lax.broadcasted_iota(jnp.int32, (dk, per), 1) + place * per
    )
    head_out[...] = mm(jnp.broadcast_to(head, (8, dk)), spot.astype(BF))[0:1]
    for i in range(3):
        block = place * 3 + i
        kind = block // heads
        source = block - kind * heads
        lanes = pl.ds(pl.multiple_of(kind * dk, dk), dk)
        conv_out[:, i * dk : (i + 1) * dk] = ref[source, pl.ds(part, 16), lanes].astype(F32)[0 : conv_out.shape[0]]
    weight_rows = beta_ref[...].astype(F32)
    gain = jnp.broadcast_to(sums, (sums.shape[0], 128)).T[0:1]
    gain = gain + jnp.sum(beta_rows * weight_rows, 0, keepdims=True)
    gain_out[0:1, :] = gain / gain_ref[0:1, :].astype(F32)
    gain_out[1:2, :] = second_ref[...]


def local_call(kernel, outs, args, scratch=(), smem=0, us=1, mib=56, name=None):
    space = [pl.BlockSpec(memory_space=pltpu.SMEM)] * smem
    space += [pl.BlockSpec(memory_space=pltpu.VMEM)] * (len(args) - smem)
    return pl.pallas_call(
        kernel,
        out_shape=tuple(outs),
        in_specs=space,
        out_specs=tuple(pl.BlockSpec(memory_space=pltpu.VMEM) for _ in outs),
        scratch_shapes=list(scratch),
        compiler_params=pltpu.CompilerParams(vmem_limit_bytes=mib * 2**20),
        cost_estimate=pl.CostEstimate(flops=us * 10**9, bytes_accessed=1024, transcendentals=0),
        name=name,
    )(*args)


def head_plan(
    block_input,
    cotangent,
    doc_starts,
    qkv_weight,
    beta_weight,
    conv_weight,
    norm_gains,
    head_gain,
    out_weight,
    gate_up_weight,
    down_weight,
):
    x, cot = block_input[0], cotangent[0]
    starts = doc_starts[0]
    size, width = x.shape
    n_seq, n_row = lax.axis_size("seq"), lax.axis_size("row")
    place, row = lax.axis_index("seq"), lax.axis_index("row")
    half = n_seq // 2
    z, side = place // 2, place % 2
    total = n_seq * size
    where_at = jnp.stack([place, row])
    taps = conv_weight.shape[0]
    hidden = down_weight.shape[0]
    wide = -(-hidden // 128) * 128
    shape = jax.ShapeDtypeStruct

    def flip(v):
        return lax.ppermute(v, "seq", [(s, s ^ 1) for s in range(n_seq)])

    def roll(v, k):
        return lax.ppermute(v, "seq", [(s, (s // 2 + k) % half * 2 + s % 2) for s in range(n_seq)])

    def core(v):
        return lax.ppermute(v, "row", [(r, r ^ 1) for r in range(n_row)])

    def across(v):
        return lax.ppermute(v, "row", [(r, r ^ 2) for r in range(n_row)])

    def group_gather(v):
        y, s = across(v), flip(v)
        four = [v, y, s, flip(y)]
        return [*four, core(jnp.stack(four))]

    def row_sum(same, other):
        mine = same.astype(F32) + core(other).astype(F32)
        return mine[0], mine[1].astype(BF)

    def row_relative(v):
        y = across(v)
        return [v, core(v), y, core(y)]

    def stage(*values):
        return lax.optimization_barrier(values)

    def line(v, step, t):
        ends = range(t - 1, half - 1) if step > 0 else range(1, half - t + 1)
        return lax.ppermute(
            v, "seq", [(2 * a + j, 2 * (a + step) + j) for a in ends for j in range(2)]
        )

    part_rows = size // n_row
    dk = width // n_seq
    lead_rows = 3 * part_rows + 48
    row_x = lax.all_gather(x, "seq", tiled=True)
    (payload,) = local_call(
        lead_kernel,
        [shape((n_seq, lead_rows, dk), BF)],
        [where_at, qkv_weight, conv_weight, norm_gains, head_gain.reshape(1, -1), beta_weight.T],
        scratch=[pltpu.VMEM((48, dk), F32)],
        smem=1,
        us=2,
        name="lead",
    )

    rows3 = shape((3 * size, 256), BF)
    pack_rows = 6 * size + 4 * SLOT
    own_cols, other_cols, down_rows = local_call(
        columns_kernel,
        [rows3, rows3, shape((4 * SLOT, 256), BF)],
        [where_at, gate_up_weight, down_weight],
        scratch=[pltpu.VMEM((size, 2 * wide), F32)] * 2,
        smem=1,
        us=2,
        name="columns",
    )
    pack = jnp.concatenate([own_cols, flip(other_cols), down_rows], 0)
    got = lax.all_to_all(payload, "seq", 0, 0)
    got_y = across(got)
    got_cores = core(jnp.stack([got, got_y]))
    out_part = lax.dynamic_slice_in_dim(out_weight, row * part_rows, part_rows, 0)
    out_part = jnp.broadcast_to(out_part[None], (n_seq, part_rows, width))
    groups_z = [[2 * a + j for a in range(half)] for j in range(2)]
    packs = lax.all_gather(pack, "seq", axis_index_groups=groups_z)
    out_part = lax.all_to_all(stage(out_part, pack)[0], "seq", 0, 0)
    row_x, got, got_y, got_cores, out_part, cot, _ = stage(row_x, got, got_y, got_cores, out_part, cot, pack)
    cot_y, cot_x = across(cot), flip(cot)
    out_y = across(out_part)
    square = shape((n_seq, size, dk), F32)
    (
        w_head,
        act1,
        proj,
        rates,
        outs,
        act2,
        inverse,
        w_mat,
        att,
        p_mat,
        u_mat,
        states,
        conv,
        gains,
        beta,
        head,
    ) = local_call(
        functools.partial(front_kernel, taps),
        [
            shape((width, 3 * dk), BF),
            shape((total, width), BF),
            shape((total, 3 * dk), BF),
            shape((total, dk), F32),
            shape((total, dk), F32),
            shape((n_seq, size, dk), BF),
            square,
            square,
            square,
            square,
            square,
            square,
            shape((8, 3 * dk), F32),
            shape((8, width), F32),
            shape((8, width), BF),
            shape((8, dk), F32),
        ],
        [where_at, starts, row_x, got, got_y, got_cores],
        scratch=[
            pltpu.VMEM((RIM + total, 3 * dk), F32),
            pltpu.VMEM((n_seq, size, size), F32),
            pltpu.VMEM((n_seq, size, size), F32),
            pltpu.VMEM((total, dk), BF),
            pltpu.VMEM((total, dk), BF),
            pltpu.VMEM((total, dk), BF),
            pltpu.VMEM((n_seq, dk, dk), F32),
        ],
        smem=2,
        us=4,
        name="front",
    )
    act2, cot_y, cot_x, out_y = stage(act2, cot_y, cot_x, out_y)
    act2 = lax.all_to_all(act2, "seq", 0, 0)
    cot_four = [cot, cot_y, cot_x, flip(cot_y)]
    out_cores = core(jnp.stack([out_part, out_y]))
    act2, out_cores, cot_four[3] = stage(act2, out_cores, cot_four[3])
    cot_all = [*cot_four, core(jnp.stack(cot_four))]
    resid, act3, w_out = local_call(
        mid_kernel,
        [shape((size, width), F32), shape((size, width), BF), shape((width, width), BF)],
        [where_at, act2, out_part, out_y, out_cores, x, gains],
        smem=1,
        us=1,
        mib=24,
        name="mid",
    )
    four = shape((4, size, width), BF)
    d_own, d_next, act4, d_gu, act3_all, cot_all, w_down = local_call(
        functools.partial(feed_kernel, hidden),
        [
            four,
            four,
            shape((total, wide), BF),
            shape((total, 2 * wide), BF),
            shape((total, width), BF),
            shape((total, width), BF),
            shape((wide, width), BF),
        ],
        [where_at, *group_gather(act3), *cot_all, packs],
        scratch=[pltpu.VMEM((width, 2 * wide), BF), pltpu.VMEM((wide, width), F32)],
        smem=1,
        us=3,
        mib=24,
        name="feed",
    )
    d_got, d_own, act4, d_gu, act3_all, cot_all = stage(core(d_next), d_own, act4, d_gu, act3_all, cot_all)
    mid_row = size // 2
    top, low = slice(0, mid_row), slice(mid_row, size)

    def core_sum(i, part):
        return d_own[i, part].astype(F32) + d_got[i, part].astype(F32)

    d_x = flip(jnp.stack([core_sum(2, top), core_sum(3, top)]).astype(BF))
    d_y = across(jnp.stack([core_sum(1, low), core_sum(3, low)]).astype(BF))
    (grads,) = local_call(
        functools.partial(grads_kernel, hidden),
        [shape((half, pack_rows, 256), BF)],
        [where_at, act3_all, cot_all, act4, d_gu],
        scratch=[pltpu.VMEM((wide, width), F32)],
        smem=1,
        us=3,
        mib=24,
        name="grads",
    )
    d_x, d_y, grads, act4 = stage(d_x, d_y, grads, act4)
    grads = lax.psum_scatter(grads, "seq", scatter_dimension=0, axis_index_groups=groups_z)
    d_top = across((core_sum(1, top) + d_x[1].astype(F32)).astype(BF))
    d_bottom = flip((core_sum(2, low) + d_y[1].astype(F32)).astype(BF))
    d_top, d_bottom, act4 = stage(d_top, d_bottom, act4)
    d_resid, d_low, d_act2 = local_call(
        functools.partial(turn_kernel, n_seq),
        [shape((size, width), F32), shape((size, width), BF), shape((n_seq, size, dk), BF)],
        [d_own, d_got, d_x, d_y, d_top, d_bottom, resid, cot, gains, w_out],
        us=1,
        mib=24,
        name="turn",
    )
    d_act2 = lax.all_to_all(d_act2, "seq", 0, 0)
    out_shape = shape((2, n_seq, part_rows, width), BF)
    out_same, out_other = local_call(
        out_grad_kernel,
        [out_shape, out_shape],
        [where_at, act2, d_low],
        scratch=[pltpu.VMEM((width, width), F32)],
        smem=1,
        us=3,
        name="out_grad",
    )
    mixed_own, mixed_next = local_call(
        mixed_kernel, [four, four], [where_at, act4, w_down], smem=1, us=5, name="mixed"
    )
    d_act2, out_same, out_other, mixed_own, mixed_next = stage(d_act2, out_same, out_other, mixed_own, mixed_next)
    mixed_got = core(mixed_next)
    out_got = core(out_other)
    d_proj, parts, d_log, g_conv, g_head = local_call(
        functools.partial(back_kernel, taps),
        [
            shape((total, 3 * dk), BF),
            shape((total, width), BF),
            shape((n_seq, size), F32),
            shape((8, 3 * dk), F32),
            shape((8, dk), F32),
        ],
        [
            where_at,
            starts,
            d_act2,
            outs,
            head,
            conv,
            proj,
            rates,
            inverse,
            w_mat,
            att,
            p_mat,
            u_mat,
            states,
            w_head,
            beta,
        ],
        scratch=[
            pltpu.VMEM((total, dk), F32),
            pltpu.VMEM((RIM + total, 3 * dk), F32),
            pltpu.VMEM((total, 3 * dk), F32),
            pltpu.VMEM((RIM + total, 3 * dk), F32),
            pltpu.VMEM((total, dk), F32),
            pltpu.VMEM((total, dk), F32),
            pltpu.VMEM((n_seq, dk, dk), F32),
            pltpu.VMEM((n_seq, dk, dk), F32),
            pltpu.VMEM((total, dk), BF),
            pltpu.VMEM((total, dk), BF),
        ],
        smem=2,
        us=5,
        name="back",
    )
    d_proj, parts, d_log, g_conv, g_head, out_got, mixed_got, grads = stage(
        d_proj, parts, d_log, g_conv, g_head, out_got, mixed_got, grads
    )
    mixed_both = [mixed_own[i].astype(F32) + mixed_got[i].astype(F32) for i in range(4)]
    mixed_x = flip(jnp.stack([mixed_both[2], mixed_both[3]]).astype(BF))
    d_act1 = lax.psum_scatter(parts, "seq", scatter_dimension=0, tiled=True)
    out_mine = out_same[0].astype(F32) + out_got[0].astype(F32)
    out_y = across((out_same[1].astype(F32) + out_got[1].astype(F32)).astype(BF))
    out_piece = lax.all_to_all((out_mine + out_y.astype(F32)).astype(BF), "seq", 0, 0)
    out_piece = out_piece.astype(F32).sum(0).astype(BF)
    out_y = across(out_piece)
    out_cores = core(jnp.stack([out_piece, out_y]))
    mixed_y = across((mixed_both[1] + mixed_x[1].astype(F32)).astype(BF))
    mixed = (resid + mixed_both[0] + mixed_x[0].astype(F32) + mixed_y.astype(F32)).astype(BF)
    gu_rows = 3 * size
    gu_other = flip(grads[gu_rows : 2 * gu_rows])
    feed_part = jnp.concatenate([grads[:gu_rows], gu_other, grads[2 * gu_rows :]], 0)
    feed_y = across(feed_part)
    feed_cores = core(jnp.stack([feed_part, feed_y]))
    cut_shape = shape((2, n_seq, part_rows + 16, 3 * dk), BF)
    qkv_same, qkv_other = local_call(
        qkv_grad_kernel,
        [cut_shape, cut_shape],
        [where_at, act1, d_proj, d_log, g_conv, g_head],
        scratch=[pltpu.VMEM((width, 3 * dk), F32), pltpu.VMEM((n_seq, 16, 3 * dk), F32)],
        smem=1,
        us=5,
        name="qkv_grad",
    )
    qkv_got = core(qkv_other)
    qkv_mine = qkv_same[0].astype(F32) + qkv_got[0].astype(F32)
    qkv_y = across((qkv_same[1].astype(F32) + qkv_got[1].astype(F32)).astype(BF))
    qkv_piece = lax.all_to_all((qkv_mine + qkv_y.astype(F32)).astype(BF), "seq", 0, 0)
    qkv_y = across(qkv_piece)
    qkv_cores = core(jnp.stack([qkv_piece, qkv_y]))
    (input_gradient,) = local_call(
        last_kernel,
        [shape((size, width), BF)],
        [d_act1, x, gains, d_resid],
        us=3,
        mib=24,
        name="last",
    )
    red_gu, red_down, second_gain = local_call(
        lay_feed_kernel,
        [
            shape((size, 2 * n_seq * hidden), F32),
            shape((hidden, width), F32),
            shape((1, size), F32),
        ],
        [where_at, feed_part, feed_y, feed_cores, gate_up_weight, norm_gains],
        scratch=[pltpu.VMEM((n_row, 2, size, 2 * wide), BF)],
        smem=1,
        us=3,
        mib=24,
        name="lay_feed",
    )
    red_qkv, red_out, red_gains, red_conv, red_beta, red_head = local_call(
        lay_mix_kernel,
        [
            shape((size, 3 * width), F32),
            shape((size, width), F32),
            shape((2, size), F32),
            shape((taps, 3 * dk), F32),
            shape((n_seq, dk), F32),
            shape((1, head_gain.shape[0]), F32),
        ],
        [where_at, qkv_piece, qkv_y, qkv_cores, out_piece, out_y, out_cores, qkv_weight, beta_weight.T, norm_gains, second_gain],
        smem=1,
        us=3,
        mib=24,
        name="lay_mix",
    )
    red_beta = red_beta.T
    red_head = red_head[0]
    return (
        mixed[None],
        input_gradient[None],
        red_qkv,
        red_beta,
        red_conv,
        red_gains,
        red_head,
        red_out,
        red_gu,
        red_down,
    )


def plan(block_input, *rest):
    seq, row = lax.axis_size("seq"), lax.axis_size("row")
    if seq == H and row * 2 == H and block_input.shape[1] == DK:
        return head_plan(block_input, *rest)
    return on_device(block_input, *rest)


def solution(mesh):
    in_specs = (
        P("row", "seq", None),
        P("row", "seq", None),
        P("row", None),
        P("seq", None),
        P("seq", None),
        P(None, "seq"),
        P(None, "seq"),
        P("seq"),
        P("seq", None),
        P("seq", None),
        P("seq", None),
    )
    out_specs = (
        P("row", "seq", None),
        P("row", "seq", None),
        P("seq", None),
        P("seq", None),
        P(None, "seq"),
        P(None, "seq"),
        P("seq"),
        P("seq", None),
        P("seq", None),
        P("seq", None),
    )
    return jax.shard_map(
        plan, mesh=mesh, in_specs=in_specs, out_specs=out_specs, check_vma=False
    )
```

```python
import functools

import jax
import jax.numpy as jnp
from jax import lax
from jax.experimental import pallas as pl
from jax.experimental.pallas import tpu as pltpu
from jax.sharding import PartitionSpec as P

H = 8
DK = 128
GROUP = 64


EPS_NORM = 1e-06
EPS_HEAD = 1e-05
EPS_UNIT = 1e-06
HIGH = lax.Precision.HIGHEST


def shifted(block, axis, distance):
    devices = range(lax.axis_size(axis))
    route = [(i - distance, i) for i in devices if i - distance in devices]
    return lax.ppermute(block, axis, route)


def dotf(first_op, second_op):
    return jnp.matmul(first_op, second_op, precision=HIGH)


def swap_last(matrix):
    return jnp.swapaxes(matrix, -1, -2)


def tok_dot(first_op, second_op):
    return lax.dot_general(
        first_op, second_op, (((0,), (0,)), ((), ())), preferred_element_type=jnp.float32
    )


def back_dot(first_op, second_op):
    return lax.dot_general(
        first_op, second_op, (((1,), (1,)), ((), ())), preferred_element_type=jnp.float32
    )


def unit_inverse(lower):
    identity = jnp.eye(lower.shape[-1], dtype=lower.dtype)
    power = lower
    result = identity - lower
    for step_index in range(lower.shape[-1].bit_length() - 2):
        power = dotf(power, power)
        result = dotf(result, identity + power)
    return result


def doc_index(positions, starts):
    return jnp.sum((starts[None, :] <= positions[:, None]).astype(jnp.int32), axis=1) - 1


def root_mean_square_backward(grad_in, normed, inverse):
    return inverse * (grad_in - normed * jnp.mean(grad_in * normed, -1, keepdims=True))


def silu_back(grad_in, pre):
    sig = jax.nn.sigmoid(pre)
    return grad_in * sig * (1.0 + pre * (1.0 - sig))


def on_device(
    block_input,
    cotangent,
    doc_starts,
    qkv_weight,
    beta_weight,
    conv_weight,
    norm_gains,
    head_gain,
    out_weight,
    gate_up_weight,
    down_weight,
):
    token_rows = block_input[0].astype(jnp.float32)
    cot_low = cotangent[0]
    seq_len = token_rows.shape[0]
    width = token_rows.shape[1]
    n_groups = seq_len // GROUP
    scale = DK ** (-0.5)
    w_qkv, w_beta, w_conv, w_gains, w_head, w_out, w_gu, w_down = (
        lax.all_gather(qkv_weight, "seq", axis=0, tiled=True),
        lax.all_gather(beta_weight, "seq", axis=0, tiled=True),
        lax.all_gather(conv_weight, "seq", axis=1, tiled=True),
        lax.all_gather(norm_gains, "seq", axis=1, tiled=True),
        lax.all_gather(head_gain, "seq", axis=0, tiled=True),
        lax.all_gather(out_weight, "seq", axis=0, tiled=True),
        lax.all_gather(gate_up_weight, "seq", axis=0, tiled=True),
        lax.all_gather(down_weight, "seq", axis=0, tiled=True),
    )
    conv_f = w_conv.astype(jnp.float32)
    float_gains = w_gains.astype(jnp.float32)
    head_f = w_head.astype(jnp.float32)
    seq_count = lax.axis_size("seq")
    seq_place = lax.axis_index("seq")
    starts = doc_starts[0]
    positions = seq_place * seq_len + jnp.arange(seq_len, dtype=jnp.int32)
    doc = doc_index(positions, starts)
    rim = conv_f.shape[0] - 1
    rim_doc = doc_index(seq_place * seq_len - rim + jnp.arange(rim, dtype=jnp.int32), starts)
    first_inverse_norm = lax.rsqrt(jnp.mean(token_rows * token_rows, -1, keepdims=True) + EPS_NORM)
    normalized_input = token_rows * first_inverse_norm
    first_activation = (normalized_input * float_gains[0]).astype(jnp.bfloat16)
    proj = jnp.dot(first_activation, w_qkv, preferred_element_type=jnp.float32).astype(jnp.bfloat16)
    rates_tok = jax.nn.sigmoid(
        jnp.dot(first_activation, w_beta, preferred_element_type=jnp.float32)
    )
    rim_vals = shifted(proj[seq_len - rim :], "seq", 1)
    extended = jnp.concatenate([rim_vals, proj], 0).astype(jnp.float32)
    ext_doc = jnp.concatenate([rim_doc, doc])
    matches = [
        (ext_doc[rim - tap : rim - tap + seq_len] == doc).astype(jnp.float32)[:, None]
        for tap in range(rim + 1)
    ]
    pre = jnp.zeros((seq_len, extended.shape[1]), jnp.float32)
    for tap in range(rim + 1):
        pre = pre + conv_f[tap] * extended[rim - tap : rim - tap + seq_len] * matches[tap]
    act = jax.nn.silu(pre)
    q_raw = act[:, :width].reshape(seq_len, H, DK)
    k_raw = act[:, width : 2 * width].reshape(seq_len, H, DK)
    v_raw = act[:, 2 * width :].reshape(seq_len, H, DK)
    q_inv = lax.rsqrt(jnp.sum(q_raw * q_raw, -1, keepdims=True) + EPS_UNIT)
    k_inv = lax.rsqrt(jnp.sum(k_raw * k_raw, -1, keepdims=True) + EPS_UNIT)
    q_unit = q_raw * q_inv
    k_unit = k_raw * k_inv

    def to_groups(arr):
        return (
            arr.astype(jnp.bfloat16)
            .astype(jnp.float32)
            .reshape(n_groups, GROUP, H, DK)
            .transpose(0, 2, 1, 3)
        )

    scaled_q = to_groups(q_unit) * scale
    keys = to_groups(k_unit)
    values = to_groups(v_raw)
    rates = rates_tok.reshape(n_groups, GROUP, H).transpose(0, 2, 1)
    block_doc = doc.reshape(n_groups, GROUP)
    prev_doc = doc_index(
        seq_place * seq_len + jnp.arange(n_groups, dtype=jnp.int32) * GROUP - 1, starts
    )
    places = jnp.arange(GROUP)
    same = block_doc[:, :, None] == block_doc[:, None, :]
    strict = ((places[:, None] > places[None, :])[None] & same)[:, None].astype(jnp.float32)
    incl = ((places[:, None] >= places[None, :])[None] & same)[:, None].astype(jnp.float32)
    keep = (block_doc == prev_doc[:, None]).astype(jnp.float32)[:, None, :, None]
    tail = (block_doc == block_doc[:, -1:]).astype(jnp.float32)[:, None, :, None]
    whole = keep[:, 0, -1, 0]
    scaled = keys * rates[..., None]
    lower = jnp.einsum("nhid,nhjd->nhij", scaled, keys, precision=HIGH) * strict
    inverse = unit_inverse(lower)
    w_mat = dotf(inverse, scaled)
    base = dotf(inverse, values * rates[..., None])
    eye_heads = jnp.broadcast_to(jnp.eye(DK, dtype=jnp.float32), (H, DK, DK))
    zero_heads = jnp.zeros((H, DK, DK), jnp.float32)

    def chain_step(maps, inputs):
        c_keys, c_w, c_base, c_keep, c_tail, c_whole = inputs
        mixed_maps = dotf(c_w[None], maps)
        reduce_part = jnp.einsum(
            "hcd,shce->shde", c_keys * (c_tail * c_keep), mixed_maps, precision=HIGH
        )
        maps = c_whole * maps - reduce_part
        shift_add = jnp.einsum("hcd,hce->hde", c_keys * c_tail, c_base, precision=HIGH)
        return (jnp.stack([maps[0], maps[1] + shift_add]), None)

    block_maps, unused = lax.scan(
        chain_step, jnp.stack([eye_heads, zero_heads]), (keys, w_mat, base, keep, tail, whole)
    )
    every_map, every_shift = (
        lax.all_gather(block_maps[0][None].astype(jnp.bfloat16), "seq", axis=0, tiled=True).astype(
            jnp.float32
        ),
        lax.all_gather(block_maps[1][None].astype(jnp.bfloat16), "seq", axis=0, tiled=True).astype(
            jnp.float32
        ),
    )

    def apply_map(position, state):
        return jnp.where(
            position < seq_place, dotf(every_map[position], state) + every_shift[position], state
        )

    state_in = lax.fori_loop(0, seq_count, apply_map, zero_heads)

    def out_step(state, inputs):
        c_q, c_keys, c_w, c_base, c_keep, c_tail, c_whole, c_incl = inputs
        pseudo = c_base - c_keep * dotf(c_w, state)
        scores = jnp.einsum("hid,hjd->hij", c_q, c_keys, precision=HIGH) * c_incl
        output = c_keep * dotf(c_q, state) + dotf(scores, pseudo)
        new_state = c_whole * state + jnp.einsum(
            "hcd,hce->hde", c_keys * c_tail, pseudo, precision=HIGH
        )
        return (new_state, (output, state))

    last_state, (outputs, block_states) = lax.scan(
        out_step, state_in, (scaled_q, keys, w_mat, base, keep, tail, whole, incl)
    )
    mixed_o = outputs.transpose(0, 2, 1, 3).reshape(seq_len, H, DK)
    head_inv = lax.rsqrt(jnp.mean(mixed_o * mixed_o, -1, keepdims=True) + EPS_HEAD)
    ohat = mixed_o * head_inv
    act_two = (ohat * head_f).reshape(seq_len, width).astype(jnp.bfloat16)
    resid = token_rows + jnp.dot(act_two, w_out, preferred_element_type=jnp.float32)
    inv_two = lax.rsqrt(jnp.mean(resid * resid, -1, keepdims=True) + EPS_NORM)
    rhat = resid * inv_two
    act_three = (rhat * float_gains[1]).astype(jnp.bfloat16)
    gate_up = jnp.dot(act_three, w_gu, preferred_element_type=jnp.float32)
    hidden_units = gate_up.shape[1] // 2
    gate = gate_up[:, :hidden_units]
    up_part = gate_up[:, hidden_units:]
    act_four = (jax.nn.silu(gate) * up_part).astype(jnp.bfloat16)
    mixed = (resid + jnp.dot(act_four, w_down, preferred_element_type=jnp.float32)).astype(
        jnp.bfloat16
    )
    grad_down = tok_dot(act_four, cot_low)
    d_act_four = back_dot(cot_low, w_down)
    d_gate = silu_back(d_act_four * up_part, gate)
    d_up = d_act_four * jax.nn.silu(gate)
    d_gate_up = jnp.concatenate([d_gate, d_up], 1).astype(jnp.bfloat16)
    grad_gate_up = tok_dot(act_three, d_gate_up)
    d_act_three = back_dot(d_gate_up, w_gu)
    grad_gain_two = jnp.sum(d_act_three * rhat, 0)
    residual_gradient = cot_low.astype(jnp.float32) + root_mean_square_backward(
        d_act_three * float_gains[1], rhat, inv_two
    )
    d_resid_low = residual_gradient.astype(jnp.bfloat16)
    grad_out = tok_dot(act_two, d_resid_low)
    d_act_two = back_dot(d_resid_low, w_out).reshape(seq_len, H, DK)
    grad_head = jnp.sum(d_act_two * ohat, (0, 1))
    d_mixed_o = root_mean_square_backward(d_act_two * head_f, ohat, head_inv)
    d_out_groups = d_mixed_o.reshape(n_groups, GROUP, H, DK).transpose(0, 2, 1, 3)

    def state_grad(grad_state, inputs):
        c_q, c_keys, c_scaled, c_inverse, c_keep, c_tail, c_whole, c_incl, c_dout = inputs
        scores = jnp.einsum("hid,hjd->hij", c_q, c_keys, precision=HIGH) * c_incl
        d_pseudo = jnp.einsum("hij,hid->hjd", scores, c_dout, precision=HIGH) + c_tail * dotf(
            c_keys, grad_state
        )
        d_res = jnp.einsum("hij,hid->hjd", c_inverse, d_pseudo, precision=HIGH)
        prior = (
            jnp.einsum("hcd,hce->hde", c_q * c_keep, c_dout, precision=HIGH) + c_whole * grad_state
        )
        return (prior - jnp.einsum("hcd,hce->hde", c_scaled * c_keep, d_res, precision=HIGH), None)

    local_grad, unused = lax.scan(
        state_grad,
        zero_heads,
        (scaled_q, keys, scaled, inverse, keep, tail, whole, incl, d_out_groups),
        reverse=True,
    )
    back_maps = swap_last(block_maps[0])
    every_back, every_grad = (
        lax.all_gather(back_maps[None].astype(jnp.bfloat16), "seq", axis=0, tiled=True).astype(
            jnp.float32
        ),
        lax.all_gather(local_grad[None].astype(jnp.bfloat16), "seq", axis=0, tiled=True).astype(
            jnp.float32
        ),
    )

    def apply_back(step_index, grad_state):
        position = seq_count - 1 - step_index
        return jnp.where(
            position > seq_place,
            dotf(every_back[position], grad_state) + every_grad[position],
            grad_state,
        )

    grad_state_out = lax.fori_loop(0, seq_count, apply_back, zero_heads)

    def full_back(grad_state, inputs):
        (
            c_q,
            c_keys,
            c_values,
            c_rates,
            c_scaled,
            c_inverse,
            c_w,
            c_base,
            c_keep,
            c_tail,
            c_whole,
            c_strict,
            c_incl,
            c_dout,
            c_state,
        ) = inputs
        pseudo = c_base - c_keep * dotf(c_w, c_state)
        scores = jnp.einsum("hid,hjd->hij", c_q, c_keys, precision=HIGH) * c_incl
        d_pseudo = jnp.einsum("hij,hid->hjd", scores, c_dout, precision=HIGH) + c_tail * dotf(
            c_keys, grad_state
        )
        d_res = jnp.einsum("hij,hid->hjd", c_inverse, d_pseudo, precision=HIGH)
        prior = (
            jnp.einsum("hcd,hce->hde", c_q * c_keep, c_dout, precision=HIGH) + c_whole * grad_state
        )
        prior = prior - jnp.einsum("hcd,hce->hde", c_scaled * c_keep, d_res, precision=HIGH)
        d_scores = jnp.einsum("hid,hjd->hij", c_dout, pseudo, precision=HIGH) * c_incl
        d_query = c_keep * dotf(c_dout, swap_last(c_state)) + dotf(d_scores, c_keys)
        d_keys = jnp.einsum("hij,hid->hjd", d_scores, c_q, precision=HIGH) + c_tail * dotf(
            pseudo, swap_last(grad_state)
        )
        d_lower = -jnp.einsum("hid,hjd->hij", d_res, pseudo, precision=HIGH) * c_strict
        d_scaled = -c_keep * dotf(d_res, swap_last(c_state)) + dotf(d_lower, c_keys)
        d_keys = (
            d_keys
            + jnp.einsum("hij,hid->hjd", d_lower, c_scaled, precision=HIGH)
            + c_rates[..., None] * d_scaled
        )
        d_values = c_rates[..., None] * d_res
        d_rates = jnp.sum(d_res * c_values, -1) + jnp.sum(d_scaled * c_keys, -1)
        return (prior, (d_query * scale, d_keys, d_values, d_rates))

    first_grad, (d_q_groups, d_k_groups, d_v_groups, d_rate_groups) = lax.scan(
        full_back,
        grad_state_out,
        (
            scaled_q,
            keys,
            values,
            rates,
            scaled,
            inverse,
            w_mat,
            base,
            keep,
            tail,
            whole,
            strict,
            incl,
            d_out_groups,
            block_states,
        ),
        reverse=True,
    )

    def from_groups(arr):
        return arr.transpose(0, 2, 1, 3).reshape(seq_len, H, DK)

    d_q_unit = from_groups(d_q_groups)
    d_k_unit = from_groups(d_k_groups)
    d_q_raw = q_inv * (d_q_unit - q_unit * jnp.sum(d_q_unit * q_unit, -1, keepdims=True))
    d_k_raw = k_inv * (d_k_unit - k_unit * jnp.sum(d_k_unit * k_unit, -1, keepdims=True))
    d_act = jnp.concatenate(
        [
            d_q_raw.reshape(seq_len, width),
            d_k_raw.reshape(seq_len, width),
            from_groups(d_v_groups).reshape(seq_len, width),
        ],
        1,
    )
    d_pre = silu_back(d_act, pre)
    d_extended = jnp.zeros((seq_len + rim, d_pre.shape[1]), jnp.float32)
    conv_grads = []
    for tap in range(rim + 1):
        masked = d_pre * matches[tap]
        d_extended = d_extended + jnp.pad(conv_f[tap] * masked, ((rim - tap, tap), (0, 0)))
        conv_grads.append(jnp.sum(masked * extended[rim - tap : rim - tap + seq_len], 0))
    grad_conv = jnp.stack(conv_grads)
    rim_back = shifted(d_extended[:rim].astype(jnp.bfloat16), "seq", -1).astype(jnp.float32)
    d_proj = (d_extended[rim:] + jnp.pad(rim_back, ((seq_len - rim, 0), (0, 0)))).astype(
        jnp.bfloat16
    )
    d_rates_tok = d_rate_groups.transpose(0, 2, 1).reshape(seq_len, H)
    d_logits = (d_rates_tok * rates_tok * (1.0 - rates_tok)).astype(jnp.bfloat16)
    grad_qkv = tok_dot(first_activation, d_proj)
    grad_beta = tok_dot(first_activation, d_logits)
    first_activation_gradient = back_dot(d_proj, w_qkv) + back_dot(d_logits, w_beta)
    first_gain_gradient = jnp.sum(first_activation_gradient * normalized_input, 0)
    block_input_gradient = (
        residual_gradient
        + root_mean_square_backward(
            first_activation_gradient * float_gains[0], normalized_input, first_inverse_norm
        )
    ).astype(jnp.bfloat16)
    grad_gains = jnp.stack([first_gain_gradient, grad_gain_two])
    red_qkv, red_beta, red_conv, red_gains, red_head, red_out, red_gu, red_down = (
        lax.psum_scatter(
            grad_qkv.astype(jnp.bfloat16), "seq", scatter_dimension=0, tiled=True
        ).astype(jnp.float32),
        lax.psum_scatter(
            grad_beta.astype(jnp.bfloat16), "seq", scatter_dimension=0, tiled=True
        ).astype(jnp.float32),
        lax.psum_scatter(
            grad_conv.astype(jnp.bfloat16), "seq", scatter_dimension=1, tiled=True
        ).astype(jnp.float32),
        lax.psum_scatter(
            grad_gains.astype(jnp.bfloat16), "seq", scatter_dimension=1, tiled=True
        ).astype(jnp.float32),
        lax.psum_scatter(
            grad_head.astype(jnp.bfloat16), "seq", scatter_dimension=0, tiled=True
        ).astype(jnp.float32),
        lax.psum_scatter(
            grad_out.astype(jnp.bfloat16), "seq", scatter_dimension=0, tiled=True
        ).astype(jnp.float32),
        lax.psum_scatter(
            grad_gate_up.astype(jnp.bfloat16), "seq", scatter_dimension=0, tiled=True
        ).astype(jnp.float32),
        lax.psum_scatter(
            grad_down.astype(jnp.bfloat16), "seq", scatter_dimension=0, tiled=True
        ).astype(jnp.float32),
    )
    red_qkv, red_beta, red_conv, red_gains, red_head, red_out, red_gu, red_down = (
        lax.psum(red_qkv.astype(jnp.bfloat16), "row").astype(jnp.float32),
        lax.psum(red_beta.astype(jnp.bfloat16), "row").astype(jnp.float32),
        lax.psum(red_conv.astype(jnp.bfloat16), "row").astype(jnp.float32),
        lax.psum(red_gains.astype(jnp.bfloat16), "row").astype(jnp.float32),
        lax.psum(red_head.astype(jnp.bfloat16), "row").astype(jnp.float32),
        lax.psum(red_out.astype(jnp.bfloat16), "row").astype(jnp.float32),
        lax.psum(red_gu.astype(jnp.bfloat16), "row").astype(jnp.float32),
        lax.psum(red_down.astype(jnp.bfloat16), "row").astype(jnp.float32),
    )
    return (
        mixed[None],
        block_input_gradient[None],
        red_qkv,
        red_beta,
        red_conv,
        red_gains,
        red_head,
        red_out,
        red_gu,
        red_down,
    )


BF = jnp.bfloat16
F32 = jnp.float32
RIM = 8
NN = (((1,), (0,)), ((), ()))
NT = (((1,), (1,)), ((), ()))
TN = (((0,), (0,)), ((), ()))


def dot_low(a, b, dims=NN):
    return lax.dot_general(a, b, dims, preferred_element_type=F32)


def parts_of(a):
    if a.dtype == BF:
        return (a,)
    high = a.astype(BF)
    return high, (a - high.astype(F32)).astype(BF)


def mm(a, b, dims=NN):
    a_parts, b_parts = parts_of(a), parts_of(b)
    total = dot_low(a_parts[0], b_parts[0], dims)
    if len(b_parts) > 1:
        total = total + dot_low(a_parts[0], b_parts[1], dims)
    if len(a_parts) > 1:
        total = total + dot_low(a_parts[1], b_parts[0], dims)
    return total


def mm1(a, b, dims=NN):
    return dot_low(a.astype(BF), b.astype(BF), dims)


def begin_of(pos, starts_ref):
    begin = jnp.zeros_like(pos)
    for i in range(starts_ref.shape[0]):
        begin = jnp.maximum(begin, jnp.where(pos >= starts_ref[i], starts_ref[i], 0))
    return begin


def begin_at(pos, starts_ref):
    begin = jnp.int32(0)
    for i in range(starts_ref.shape[0]):
        begin = jnp.maximum(begin, jnp.where(starts_ref[i] <= pos, starts_ref[i], 0))
    return begin


def mark_table(chunks, size, taps, starts_ref):
    pos = lax.broadcasted_iota(jnp.int32, (chunks, size), 0) * size
    pos = pos + lax.broadcasted_iota(jnp.int32, (chunks, size), 1)
    rows = begin_of(pos, starts_ref)
    later = [
        ((begin_of(pos + tap, starts_ref) <= pos) & (pos + tap < chunks * size)).astype(F32)
        for tap in range(1, taps)
    ]
    down = lax.broadcasted_iota(jnp.int32, (size, size), 0)
    eye = (down == lax.broadcasted_iota(jnp.int32, (size, size), 1)).astype(BF)
    rows = rows.astype(F32)
    return rows, mm(eye, rows, NT), [mm(eye, v, NT) for v in later]


def chunk_marks(n, size, table, starts_ref):
    first = n * size
    col = table[1][:, n : n + 1]
    last = begin_at(first + size - 1, starts_ref)
    keep = (col < float(first)).astype(F32)
    tail = (col == last.astype(F32)).astype(F32)
    whole = (last < first).astype(F32)
    return col, keep, tail, whole


def chunk_masks(n, size, col, table):
    here = lax.broadcasted_iota(jnp.int32, (size, size), 0)
    there = lax.broadcasted_iota(jnp.int32, (size, size), 1)
    same = col == table[0][n : n + 1]
    return here, there, same & (here > there), same & (here >= there)


def conv_chunk(n, size, pad, conv, col):
    depth = (n * size + lax.broadcasted_iota(jnp.int32, (size, 1), 0)).astype(F32) - col
    pre = conv[0:1, :] * pad[pl.ds(RIM + n * size, size), :]
    for tap in range(1, conv.shape[0]):
        match = (depth >= float(tap)).astype(F32)
        pre = pre + conv[tap : tap + 1, :] * pad[pl.ds(RIM - tap + n * size, size), :] * match
    return pre


def front_kernel(taps, place_ref, starts_ref, *refs):
    n_seq = refs[-1].shape[0]
    n_row = n_seq // 2
    top_ref, low_refs = refs[0], refs[1 : 1 + n_seq]
    got_ref, got_y_ref, got_cores_ref = refs[1 + n_seq : 4 + n_seq]
    got_refs = (got_ref, got_cores_ref.at[0], got_y_ref, got_cores_ref.at[1])
    (
        weight_ref,
        act1_ref,
        proj_ref,
        rates_ref,
        o_ref,
        act2_ref,
        inv_ref,
        w_ref,
        att_ref,
        p_ref,
        u_ref,
        s_ref,
        conv_ref,
        gains_ref,
        beta_ref,
        head_ref,
        pad,
        lower,
        tmp,
        q_scr,
        k_scr,
        v_scr,
        low_rows,
        add,
    ) = refs[4 + n_seq :]
    place, row = place_ref[0], place_ref[1]
    size = s_ref.shape[1]
    part_rows = size // n_row
    dk = o_ref.shape[1]
    base = 3 * part_rows
    gains = jnp.concatenate([got_ref[s, base + 4 : base + 6, :] for s in range(n_seq)], 1).astype(F32)
    gains_ref[...] = jnp.zeros_like(gains_ref)
    gains_ref[0:2, :] = gains
    beta = jnp.concatenate([got_ref[s, base + 8 : base + 16, :] for s in range(n_seq)], 1)
    beta_ref[...] = beta
    head_gain = got_ref[0, base + 6 : base + 7, :].astype(F32)
    for s in range(1, n_seq):
        head_gain = head_gain + got_ref[s, base + 6 : base + 7, :].astype(F32)
    head_ref[...] = jnp.broadcast_to(head_gain, head_ref.shape)
    conv_parts = []
    for part in range(3):
        block = part * n_seq + place
        shard = block // 3
        offset = pl.multiple_of(base + (block - shard * 3) * 16, 16)
        conv_parts.append(got_ref[shard, pl.ds(offset, 16), :][0:8])
    conv = jnp.concatenate(conv_parts, 1).astype(F32)
    conv_ref[...] = conv
    conv = conv[0:taps]
    for m, ref in enumerate(got_refs):
        for s in range(n_seq):
            at = pl.multiple_of(s * size + (row ^ m) * part_rows, part_rows)
            for kind in range(3):
                block = ref[s, kind * part_rows : (kind + 1) * part_rows, :]
                weight_ref[pl.ds(at, part_rows), kind * dk : (kind + 1) * dk] = block
    weight = weight_ref[...]
    lanes = lax.broadcasted_iota(jnp.int32, (2 * size, 8), 1)
    half = n_seq // 2
    z, side = place // 2, lax.rem(place, 2)
    for i, ref in enumerate(low_refs):
        chunk = lax.rem(z - i // 2 + half, half) * 2 + (side if i % 2 == 0 else 1 - side)
        at = pl.multiple_of(chunk * (size // 2), size // 2)
        low_rows[pl.ds(at, size // 2), :] = ref[...]
    pad[0:RIM, :] = jnp.zeros((RIM, 3 * dk), F32)
    for n in range(0, n_seq, 2):
        rows_at = pl.ds(n * size, 2 * size)
        part = size // 2
        rows = jnp.concatenate(
            [
                top_ref[n * part : (n + 1) * part, :],
                low_rows[n * part : (n + 1) * part, :],
                top_ref[(n + 1) * part : (n + 2) * part, :],
                low_rows[(n + 1) * part : (n + 2) * part, :],
            ],
            0,
        ).astype(F32)
        inv = lax.rsqrt(jnp.mean(rows * rows, -1, keepdims=True) + EPS_NORM)
        act = ((rows * inv) * gains[0:1]).astype(BF)
        act1_ref[rows_at, :] = act
        proj = dot_low(act, weight).astype(BF)
        proj_ref[rows_at, :] = proj
        pad[pl.ds(RIM + n * size, 2 * size), :] = proj.astype(F32)
        logits = dot_low(act, beta, NT)
        rate = jax.nn.sigmoid(jnp.sum(jnp.where(lanes == place, logits, 0.0), 1, keepdims=True))
        rates_ref[rows_at, :] = jnp.broadcast_to(rate, (2 * size, dk))
    table = mark_table(n_seq, size, taps, starts_ref)
    marks = []
    for n in range(n_seq):
        at = n * size
        col, keep, tail, whole = chunk_marks(n, size, table, starts_ref)
        marks.append((keep, tail, whole))
        pre = conv_chunk(n, size, pad, conv, col)
        act = pre * jax.nn.sigmoid(pre)
        q_raw, k_raw, v_raw = act[:, :dk], act[:, dk : 2 * dk], act[:, 2 * dk :]
        q = (q_raw * lax.rsqrt(jnp.sum(q_raw * q_raw, -1, keepdims=True) + EPS_UNIT)).astype(BF)
        key = (k_raw * lax.rsqrt(jnp.sum(k_raw * k_raw, -1, keepdims=True) + EPS_UNIT)).astype(BF)
        q_scr[pl.ds(at, size), :] = q
        k_scr[pl.ds(at, size), :] = key
        v_scr[pl.ds(at, size), :] = v_raw.astype(BF)
        here, there, strict, incl = chunk_masks(n, size, col, table)
        rate = rates_ref[pl.ds(at, size), :]
        low = jnp.where(strict, dot_low(key, key, NT) * rate, 0.0)
        att_ref[n] = jnp.where(incl, dot_low(q, key, NT) * (dk**-0.5), 0.0)
        lower[n] = low
        eye = (here == there).astype(F32)
        inv_ref[n] = eye - jnp.where((here // 2) == (there // 2), low, 0.0)
    span = 2
    while span < size:
        here = lax.broadcasted_iota(jnp.int32, (size, size), 0)
        there = lax.broadcasted_iota(jnp.int32, (size, size), 1)
        cross = ((here // (2 * span)) == (there // (2 * span))) & ((here // span) != (there // span))
        for n in range(n_seq):
            tmp[n] = mm(inv_ref[n], jnp.where(cross, lower[n], 0.0))
        for n in range(n_seq):
            inv_ref[n] = inv_ref[n] - mm(tmp[n], inv_ref[n])
        span *= 2
    for n in range(n_seq):
        keep, tail, whole = marks[n]
        rows = pl.ds(n * size, size)
        rate = rates_ref[rows, :]
        key = k_scr[rows, :]
        inv = inv_ref[n]
        w = mm(inv, rate * key.astype(F32))
        base = mm(inv, rate * v_scr[rows, :].astype(F32))
        w_ref[n] = w
        u_ref[n] = base
        p_ref[n] = mm(key, (tail * keep) * w, TN)
        add[n] = mm(key, tail * base, TN)
    state = jnp.zeros((dk, dk), F32)
    for n in range(n_seq):
        s_ref[n] = state
        if n + 1 < n_seq:
            state = marks[n][2] * state - mm(p_ref[n], state) + add[n]
    for n in range(n_seq):
        keep, tail, whole = marks[n]
        rows = pl.ds(n * size, size)
        state = s_ref[n]
        u = u_ref[n] - keep * mm(w_ref[n], state)
        u_ref[n] = u
        out = (keep * (dk**-0.5)) * mm(q_scr[rows, :], state) + mm(att_ref[n], u)
        o_ref[rows, :] = out
        inv = lax.rsqrt(jnp.mean(out * out, -1, keepdims=True) + EPS_HEAD)
        act2_ref[n] = ((out * inv) * head_gain).astype(BF)


def back_kernel(taps, place_ref, starts_ref, *refs):
    (
        dact_ref,
        o_ref,
        head_ref,
        conv_ref,
        proj_ref,
        rates_ref,
        inv_ref,
        w_ref,
        att_ref,
        p_ref,
        u_ref,
        s_ref,
        weight_ref,
        beta_ref,
        dproj_ref,
        part_ref,
        dlog_ref,
        gconv_ref,
        ghead_ref,
        logit_scr,
        pad,
        pre_scr,
        dpre,
        do_scr,
        g_scr,
        add,
        x_scr,
        q_scr,
        k_scr,
    ) = refs
    n_seq, size, dk = dact_ref.shape
    scale = dk**-0.5
    place = place_ref[0]
    beta_all = beta_ref[...].astype(F32)
    beta_lane = lax.broadcasted_iota(jnp.int32, beta_all.shape, 0) == place
    beta_row = jnp.sum(jnp.where(beta_lane, beta_all, 0.0), 0, keepdims=True)
    head_gain = head_ref[0:1, :]
    conv = conv_ref[0:taps, :]
    total = n_seq * size
    pad[0:RIM, :] = jnp.zeros((RIM, 3 * dk), F32)
    pad[pl.ds(RIM, total), :] = proj_ref[...].astype(F32)
    dpre[pl.ds(total, RIM), :] = jnp.zeros((RIM, 3 * dk), F32)
    table = mark_table(n_seq, size, taps, starts_ref)
    marks = []
    ghead = jnp.zeros((1, dk), F32)
    for n in range(n_seq):
        rows = pl.ds(n * size, size)
        col, keep, tail, whole = chunk_marks(n, size, table, starts_ref)
        marks.append((col, keep, tail, whole))
        pre = conv_chunk(n, size, pad, conv, col)
        pre_scr[rows, :] = pre
        act = pre * jax.nn.sigmoid(pre)
        q_raw, k_raw = act[:, :dk], act[:, dk : 2 * dk]
        q = (q_raw * lax.rsqrt(jnp.sum(q_raw * q_raw, -1, keepdims=True) + EPS_UNIT)).astype(BF)
        key = (k_raw * lax.rsqrt(jnp.sum(k_raw * k_raw, -1, keepdims=True) + EPS_UNIT)).astype(BF)
        q_scr[rows, :] = q
        k_scr[rows, :] = key
        out = o_ref[rows, :]
        inv = lax.rsqrt(jnp.mean(out * out, -1, keepdims=True) + EPS_HEAD)
        ohat = out * inv
        d_act2 = dact_ref[n].astype(F32)
        ghead = ghead + jnp.sum(d_act2 * ohat, 0, keepdims=True)
        lean = d_act2 * head_gain
        d_out = inv * (lean - ohat * jnp.mean(lean * ohat, -1, keepdims=True))
        do_scr[rows, :] = d_out
        g_scr[rows, :] = mm(att_ref[n], d_out, TN)
    ghead_ref[...] = jnp.broadcast_to(ghead, ghead_ref.shape)
    for n in range(n_seq):
        rows = pl.ds(n * size, size)
        col, keep, tail, whole = marks[n]
        add[n] = mm(q_scr[rows, :], (scale * keep) * do_scr[rows, :], TN) - mm(w_ref[n], keep * g_scr[rows, :], TN)
    grad = jnp.zeros((dk, dk), F32)
    for n in range(n_seq - 1, -1, -1):
        x_scr[n] = grad
        if n > 0:
            grad = marks[n][3] * grad - mm(p_ref[n], grad, TN) + add[n]
    gconv = [jnp.zeros((1, 3 * dk), F32) for _ in range(taps)]
    for n in range(n_seq - 1, -1, -1):
        rows = pl.ds(n * size, size)
        col, keep, tail, whole = marks[n]
        here, there, strict, incl = chunk_masks(n, size, col, table)
        rate = rates_ref[rows, :]
        key, q = k_scr[rows, :], q_scr[rows, :]
        key_f, q_f = key.astype(F32), q.astype(F32)
        pre = pre_scr[rows, :]
        sig = jax.nn.sigmoid(pre)
        act = pre * sig
        value = act[:, 2 * dk :].astype(BF).astype(F32)
        grad, state, u = x_scr[n], s_ref[n], u_ref[n]
        d_out = do_scr[rows, :]
        d_u = g_scr[rows, :] + tail * mm(key, grad)
        d_r = mm(inv_ref[n], d_u, TN)
        d_att = jnp.where(incl, mm(d_out, u, NT), 0.0)
        d_low = jnp.where(strict, -mm(d_r, u, NT), 0.0)
        d_q = keep * mm(d_out, state, NT) + mm(d_att, key)
        d_kb = mm(d_low, key) - keep * mm(d_r, state, NT)
        d_k = (
            scale * mm(d_att, q, TN)
            + mm(d_low, rate * key_f, TN)
            + tail * mm(u, grad, NT)
            + rate * d_kb
        )
        d_v = rate * d_r
        d_rate = jnp.sum(d_r * value + d_kb * key_f, -1, keepdims=True)
        d_q = d_q * scale
        q_raw, k_raw = act[:, :dk], act[:, dk : 2 * dk]
        q_inv = lax.rsqrt(jnp.sum(q_raw * q_raw, -1, keepdims=True) + EPS_UNIT)
        k_inv = lax.rsqrt(jnp.sum(k_raw * k_raw, -1, keepdims=True) + EPS_UNIT)
        q_unit, k_unit = q_raw * q_inv, k_raw * k_inv
        d_q = q_inv * (d_q - q_unit * jnp.sum(d_q * q_unit, -1, keepdims=True))
        d_k = k_inv * (d_k - k_unit * jnp.sum(d_k * k_unit, -1, keepdims=True))
        d_act = jnp.concatenate([d_q, d_k, d_v], 1)
        d_pre = d_act * sig * (1.0 + pre * (1.0 - sig))
        dpre[rows, :] = d_pre
        depth = (n * size + lax.broadcasted_iota(jnp.int32, (size, 1), 0)).astype(F32) - col
        d_proj = conv[0:1, :] * d_pre
        gconv[0] = gconv[0] + jnp.sum(d_pre * pad[pl.ds(RIM + n * size, size), :], 0, keepdims=True)
        for tap in range(1, taps):
            match = table[2][tap - 1][:, n : n + 1]
            d_proj = d_proj + conv[tap : tap + 1, :] * dpre[pl.ds(n * size + tap, size), :] * match
            reach = (depth >= float(tap)).astype(F32)
            gconv[tap] = gconv[tap] + jnp.sum(
                d_pre * reach * pad[pl.ds(RIM - tap + n * size, size), :], 0, keepdims=True
            )
        d_proj = d_proj.astype(BF)
        dproj_ref[rows, :] = d_proj
        one_rate = rate[:, 0:1]
        d_logit = (d_rate * one_rate * (1.0 - one_rate)).astype(BF).astype(F32)
        logit_scr[rows, :] = jnp.broadcast_to(d_logit, (size, dk))
        dlog_ref[pl.ds(n, 1), :] = jnp.broadcast_to(d_logit, (size, dk)).T[0:1]
    for n in range(0, n_seq, 2):
        rows = pl.ds(n * size, 2 * size)
        d_act1 = dot_low(dproj_ref[rows, :], weight_ref[...], NT) + logit_scr[rows, 0:1] * beta_row
        part_ref[rows, :] = d_act1.astype(BF)
    gconv_ref[...] = jnp.zeros_like(gconv_ref)
    for tap in range(taps):
        gconv_ref[tap : tap + 1, :] = gconv[tap]


def lead_kernel(place_ref, qkv_ref, conv_ref, gains_ref, head_ref, beta_ref, out_ref, rows):
    place, row = place_ref[0], place_ref[1]
    heads, dk = out_ref.shape[0], out_ref.shape[2]
    part = dk // 4
    from_row = pl.ds(pl.multiple_of(row * part, part), part)
    per = head_ref.shape[1]
    down = lax.broadcasted_iota(jnp.int32, (dk, dk), 0)
    along = lax.broadcasted_iota(jnp.int32, (dk, dk), 1)
    spot = (along == down + place * per)[0:per].astype(BF)
    rows[...] = jnp.zeros_like(rows)
    taps = conv_ref.shape[0]
    for kind in range(3):
        rows[kind * 16 : kind * 16 + taps, :] = conv_ref[:, kind * dk : (kind + 1) * dk].astype(F32)
    rows[4:6, :] = gains_ref[...].astype(F32)
    rows[6:7, :] = dot_low(jnp.broadcast_to(head_ref[...], (16, per)), spot)[0:1]
    rows[8:16, :] = beta_ref[...].astype(F32)
    small = rows[...].astype(BF)
    for h in range(heads):
        for kind in range(3):
            block = qkv_ref[from_row, pl.ds((kind * heads + h) * dk, dk)]
            out_ref[h, kind * part : (kind + 1) * part, :] = block
        out_ref[h, 3 * part : 3 * part + 48, :] = small


SLOT = 96


def columns_kernel(place_ref, gu_ref, down_ref, own_ref, other_ref, rows_ref, wide_own, wide_other):
    side, row = lax.rem(place_ref[0], 2), place_ref[1]
    size, lanes = gu_ref.shape[0], own_ref.shape[1]
    hidden = down_ref.shape[0]
    part, wide = hidden // 4, wide_own.shape[1] // 2
    for ref in (wide_own, wide_other):
        for kind in range(2):
            ref[:, kind * wide + wide - 128 : (kind + 1) * wide] = jnp.zeros((size, 128), F32)

    def take(x, r):
        for ref, block in ((wide_own, x), (wide_other, 1 - x)):
            for kind in range(2):
                for z in range(4):
                    at = (kind * 8 + z * 2 + block) * hidden + r * part
                    to = kind * wide + z * part
                    ref[:, to : to + part] = gu_ref[:, at : at + part].astype(F32)
        for j in range(down_ref.shape[1] // lanes):
            block = down_ref[r * part : (r + 1) * part, j * lanes : (j + 1) * lanes].astype(F32)
            block = jnp.concatenate([block, jnp.zeros((SLOT - part, lanes), F32)], 0)
            rows_ref[j * SLOT : (j + 1) * SLOT, :] = block.astype(BF)

    for x in range(2):
        for r in range(4):
            pl.when((side == x) & (row == r))(functools.partial(take, x, r))
    for ref, out in ((wide_own, own_ref), (wide_other, other_ref)):
        for j in range(2 * wide // lanes):
            out[j * size : (j + 1) * size, :] = ref[:, j * lanes : (j + 1) * lanes].astype(BF)


def mid_kernel(place_ref, act2_ref, own_ref, y_ref, cores_ref, x_ref, gains_ref, resid_ref, act3_ref, weight_ref):
    row = place_ref[1]
    heads, size, dk = act2_ref.shape
    part = dk // 4
    for m in range(4):
        ref = (own_ref, cores_ref.at[0], y_ref, cores_ref.at[1])[m]
        for s in range(heads):
            at = pl.multiple_of((s * 4 + (row ^ m)) * part, part)
            weight_ref[pl.ds(at, part), :] = ref[s]
    act2 = jnp.concatenate([act2_ref[h] for h in range(heads)], 1)
    resid = x_ref[...].astype(F32) + dot_low(act2, weight_ref[...])
    resid_ref[...] = resid
    inv = lax.rsqrt(jnp.mean(resid * resid, -1, keepdims=True) + EPS_NORM)
    act3_ref[...] = ((resid * inv) * gains_ref[1:2, :]).astype(BF)


GROUP_BITS = (0, 2, 4, 6, 1, 3, 5, 7)


def store_part(bits, block, own_ref, next_ref):
    @pl.when((bits & 1) == 0)
    def _():
        own_ref[bits >> 1] = block

    @pl.when((bits & 1) == 1)
    def _():
        next_ref[bits >> 1] = block


def mixed_kernel(place_ref, act4_ref, down_ref, own_ref, next_ref):
    me = lax.rem(place_ref[0], 2) * 4 + place_ref[1]
    size = own_ref.shape[1]
    for i in range(4):
        parts = dot_low(act4_ref[pl.ds(i * 2 * size, 2 * size), :], down_ref[...]).astype(BF)
        for half in range(2):
            store_part(me ^ (2 * i + half), parts[half * size : (half + 1) * size], own_ref, next_ref)


def feed_kernel(hidden, place_ref, *refs):
    act3_refs, core_ref, cot_refs, cot_core_ref, packs_ref = refs[0:4], refs[4], refs[5:9], refs[9], refs[10]
    own_ref, next_ref, act4_ref, dgu_ref, act3_ref, cot_ref, down_ref, gu, down32 = refs[11:]
    place, row = place_ref[0], place_ref[1]
    side = lax.rem(place, 2)
    me = side * 4 + row
    size, width = act3_refs[0].shape
    wide = act4_ref.shape[1]
    lanes = packs_ref.shape[2]
    slot, part = 96, hidden // 4
    gu_rows = gu.shape[0] // 4
    n_cols = gu.shape[1] // lanes
    down32[hidden:wide, :] = jnp.zeros((wide - hidden, width), F32)

    for src in range(4):
        for i in range(2):
            shard = src * 2 + (side if i == 0 else 1 - side)
            rows = pl.ds(pl.multiple_of(shard * size, size), size)
            for j in range(n_cols):
                from_rows = pl.ds((i * n_cols + j) * size, size)
                gu[rows, j * lanes : (j + 1) * lanes] = packs_ref[src, from_rows, :]
        for j in range(width // lanes):
            block = packs_ref[src, pl.ds(n_cols * gu_rows + j * slot, slot), :].astype(F32)
            down32[src * part : (src + 1) * part, j * lanes : (j + 1) * lanes] = block[0:part]
    down_ref[...] = down32[...].astype(BF)
    for i, bits in enumerate(GROUP_BITS):
        at = pl.multiple_of((me ^ bits) * size, size)
        act3_ref[pl.ds(at, size), :] = act3_refs[i][...] if i < 4 else core_ref[i - 4]
        cot_ref[pl.ds(at, size), :] = cot_refs[i][...] if i < 4 else cot_core_ref[i - 4]
    for i in range(4):
        rows = pl.ds(i * 2 * size, 2 * size)
        act3 = act3_ref[rows, :]
        cot = cot_ref[rows, :]
        gate_up = dot_low(act3, gu[...])
        gate, up = gate_up[:, :wide], gate_up[:, wide:]
        sig = jax.nn.sigmoid(gate)
        silu = gate * sig
        act4_ref[rows, :] = (silu * up).astype(BF)
        d_act4 = dot_low(cot, down_ref[...], NT)
        d_gate = d_act4 * up * sig * (1.0 + gate * (1.0 - sig))
        d_gu = jnp.concatenate([d_gate, d_act4 * silu], 1).astype(BF)
        dgu_ref[rows, :] = d_gu
        parts = dot_low(d_gu, gu[...], NT).astype(BF)
        for half in range(2):
            store_part(me ^ (2 * i + half), parts[half * size : (half + 1) * size], own_ref, next_ref)


def grads_kernel(hidden, place_ref, act3_ref, cot_ref, act4_ref, dgu_ref, out_ref, down32):
    side = lax.rem(place_ref[0], 2)
    lanes = out_ref.shape[2]
    slot, part = 96, hidden // 4
    gu_rows = act3_ref.shape[1] // 4
    n_cols = dgu_ref.shape[1] // lanes
    down32[...] = dot_low(act4_ref[...], cot_ref[...], TN)
    for k in range(4):
        at = k * gu_rows
        grad = dot_low(act3_ref[:, at : at + gu_rows], dgu_ref[...], TN).astype(BF)
        size = gu_rows // 2
        for parity in range(2):
            first = jnp.where(side == parity, 0, n_cols * size)
            for j in range(n_cols):
                rows = pl.ds(pl.multiple_of(first + j * size, size), size)
                out_ref[k, rows, :] = grad[parity * size : (parity + 1) * size, j * lanes : (j + 1) * lanes]
        rows = pl.ds(k * part, part)
        for j in range(cot_ref.shape[1] // lanes):
            block = down32[rows, j * lanes : (j + 1) * lanes]
            block = jnp.concatenate([block, jnp.zeros((slot - part, lanes), F32)], 0)
            out_ref[k, pl.ds(n_cols * gu_rows + j * slot, slot), :] = block.astype(BF)


def out_grad_kernel(place_ref, act2_ref, low_ref, same_ref, other_ref, full):
    row = place_ref[1]
    heads, _, dk = act2_ref.shape
    part = dk // 4
    for h in range(heads):
        full[h * dk : (h + 1) * dk, :] = dot_low(act2_ref[h], low_ref[...], TN)
    for m in range(4):
        ref = same_ref if m % 2 == 0 else other_ref
        for h in range(heads):
            at = pl.multiple_of(h * dk + (row ^ m) * part, part)
            ref[m // 2, h] = full[pl.ds(at, part), :].astype(BF)


def qkv_grad_kernel(place_ref, act1_ref, dproj_ref, dlog_ref, gconv_ref, ghead_ref, same_ref, other_ref, full, rows):
    row = place_ref[1]
    shards, total, cols = same_ref.shape[1:]
    dk = cols // 3
    part = total - 16
    for h in range(shards):
        lanes = pl.ds(h * dk, dk)
        full[h * dk : (h + 1) * dk, :] = dot_low(act1_ref[:, lanes], dproj_ref[...], TN)
    g_beta = None
    dlog = dlog_ref[...].astype(BF)
    for n in range(dlog.shape[0]):
        one = jnp.broadcast_to(dlog[n : n + 1], (16, dk))
        term = dot_low(one, act1_ref[n * dk : (n + 1) * dk, :])[0:1]
        g_beta = term if g_beta is None else g_beta + term
    rows[...] = jnp.zeros_like(rows)
    for s in range(shards):
        rows[s, 0:4, :] = gconv_ref[0:4, :]
        rows[s, 4:5, 0:dk] = g_beta[:, s * dk : (s + 1) * dk]
        rows[s, 4:5, dk : 2 * dk] = ghead_ref[0:1, :]
    for m in range(4):
        ref = same_ref if m % 2 == 0 else other_ref
        for s in range(shards):
            at = pl.multiple_of(s * dk + (row ^ m) * part, part)
            ref[m // 2, s, 0:part, :] = full[pl.ds(at, part), :].astype(BF)
            ref[m // 2, s, pl.ds(part, 16), :] = rows[s].astype(BF)


def turn_kernel(heads, own_ref, core_ref, x_ref, y_ref, top_ref, bottom_ref, resid_ref, cot_ref, gains_ref, weight_ref, dresid_ref, low_ref, dact2_ref):
    resid = resid_ref[...]
    inv = lax.rsqrt(jnp.mean(resid * resid, -1, keepdims=True) + EPS_NORM)
    rhat = resid * inv
    d_act3 = own_ref[0].astype(F32) + core_ref[0].astype(F32)
    d_act3 = d_act3 + jnp.concatenate([x_ref[0], y_ref[0]], 0).astype(F32)
    d_act3 = d_act3 + jnp.concatenate([top_ref[...], bottom_ref[...]], 0).astype(F32)
    lean = d_act3 * gains_ref[1:2, :]
    d_resid = cot_ref[...].astype(F32) + inv * (lean - rhat * jnp.mean(lean * rhat, -1, keepdims=True))
    dresid_ref[...] = d_resid
    low = d_resid.astype(BF)
    low_ref[...] = low
    d_act2 = dot_low(low, weight_ref[...], NT).astype(BF)
    dk = d_act2.shape[1] // heads
    for h in range(heads):
        dact2_ref[h] = d_act2[:, h * dk : (h + 1) * dk]


def last_kernel(part_ref, x_ref, gains_ref, dresid_ref, out_ref):
    d_act1 = part_ref[...].astype(F32)
    rows = x_ref[...].astype(F32)
    inv = lax.rsqrt(jnp.mean(rows * rows, -1, keepdims=True) + EPS_NORM)
    xhat = rows * inv
    lean = d_act1 * gains_ref[0:1, :]
    out = dresid_ref[...] + inv * (lean - xhat * jnp.mean(lean * xhat, -1, keepdims=True))
    out_ref[...] = out.astype(BF)


def row_sums(v):
    total = jnp.sum(v, 1, keepdims=True)
    return jnp.broadcast_to(total, (v.shape[0], 128)).T[0:1]


def lay_feed_kernel(place_ref, *refs):
    own_ref, y_ref, cores_ref = refs[0:3]
    packs = (own_ref, cores_ref.at[0], y_ref, cores_ref.at[1])
    weight_ref, gain_ref, gu_out, down_out, gain_out, held = refs[3:]
    side, row = lax.rem(place_ref[0], 2), place_ref[1]
    size, hidden = gain_out.shape[1], down_out.shape[0]
    lanes, slot, part = packs[0].shape[1], 96, hidden // 4
    wide = held.shape[3] // 2
    n_cols = held.shape[3] // lanes
    for m in range(4):
        for own in range(2):
            block = side if own == 0 else 1 - side
            for j in range(n_cols):
                rows = pl.ds((own * n_cols + j) * size, size)
                held[row ^ m, block, :, j * lanes : (j + 1) * lanes] = packs[m][rows, :]
        at = pl.multiple_of((row ^ m) * part, 8)
        for j in range(down_out.shape[1] // lanes):
            block = packs[m][pl.ds(2 * n_cols * size + j * slot, slot), :].astype(F32)
            down_out[pl.ds(at, part), j * lanes : (j + 1) * lanes] = block[0:part]
    total = None
    for kind in range(2):
        for m in range(4):
            for x in range(2):
                for z in range(4):
                    at = kind * wide + z * part
                    piece = held[m, x, :, at : at + part].astype(F32)
                    to = (kind * 8 + z * 2 + x) * hidden + m * part
                    gu_out[:, to : to + part] = piece
    for at in range(0, gu_out.shape[1], lanes):
        term = gu_out[:, at : at + lanes] * weight_ref[:, at : at + lanes].astype(F32)
        total = term if total is None else total + term
    gain_out[...] = row_sums(total) / gain_ref[1:2, :].astype(F32)


def lay_mix_kernel(place_ref, *refs):
    qkv_refs = (refs[0], refs[2].at[0], refs[1], refs[2].at[1])
    out_refs = (refs[3], refs[5].at[0], refs[4], refs[5].at[1])
    weight_ref, beta_ref, gain_ref, second_ref, qkv_out, out_out, gain_out, conv_out, beta_out, head_out = refs[6:]
    place, row = place_ref[0], place_ref[1]
    heads, total, cols = qkv_refs[0].shape
    dk = cols // 3
    part = total - 16
    for m in range(4):
        rows = pl.ds(pl.multiple_of((row ^ m) * part, 8), part)
        out_out[rows, :] = out_refs[m][...].astype(F32)
        for h in range(heads):
            for kind in range(3):
                lanes = pl.ds((kind * heads + h) * dk, dk)
                block = qkv_refs[m][h, 0:part, kind * dk : (kind + 1) * dk]
                qkv_out[rows, lanes] = block.astype(F32)
    sums = jnp.sum(qkv_out[...] * weight_ref[...].astype(F32), 1, keepdims=True)
    ref = qkv_refs[0]
    small = [ref[h, pl.ds(part, 16), :].astype(F32) for h in range(heads)]
    beta_rows = jnp.concatenate([v[4:5, 0:dk] for v in small], 0)
    beta_out[...] = beta_rows
    head = small[0][4:5, dk : 2 * dk]
    for v in small[1:]:
        head = head + v[4:5, dk : 2 * dk]
    per = head_out.shape[1]
    spot = lax.broadcasted_iota(jnp.int32, (dk, per), 0) == (
        lax.broadcasted_iota(jnp.int32, (dk, per), 1) + place * per
    )
    head_out[...] = mm(jnp.broadcast_to(head, (8, dk)), spot.astype(BF))[0:1]
    for i in range(3):
        block = place * 3 + i
        kind = block // heads
        source = block - kind * heads
        lanes = pl.ds(pl.multiple_of(kind * dk, dk), dk)
        conv_out[:, i * dk : (i + 1) * dk] = ref[source, pl.ds(part, 16), lanes].astype(F32)[0 : conv_out.shape[0]]
    weight_rows = beta_ref[...].astype(F32)
    gain = jnp.broadcast_to(sums, (sums.shape[0], 128)).T[0:1]
    gain = gain + jnp.sum(beta_rows * weight_rows, 0, keepdims=True)
    gain_out[0:1, :] = gain / gain_ref[0:1, :].astype(F32)
    gain_out[1:2, :] = second_ref[...]


def local_call(kernel, outs, args, scratch=(), smem=0, us=1, mib=56, name=None):
    space = [pl.BlockSpec(memory_space=pltpu.SMEM)] * smem
    space += [pl.BlockSpec(memory_space=pltpu.VMEM)] * (len(args) - smem)
    return pl.pallas_call(
        kernel,
        out_shape=tuple(outs),
        in_specs=space,
        out_specs=tuple(pl.BlockSpec(memory_space=pltpu.VMEM) for _ in outs),
        scratch_shapes=list(scratch),
        compiler_params=pltpu.CompilerParams(vmem_limit_bytes=mib * 2**20),
        cost_estimate=pl.CostEstimate(flops=us * 10**9, bytes_accessed=1024, transcendentals=0),
        name=name,
    )(*args)


def head_plan(
    block_input,
    cotangent,
    doc_starts,
    qkv_weight,
    beta_weight,
    conv_weight,
    norm_gains,
    head_gain,
    out_weight,
    gate_up_weight,
    down_weight,
):
    x, cot = block_input[0], cotangent[0]
    starts = doc_starts[0]
    size, width = x.shape
    n_seq, n_row = lax.axis_size("seq"), lax.axis_size("row")
    place, row = lax.axis_index("seq"), lax.axis_index("row")
    half = n_seq // 2
    z, side = place // 2, place % 2
    total = n_seq * size
    where_at = jnp.stack([place, row])
    taps = conv_weight.shape[0]
    hidden = down_weight.shape[0]
    wide = -(-hidden // 128) * 128
    shape = jax.ShapeDtypeStruct

    def flip(v):
        return lax.ppermute(v, "seq", [(s, s ^ 1) for s in range(n_seq)])

    def roll(v, k):
        return lax.ppermute(v, "seq", [(s, (s // 2 + k) % half * 2 + s % 2) for s in range(n_seq)])

    def core(v):
        return lax.ppermute(v, "row", [(r, r ^ 1) for r in range(n_row)])

    def across(v):
        return lax.ppermute(v, "row", [(r, r ^ 2) for r in range(n_row)])

    def group_gather(v):
        y, s = across(v), flip(v)
        four = [v, y, s, flip(y)]
        return [*four, core(jnp.stack(four))]

    def row_sum(same, other):
        mine = same.astype(F32) + core(other).astype(F32)
        return mine[0], mine[1].astype(BF)

    def row_relative(v):
        y = across(v)
        return [v, core(v), y, core(y)]

    def stage(*values):
        return lax.optimization_barrier(values)

    def line(v, step, t):
        ends = range(t - 1, half - 1) if step > 0 else range(1, half - t + 1)
        return lax.ppermute(
            v, "seq", [(2 * a + j, 2 * (a + step) + j) for a in ends for j in range(2)]
        )

    part_rows = size // n_row
    dk = width // n_seq
    lead_rows = 3 * part_rows + 48
    mid_row = size // 2
    row_top = lax.all_gather(x[:mid_row], "seq", tiled=True)
    far = {k: roll(x[mid_row:], k) for k in (2, 1, 3)}
    near = flip(x[mid_row:])
    (payload,) = local_call(
        lead_kernel,
        [shape((n_seq, lead_rows, dk), BF)],
        [where_at, qkv_weight, conv_weight, norm_gains, head_gain.reshape(1, -1), beta_weight.T],
        scratch=[pltpu.VMEM((48, dk), F32)],
        smem=1,
        us=2,
        name="lead",
    )

    rows3 = shape((3 * size, 256), BF)
    pack_rows = 6 * size + 4 * SLOT
    own_cols, other_cols, down_rows = local_call(
        columns_kernel,
        [rows3, rows3, shape((4 * SLOT, 256), BF)],
        [where_at, gate_up_weight, down_weight],
        scratch=[pltpu.VMEM((size, 2 * wide), F32)] * 2,
        smem=1,
        us=2,
        name="columns",
    )
    pack = jnp.concatenate([own_cols, flip(other_cols), down_rows], 0)
    got = lax.all_to_all(payload, "seq", 0, 0)
    got_y = across(got)
    got_cores = core(jnp.stack([got, got_y]))
    out_part = lax.dynamic_slice_in_dim(out_weight, row * part_rows, part_rows, 0)
    out_part = jnp.broadcast_to(out_part[None], (n_seq, part_rows, width))
    groups_z = [[2 * a + j for a in range(half)] for j in range(2)]
    packs = lax.all_gather(pack, "seq", axis_index_groups=groups_z)
    out_part, _, near, far[1], far[2], far[3] = stage(out_part, pack, near, far[1], far[2], far[3])
    out_part = lax.all_to_all(out_part, "seq", 0, 0)
    row_low = [x[mid_row:], near]
    for k in range(1, half):
        row_low += [far[k], flip(far[k])]
    row_top, got, got_y, got_cores, out_part, cot, _, *row_low = stage(
        row_top, got, got_y, got_cores, out_part, cot, pack, *row_low
    )
    cot_y, cot_x = across(cot), flip(cot)
    out_y = across(out_part)
    square = shape((n_seq, size, dk), F32)
    (
        w_head,
        act1,
        proj,
        rates,
        outs,
        act2,
        inverse,
        w_mat,
        att,
        p_mat,
        u_mat,
        states,
        conv,
        gains,
        beta,
        head,
    ) = local_call(
        functools.partial(front_kernel, taps),
        [
            shape((width, 3 * dk), BF),
            shape((total, width), BF),
            shape((total, 3 * dk), BF),
            shape((total, dk), F32),
            shape((total, dk), F32),
            shape((n_seq, size, dk), BF),
            square,
            square,
            square,
            square,
            square,
            square,
            shape((8, 3 * dk), F32),
            shape((8, width), F32),
            shape((8, width), BF),
            shape((8, dk), F32),
        ],
        [where_at, starts, row_top, *row_low, got, got_y, got_cores],
        scratch=[
            pltpu.VMEM((RIM + total, 3 * dk), F32),
            pltpu.VMEM((n_seq, size, size), F32),
            pltpu.VMEM((n_seq, size, size), F32),
            pltpu.VMEM((total, dk), BF),
            pltpu.VMEM((total, dk), BF),
            pltpu.VMEM((total, dk), BF),
            pltpu.VMEM((total // 2, width), BF),
            pltpu.VMEM((n_seq, dk, dk), F32),
        ],
        smem=2,
        us=4,
        name="front",
    )
    act2, cot_y, cot_x, out_y = stage(act2, cot_y, cot_x, out_y)
    act2 = lax.all_to_all(act2, "seq", 0, 0)
    cot_four = [cot, cot_y, cot_x, flip(cot_y)]
    out_cores = core(jnp.stack([out_part, out_y]))
    act2, out_cores, cot_four[3] = stage(act2, out_cores, cot_four[3])
    cot_all = [*cot_four, core(jnp.stack(cot_four))]
    resid, act3, w_out = local_call(
        mid_kernel,
        [shape((size, width), F32), shape((size, width), BF), shape((width, width), BF)],
        [where_at, act2, out_part, out_y, out_cores, x, gains],
        smem=1,
        us=1,
        mib=24,
        name="mid",
    )
    four = shape((4, size, width), BF)
    d_own, d_next, act4, d_gu, act3_all, cot_all, w_down = local_call(
        functools.partial(feed_kernel, hidden),
        [
            four,
            four,
            shape((total, wide), BF),
            shape((total, 2 * wide), BF),
            shape((total, width), BF),
            shape((total, width), BF),
            shape((wide, width), BF),
        ],
        [where_at, *group_gather(act3), *cot_all, packs],
        scratch=[pltpu.VMEM((width, 2 * wide), BF), pltpu.VMEM((wide, width), F32)],
        smem=1,
        us=3,
        mib=24,
        name="feed",
    )
    d_got, d_own, act4, d_gu, act3_all, cot_all = stage(core(d_next), d_own, act4, d_gu, act3_all, cot_all)
    top, low = slice(0, mid_row), slice(mid_row, size)

    def core_sum(i, part):
        return d_own[i, part].astype(F32) + d_got[i, part].astype(F32)

    d_x = flip(jnp.stack([core_sum(2, top), core_sum(3, top)]).astype(BF))
    d_y = across(jnp.stack([core_sum(1, low), core_sum(3, low)]).astype(BF))
    (grads,) = local_call(
        functools.partial(grads_kernel, hidden),
        [shape((half, pack_rows, 256), BF)],
        [where_at, act3_all, cot_all, act4, d_gu],
        scratch=[pltpu.VMEM((wide, width), F32)],
        smem=1,
        us=3,
        mib=24,
        name="grads",
    )
    d_x, d_y, grads, act4 = stage(d_x, d_y, grads, act4)
    grads = lax.psum_scatter(grads, "seq", scatter_dimension=0, axis_index_groups=groups_z)
    d_top = across((core_sum(1, top) + d_x[1].astype(F32)).astype(BF))
    d_bottom = flip((core_sum(2, low) + d_y[1].astype(F32)).astype(BF))
    d_top, d_bottom, act4 = stage(d_top, d_bottom, act4)
    d_resid, d_low, d_act2 = local_call(
        functools.partial(turn_kernel, n_seq),
        [shape((size, width), F32), shape((size, width), BF), shape((n_seq, size, dk), BF)],
        [d_own, d_got, d_x, d_y, d_top, d_bottom, resid, cot, gains, w_out],
        us=1,
        mib=24,
        name="turn",
    )
    d_act2 = lax.all_to_all(d_act2, "seq", 0, 0)
    out_shape = shape((2, n_seq, part_rows, width), BF)
    out_same, out_other = local_call(
        out_grad_kernel,
        [out_shape, out_shape],
        [where_at, act2, d_low],
        scratch=[pltpu.VMEM((width, width), F32)],
        smem=1,
        us=3,
        name="out_grad",
    )
    mixed_own, mixed_next = local_call(
        mixed_kernel, [four, four], [where_at, act4, w_down], smem=1, us=5, name="mixed"
    )
    d_act2, out_same, out_other, mixed_own, mixed_next = stage(d_act2, out_same, out_other, mixed_own, mixed_next)
    mixed_got = core(mixed_next)
    out_got = core(out_other)
    d_proj, parts, d_log, g_conv, g_head = local_call(
        functools.partial(back_kernel, taps),
        [
            shape((total, 3 * dk), BF),
            shape((total, width), BF),
            shape((n_seq, size), F32),
            shape((8, 3 * dk), F32),
            shape((8, dk), F32),
        ],
        [
            where_at,
            starts,
            d_act2,
            outs,
            head,
            conv,
            proj,
            rates,
            inverse,
            w_mat,
            att,
            p_mat,
            u_mat,
            states,
            w_head,
            beta,
        ],
        scratch=[
            pltpu.VMEM((total, dk), F32),
            pltpu.VMEM((RIM + total, 3 * dk), F32),
            pltpu.VMEM((total, 3 * dk), F32),
            pltpu.VMEM((RIM + total, 3 * dk), F32),
            pltpu.VMEM((total, dk), F32),
            pltpu.VMEM((total, dk), F32),
            pltpu.VMEM((n_seq, dk, dk), F32),
            pltpu.VMEM((n_seq, dk, dk), F32),
            pltpu.VMEM((total, dk), BF),
            pltpu.VMEM((total, dk), BF),
        ],
        smem=2,
        us=5,
        name="back",
    )
    d_proj, parts, d_log, g_conv, g_head, out_got, mixed_got, grads = stage(
        d_proj, parts, d_log, g_conv, g_head, out_got, mixed_got, grads
    )
    mixed_both = [mixed_own[i].astype(F32) + mixed_got[i].astype(F32) for i in range(4)]
    mixed_x = flip(jnp.stack([mixed_both[2], mixed_both[3]]).astype(BF))
    d_act1 = lax.psum_scatter(parts, "seq", scatter_dimension=0, tiled=True)
    out_mine = out_same[0].astype(F32) + out_got[0].astype(F32)
    out_y = across((out_same[1].astype(F32) + out_got[1].astype(F32)).astype(BF))
    out_piece = lax.all_to_all((out_mine + out_y.astype(F32)).astype(BF), "seq", 0, 0)
    out_piece = out_piece.astype(F32).sum(0).astype(BF)
    out_y = across(out_piece)
    out_cores = core(jnp.stack([out_piece, out_y]))
    mixed_y = across((mixed_both[1] + mixed_x[1].astype(F32)).astype(BF))
    mixed = (resid + mixed_both[0] + mixed_x[0].astype(F32) + mixed_y.astype(F32)).astype(BF)
    gu_rows = 3 * size
    gu_other = flip(grads[gu_rows : 2 * gu_rows])
    feed_part = jnp.concatenate([grads[:gu_rows], gu_other, grads[2 * gu_rows :]], 0)
    feed_y = across(feed_part)
    feed_cores = core(jnp.stack([feed_part, feed_y]))
    cut_shape = shape((2, n_seq, part_rows + 16, 3 * dk), BF)
    qkv_same, qkv_other = local_call(
        qkv_grad_kernel,
        [cut_shape, cut_shape],
        [where_at, act1, d_proj, d_log, g_conv, g_head],
        scratch=[pltpu.VMEM((width, 3 * dk), F32), pltpu.VMEM((n_seq, 16, 3 * dk), F32)],
        smem=1,
        us=5,
        name="qkv_grad",
    )
    qkv_got = core(qkv_other)
    qkv_mine = qkv_same[0].astype(F32) + qkv_got[0].astype(F32)
    qkv_y = across((qkv_same[1].astype(F32) + qkv_got[1].astype(F32)).astype(BF))
    qkv_piece = lax.all_to_all((qkv_mine + qkv_y.astype(F32)).astype(BF), "seq", 0, 0)
    qkv_y = across(qkv_piece)
    qkv_cores = core(jnp.stack([qkv_piece, qkv_y]))
    (input_gradient,) = local_call(
        last_kernel,
        [shape((size, width), BF)],
        [d_act1, x, gains, d_resid],
        us=3,
        mib=24,
        name="last",
    )
    red_gu, red_down, second_gain = local_call(
        lay_feed_kernel,
        [
            shape((size, 2 * n_seq * hidden), F32),
            shape((hidden, width), F32),
            shape((1, size), F32),
        ],
        [where_at, feed_part, feed_y, feed_cores, gate_up_weight, norm_gains],
        scratch=[pltpu.VMEM((n_row, 2, size, 2 * wide), BF)],
        smem=1,
        us=3,
        mib=24,
        name="lay_feed",
    )
    red_qkv, red_out, red_gains, red_conv, red_beta, red_head = local_call(
        lay_mix_kernel,
        [
            shape((size, 3 * width), F32),
            shape((size, width), F32),
            shape((2, size), F32),
            shape((taps, 3 * dk), F32),
            shape((n_seq, dk), F32),
            shape((1, head_gain.shape[0]), F32),
        ],
        [where_at, qkv_piece, qkv_y, qkv_cores, out_piece, out_y, out_cores, qkv_weight, beta_weight.T, norm_gains, second_gain],
        smem=1,
        us=3,
        mib=24,
        name="lay_mix",
    )
    red_beta = red_beta.T
    red_head = red_head[0]
    return (
        mixed[None],
        input_gradient[None],
        red_qkv,
        red_beta,
        red_conv,
        red_gains,
        red_head,
        red_out,
        red_gu,
        red_down,
    )


def plan(block_input, *rest):
    seq, row = lax.axis_size("seq"), lax.axis_size("row")
    if seq == H and row * 2 == H and block_input.shape[1] == DK:
        return head_plan(block_input, *rest)
    return on_device(block_input, *rest)


def solution(mesh):
    in_specs = (
        P("row", "seq", None),
        P("row", "seq", None),
        P("row", None),
        P("seq", None),
        P("seq", None),
        P(None, "seq"),
        P(None, "seq"),
        P("seq"),
        P("seq", None),
        P("seq", None),
        P("seq", None),
    )
    out_specs = (
        P("row", "seq", None),
        P("row", "seq", None),
        P("seq", None),
        P("seq", None),
        P(None, "seq"),
        P(None, "seq"),
        P("seq"),
        P("seq", None),
        P("seq", None),
        P("seq", None),
    )
    return jax.shard_map(
        plan, mesh=mesh, in_specs=in_specs, out_specs=out_specs, check_vma=False
    )
```

```python
import functools

import jax
import jax.numpy as jnp
from jax import lax
from jax.experimental import pallas as pl
from jax.experimental.pallas import tpu as pltpu
from jax.sharding import PartitionSpec as P

H = 8
DK = 128
GROUP = 64


EPS_NORM = 1e-06
EPS_HEAD = 1e-05
EPS_UNIT = 1e-06
HIGH = lax.Precision.HIGHEST


def shifted(block, axis, distance):
    devices = range(lax.axis_size(axis))
    route = [(i - distance, i) for i in devices if i - distance in devices]
    return lax.ppermute(block, axis, route)


def dotf(first_op, second_op):
    return jnp.matmul(first_op, second_op, precision=HIGH)


def swap_last(matrix):
    return jnp.swapaxes(matrix, -1, -2)


def tok_dot(first_op, second_op):
    return lax.dot_general(
        first_op, second_op, (((0,), (0,)), ((), ())), preferred_element_type=jnp.float32
    )


def back_dot(first_op, second_op):
    return lax.dot_general(
        first_op, second_op, (((1,), (1,)), ((), ())), preferred_element_type=jnp.float32
    )


def unit_inverse(lower):
    identity = jnp.eye(lower.shape[-1], dtype=lower.dtype)
    power = lower
    result = identity - lower
    for step_index in range(lower.shape[-1].bit_length() - 2):
        power = dotf(power, power)
        result = dotf(result, identity + power)
    return result


def doc_index(positions, starts):
    return jnp.sum((starts[None, :] <= positions[:, None]).astype(jnp.int32), axis=1) - 1


def root_mean_square_backward(grad_in, normed, inverse):
    return inverse * (grad_in - normed * jnp.mean(grad_in * normed, -1, keepdims=True))


def silu_back(grad_in, pre):
    sig = jax.nn.sigmoid(pre)
    return grad_in * sig * (1.0 + pre * (1.0 - sig))


def on_device(
    block_input,
    cotangent,
    doc_starts,
    qkv_weight,
    beta_weight,
    conv_weight,
    norm_gains,
    head_gain,
    out_weight,
    gate_up_weight,
    down_weight,
):
    token_rows = block_input[0].astype(jnp.float32)
    cot_low = cotangent[0]
    seq_len = token_rows.shape[0]
    width = token_rows.shape[1]
    n_groups = seq_len // GROUP
    scale = DK ** (-0.5)
    w_qkv, w_beta, w_conv, w_gains, w_head, w_out, w_gu, w_down = (
        lax.all_gather(qkv_weight, "seq", axis=0, tiled=True),
        lax.all_gather(beta_weight, "seq", axis=0, tiled=True),
        lax.all_gather(conv_weight, "seq", axis=1, tiled=True),
        lax.all_gather(norm_gains, "seq", axis=1, tiled=True),
        lax.all_gather(head_gain, "seq", axis=0, tiled=True),
        lax.all_gather(out_weight, "seq", axis=0, tiled=True),
        lax.all_gather(gate_up_weight, "seq", axis=0, tiled=True),
        lax.all_gather(down_weight, "seq", axis=0, tiled=True),
    )
    conv_f = w_conv.astype(jnp.float32)
    float_gains = w_gains.astype(jnp.float32)
    head_f = w_head.astype(jnp.float32)
    seq_count = lax.axis_size("seq")
    seq_place = lax.axis_index("seq")
    starts = doc_starts[0]
    positions = seq_place * seq_len + jnp.arange(seq_len, dtype=jnp.int32)
    doc = doc_index(positions, starts)
    rim = conv_f.shape[0] - 1
    rim_doc = doc_index(seq_place * seq_len - rim + jnp.arange(rim, dtype=jnp.int32), starts)
    first_inverse_norm = lax.rsqrt(jnp.mean(token_rows * token_rows, -1, keepdims=True) + EPS_NORM)
    normalized_input = token_rows * first_inverse_norm
    first_activation = (normalized_input * float_gains[0]).astype(jnp.bfloat16)
    proj = jnp.dot(first_activation, w_qkv, preferred_element_type=jnp.float32).astype(jnp.bfloat16)
    rates_tok = jax.nn.sigmoid(
        jnp.dot(first_activation, w_beta, preferred_element_type=jnp.float32)
    )
    rim_vals = shifted(proj[seq_len - rim :], "seq", 1)
    extended = jnp.concatenate([rim_vals, proj], 0).astype(jnp.float32)
    ext_doc = jnp.concatenate([rim_doc, doc])
    matches = [
        (ext_doc[rim - tap : rim - tap + seq_len] == doc).astype(jnp.float32)[:, None]
        for tap in range(rim + 1)
    ]
    pre = jnp.zeros((seq_len, extended.shape[1]), jnp.float32)
    for tap in range(rim + 1):
        pre = pre + conv_f[tap] * extended[rim - tap : rim - tap + seq_len] * matches[tap]
    act = jax.nn.silu(pre)
    q_raw = act[:, :width].reshape(seq_len, H, DK)
    k_raw = act[:, width : 2 * width].reshape(seq_len, H, DK)
    v_raw = act[:, 2 * width :].reshape(seq_len, H, DK)
    q_inv = lax.rsqrt(jnp.sum(q_raw * q_raw, -1, keepdims=True) + EPS_UNIT)
    k_inv = lax.rsqrt(jnp.sum(k_raw * k_raw, -1, keepdims=True) + EPS_UNIT)
    q_unit = q_raw * q_inv
    k_unit = k_raw * k_inv

    def to_groups(arr):
        return (
            arr.astype(jnp.bfloat16)
            .astype(jnp.float32)
            .reshape(n_groups, GROUP, H, DK)
            .transpose(0, 2, 1, 3)
        )

    scaled_q = to_groups(q_unit) * scale
    keys = to_groups(k_unit)
    values = to_groups(v_raw)
    rates = rates_tok.reshape(n_groups, GROUP, H).transpose(0, 2, 1)
    block_doc = doc.reshape(n_groups, GROUP)
    prev_doc = doc_index(
        seq_place * seq_len + jnp.arange(n_groups, dtype=jnp.int32) * GROUP - 1, starts
    )
    places = jnp.arange(GROUP)
    same = block_doc[:, :, None] == block_doc[:, None, :]
    strict = ((places[:, None] > places[None, :])[None] & same)[:, None].astype(jnp.float32)
    incl = ((places[:, None] >= places[None, :])[None] & same)[:, None].astype(jnp.float32)
    keep = (block_doc == prev_doc[:, None]).astype(jnp.float32)[:, None, :, None]
    tail = (block_doc == block_doc[:, -1:]).astype(jnp.float32)[:, None, :, None]
    whole = keep[:, 0, -1, 0]
    scaled = keys * rates[..., None]
    lower = jnp.einsum("nhid,nhjd->nhij", scaled, keys, precision=HIGH) * strict
    inverse = unit_inverse(lower)
    w_mat = dotf(inverse, scaled)
    base = dotf(inverse, values * rates[..., None])
    eye_heads = jnp.broadcast_to(jnp.eye(DK, dtype=jnp.float32), (H, DK, DK))
    zero_heads = jnp.zeros((H, DK, DK), jnp.float32)

    def chain_step(maps, inputs):
        c_keys, c_w, c_base, c_keep, c_tail, c_whole = inputs
        mixed_maps = dotf(c_w[None], maps)
        reduce_part = jnp.einsum(
            "hcd,shce->shde", c_keys * (c_tail * c_keep), mixed_maps, precision=HIGH
        )
        maps = c_whole * maps - reduce_part
        shift_add = jnp.einsum("hcd,hce->hde", c_keys * c_tail, c_base, precision=HIGH)
        return (jnp.stack([maps[0], maps[1] + shift_add]), None)

    block_maps, unused = lax.scan(
        chain_step, jnp.stack([eye_heads, zero_heads]), (keys, w_mat, base, keep, tail, whole)
    )
    every_map, every_shift = (
        lax.all_gather(block_maps[0][None].astype(jnp.bfloat16), "seq", axis=0, tiled=True).astype(
            jnp.float32
        ),
        lax.all_gather(block_maps[1][None].astype(jnp.bfloat16), "seq", axis=0, tiled=True).astype(
            jnp.float32
        ),
    )

    def apply_map(position, state):
        return jnp.where(
            position < seq_place, dotf(every_map[position], state) + every_shift[position], state
        )

    state_in = lax.fori_loop(0, seq_count, apply_map, zero_heads)

    def out_step(state, inputs):
        c_q, c_keys, c_w, c_base, c_keep, c_tail, c_whole, c_incl = inputs
        pseudo = c_base - c_keep * dotf(c_w, state)
        scores = jnp.einsum("hid,hjd->hij", c_q, c_keys, precision=HIGH) * c_incl
        output = c_keep * dotf(c_q, state) + dotf(scores, pseudo)
        new_state = c_whole * state + jnp.einsum(
            "hcd,hce->hde", c_keys * c_tail, pseudo, precision=HIGH
        )
        return (new_state, (output, state))

    last_state, (outputs, block_states) = lax.scan(
        out_step, state_in, (scaled_q, keys, w_mat, base, keep, tail, whole, incl)
    )
    mixed_o = outputs.transpose(0, 2, 1, 3).reshape(seq_len, H, DK)
    head_inv = lax.rsqrt(jnp.mean(mixed_o * mixed_o, -1, keepdims=True) + EPS_HEAD)
    ohat = mixed_o * head_inv
    act_two = (ohat * head_f).reshape(seq_len, width).astype(jnp.bfloat16)
    resid = token_rows + jnp.dot(act_two, w_out, preferred_element_type=jnp.float32)
    inv_two = lax.rsqrt(jnp.mean(resid * resid, -1, keepdims=True) + EPS_NORM)
    rhat = resid * inv_two
    act_three = (rhat * float_gains[1]).astype(jnp.bfloat16)
    gate_up = jnp.dot(act_three, w_gu, preferred_element_type=jnp.float32)
    hidden_units = gate_up.shape[1] // 2
    gate = gate_up[:, :hidden_units]
    up_part = gate_up[:, hidden_units:]
    act_four = (jax.nn.silu(gate) * up_part).astype(jnp.bfloat16)
    mixed = (resid + jnp.dot(act_four, w_down, preferred_element_type=jnp.float32)).astype(
        jnp.bfloat16
    )
    grad_down = tok_dot(act_four, cot_low)
    d_act_four = back_dot(cot_low, w_down)
    d_gate = silu_back(d_act_four * up_part, gate)
    d_up = d_act_four * jax.nn.silu(gate)
    d_gate_up = jnp.concatenate([d_gate, d_up], 1).astype(jnp.bfloat16)
    grad_gate_up = tok_dot(act_three, d_gate_up)
    d_act_three = back_dot(d_gate_up, w_gu)
    grad_gain_two = jnp.sum(d_act_three * rhat, 0)
    residual_gradient = cot_low.astype(jnp.float32) + root_mean_square_backward(
        d_act_three * float_gains[1], rhat, inv_two
    )
    d_resid_low = residual_gradient.astype(jnp.bfloat16)
    grad_out = tok_dot(act_two, d_resid_low)
    d_act_two = back_dot(d_resid_low, w_out).reshape(seq_len, H, DK)
    grad_head = jnp.sum(d_act_two * ohat, (0, 1))
    d_mixed_o = root_mean_square_backward(d_act_two * head_f, ohat, head_inv)
    d_out_groups = d_mixed_o.reshape(n_groups, GROUP, H, DK).transpose(0, 2, 1, 3)

    def state_grad(grad_state, inputs):
        c_q, c_keys, c_scaled, c_inverse, c_keep, c_tail, c_whole, c_incl, c_dout = inputs
        scores = jnp.einsum("hid,hjd->hij", c_q, c_keys, precision=HIGH) * c_incl
        d_pseudo = jnp.einsum("hij,hid->hjd", scores, c_dout, precision=HIGH) + c_tail * dotf(
            c_keys, grad_state
        )
        d_res = jnp.einsum("hij,hid->hjd", c_inverse, d_pseudo, precision=HIGH)
        prior = (
            jnp.einsum("hcd,hce->hde", c_q * c_keep, c_dout, precision=HIGH) + c_whole * grad_state
        )
        return (prior - jnp.einsum("hcd,hce->hde", c_scaled * c_keep, d_res, precision=HIGH), None)

    local_grad, unused = lax.scan(
        state_grad,
        zero_heads,
        (scaled_q, keys, scaled, inverse, keep, tail, whole, incl, d_out_groups),
        reverse=True,
    )
    back_maps = swap_last(block_maps[0])
    every_back, every_grad = (
        lax.all_gather(back_maps[None].astype(jnp.bfloat16), "seq", axis=0, tiled=True).astype(
            jnp.float32
        ),
        lax.all_gather(local_grad[None].astype(jnp.bfloat16), "seq", axis=0, tiled=True).astype(
            jnp.float32
        ),
    )

    def apply_back(step_index, grad_state):
        position = seq_count - 1 - step_index
        return jnp.where(
            position > seq_place,
            dotf(every_back[position], grad_state) + every_grad[position],
            grad_state,
        )

    grad_state_out = lax.fori_loop(0, seq_count, apply_back, zero_heads)

    def full_back(grad_state, inputs):
        (
            c_q,
            c_keys,
            c_values,
            c_rates,
            c_scaled,
            c_inverse,
            c_w,
            c_base,
            c_keep,
            c_tail,
            c_whole,
            c_strict,
            c_incl,
            c_dout,
            c_state,
        ) = inputs
        pseudo = c_base - c_keep * dotf(c_w, c_state)
        scores = jnp.einsum("hid,hjd->hij", c_q, c_keys, precision=HIGH) * c_incl
        d_pseudo = jnp.einsum("hij,hid->hjd", scores, c_dout, precision=HIGH) + c_tail * dotf(
            c_keys, grad_state
        )
        d_res = jnp.einsum("hij,hid->hjd", c_inverse, d_pseudo, precision=HIGH)
        prior = (
            jnp.einsum("hcd,hce->hde", c_q * c_keep, c_dout, precision=HIGH) + c_whole * grad_state
        )
        prior = prior - jnp.einsum("hcd,hce->hde", c_scaled * c_keep, d_res, precision=HIGH)
        d_scores = jnp.einsum("hid,hjd->hij", c_dout, pseudo, precision=HIGH) * c_incl
        d_query = c_keep * dotf(c_dout, swap_last(c_state)) + dotf(d_scores, c_keys)
        d_keys = jnp.einsum("hij,hid->hjd", d_scores, c_q, precision=HIGH) + c_tail * dotf(
            pseudo, swap_last(grad_state)
        )
        d_lower = -jnp.einsum("hid,hjd->hij", d_res, pseudo, precision=HIGH) * c_strict
        d_scaled = -c_keep * dotf(d_res, swap_last(c_state)) + dotf(d_lower, c_keys)
        d_keys = (
            d_keys
            + jnp.einsum("hij,hid->hjd", d_lower, c_scaled, precision=HIGH)
            + c_rates[..., None] * d_scaled
        )
        d_values = c_rates[..., None] * d_res
        d_rates = jnp.sum(d_res * c_values, -1) + jnp.sum(d_scaled * c_keys, -1)
        return (prior, (d_query * scale, d_keys, d_values, d_rates))

    first_grad, (d_q_groups, d_k_groups, d_v_groups, d_rate_groups) = lax.scan(
        full_back,
        grad_state_out,
        (
            scaled_q,
            keys,
            values,
            rates,
            scaled,
            inverse,
            w_mat,
            base,
            keep,
            tail,
            whole,
            strict,
            incl,
            d_out_groups,
            block_states,
        ),
        reverse=True,
    )

    def from_groups(arr):
        return arr.transpose(0, 2, 1, 3).reshape(seq_len, H, DK)

    d_q_unit = from_groups(d_q_groups)
    d_k_unit = from_groups(d_k_groups)
    d_q_raw = q_inv * (d_q_unit - q_unit * jnp.sum(d_q_unit * q_unit, -1, keepdims=True))
    d_k_raw = k_inv * (d_k_unit - k_unit * jnp.sum(d_k_unit * k_unit, -1, keepdims=True))
    d_act = jnp.concatenate(
        [
            d_q_raw.reshape(seq_len, width),
            d_k_raw.reshape(seq_len, width),
            from_groups(d_v_groups).reshape(seq_len, width),
        ],
        1,
    )
    d_pre = silu_back(d_act, pre)
    d_extended = jnp.zeros((seq_len + rim, d_pre.shape[1]), jnp.float32)
    conv_grads = []
    for tap in range(rim + 1):
        masked = d_pre * matches[tap]
        d_extended = d_extended + jnp.pad(conv_f[tap] * masked, ((rim - tap, tap), (0, 0)))
        conv_grads.append(jnp.sum(masked * extended[rim - tap : rim - tap + seq_len], 0))
    grad_conv = jnp.stack(conv_grads)
    rim_back = shifted(d_extended[:rim].astype(jnp.bfloat16), "seq", -1).astype(jnp.float32)
    d_proj = (d_extended[rim:] + jnp.pad(rim_back, ((seq_len - rim, 0), (0, 0)))).astype(
        jnp.bfloat16
    )
    d_rates_tok = d_rate_groups.transpose(0, 2, 1).reshape(seq_len, H)
    d_logits = (d_rates_tok * rates_tok * (1.0 - rates_tok)).astype(jnp.bfloat16)
    grad_qkv = tok_dot(first_activation, d_proj)
    grad_beta = tok_dot(first_activation, d_logits)
    first_activation_gradient = back_dot(d_proj, w_qkv) + back_dot(d_logits, w_beta)
    first_gain_gradient = jnp.sum(first_activation_gradient * normalized_input, 0)
    block_input_gradient = (
        residual_gradient
        + root_mean_square_backward(
            first_activation_gradient * float_gains[0], normalized_input, first_inverse_norm
        )
    ).astype(jnp.bfloat16)
    grad_gains = jnp.stack([first_gain_gradient, grad_gain_two])
    red_qkv, red_beta, red_conv, red_gains, red_head, red_out, red_gu, red_down = (
        lax.psum_scatter(
            grad_qkv.astype(jnp.bfloat16), "seq", scatter_dimension=0, tiled=True
        ).astype(jnp.float32),
        lax.psum_scatter(
            grad_beta.astype(jnp.bfloat16), "seq", scatter_dimension=0, tiled=True
        ).astype(jnp.float32),
        lax.psum_scatter(
            grad_conv.astype(jnp.bfloat16), "seq", scatter_dimension=1, tiled=True
        ).astype(jnp.float32),
        lax.psum_scatter(
            grad_gains.astype(jnp.bfloat16), "seq", scatter_dimension=1, tiled=True
        ).astype(jnp.float32),
        lax.psum_scatter(
            grad_head.astype(jnp.bfloat16), "seq", scatter_dimension=0, tiled=True
        ).astype(jnp.float32),
        lax.psum_scatter(
            grad_out.astype(jnp.bfloat16), "seq", scatter_dimension=0, tiled=True
        ).astype(jnp.float32),
        lax.psum_scatter(
            grad_gate_up.astype(jnp.bfloat16), "seq", scatter_dimension=0, tiled=True
        ).astype(jnp.float32),
        lax.psum_scatter(
            grad_down.astype(jnp.bfloat16), "seq", scatter_dimension=0, tiled=True
        ).astype(jnp.float32),
    )
    red_qkv, red_beta, red_conv, red_gains, red_head, red_out, red_gu, red_down = (
        lax.psum(red_qkv.astype(jnp.bfloat16), "row").astype(jnp.float32),
        lax.psum(red_beta.astype(jnp.bfloat16), "row").astype(jnp.float32),
        lax.psum(red_conv.astype(jnp.bfloat16), "row").astype(jnp.float32),
        lax.psum(red_gains.astype(jnp.bfloat16), "row").astype(jnp.float32),
        lax.psum(red_head.astype(jnp.bfloat16), "row").astype(jnp.float32),
        lax.psum(red_out.astype(jnp.bfloat16), "row").astype(jnp.float32),
        lax.psum(red_gu.astype(jnp.bfloat16), "row").astype(jnp.float32),
        lax.psum(red_down.astype(jnp.bfloat16), "row").astype(jnp.float32),
    )
    return (
        mixed[None],
        block_input_gradient[None],
        red_qkv,
        red_beta,
        red_conv,
        red_gains,
        red_head,
        red_out,
        red_gu,
        red_down,
    )


BF = jnp.bfloat16
F32 = jnp.float32
RIM = 8
NN = (((1,), (0,)), ((), ()))
NT = (((1,), (1,)), ((), ()))
TN = (((0,), (0,)), ((), ()))


def dot_low(a, b, dims=NN):
    return lax.dot_general(a, b, dims, preferred_element_type=F32)


def parts_of(a):
    if a.dtype == BF:
        return (a,)
    high = a.astype(BF)
    return high, (a - high.astype(F32)).astype(BF)


def mm(a, b, dims=NN):
    a_parts, b_parts = parts_of(a), parts_of(b)
    total = dot_low(a_parts[0], b_parts[0], dims)
    if len(b_parts) > 1:
        total = total + dot_low(a_parts[0], b_parts[1], dims)
    if len(a_parts) > 1:
        total = total + dot_low(a_parts[1], b_parts[0], dims)
    return total


def mm1(a, b, dims=NN):
    return dot_low(a.astype(BF), b.astype(BF), dims)


def begin_of(pos, starts_ref):
    begin = jnp.zeros_like(pos)
    for i in range(starts_ref.shape[0]):
        begin = jnp.maximum(begin, jnp.where(pos >= starts_ref[i], starts_ref[i], 0))
    return begin


def begin_at(pos, starts_ref):
    begin = jnp.int32(0)
    for i in range(starts_ref.shape[0]):
        begin = jnp.maximum(begin, jnp.where(starts_ref[i] <= pos, starts_ref[i], 0))
    return begin


def mark_table(chunks, size, taps, starts_ref):
    pos = lax.broadcasted_iota(jnp.int32, (chunks, size), 0) * size
    pos = pos + lax.broadcasted_iota(jnp.int32, (chunks, size), 1)
    rows = begin_of(pos, starts_ref)
    later = [
        ((begin_of(pos + tap, starts_ref) <= pos) & (pos + tap < chunks * size)).astype(F32)
        for tap in range(1, taps)
    ]
    down = lax.broadcasted_iota(jnp.int32, (size, size), 0)
    eye = (down == lax.broadcasted_iota(jnp.int32, (size, size), 1)).astype(BF)
    rows = rows.astype(F32)
    return rows, mm(eye, rows, NT), [mm(eye, v, NT) for v in later]


def chunk_marks(n, size, table, starts_ref):
    first = n * size
    col = table[1][:, n : n + 1]
    last = begin_at(first + size - 1, starts_ref)
    keep = (col < float(first)).astype(F32)
    tail = (col == last.astype(F32)).astype(F32)
    whole = (last < first).astype(F32)
    return col, keep, tail, whole


def chunk_masks(n, size, col, table):
    here = lax.broadcasted_iota(jnp.int32, (size, size), 0)
    there = lax.broadcasted_iota(jnp.int32, (size, size), 1)
    same = col == table[0][n : n + 1]
    return here, there, same & (here > there), same & (here >= there)


def conv_chunk(n, size, pad, conv, col):
    depth = (n * size + lax.broadcasted_iota(jnp.int32, (size, 1), 0)).astype(F32) - col
    pre = conv[0:1, :] * pad[pl.ds(RIM + n * size, size), :]
    for tap in range(1, conv.shape[0]):
        match = (depth >= float(tap)).astype(F32)
        pre = pre + conv[tap : tap + 1, :] * pad[pl.ds(RIM - tap + n * size, size), :] * match
    return pre


def front_kernel(taps, place_ref, starts_ref, *refs):
    n_seq = refs[-1].shape[0]
    n_row = n_seq // 2
    top_ref, low_refs = refs[0], refs[1 : 1 + n_seq]
    got_ref, got_y_ref, got_cores_ref = refs[1 + n_seq : 4 + n_seq]
    got_refs = (got_ref, got_cores_ref.at[0], got_y_ref, got_cores_ref.at[1])
    (
        weight_ref,
        act1_ref,
        proj_ref,
        rates_ref,
        o_ref,
        act2_ref,
        inv_ref,
        w_ref,
        att_ref,
        p_ref,
        u_ref,
        s_ref,
        conv_ref,
        gains_ref,
        beta_ref,
        head_ref,
        pad,
        lower,
        tmp,
        q_scr,
        k_scr,
        v_scr,
        low_rows,
        add,
    ) = refs[4 + n_seq :]
    place, row = place_ref[0], place_ref[1]
    size = s_ref.shape[1]
    part_rows = size // n_row
    dk = o_ref.shape[1]
    base = 3 * part_rows
    gains = jnp.concatenate([got_ref[s, base + 4 : base + 6, :] for s in range(n_seq)], 1).astype(F32)
    gains_ref[...] = jnp.zeros_like(gains_ref)
    gains_ref[0:2, :] = gains
    beta = jnp.concatenate([got_ref[s, base + 8 : base + 16, :] for s in range(n_seq)], 1)
    beta_ref[...] = beta
    head_gain = got_ref[0, base + 6 : base + 7, :].astype(F32)
    for s in range(1, n_seq):
        head_gain = head_gain + got_ref[s, base + 6 : base + 7, :].astype(F32)
    head_ref[...] = jnp.broadcast_to(head_gain, head_ref.shape)
    conv_parts = []
    for part in range(3):
        block = part * n_seq + place
        shard = block // 3
        offset = pl.multiple_of(base + (block - shard * 3) * 16, 16)
        conv_parts.append(got_ref[shard, pl.ds(offset, 16), :][0:8])
    conv = jnp.concatenate(conv_parts, 1).astype(F32)
    conv_ref[...] = conv
    conv = conv[0:taps]
    for m, ref in enumerate(got_refs):
        for s in range(n_seq):
            at = pl.multiple_of(s * size + (row ^ m) * part_rows, part_rows)
            for kind in range(3):
                block = ref[s, kind * part_rows : (kind + 1) * part_rows, :]
                weight_ref[pl.ds(at, part_rows), kind * dk : (kind + 1) * dk] = block
    weight = weight_ref[...]
    lanes = lax.broadcasted_iota(jnp.int32, (2 * size, 8), 1)
    half = n_seq // 2
    z, side = place // 2, lax.rem(place, 2)
    for i, ref in enumerate(low_refs):
        chunk = lax.rem(z - i // 2 + half, half) * 2 + (side if i % 2 == 0 else 1 - side)
        at = pl.multiple_of(chunk * (size // 2), size // 2)
        low_rows[pl.ds(at, size // 2), :] = ref[...]
    pad[0:RIM, :] = jnp.zeros((RIM, 3 * dk), F32)
    for n in range(0, n_seq, 2):
        rows_at = pl.ds(n * size, 2 * size)
        part = size // 2
        rows = jnp.concatenate(
            [
                top_ref[n * part : (n + 1) * part, :],
                low_rows[n * part : (n + 1) * part, :],
                top_ref[(n + 1) * part : (n + 2) * part, :],
                low_rows[(n + 1) * part : (n + 2) * part, :],
            ],
            0,
        ).astype(F32)
        inv = lax.rsqrt(jnp.mean(rows * rows, -1, keepdims=True) + EPS_NORM)
        act = ((rows * inv) * gains[0:1]).astype(BF)
        act1_ref[rows_at, :] = act
        proj = dot_low(act, weight).astype(BF)
        proj_ref[rows_at, :] = proj
        pad[pl.ds(RIM + n * size, 2 * size), :] = proj.astype(F32)
        logits = dot_low(act, beta, NT)
        rate = jax.nn.sigmoid(jnp.sum(jnp.where(lanes == place, logits, 0.0), 1, keepdims=True))
        rates_ref[rows_at, :] = jnp.broadcast_to(rate, (2 * size, dk))
    table = mark_table(n_seq, size, taps, starts_ref)
    marks = []
    for n in range(n_seq):
        at = n * size
        col, keep, tail, whole = chunk_marks(n, size, table, starts_ref)
        marks.append((keep, tail, whole))
        pre = conv_chunk(n, size, pad, conv, col)
        act = pre * jax.nn.sigmoid(pre)
        q_raw, k_raw, v_raw = act[:, :dk], act[:, dk : 2 * dk], act[:, 2 * dk :]
        q = (q_raw * lax.rsqrt(jnp.sum(q_raw * q_raw, -1, keepdims=True) + EPS_UNIT)).astype(BF)
        key = (k_raw * lax.rsqrt(jnp.sum(k_raw * k_raw, -1, keepdims=True) + EPS_UNIT)).astype(BF)
        q_scr[pl.ds(at, size), :] = q
        k_scr[pl.ds(at, size), :] = key
        v_scr[pl.ds(at, size), :] = v_raw.astype(BF)
        here, there, strict, incl = chunk_masks(n, size, col, table)
        rate = rates_ref[pl.ds(at, size), :]
        low = jnp.where(strict, dot_low(key, key, NT) * rate, 0.0)
        att_ref[n] = jnp.where(incl, dot_low(q, key, NT) * (dk**-0.5), 0.0)
        lower[n] = low
        eye = (here == there).astype(F32)
        inv_ref[n] = eye - jnp.where((here // 2) == (there // 2), low, 0.0)
    span = 2
    while span < size:
        here = lax.broadcasted_iota(jnp.int32, (size, size), 0)
        there = lax.broadcasted_iota(jnp.int32, (size, size), 1)
        cross = ((here // (2 * span)) == (there // (2 * span))) & ((here // span) != (there // span))
        for n in range(n_seq):
            tmp[n] = mm1(inv_ref[n], jnp.where(cross, lower[n], 0.0))
        for n in range(n_seq):
            inv_ref[n] = inv_ref[n] - mm1(tmp[n], inv_ref[n])
        span *= 2
    for n in range(n_seq):
        keep, tail, whole = marks[n]
        rows = pl.ds(n * size, size)
        rate = rates_ref[rows, :]
        key = k_scr[rows, :]
        inv = inv_ref[n]
        w = mm(inv, rate * key.astype(F32))
        base = mm(inv, rate * v_scr[rows, :].astype(F32))
        w_ref[n] = w
        u_ref[n] = base
        p_ref[n] = mm(key, (tail * keep) * w, TN)
        add[n] = mm(key, tail * base, TN)
    state = jnp.zeros((dk, dk), F32)
    for n in range(n_seq):
        s_ref[n] = state
        if n + 1 < n_seq:
            state = marks[n][2] * state - mm(p_ref[n], state) + add[n]
    for n in range(n_seq):
        keep, tail, whole = marks[n]
        rows = pl.ds(n * size, size)
        state = s_ref[n]
        u = u_ref[n] - keep * mm(w_ref[n], state)
        u_ref[n] = u
        out = (keep * (dk**-0.5)) * mm(q_scr[rows, :], state) + mm(att_ref[n], u)
        o_ref[rows, :] = out
        inv = lax.rsqrt(jnp.mean(out * out, -1, keepdims=True) + EPS_HEAD)
        act2_ref[n] = ((out * inv) * head_gain).astype(BF)


def back_kernel(taps, place_ref, starts_ref, *refs):
    (
        dact_ref,
        o_ref,
        head_ref,
        conv_ref,
        proj_ref,
        rates_ref,
        inv_ref,
        w_ref,
        att_ref,
        p_ref,
        u_ref,
        s_ref,
        weight_ref,
        beta_ref,
        dproj_ref,
        part_ref,
        dlog_ref,
        gconv_ref,
        ghead_ref,
        logit_scr,
        pad,
        pre_scr,
        dpre,
        do_scr,
        g_scr,
        add,
        x_scr,
        q_scr,
        k_scr,
    ) = refs
    n_seq, size, dk = dact_ref.shape
    scale = dk**-0.5
    place = place_ref[0]
    beta_all = beta_ref[...].astype(F32)
    beta_lane = lax.broadcasted_iota(jnp.int32, beta_all.shape, 0) == place
    beta_row = jnp.sum(jnp.where(beta_lane, beta_all, 0.0), 0, keepdims=True)
    head_gain = head_ref[0:1, :]
    conv = conv_ref[0:taps, :]
    total = n_seq * size
    pad[0:RIM, :] = jnp.zeros((RIM, 3 * dk), F32)
    pad[pl.ds(RIM, total), :] = proj_ref[...].astype(F32)
    dpre[pl.ds(total, RIM), :] = jnp.zeros((RIM, 3 * dk), F32)
    table = mark_table(n_seq, size, taps, starts_ref)
    marks = []
    ghead = jnp.zeros((1, dk), F32)
    for n in range(n_seq):
        rows = pl.ds(n * size, size)
        col, keep, tail, whole = chunk_marks(n, size, table, starts_ref)
        marks.append((col, keep, tail, whole))
        pre = conv_chunk(n, size, pad, conv, col)
        pre_scr[rows, :] = pre
        act = pre * jax.nn.sigmoid(pre)
        q_raw, k_raw = act[:, :dk], act[:, dk : 2 * dk]
        q = (q_raw * lax.rsqrt(jnp.sum(q_raw * q_raw, -1, keepdims=True) + EPS_UNIT)).astype(BF)
        key = (k_raw * lax.rsqrt(jnp.sum(k_raw * k_raw, -1, keepdims=True) + EPS_UNIT)).astype(BF)
        q_scr[rows, :] = q
        k_scr[rows, :] = key
        out = o_ref[rows, :]
        inv = lax.rsqrt(jnp.mean(out * out, -1, keepdims=True) + EPS_HEAD)
        ohat = out * inv
        d_act2 = dact_ref[n].astype(F32)
        ghead = ghead + jnp.sum(d_act2 * ohat, 0, keepdims=True)
        lean = d_act2 * head_gain
        d_out = inv * (lean - ohat * jnp.mean(lean * ohat, -1, keepdims=True))
        do_scr[rows, :] = d_out
        g_scr[rows, :] = mm1(att_ref[n], d_out, TN)
    ghead_ref[...] = jnp.broadcast_to(ghead, ghead_ref.shape)
    for n in range(n_seq):
        rows = pl.ds(n * size, size)
        col, keep, tail, whole = marks[n]
        add[n] = mm1(q_scr[rows, :], (scale * keep) * do_scr[rows, :], TN) - mm1(w_ref[n], keep * g_scr[rows, :], TN)
    grad = jnp.zeros((dk, dk), F32)
    for n in range(n_seq - 1, -1, -1):
        x_scr[n] = grad
        if n > 0:
            grad = marks[n][3] * grad - mm(p_ref[n], grad, TN) + add[n]
    gconv = [jnp.zeros((1, 3 * dk), F32) for _ in range(taps)]
    for n in range(n_seq - 1, -1, -1):
        rows = pl.ds(n * size, size)
        col, keep, tail, whole = marks[n]
        here, there, strict, incl = chunk_masks(n, size, col, table)
        rate = rates_ref[rows, :]
        key, q = k_scr[rows, :], q_scr[rows, :]
        key_f, q_f = key.astype(F32), q.astype(F32)
        pre = pre_scr[rows, :]
        sig = jax.nn.sigmoid(pre)
        act = pre * sig
        value = act[:, 2 * dk :].astype(BF).astype(F32)
        grad, state, u = x_scr[n], s_ref[n], u_ref[n]
        d_out = do_scr[rows, :]
        d_u = g_scr[rows, :] + tail * mm1(key, grad)
        d_r = mm1(inv_ref[n], d_u, TN)
        d_att = jnp.where(incl, mm1(d_out, u, NT), 0.0)
        d_low = jnp.where(strict, -mm1(d_r, u, NT), 0.0)
        d_q = keep * mm1(d_out, state, NT) + mm1(d_att, key)
        d_kb = mm1(d_low, key) - keep * mm1(d_r, state, NT)
        d_k = (
            scale * mm1(d_att, q, TN)
            + mm1(d_low, rate * key_f, TN)
            + tail * mm1(u, grad, NT)
            + rate * d_kb
        )
        d_v = rate * d_r
        d_rate = jnp.sum(d_r * value + d_kb * key_f, -1, keepdims=True)
        d_q = d_q * scale
        q_raw, k_raw = act[:, :dk], act[:, dk : 2 * dk]
        q_inv = lax.rsqrt(jnp.sum(q_raw * q_raw, -1, keepdims=True) + EPS_UNIT)
        k_inv = lax.rsqrt(jnp.sum(k_raw * k_raw, -1, keepdims=True) + EPS_UNIT)
        q_unit, k_unit = q_raw * q_inv, k_raw * k_inv
        d_q = q_inv * (d_q - q_unit * jnp.sum(d_q * q_unit, -1, keepdims=True))
        d_k = k_inv * (d_k - k_unit * jnp.sum(d_k * k_unit, -1, keepdims=True))
        d_act = jnp.concatenate([d_q, d_k, d_v], 1)
        d_pre = d_act * sig * (1.0 + pre * (1.0 - sig))
        dpre[rows, :] = d_pre
        depth = (n * size + lax.broadcasted_iota(jnp.int32, (size, 1), 0)).astype(F32) - col
        d_proj = conv[0:1, :] * d_pre
        gconv[0] = gconv[0] + jnp.sum(d_pre * pad[pl.ds(RIM + n * size, size), :], 0, keepdims=True)
        for tap in range(1, taps):
            match = table[2][tap - 1][:, n : n + 1]
            d_proj = d_proj + conv[tap : tap + 1, :] * dpre[pl.ds(n * size + tap, size), :] * match
            reach = (depth >= float(tap)).astype(F32)
            gconv[tap] = gconv[tap] + jnp.sum(
                d_pre * reach * pad[pl.ds(RIM - tap + n * size, size), :], 0, keepdims=True
            )
        d_proj = d_proj.astype(BF)
        dproj_ref[rows, :] = d_proj
        one_rate = rate[:, 0:1]
        d_logit = (d_rate * one_rate * (1.0 - one_rate)).astype(BF).astype(F32)
        logit_scr[rows, :] = jnp.broadcast_to(d_logit, (size, dk))
        dlog_ref[pl.ds(n, 1), :] = jnp.broadcast_to(d_logit, (size, dk)).T[0:1]
    for n in range(0, n_seq, 2):
        rows = pl.ds(n * size, 2 * size)
        d_act1 = dot_low(dproj_ref[rows, :], weight_ref[...], NT) + logit_scr[rows, 0:1] * beta_row
        part_ref[rows, :] = d_act1.astype(BF)
    gconv_ref[...] = jnp.zeros_like(gconv_ref)
    for tap in range(taps):
        gconv_ref[tap : tap + 1, :] = gconv[tap]


def lead_kernel(place_ref, qkv_ref, conv_ref, gains_ref, head_ref, beta_ref, out_ref, rows):
    place, row = place_ref[0], place_ref[1]
    heads, dk = out_ref.shape[0], out_ref.shape[2]
    part = dk // 4
    from_row = pl.ds(pl.multiple_of(row * part, part), part)
    per = head_ref.shape[1]
    down = lax.broadcasted_iota(jnp.int32, (dk, dk), 0)
    along = lax.broadcasted_iota(jnp.int32, (dk, dk), 1)
    spot = (along == down + place * per)[0:per].astype(BF)
    rows[...] = jnp.zeros_like(rows)
    taps = conv_ref.shape[0]
    for kind in range(3):
        rows[kind * 16 : kind * 16 + taps, :] = conv_ref[:, kind * dk : (kind + 1) * dk].astype(F32)
    rows[4:6, :] = gains_ref[...].astype(F32)
    rows[6:7, :] = dot_low(jnp.broadcast_to(head_ref[...], (16, per)), spot)[0:1]
    rows[8:16, :] = beta_ref[...].astype(F32)
    small = rows[...].astype(BF)
    for h in range(heads):
        for kind in range(3):
            block = qkv_ref[from_row, pl.ds((kind * heads + h) * dk, dk)]
            out_ref[h, kind * part : (kind + 1) * part, :] = block
        out_ref[h, 3 * part : 3 * part + 48, :] = small


SLOT = 96


def columns_kernel(place_ref, gu_ref, down_ref, own_ref, other_ref, rows_ref, wide_own, wide_other):
    side, row = lax.rem(place_ref[0], 2), place_ref[1]
    size, lanes = gu_ref.shape[0], own_ref.shape[1]
    hidden = down_ref.shape[0]
    part, wide = hidden // 4, wide_own.shape[1] // 2
    for ref in (wide_own, wide_other):
        for kind in range(2):
            ref[:, kind * wide + wide - 128 : (kind + 1) * wide] = jnp.zeros((size, 128), F32)

    def take(x, r):
        for ref, block in ((wide_own, x), (wide_other, 1 - x)):
            for kind in range(2):
                for z in range(4):
                    at = (kind * 8 + z * 2 + block) * hidden + r * part
                    to = kind * wide + z * part
                    ref[:, to : to + part] = gu_ref[:, at : at + part].astype(F32)
        for j in range(down_ref.shape[1] // lanes):
            block = down_ref[r * part : (r + 1) * part, j * lanes : (j + 1) * lanes].astype(F32)
            block = jnp.concatenate([block, jnp.zeros((SLOT - part, lanes), F32)], 0)
            rows_ref[j * SLOT : (j + 1) * SLOT, :] = block.astype(BF)

    for x in range(2):
        for r in range(4):
            pl.when((side == x) & (row == r))(functools.partial(take, x, r))
    for ref, out in ((wide_own, own_ref), (wide_other, other_ref)):
        for j in range(2 * wide // lanes):
            out[j * size : (j + 1) * size, :] = ref[:, j * lanes : (j + 1) * lanes].astype(BF)


def mid_kernel(place_ref, act2_ref, own_ref, y_ref, cores_ref, x_ref, gains_ref, resid_ref, act3_ref, weight_ref):
    row = place_ref[1]
    heads, size, dk = act2_ref.shape
    part = dk // 4
    for m in range(4):
        ref = (own_ref, cores_ref.at[0], y_ref, cores_ref.at[1])[m]
        for s in range(heads):
            at = pl.multiple_of((s * 4 + (row ^ m)) * part, part)
            weight_ref[pl.ds(at, part), :] = ref[s]
    act2 = jnp.concatenate([act2_ref[h] for h in range(heads)], 1)
    resid = x_ref[...].astype(F32) + dot_low(act2, weight_ref[...])
    resid_ref[...] = resid
    inv = lax.rsqrt(jnp.mean(resid * resid, -1, keepdims=True) + EPS_NORM)
    act3_ref[...] = ((resid * inv) * gains_ref[1:2, :]).astype(BF)


GROUP_BITS = (0, 2, 4, 6, 1, 3, 5, 7)


def store_part(bits, block, own_ref, next_ref):
    @pl.when((bits & 1) == 0)
    def _():
        own_ref[bits >> 1] = block

    @pl.when((bits & 1) == 1)
    def _():
        next_ref[bits >> 1] = block


def mixed_kernel(place_ref, act4_ref, down_ref, own_ref, next_ref):
    me = lax.rem(place_ref[0], 2) * 4 + place_ref[1]
    size = own_ref.shape[1]
    for i in range(4):
        parts = dot_low(act4_ref[pl.ds(i * 2 * size, 2 * size), :], down_ref[...]).astype(BF)
        for half in range(2):
            store_part(me ^ (2 * i + half), parts[half * size : (half + 1) * size], own_ref, next_ref)


def feed_kernel(hidden, place_ref, *refs):
    act3_refs, core_ref, cot_refs, cot_core_ref, packs_ref = refs[0:4], refs[4], refs[5:9], refs[9], refs[10]
    own_ref, next_ref, act4_ref, dgu_ref, act3_ref, cot_ref, down_ref, gu, down32 = refs[11:]
    place, row = place_ref[0], place_ref[1]
    side = lax.rem(place, 2)
    me = side * 4 + row
    size, width = act3_refs[0].shape
    wide = act4_ref.shape[1]
    lanes = packs_ref.shape[2]
    slot, part = 96, hidden // 4
    gu_rows = gu.shape[0] // 4
    n_cols = gu.shape[1] // lanes
    down32[hidden:wide, :] = jnp.zeros((wide - hidden, width), F32)

    for src in range(4):
        for i in range(2):
            shard = src * 2 + (side if i == 0 else 1 - side)
            rows = pl.ds(pl.multiple_of(shard * size, size), size)
            for j in range(n_cols):
                from_rows = pl.ds((i * n_cols + j) * size, size)
                gu[rows, j * lanes : (j + 1) * lanes] = packs_ref[src, from_rows, :]
        for j in range(width // lanes):
            block = packs_ref[src, pl.ds(n_cols * gu_rows + j * slot, slot), :].astype(F32)
            down32[src * part : (src + 1) * part, j * lanes : (j + 1) * lanes] = block[0:part]
    down_ref[...] = down32[...].astype(BF)
    for i, bits in enumerate(GROUP_BITS):
        at = pl.multiple_of((me ^ bits) * size, size)
        act3_ref[pl.ds(at, size), :] = act3_refs[i][...] if i < 4 else core_ref[i - 4]
        cot_ref[pl.ds(at, size), :] = cot_refs[i][...] if i < 4 else cot_core_ref[i - 4]
    for i in range(4):
        rows = pl.ds(i * 2 * size, 2 * size)
        act3 = act3_ref[rows, :]
        cot = cot_ref[rows, :]
        gate_up = dot_low(act3, gu[...])
        gate, up = gate_up[:, :wide], gate_up[:, wide:]
        sig = jax.nn.sigmoid(gate)
        silu = gate * sig
        act4_ref[rows, :] = (silu * up).astype(BF)
        d_act4 = dot_low(cot, down_ref[...], NT)
        d_gate = d_act4 * up * sig * (1.0 + gate * (1.0 - sig))
        d_gu = jnp.concatenate([d_gate, d_act4 * silu], 1).astype(BF)
        dgu_ref[rows, :] = d_gu
        parts = dot_low(d_gu, gu[...], NT).astype(BF)
        for half in range(2):
            store_part(me ^ (2 * i + half), parts[half * size : (half + 1) * size], own_ref, next_ref)


def grads_kernel(hidden, place_ref, act3_ref, cot_ref, act4_ref, dgu_ref, out_ref, down32):
    side = lax.rem(place_ref[0], 2)
    lanes = out_ref.shape[2]
    slot, part = 96, hidden // 4
    gu_rows = act3_ref.shape[1] // 4
    n_cols = dgu_ref.shape[1] // lanes
    down32[...] = dot_low(act4_ref[...], cot_ref[...], TN)
    for k in range(4):
        at = k * gu_rows
        grad = dot_low(act3_ref[:, at : at + gu_rows], dgu_ref[...], TN).astype(BF)
        size = gu_rows // 2
        for parity in range(2):
            first = jnp.where(side == parity, 0, n_cols * size)
            for j in range(n_cols):
                rows = pl.ds(pl.multiple_of(first + j * size, size), size)
                out_ref[k, rows, :] = grad[parity * size : (parity + 1) * size, j * lanes : (j + 1) * lanes]
        rows = pl.ds(k * part, part)
        for j in range(cot_ref.shape[1] // lanes):
            block = down32[rows, j * lanes : (j + 1) * lanes]
            block = jnp.concatenate([block, jnp.zeros((slot - part, lanes), F32)], 0)
            out_ref[k, pl.ds(n_cols * gu_rows + j * slot, slot), :] = block.astype(BF)


def out_grad_kernel(place_ref, act2_ref, low_ref, same_ref, other_ref, full):
    row = place_ref[1]
    heads, _, dk = act2_ref.shape
    part = dk // 4
    for h in range(heads):
        full[h * dk : (h + 1) * dk, :] = dot_low(act2_ref[h], low_ref[...], TN)
    for m in range(4):
        ref = same_ref if m % 2 == 0 else other_ref
        for h in range(heads):
            at = pl.multiple_of(h * dk + (row ^ m) * part, part)
            ref[m // 2, h] = full[pl.ds(at, part), :].astype(BF)


def qkv_grad_kernel(place_ref, act1_ref, dproj_ref, dlog_ref, gconv_ref, ghead_ref, same_ref, other_ref, full, rows):
    row = place_ref[1]
    shards, total, cols = same_ref.shape[1:]
    dk = cols // 3
    part = total - 16
    for h in range(shards):
        lanes = pl.ds(h * dk, dk)
        full[h * dk : (h + 1) * dk, :] = dot_low(act1_ref[:, lanes], dproj_ref[...], TN)
    g_beta = None
    dlog = dlog_ref[...].astype(BF)
    for n in range(dlog.shape[0]):
        one = jnp.broadcast_to(dlog[n : n + 1], (16, dk))
        term = dot_low(one, act1_ref[n * dk : (n + 1) * dk, :])[0:1]
        g_beta = term if g_beta is None else g_beta + term
    rows[...] = jnp.zeros_like(rows)
    for s in range(shards):
        rows[s, 0:4, :] = gconv_ref[0:4, :]
        rows[s, 4:5, 0:dk] = g_beta[:, s * dk : (s + 1) * dk]
        rows[s, 4:5, dk : 2 * dk] = ghead_ref[0:1, :]
    for m in range(4):
        ref = same_ref if m % 2 == 0 else other_ref
        for s in range(shards):
            at = pl.multiple_of(s * dk + (row ^ m) * part, part)
            ref[m // 2, s, 0:part, :] = full[pl.ds(at, part), :].astype(BF)
            ref[m // 2, s, pl.ds(part, 16), :] = rows[s].astype(BF)


def turn_kernel(heads, own_ref, core_ref, x_ref, y_ref, top_ref, bottom_ref, resid_ref, cot_ref, gains_ref, weight_ref, dresid_ref, low_ref, dact2_ref):
    resid = resid_ref[...]
    inv = lax.rsqrt(jnp.mean(resid * resid, -1, keepdims=True) + EPS_NORM)
    rhat = resid * inv
    d_act3 = own_ref[0].astype(F32) + core_ref[0].astype(F32)
    d_act3 = d_act3 + jnp.concatenate([x_ref[0], y_ref[0]], 0).astype(F32)
    d_act3 = d_act3 + jnp.concatenate([top_ref[...], bottom_ref[...]], 0).astype(F32)
    lean = d_act3 * gains_ref[1:2, :]
    d_resid = cot_ref[...].astype(F32) + inv * (lean - rhat * jnp.mean(lean * rhat, -1, keepdims=True))
    dresid_ref[...] = d_resid
    low = d_resid.astype(BF)
    low_ref[...] = low
    d_act2 = dot_low(low, weight_ref[...], NT).astype(BF)
    dk = d_act2.shape[1] // heads
    for h in range(heads):
        dact2_ref[h] = d_act2[:, h * dk : (h + 1) * dk]


def last_kernel(part_ref, x_ref, gains_ref, dresid_ref, out_ref):
    d_act1 = part_ref[...].astype(F32)
    rows = x_ref[...].astype(F32)
    inv = lax.rsqrt(jnp.mean(rows * rows, -1, keepdims=True) + EPS_NORM)
    xhat = rows * inv
    lean = d_act1 * gains_ref[0:1, :]
    out = dresid_ref[...] + inv * (lean - xhat * jnp.mean(lean * xhat, -1, keepdims=True))
    out_ref[...] = out.astype(BF)


def row_sums(v):
    total = jnp.sum(v, 1, keepdims=True)
    return jnp.broadcast_to(total, (v.shape[0], 128)).T[0:1]


def lay_feed_kernel(place_ref, *refs):
    own_ref, y_ref, cores_ref = refs[0:3]
    packs = (own_ref, cores_ref.at[0], y_ref, cores_ref.at[1])
    weight_ref, gain_ref, gu_out, down_out, gain_out, held = refs[3:]
    side, row = lax.rem(place_ref[0], 2), place_ref[1]
    size, hidden = gain_out.shape[1], down_out.shape[0]
    lanes, slot, part = packs[0].shape[1], 96, hidden // 4
    wide = held.shape[3] // 2
    n_cols = held.shape[3] // lanes
    for m in range(4):
        for own in range(2):
            block = side if own == 0 else 1 - side
            for j in range(n_cols):
                rows = pl.ds((own * n_cols + j) * size, size)
                held[row ^ m, block, :, j * lanes : (j + 1) * lanes] = packs[m][rows, :]
        at = pl.multiple_of((row ^ m) * part, 8)
        for j in range(down_out.shape[1] // lanes):
            block = packs[m][pl.ds(2 * n_cols * size + j * slot, slot), :].astype(F32)
            down_out[pl.ds(at, part), j * lanes : (j + 1) * lanes] = block[0:part]
    total = None
    for kind in range(2):
        for m in range(4):
            for x in range(2):
                for z in range(4):
                    at = kind * wide + z * part
                    piece = held[m, x, :, at : at + part].astype(F32)
                    to = (kind * 8 + z * 2 + x) * hidden + m * part
                    gu_out[:, to : to + part] = piece
    for at in range(0, gu_out.shape[1], lanes):
        term = gu_out[:, at : at + lanes] * weight_ref[:, at : at + lanes].astype(F32)
        total = term if total is None else total + term
    gain_out[...] = row_sums(total) / gain_ref[1:2, :].astype(F32)


def lay_mix_kernel(place_ref, *refs):
    qkv_refs = (refs[0], refs[2].at[0], refs[1], refs[2].at[1])
    out_refs = (refs[3], refs[5].at[0], refs[4], refs[5].at[1])
    weight_ref, beta_ref, gain_ref, second_ref, qkv_out, out_out, gain_out, conv_out, beta_out, head_out = refs[6:]
    place, row = place_ref[0], place_ref[1]
    heads, total, cols = qkv_refs[0].shape
    dk = cols // 3
    part = total - 16
    for m in range(4):
        rows = pl.ds(pl.multiple_of((row ^ m) * part, 8), part)
        out_out[rows, :] = out_refs[m][...].astype(F32)
        for h in range(heads):
            for kind in range(3):
                lanes = pl.ds((kind * heads + h) * dk, dk)
                block = qkv_refs[m][h, 0:part, kind * dk : (kind + 1) * dk]
                qkv_out[rows, lanes] = block.astype(F32)
    sums = jnp.sum(qkv_out[...] * weight_ref[...].astype(F32), 1, keepdims=True)
    ref = qkv_refs[0]
    small = [ref[h, pl.ds(part, 16), :].astype(F32) for h in range(heads)]
    beta_rows = jnp.concatenate([v[4:5, 0:dk] for v in small], 0)
    beta_out[...] = beta_rows
    head = small[0][4:5, dk : 2 * dk]
    for v in small[1:]:
        head = head + v[4:5, dk : 2 * dk]
    per = head_out.shape[1]
    spot = lax.broadcasted_iota(jnp.int32, (dk, per), 0) == (
        lax.broadcasted_iota(jnp.int32, (dk, per), 1) + place * per
    )
    head_out[...] = mm(jnp.broadcast_to(head, (8, dk)), spot.astype(BF))[0:1]
    for i in range(3):
        block = place * 3 + i
        kind = block // heads
        source = block - kind * heads
        lanes = pl.ds(pl.multiple_of(kind * dk, dk), dk)
        conv_out[:, i * dk : (i + 1) * dk] = ref[source, pl.ds(part, 16), lanes].astype(F32)[0 : conv_out.shape[0]]
    weight_rows = beta_ref[...].astype(F32)
    gain = jnp.broadcast_to(sums, (sums.shape[0], 128)).T[0:1]
    gain = gain + jnp.sum(beta_rows * weight_rows, 0, keepdims=True)
    gain_out[0:1, :] = gain / gain_ref[0:1, :].astype(F32)
    gain_out[1:2, :] = second_ref[...]


def local_call(kernel, outs, args, scratch=(), smem=0, us=1, mib=56, name=None):
    space = [pl.BlockSpec(memory_space=pltpu.SMEM)] * smem
    space += [pl.BlockSpec(memory_space=pltpu.VMEM)] * (len(args) - smem)
    return pl.pallas_call(
        kernel,
        out_shape=tuple(outs),
        in_specs=space,
        out_specs=tuple(pl.BlockSpec(memory_space=pltpu.VMEM) for _ in outs),
        scratch_shapes=list(scratch),
        compiler_params=pltpu.CompilerParams(vmem_limit_bytes=mib * 2**20),
        cost_estimate=pl.CostEstimate(flops=us * 10**9, bytes_accessed=1024, transcendentals=0),
        name=name,
    )(*args)


def head_plan(
    block_input,
    cotangent,
    doc_starts,
    qkv_weight,
    beta_weight,
    conv_weight,
    norm_gains,
    head_gain,
    out_weight,
    gate_up_weight,
    down_weight,
):
    x, cot = block_input[0], cotangent[0]
    starts = doc_starts[0]
    size, width = x.shape
    n_seq, n_row = lax.axis_size("seq"), lax.axis_size("row")
    place, row = lax.axis_index("seq"), lax.axis_index("row")
    half = n_seq // 2
    z, side = place // 2, place % 2
    total = n_seq * size
    where_at = jnp.stack([place, row])
    taps = conv_weight.shape[0]
    hidden = down_weight.shape[0]
    wide = -(-hidden // 128) * 128
    shape = jax.ShapeDtypeStruct

    def flip(v):
        return lax.ppermute(v, "seq", [(s, s ^ 1) for s in range(n_seq)])

    def roll(v, k):
        return lax.ppermute(v, "seq", [(s, (s // 2 + k) % half * 2 + s % 2) for s in range(n_seq)])

    def core(v):
        return lax.ppermute(v, "row", [(r, r ^ 1) for r in range(n_row)])

    def across(v):
        return lax.ppermute(v, "row", [(r, r ^ 2) for r in range(n_row)])

    def group_gather(v):
        y, s = across(v), flip(v)
        four = [v, y, s, flip(y)]
        return [*four, core(jnp.stack(four))]

    def row_sum(same, other):
        mine = same.astype(F32) + core(other).astype(F32)
        return mine[0], mine[1].astype(BF)

    def row_relative(v):
        y = across(v)
        return [v, core(v), y, core(y)]

    def stage(*values):
        return lax.optimization_barrier(values)

    def line(v, step, t):
        ends = range(t - 1, half - 1) if step > 0 else range(1, half - t + 1)
        return lax.ppermute(
            v, "seq", [(2 * a + j, 2 * (a + step) + j) for a in ends for j in range(2)]
        )

    part_rows = size // n_row
    dk = width // n_seq
    lead_rows = 3 * part_rows + 48
    mid_row = size // 2
    row_top = lax.all_gather(x[:mid_row], "seq", tiled=True)
    far = {k: roll(x[mid_row:], k) for k in (2, 1, 3)}
    near = flip(x[mid_row:])
    (payload,) = local_call(
        lead_kernel,
        [shape((n_seq, lead_rows, dk), BF)],
        [where_at, qkv_weight, conv_weight, norm_gains, head_gain.reshape(1, -1), beta_weight.T],
        scratch=[pltpu.VMEM((48, dk), F32)],
        smem=1,
        us=2,
        name="lead",
    )

    rows3 = shape((3 * size, 256), BF)
    pack_rows = 6 * size + 4 * SLOT
    own_cols, other_cols, down_rows = local_call(
        columns_kernel,
        [rows3, rows3, shape((4 * SLOT, 256), BF)],
        [where_at, gate_up_weight, down_weight],
        scratch=[pltpu.VMEM((size, 2 * wide), F32)] * 2,
        smem=1,
        us=2,
        name="columns",
    )
    pack = jnp.concatenate([own_cols, flip(other_cols), down_rows], 0)
    got = lax.all_to_all(payload, "seq", 0, 0)
    got_y = across(got)
    got_cores = core(jnp.stack([got, got_y]))
    out_part = lax.dynamic_slice_in_dim(out_weight, row * part_rows, part_rows, 0)
    out_part = jnp.broadcast_to(out_part[None], (n_seq, part_rows, width))
    groups_z = [[2 * a + j for a in range(half)] for j in range(2)]
    packs = lax.all_gather(pack, "seq", axis_index_groups=groups_z)
    out_part, _, near, far[1], far[2], far[3] = stage(out_part, pack, near, far[1], far[2], far[3])
    out_part = lax.all_to_all(out_part, "seq", 0, 0)
    row_low = [x[mid_row:], near]
    for k in range(1, half):
        row_low += [far[k], flip(far[k])]
    row_top, got, got_y, got_cores, out_part, cot, _, *row_low = stage(
        row_top, got, got_y, got_cores, out_part, cot, pack, *row_low
    )
    cot_y, cot_x = across(cot), flip(cot)
    out_y = across(out_part)
    square = shape((n_seq, size, dk), F32)
    (
        w_head,
        act1,
        proj,
        rates,
        outs,
        act2,
        inverse,
        w_mat,
        att,
        p_mat,
        u_mat,
        states,
        conv,
        gains,
        beta,
        head,
    ) = local_call(
        functools.partial(front_kernel, taps),
        [
            shape((width, 3 * dk), BF),
            shape((total, width), BF),
            shape((total, 3 * dk), BF),
            shape((total, dk), F32),
            shape((total, dk), F32),
            shape((n_seq, size, dk), BF),
            square,
            square,
            square,
            square,
            square,
            square,
            shape((8, 3 * dk), F32),
            shape((8, width), F32),
            shape((8, width), BF),
            shape((8, dk), F32),
        ],
        [where_at, starts, row_top, *row_low, got, got_y, got_cores],
        scratch=[
            pltpu.VMEM((RIM + total, 3 * dk), F32),
            pltpu.VMEM((n_seq, size, size), F32),
            pltpu.VMEM((n_seq, size, size), F32),
            pltpu.VMEM((total, dk), BF),
            pltpu.VMEM((total, dk), BF),
            pltpu.VMEM((total, dk), BF),
            pltpu.VMEM((total // 2, width), BF),
            pltpu.VMEM((n_seq, dk, dk), F32),
        ],
        smem=2,
        us=4,
        name="front",
    )
    act2, cot_y, cot_x, out_y = stage(act2, cot_y, cot_x, out_y)
    act2 = lax.all_to_all(act2, "seq", 0, 0)
    cot_four = [cot, cot_y, cot_x, flip(cot_y)]
    out_cores = core(jnp.stack([out_part, out_y]))
    act2, out_cores, cot_four[3] = stage(act2, out_cores, cot_four[3])
    cot_all = [*cot_four, core(jnp.stack(cot_four))]
    resid, act3, w_out = local_call(
        mid_kernel,
        [shape((size, width), F32), shape((size, width), BF), shape((width, width), BF)],
        [where_at, act2, out_part, out_y, out_cores, x, gains],
        smem=1,
        us=1,
        mib=24,
        name="mid",
    )
    four = shape((4, size, width), BF)
    d_own, d_next, act4, d_gu, act3_all, cot_all, w_down = local_call(
        functools.partial(feed_kernel, hidden),
        [
            four,
            four,
            shape((total, wide), BF),
            shape((total, 2 * wide), BF),
            shape((total, width), BF),
            shape((total, width), BF),
            shape((wide, width), BF),
        ],
        [where_at, *group_gather(act3), *cot_all, packs],
        scratch=[pltpu.VMEM((width, 2 * wide), BF), pltpu.VMEM((wide, width), F32)],
        smem=1,
        us=3,
        mib=24,
        name="feed",
    )
    d_got = core(d_next)
    (grads,) = local_call(
        functools.partial(grads_kernel, hidden),
        [shape((half, pack_rows, 256), BF)],
        [where_at, act3_all, cot_all, act4, d_gu],
        scratch=[pltpu.VMEM((wide, width), F32)],
        smem=1,
        us=3,
        mib=24,
        name="grads",
    )
    d_got, d_own, act4, grads = stage(d_got, d_own, act4, grads)
    grads = lax.psum_scatter(grads, "seq", scatter_dimension=0, axis_index_groups=groups_z)
    top, low = slice(0, mid_row), slice(mid_row, size)

    def core_sum(i, part):
        return d_own[i, part].astype(F32) + d_got[i, part].astype(F32)

    d_x = flip(jnp.stack([core_sum(2, top), core_sum(3, top)]).astype(BF))
    d_y = across(jnp.stack([core_sum(1, low), core_sum(3, low)]).astype(BF))
    mixed_own, mixed_next = local_call(
        mixed_kernel, [four, four], [where_at, act4, w_down], smem=1, us=5, name="mixed"
    )
    d_x, d_y, mixed_own, mixed_next = stage(d_x, d_y, mixed_own, mixed_next)
    d_top = across((core_sum(1, top) + d_x[1].astype(F32)).astype(BF))
    d_bottom = flip((core_sum(2, low) + d_y[1].astype(F32)).astype(BF))
    d_resid, d_low, d_act2 = local_call(
        functools.partial(turn_kernel, n_seq),
        [shape((size, width), F32), shape((size, width), BF), shape((n_seq, size, dk), BF)],
        [d_own, d_got, d_x, d_y, d_top, d_bottom, resid, cot, gains, w_out],
        us=1,
        mib=24,
        name="turn",
    )
    d_act2 = lax.all_to_all(d_act2, "seq", 0, 0)
    out_shape = shape((2, n_seq, part_rows, width), BF)
    out_same, out_other = local_call(
        out_grad_kernel,
        [out_shape, out_shape],
        [where_at, act2, d_low],
        scratch=[pltpu.VMEM((width, width), F32)],
        smem=1,
        us=3,
        name="out_grad",
    )
    d_act2, out_same, out_other, mixed_own, mixed_next = stage(d_act2, out_same, out_other, mixed_own, mixed_next)
    mixed_got = core(mixed_next)
    out_got = core(out_other)
    d_proj, parts, d_log, g_conv, g_head = local_call(
        functools.partial(back_kernel, taps),
        [
            shape((total, 3 * dk), BF),
            shape((total, width), BF),
            shape((n_seq, size), F32),
            shape((8, 3 * dk), F32),
            shape((8, dk), F32),
        ],
        [
            where_at,
            starts,
            d_act2,
            outs,
            head,
            conv,
            proj,
            rates,
            inverse,
            w_mat,
            att,
            p_mat,
            u_mat,
            states,
            w_head,
            beta,
        ],
        scratch=[
            pltpu.VMEM((total, dk), F32),
            pltpu.VMEM((RIM + total, 3 * dk), F32),
            pltpu.VMEM((total, 3 * dk), F32),
            pltpu.VMEM((RIM + total, 3 * dk), F32),
            pltpu.VMEM((total, dk), F32),
            pltpu.VMEM((total, dk), F32),
            pltpu.VMEM((n_seq, dk, dk), F32),
            pltpu.VMEM((n_seq, dk, dk), F32),
            pltpu.VMEM((total, dk), BF),
            pltpu.VMEM((total, dk), BF),
        ],
        smem=2,
        us=14,
        name="back",
    )
    d_proj, parts, d_log, g_conv, g_head, out_got, mixed_got, grads = stage(
        d_proj, parts, d_log, g_conv, g_head, out_got, mixed_got, grads
    )
    mixed_both = [mixed_own[i].astype(F32) + mixed_got[i].astype(F32) for i in range(4)]
    mixed_x = flip(jnp.stack([mixed_both[2], mixed_both[3]]).astype(BF))
    d_act1 = lax.psum_scatter(parts, "seq", scatter_dimension=0, tiled=True)
    out_mine = out_same[0].astype(F32) + out_got[0].astype(F32)
    out_y = across((out_same[1].astype(F32) + out_got[1].astype(F32)).astype(BF))
    out_piece = lax.all_to_all((out_mine + out_y.astype(F32)).astype(BF), "seq", 0, 0)
    out_piece = out_piece.astype(F32).sum(0).astype(BF)
    out_y = across(out_piece)
    out_cores = core(jnp.stack([out_piece, out_y]))
    mixed_y = across((mixed_both[1] + mixed_x[1].astype(F32)).astype(BF))
    mixed = (resid + mixed_both[0] + mixed_x[0].astype(F32) + mixed_y.astype(F32)).astype(BF)
    gu_rows = 3 * size
    gu_other = flip(grads[gu_rows : 2 * gu_rows])
    feed_part = jnp.concatenate([grads[:gu_rows], gu_other, grads[2 * gu_rows :]], 0)
    feed_y = across(feed_part)
    feed_cores = core(jnp.stack([feed_part, feed_y]))
    cut_shape = shape((2, n_seq, part_rows + 16, 3 * dk), BF)
    qkv_same, qkv_other = local_call(
        qkv_grad_kernel,
        [cut_shape, cut_shape],
        [where_at, act1, d_proj, d_log, g_conv, g_head],
        scratch=[pltpu.VMEM((width, 3 * dk), F32), pltpu.VMEM((n_seq, 16, 3 * dk), F32)],
        smem=1,
        us=5,
        name="qkv_grad",
    )
    qkv_got = core(qkv_other)
    qkv_mine = qkv_same[0].astype(F32) + qkv_got[0].astype(F32)
    qkv_y = across((qkv_same[1].astype(F32) + qkv_got[1].astype(F32)).astype(BF))
    qkv_piece = lax.all_to_all((qkv_mine + qkv_y.astype(F32)).astype(BF), "seq", 0, 0)
    qkv_y = across(qkv_piece)
    qkv_cores = core(jnp.stack([qkv_piece, qkv_y]))
    (input_gradient,) = local_call(
        last_kernel,
        [shape((size, width), BF)],
        [d_act1, x, gains, d_resid],
        us=3,
        mib=24,
        name="last",
    )
    red_gu, red_down, second_gain = local_call(
        lay_feed_kernel,
        [
            shape((size, 2 * n_seq * hidden), F32),
            shape((hidden, width), F32),
            shape((1, size), F32),
        ],
        [where_at, feed_part, feed_y, feed_cores, gate_up_weight, norm_gains],
        scratch=[pltpu.VMEM((n_row, 2, size, 2 * wide), BF)],
        smem=1,
        us=0,
        mib=24,
        name="lay_feed",
    )
    red_qkv, red_out, red_gains, red_conv, red_beta, red_head = local_call(
        lay_mix_kernel,
        [
            shape((size, 3 * width), F32),
            shape((size, width), F32),
            shape((2, size), F32),
            shape((taps, 3 * dk), F32),
            shape((n_seq, dk), F32),
            shape((1, head_gain.shape[0]), F32),
        ],
        [where_at, qkv_piece, qkv_y, qkv_cores, out_piece, out_y, out_cores, qkv_weight, beta_weight.T, norm_gains, second_gain],
        smem=1,
        us=3,
        mib=24,
        name="lay_mix",
    )
    red_beta = red_beta.T
    red_head = red_head[0]
    return (
        mixed[None],
        input_gradient[None],
        red_qkv,
        red_beta,
        red_conv,
        red_gains,
        red_head,
        red_out,
        red_gu,
        red_down,
    )


def plan(block_input, *rest):
    seq, row = lax.axis_size("seq"), lax.axis_size("row")
    if seq == H and row * 2 == H and block_input.shape[1] == DK:
        return head_plan(block_input, *rest)
    return on_device(block_input, *rest)


def solution(mesh):
    in_specs = (
        P("row", "seq", None),
        P("row", "seq", None),
        P("row", None),
        P("seq", None),
        P("seq", None),
        P(None, "seq"),
        P(None, "seq"),
        P("seq"),
        P("seq", None),
        P("seq", None),
        P("seq", None),
    )
    out_specs = (
        P("row", "seq", None),
        P("row", "seq", None),
        P("seq", None),
        P("seq", None),
        P(None, "seq"),
        P(None, "seq"),
        P("seq"),
        P("seq", None),
        P("seq", None),
        P("seq", None),
    )
    return jax.shard_map(
        plan, mesh=mesh, in_specs=in_specs, out_specs=out_specs, check_vma=False
    )
```

```python
import functools

import jax
import jax.numpy as jnp
from jax import lax
from jax.experimental import pallas as pl
from jax.experimental.pallas import tpu as pltpu
from jax.sharding import PartitionSpec as P

H = 8
DK = 128
GROUP = 64


EPS_NORM = 1e-06
EPS_HEAD = 1e-05
EPS_UNIT = 1e-06
HIGH = lax.Precision.HIGHEST


def shifted(block, axis, distance):
    devices = range(lax.axis_size(axis))
    route = [(i - distance, i) for i in devices if i - distance in devices]
    return lax.ppermute(block, axis, route)


def dotf(first_op, second_op):
    return jnp.matmul(first_op, second_op, precision=HIGH)


def swap_last(matrix):
    return jnp.swapaxes(matrix, -1, -2)


def tok_dot(first_op, second_op):
    return lax.dot_general(
        first_op, second_op, (((0,), (0,)), ((), ())), preferred_element_type=jnp.float32
    )


def back_dot(first_op, second_op):
    return lax.dot_general(
        first_op, second_op, (((1,), (1,)), ((), ())), preferred_element_type=jnp.float32
    )


def unit_inverse(lower):
    identity = jnp.eye(lower.shape[-1], dtype=lower.dtype)
    power = lower
    result = identity - lower
    for step_index in range(lower.shape[-1].bit_length() - 2):
        power = dotf(power, power)
        result = dotf(result, identity + power)
    return result


def doc_index(positions, starts):
    return jnp.sum((starts[None, :] <= positions[:, None]).astype(jnp.int32), axis=1) - 1


def root_mean_square_backward(grad_in, normed, inverse):
    return inverse * (grad_in - normed * jnp.mean(grad_in * normed, -1, keepdims=True))


def silu_back(grad_in, pre):
    sig = jax.nn.sigmoid(pre)
    return grad_in * sig * (1.0 + pre * (1.0 - sig))


def on_device(
    block_input,
    cotangent,
    doc_starts,
    qkv_weight,
    beta_weight,
    conv_weight,
    norm_gains,
    head_gain,
    out_weight,
    gate_up_weight,
    down_weight,
):
    token_rows = block_input[0].astype(jnp.float32)
    cot_low = cotangent[0]
    seq_len = token_rows.shape[0]
    width = token_rows.shape[1]
    n_groups = seq_len // GROUP
    scale = DK ** (-0.5)
    w_qkv, w_beta, w_conv, w_gains, w_head, w_out, w_gu, w_down = (
        lax.all_gather(qkv_weight, "seq", axis=0, tiled=True),
        lax.all_gather(beta_weight, "seq", axis=0, tiled=True),
        lax.all_gather(conv_weight, "seq", axis=1, tiled=True),
        lax.all_gather(norm_gains, "seq", axis=1, tiled=True),
        lax.all_gather(head_gain, "seq", axis=0, tiled=True),
        lax.all_gather(out_weight, "seq", axis=0, tiled=True),
        lax.all_gather(gate_up_weight, "seq", axis=0, tiled=True),
        lax.all_gather(down_weight, "seq", axis=0, tiled=True),
    )
    conv_f = w_conv.astype(jnp.float32)
    float_gains = w_gains.astype(jnp.float32)
    head_f = w_head.astype(jnp.float32)
    seq_count = lax.axis_size("seq")
    seq_place = lax.axis_index("seq")
    starts = doc_starts[0]
    positions = seq_place * seq_len + jnp.arange(seq_len, dtype=jnp.int32)
    doc = doc_index(positions, starts)
    rim = conv_f.shape[0] - 1
    rim_doc = doc_index(seq_place * seq_len - rim + jnp.arange(rim, dtype=jnp.int32), starts)
    first_inverse_norm = lax.rsqrt(jnp.mean(token_rows * token_rows, -1, keepdims=True) + EPS_NORM)
    normalized_input = token_rows * first_inverse_norm
    first_activation = (normalized_input * float_gains[0]).astype(jnp.bfloat16)
    proj = jnp.dot(first_activation, w_qkv, preferred_element_type=jnp.float32).astype(jnp.bfloat16)
    rates_tok = jax.nn.sigmoid(
        jnp.dot(first_activation, w_beta, preferred_element_type=jnp.float32)
    )
    rim_vals = shifted(proj[seq_len - rim :], "seq", 1)
    extended = jnp.concatenate([rim_vals, proj], 0).astype(jnp.float32)
    ext_doc = jnp.concatenate([rim_doc, doc])
    matches = [
        (ext_doc[rim - tap : rim - tap + seq_len] == doc).astype(jnp.float32)[:, None]
        for tap in range(rim + 1)
    ]
    pre = jnp.zeros((seq_len, extended.shape[1]), jnp.float32)
    for tap in range(rim + 1):
        pre = pre + conv_f[tap] * extended[rim - tap : rim - tap + seq_len] * matches[tap]
    act = jax.nn.silu(pre)
    q_raw = act[:, :width].reshape(seq_len, H, DK)
    k_raw = act[:, width : 2 * width].reshape(seq_len, H, DK)
    v_raw = act[:, 2 * width :].reshape(seq_len, H, DK)
    q_inv = lax.rsqrt(jnp.sum(q_raw * q_raw, -1, keepdims=True) + EPS_UNIT)
    k_inv = lax.rsqrt(jnp.sum(k_raw * k_raw, -1, keepdims=True) + EPS_UNIT)
    q_unit = q_raw * q_inv
    k_unit = k_raw * k_inv

    def to_groups(arr):
        return (
            arr.astype(jnp.bfloat16)
            .astype(jnp.float32)
            .reshape(n_groups, GROUP, H, DK)
            .transpose(0, 2, 1, 3)
        )

    scaled_q = to_groups(q_unit) * scale
    keys = to_groups(k_unit)
    values = to_groups(v_raw)
    rates = rates_tok.reshape(n_groups, GROUP, H).transpose(0, 2, 1)
    block_doc = doc.reshape(n_groups, GROUP)
    prev_doc = doc_index(
        seq_place * seq_len + jnp.arange(n_groups, dtype=jnp.int32) * GROUP - 1, starts
    )
    places = jnp.arange(GROUP)
    same = block_doc[:, :, None] == block_doc[:, None, :]
    strict = ((places[:, None] > places[None, :])[None] & same)[:, None].astype(jnp.float32)
    incl = ((places[:, None] >= places[None, :])[None] & same)[:, None].astype(jnp.float32)
    keep = (block_doc == prev_doc[:, None]).astype(jnp.float32)[:, None, :, None]
    tail = (block_doc == block_doc[:, -1:]).astype(jnp.float32)[:, None, :, None]
    whole = keep[:, 0, -1, 0]
    scaled = keys * rates[..., None]
    lower = jnp.einsum("nhid,nhjd->nhij", scaled, keys, precision=HIGH) * strict
    inverse = unit_inverse(lower)
    w_mat = dotf(inverse, scaled)
    base = dotf(inverse, values * rates[..., None])
    eye_heads = jnp.broadcast_to(jnp.eye(DK, dtype=jnp.float32), (H, DK, DK))
    zero_heads = jnp.zeros((H, DK, DK), jnp.float32)

    def chain_step(maps, inputs):
        c_keys, c_w, c_base, c_keep, c_tail, c_whole = inputs
        mixed_maps = dotf(c_w[None], maps)
        reduce_part = jnp.einsum(
            "hcd,shce->shde", c_keys * (c_tail * c_keep), mixed_maps, precision=HIGH
        )
        maps = c_whole * maps - reduce_part
        shift_add = jnp.einsum("hcd,hce->hde", c_keys * c_tail, c_base, precision=HIGH)
        return (jnp.stack([maps[0], maps[1] + shift_add]), None)

    block_maps, unused = lax.scan(
        chain_step, jnp.stack([eye_heads, zero_heads]), (keys, w_mat, base, keep, tail, whole)
    )
    every_map, every_shift = (
        lax.all_gather(block_maps[0][None].astype(jnp.bfloat16), "seq", axis=0, tiled=True).astype(
            jnp.float32
        ),
        lax.all_gather(block_maps[1][None].astype(jnp.bfloat16), "seq", axis=0, tiled=True).astype(
            jnp.float32
        ),
    )

    def apply_map(position, state):
        return jnp.where(
            position < seq_place, dotf(every_map[position], state) + every_shift[position], state
        )

    state_in = lax.fori_loop(0, seq_count, apply_map, zero_heads)

    def out_step(state, inputs):
        c_q, c_keys, c_w, c_base, c_keep, c_tail, c_whole, c_incl = inputs
        pseudo = c_base - c_keep * dotf(c_w, state)
        scores = jnp.einsum("hid,hjd->hij", c_q, c_keys, precision=HIGH) * c_incl
        output = c_keep * dotf(c_q, state) + dotf(scores, pseudo)
        new_state = c_whole * state + jnp.einsum(
            "hcd,hce->hde", c_keys * c_tail, pseudo, precision=HIGH
        )
        return (new_state, (output, state))

    last_state, (outputs, block_states) = lax.scan(
        out_step, state_in, (scaled_q, keys, w_mat, base, keep, tail, whole, incl)
    )
    mixed_o = outputs.transpose(0, 2, 1, 3).reshape(seq_len, H, DK)
    head_inv = lax.rsqrt(jnp.mean(mixed_o * mixed_o, -1, keepdims=True) + EPS_HEAD)
    ohat = mixed_o * head_inv
    act_two = (ohat * head_f).reshape(seq_len, width).astype(jnp.bfloat16)
    resid = token_rows + jnp.dot(act_two, w_out, preferred_element_type=jnp.float32)
    inv_two = lax.rsqrt(jnp.mean(resid * resid, -1, keepdims=True) + EPS_NORM)
    rhat = resid * inv_two
    act_three = (rhat * float_gains[1]).astype(jnp.bfloat16)
    gate_up = jnp.dot(act_three, w_gu, preferred_element_type=jnp.float32)
    hidden_units = gate_up.shape[1] // 2
    gate = gate_up[:, :hidden_units]
    up_part = gate_up[:, hidden_units:]
    act_four = (jax.nn.silu(gate) * up_part).astype(jnp.bfloat16)
    mixed = (resid + jnp.dot(act_four, w_down, preferred_element_type=jnp.float32)).astype(
        jnp.bfloat16
    )
    grad_down = tok_dot(act_four, cot_low)
    d_act_four = back_dot(cot_low, w_down)
    d_gate = silu_back(d_act_four * up_part, gate)
    d_up = d_act_four * jax.nn.silu(gate)
    d_gate_up = jnp.concatenate([d_gate, d_up], 1).astype(jnp.bfloat16)
    grad_gate_up = tok_dot(act_three, d_gate_up)
    d_act_three = back_dot(d_gate_up, w_gu)
    grad_gain_two = jnp.sum(d_act_three * rhat, 0)
    residual_gradient = cot_low.astype(jnp.float32) + root_mean_square_backward(
        d_act_three * float_gains[1], rhat, inv_two
    )
    d_resid_low = residual_gradient.astype(jnp.bfloat16)
    grad_out = tok_dot(act_two, d_resid_low)
    d_act_two = back_dot(d_resid_low, w_out).reshape(seq_len, H, DK)
    grad_head = jnp.sum(d_act_two * ohat, (0, 1))
    d_mixed_o = root_mean_square_backward(d_act_two * head_f, ohat, head_inv)
    d_out_groups = d_mixed_o.reshape(n_groups, GROUP, H, DK).transpose(0, 2, 1, 3)

    def state_grad(grad_state, inputs):
        c_q, c_keys, c_scaled, c_inverse, c_keep, c_tail, c_whole, c_incl, c_dout = inputs
        scores = jnp.einsum("hid,hjd->hij", c_q, c_keys, precision=HIGH) * c_incl
        d_pseudo = jnp.einsum("hij,hid->hjd", scores, c_dout, precision=HIGH) + c_tail * dotf(
            c_keys, grad_state
        )
        d_res = jnp.einsum("hij,hid->hjd", c_inverse, d_pseudo, precision=HIGH)
        prior = (
            jnp.einsum("hcd,hce->hde", c_q * c_keep, c_dout, precision=HIGH) + c_whole * grad_state
        )
        return (prior - jnp.einsum("hcd,hce->hde", c_scaled * c_keep, d_res, precision=HIGH), None)

    local_grad, unused = lax.scan(
        state_grad,
        zero_heads,
        (scaled_q, keys, scaled, inverse, keep, tail, whole, incl, d_out_groups),
        reverse=True,
    )
    back_maps = swap_last(block_maps[0])
    every_back, every_grad = (
        lax.all_gather(back_maps[None].astype(jnp.bfloat16), "seq", axis=0, tiled=True).astype(
            jnp.float32
        ),
        lax.all_gather(local_grad[None].astype(jnp.bfloat16), "seq", axis=0, tiled=True).astype(
            jnp.float32
        ),
    )

    def apply_back(step_index, grad_state):
        position = seq_count - 1 - step_index
        return jnp.where(
            position > seq_place,
            dotf(every_back[position], grad_state) + every_grad[position],
            grad_state,
        )

    grad_state_out = lax.fori_loop(0, seq_count, apply_back, zero_heads)

    def full_back(grad_state, inputs):
        (
            c_q,
            c_keys,
            c_values,
            c_rates,
            c_scaled,
            c_inverse,
            c_w,
            c_base,
            c_keep,
            c_tail,
            c_whole,
            c_strict,
            c_incl,
            c_dout,
            c_state,
        ) = inputs
        pseudo = c_base - c_keep * dotf(c_w, c_state)
        scores = jnp.einsum("hid,hjd->hij", c_q, c_keys, precision=HIGH) * c_incl
        d_pseudo = jnp.einsum("hij,hid->hjd", scores, c_dout, precision=HIGH) + c_tail * dotf(
            c_keys, grad_state
        )
        d_res = jnp.einsum("hij,hid->hjd", c_inverse, d_pseudo, precision=HIGH)
        prior = (
            jnp.einsum("hcd,hce->hde", c_q * c_keep, c_dout, precision=HIGH) + c_whole * grad_state
        )
        prior = prior - jnp.einsum("hcd,hce->hde", c_scaled * c_keep, d_res, precision=HIGH)
        d_scores = jnp.einsum("hid,hjd->hij", c_dout, pseudo, precision=HIGH) * c_incl
        d_query = c_keep * dotf(c_dout, swap_last(c_state)) + dotf(d_scores, c_keys)
        d_keys = jnp.einsum("hij,hid->hjd", d_scores, c_q, precision=HIGH) + c_tail * dotf(
            pseudo, swap_last(grad_state)
        )
        d_lower = -jnp.einsum("hid,hjd->hij", d_res, pseudo, precision=HIGH) * c_strict
        d_scaled = -c_keep * dotf(d_res, swap_last(c_state)) + dotf(d_lower, c_keys)
        d_keys = (
            d_keys
            + jnp.einsum("hij,hid->hjd", d_lower, c_scaled, precision=HIGH)
            + c_rates[..., None] * d_scaled
        )
        d_values = c_rates[..., None] * d_res
        d_rates = jnp.sum(d_res * c_values, -1) + jnp.sum(d_scaled * c_keys, -1)
        return (prior, (d_query * scale, d_keys, d_values, d_rates))

    first_grad, (d_q_groups, d_k_groups, d_v_groups, d_rate_groups) = lax.scan(
        full_back,
        grad_state_out,
        (
            scaled_q,
            keys,
            values,
            rates,
            scaled,
            inverse,
            w_mat,
            base,
            keep,
            tail,
            whole,
            strict,
            incl,
            d_out_groups,
            block_states,
        ),
        reverse=True,
    )

    def from_groups(arr):
        return arr.transpose(0, 2, 1, 3).reshape(seq_len, H, DK)

    d_q_unit = from_groups(d_q_groups)
    d_k_unit = from_groups(d_k_groups)
    d_q_raw = q_inv * (d_q_unit - q_unit * jnp.sum(d_q_unit * q_unit, -1, keepdims=True))
    d_k_raw = k_inv * (d_k_unit - k_unit * jnp.sum(d_k_unit * k_unit, -1, keepdims=True))
    d_act = jnp.concatenate(
        [
            d_q_raw.reshape(seq_len, width),
            d_k_raw.reshape(seq_len, width),
            from_groups(d_v_groups).reshape(seq_len, width),
        ],
        1,
    )
    d_pre = silu_back(d_act, pre)
    d_extended = jnp.zeros((seq_len + rim, d_pre.shape[1]), jnp.float32)
    conv_grads = []
    for tap in range(rim + 1):
        masked = d_pre * matches[tap]
        d_extended = d_extended + jnp.pad(conv_f[tap] * masked, ((rim - tap, tap), (0, 0)))
        conv_grads.append(jnp.sum(masked * extended[rim - tap : rim - tap + seq_len], 0))
    grad_conv = jnp.stack(conv_grads)
    rim_back = shifted(d_extended[:rim].astype(jnp.bfloat16), "seq", -1).astype(jnp.float32)
    d_proj = (d_extended[rim:] + jnp.pad(rim_back, ((seq_len - rim, 0), (0, 0)))).astype(
        jnp.bfloat16
    )
    d_rates_tok = d_rate_groups.transpose(0, 2, 1).reshape(seq_len, H)
    d_logits = (d_rates_tok * rates_tok * (1.0 - rates_tok)).astype(jnp.bfloat16)
    grad_qkv = tok_dot(first_activation, d_proj)
    grad_beta = tok_dot(first_activation, d_logits)
    first_activation_gradient = back_dot(d_proj, w_qkv) + back_dot(d_logits, w_beta)
    first_gain_gradient = jnp.sum(first_activation_gradient * normalized_input, 0)
    block_input_gradient = (
        residual_gradient
        + root_mean_square_backward(
            first_activation_gradient * float_gains[0], normalized_input, first_inverse_norm
        )
    ).astype(jnp.bfloat16)
    grad_gains = jnp.stack([first_gain_gradient, grad_gain_two])
    red_qkv, red_beta, red_conv, red_gains, red_head, red_out, red_gu, red_down = (
        lax.psum_scatter(
            grad_qkv.astype(jnp.bfloat16), "seq", scatter_dimension=0, tiled=True
        ).astype(jnp.float32),
        lax.psum_scatter(
            grad_beta.astype(jnp.bfloat16), "seq", scatter_dimension=0, tiled=True
        ).astype(jnp.float32),
        lax.psum_scatter(
            grad_conv.astype(jnp.bfloat16), "seq", scatter_dimension=1, tiled=True
        ).astype(jnp.float32),
        lax.psum_scatter(
            grad_gains.astype(jnp.bfloat16), "seq", scatter_dimension=1, tiled=True
        ).astype(jnp.float32),
        lax.psum_scatter(
            grad_head.astype(jnp.bfloat16), "seq", scatter_dimension=0, tiled=True
        ).astype(jnp.float32),
        lax.psum_scatter(
            grad_out.astype(jnp.bfloat16), "seq", scatter_dimension=0, tiled=True
        ).astype(jnp.float32),
        lax.psum_scatter(
            grad_gate_up.astype(jnp.bfloat16), "seq", scatter_dimension=0, tiled=True
        ).astype(jnp.float32),
        lax.psum_scatter(
            grad_down.astype(jnp.bfloat16), "seq", scatter_dimension=0, tiled=True
        ).astype(jnp.float32),
    )
    red_qkv, red_beta, red_conv, red_gains, red_head, red_out, red_gu, red_down = (
        lax.psum(red_qkv.astype(jnp.bfloat16), "row").astype(jnp.float32),
        lax.psum(red_beta.astype(jnp.bfloat16), "row").astype(jnp.float32),
        lax.psum(red_conv.astype(jnp.bfloat16), "row").astype(jnp.float32),
        lax.psum(red_gains.astype(jnp.bfloat16), "row").astype(jnp.float32),
        lax.psum(red_head.astype(jnp.bfloat16), "row").astype(jnp.float32),
        lax.psum(red_out.astype(jnp.bfloat16), "row").astype(jnp.float32),
        lax.psum(red_gu.astype(jnp.bfloat16), "row").astype(jnp.float32),
        lax.psum(red_down.astype(jnp.bfloat16), "row").astype(jnp.float32),
    )
    return (
        mixed[None],
        block_input_gradient[None],
        red_qkv,
        red_beta,
        red_conv,
        red_gains,
        red_head,
        red_out,
        red_gu,
        red_down,
    )


BF = jnp.bfloat16
F32 = jnp.float32
RIM = 8
NN = (((1,), (0,)), ((), ()))
NT = (((1,), (1,)), ((), ()))
TN = (((0,), (0,)), ((), ()))


def dot_low(a, b, dims=NN):
    return lax.dot_general(a, b, dims, preferred_element_type=F32)


def parts_of(a):
    if a.dtype == BF:
        return (a,)
    high = a.astype(BF)
    return high, (a - high.astype(F32)).astype(BF)


def mm(a, b, dims=NN):
    a_parts, b_parts = parts_of(a), parts_of(b)
    total = dot_low(a_parts[0], b_parts[0], dims)
    if len(b_parts) > 1:
        total = total + dot_low(a_parts[0], b_parts[1], dims)
    if len(a_parts) > 1:
        total = total + dot_low(a_parts[1], b_parts[0], dims)
    return total


def mm1(a, b, dims=NN):
    return dot_low(a.astype(BF), b.astype(BF), dims)


def begin_of(pos, starts_ref):
    begin = jnp.zeros_like(pos)
    for i in range(starts_ref.shape[0]):
        begin = jnp.maximum(begin, jnp.where(pos >= starts_ref[i], starts_ref[i], 0))
    return begin


def begin_at(pos, starts_ref):
    begin = jnp.int32(0)
    for i in range(starts_ref.shape[0]):
        begin = jnp.maximum(begin, jnp.where(starts_ref[i] <= pos, starts_ref[i], 0))
    return begin


def mark_table(chunks, size, taps, starts_ref):
    pos = lax.broadcasted_iota(jnp.int32, (chunks, size), 0) * size
    pos = pos + lax.broadcasted_iota(jnp.int32, (chunks, size), 1)
    rows = begin_of(pos, starts_ref)
    later = [
        ((begin_of(pos + tap, starts_ref) <= pos) & (pos + tap < chunks * size)).astype(F32)
        for tap in range(1, taps)
    ]
    down = lax.broadcasted_iota(jnp.int32, (size, size), 0)
    eye = (down == lax.broadcasted_iota(jnp.int32, (size, size), 1)).astype(BF)
    rows = rows.astype(F32)
    return rows, mm(eye, rows, NT), [mm(eye, v, NT) for v in later]


def chunk_marks(n, size, table, starts_ref):
    first = n * size
    col = table[1][:, n : n + 1]
    last = begin_at(first + size - 1, starts_ref)
    keep = (col < float(first)).astype(F32)
    tail = (col == last.astype(F32)).astype(F32)
    whole = (last < first).astype(F32)
    return col, keep, tail, whole


def chunk_masks(n, size, col, table):
    here = lax.broadcasted_iota(jnp.int32, (size, size), 0)
    there = lax.broadcasted_iota(jnp.int32, (size, size), 1)
    same = col == table[0][n : n + 1]
    return here, there, same & (here > there), same & (here >= there)


def conv_chunk(n, size, pad, conv, col):
    depth = (n * size + lax.broadcasted_iota(jnp.int32, (size, 1), 0)).astype(F32) - col
    pre = conv[0:1, :] * pad[pl.ds(RIM + n * size, size), :]
    for tap in range(1, conv.shape[0]):
        match = (depth >= float(tap)).astype(F32)
        pre = pre + conv[tap : tap + 1, :] * pad[pl.ds(RIM - tap + n * size, size), :] * match
    return pre


def front_kernel(taps, place_ref, starts_ref, *refs):
    n_seq = refs[-1].shape[0]
    n_row = n_seq // 2
    top_ref, low_refs = refs[0], refs[1 : 1 + n_seq]
    got_ref, got_y_ref, got_cores_ref = refs[1 + n_seq : 4 + n_seq]
    got_refs = (got_ref, got_cores_ref.at[0], got_y_ref, got_cores_ref.at[1])
    (
        weight_ref,
        act1_ref,
        proj_ref,
        rates_ref,
        o_ref,
        act2_ref,
        inv_ref,
        w_ref,
        att_ref,
        p_ref,
        u_ref,
        s_ref,
        conv_ref,
        gains_ref,
        beta_ref,
        head_ref,
        pad,
        lower,
        tmp,
        q_scr,
        k_scr,
        v_scr,
        low_rows,
        add,
    ) = refs[4 + n_seq :]
    place, row = place_ref[0], place_ref[1]
    size = s_ref.shape[1]
    part_rows = size // n_row
    dk = o_ref.shape[1]
    base = 3 * part_rows
    gains = jnp.concatenate([got_ref[s, base + 4 : base + 6, :] for s in range(n_seq)], 1).astype(F32)
    gains_ref[...] = jnp.zeros_like(gains_ref)
    gains_ref[0:2, :] = gains
    beta = jnp.concatenate([got_ref[s, base + 8 : base + 16, :] for s in range(n_seq)], 1)
    beta_ref[...] = beta
    head_gain = got_ref[0, base + 6 : base + 7, :].astype(F32)
    for s in range(1, n_seq):
        head_gain = head_gain + got_ref[s, base + 6 : base + 7, :].astype(F32)
    head_ref[...] = jnp.broadcast_to(head_gain, head_ref.shape)
    conv_parts = []
    for part in range(3):
        block = part * n_seq + place
        shard = block // 3
        offset = pl.multiple_of(base + (block - shard * 3) * 16, 16)
        conv_parts.append(got_ref[shard, pl.ds(offset, 16), :][0:8])
    conv = jnp.concatenate(conv_parts, 1).astype(F32)
    conv_ref[...] = conv
    conv = conv[0:taps]
    for m, ref in enumerate(got_refs):
        for s in range(n_seq):
            at = pl.multiple_of(s * size + (row ^ m) * part_rows, part_rows)
            for kind in range(3):
                block = ref[s, kind * part_rows : (kind + 1) * part_rows, :]
                weight_ref[pl.ds(at, part_rows), kind * dk : (kind + 1) * dk] = block
    weight = weight_ref[...]
    lanes = lax.broadcasted_iota(jnp.int32, (2 * size, 8), 1)
    half = n_seq // 2
    z, side = place // 2, lax.rem(place, 2)
    for i, ref in enumerate(low_refs):
        chunk = lax.rem(z - i // 2 + half, half) * 2 + (side if i % 2 == 0 else 1 - side)
        at = pl.multiple_of(chunk * (size // 2), size // 2)
        low_rows[pl.ds(at, size // 2), :] = ref[...]
    pad[0:RIM, :] = jnp.zeros((RIM, 3 * dk), F32)
    for n in range(0, n_seq, 2):
        rows_at = pl.ds(n * size, 2 * size)
        part = size // 2
        rows = jnp.concatenate(
            [
                top_ref[n * part : (n + 1) * part, :],
                low_rows[n * part : (n + 1) * part, :],
                top_ref[(n + 1) * part : (n + 2) * part, :],
                low_rows[(n + 1) * part : (n + 2) * part, :],
            ],
            0,
        ).astype(F32)
        inv = lax.rsqrt(jnp.mean(rows * rows, -1, keepdims=True) + EPS_NORM)
        act = ((rows * inv) * gains[0:1]).astype(BF)
        act1_ref[rows_at, :] = act
        proj = dot_low(act, weight).astype(BF)
        proj_ref[rows_at, :] = proj
        pad[pl.ds(RIM + n * size, 2 * size), :] = proj.astype(F32)
        logits = dot_low(act, beta, NT)
        rate = jax.nn.sigmoid(jnp.sum(jnp.where(lanes == place, logits, 0.0), 1, keepdims=True))
        rates_ref[rows_at, :] = jnp.broadcast_to(rate, (2 * size, dk))
    table = mark_table(n_seq, size, taps, starts_ref)
    marks = []
    for n in range(n_seq):
        at = n * size
        col, keep, tail, whole = chunk_marks(n, size, table, starts_ref)
        marks.append((keep, tail, whole))
        pre = conv_chunk(n, size, pad, conv, col)
        act = pre * jax.nn.sigmoid(pre)
        q_raw, k_raw, v_raw = act[:, :dk], act[:, dk : 2 * dk], act[:, 2 * dk :]
        q = (q_raw * lax.rsqrt(jnp.sum(q_raw * q_raw, -1, keepdims=True) + EPS_UNIT)).astype(BF)
        key = (k_raw * lax.rsqrt(jnp.sum(k_raw * k_raw, -1, keepdims=True) + EPS_UNIT)).astype(BF)
        q_scr[pl.ds(at, size), :] = q
        k_scr[pl.ds(at, size), :] = key
        v_scr[pl.ds(at, size), :] = v_raw.astype(BF)
        here, there, strict, incl = chunk_masks(n, size, col, table)
        rate = rates_ref[pl.ds(at, size), :]
        low = jnp.where(strict, dot_low(key, key, NT) * rate, 0.0)
        att_ref[n] = jnp.where(incl, dot_low(q, key, NT) * (dk**-0.5), 0.0)
        lower[n] = low
        eye = (here == there).astype(F32)
        inv_ref[n] = eye - jnp.where((here // 2) == (there // 2), low, 0.0)
    span = 2
    while span < size:
        here = lax.broadcasted_iota(jnp.int32, (size, size), 0)
        there = lax.broadcasted_iota(jnp.int32, (size, size), 1)
        cross = ((here // (2 * span)) == (there // (2 * span))) & ((here // span) != (there // span))
        for n in range(n_seq):
            tmp[n] = mm1(inv_ref[n], jnp.where(cross, lower[n], 0.0))
        for n in range(n_seq):
            inv_ref[n] = inv_ref[n] - mm1(tmp[n], inv_ref[n])
        span *= 2
    for n in range(n_seq):
        keep, tail, whole = marks[n]
        rows = pl.ds(n * size, size)
        rate = rates_ref[rows, :]
        key = k_scr[rows, :]
        inv = inv_ref[n]
        w = mm(inv, rate * key.astype(F32))
        base = mm(inv, rate * v_scr[rows, :].astype(F32))
        w_ref[n] = w
        u_ref[n] = base
        p_ref[n] = mm(key, (tail * keep) * w, TN)
        add[n] = mm(key, tail * base, TN)
    state = jnp.zeros((dk, dk), F32)
    for n in range(n_seq):
        s_ref[n] = state
        if n + 1 < n_seq:
            state = marks[n][2] * state - mm(p_ref[n], state) + add[n]
    for n in range(n_seq):
        keep, tail, whole = marks[n]
        rows = pl.ds(n * size, size)
        state = s_ref[n]
        u = u_ref[n] - keep * mm(w_ref[n], state)
        u_ref[n] = u
        out = (keep * (dk**-0.5)) * mm(q_scr[rows, :], state) + mm(att_ref[n], u)
        o_ref[rows, :] = out
        inv = lax.rsqrt(jnp.mean(out * out, -1, keepdims=True) + EPS_HEAD)
        act2_ref[n] = ((out * inv) * head_gain).astype(BF)


def back_kernel(taps, place_ref, starts_ref, *refs):
    (
        dact_ref,
        o_ref,
        head_ref,
        conv_ref,
        proj_ref,
        rates_ref,
        inv_ref,
        w_ref,
        att_ref,
        p_ref,
        u_ref,
        s_ref,
        weight_ref,
        beta_ref,
        dproj_ref,
        part_ref,
        dlog_ref,
        gconv_ref,
        ghead_ref,
        logit_scr,
        pad,
        pre_scr,
        dpre,
        do_scr,
        g_scr,
        add,
        x_scr,
        q_scr,
        k_scr,
    ) = refs
    n_seq, size, dk = dact_ref.shape
    scale = dk**-0.5
    place = place_ref[0]
    beta_all = beta_ref[...].astype(F32)
    beta_lane = lax.broadcasted_iota(jnp.int32, beta_all.shape, 0) == place
    beta_row = jnp.sum(jnp.where(beta_lane, beta_all, 0.0), 0, keepdims=True)
    head_gain = head_ref[0:1, :]
    conv = conv_ref[0:taps, :]
    total = n_seq * size
    pad[0:RIM, :] = jnp.zeros((RIM, 3 * dk), F32)
    pad[pl.ds(RIM, total), :] = proj_ref[...].astype(F32)
    dpre[pl.ds(total, RIM), :] = jnp.zeros((RIM, 3 * dk), F32)
    table = mark_table(n_seq, size, taps, starts_ref)
    marks = []
    ghead = jnp.zeros((1, dk), F32)
    for n in range(n_seq):
        rows = pl.ds(n * size, size)
        col, keep, tail, whole = chunk_marks(n, size, table, starts_ref)
        marks.append((col, keep, tail, whole))
        pre = conv_chunk(n, size, pad, conv, col)
        pre_scr[rows, :] = pre
        act = pre * jax.nn.sigmoid(pre)
        q_raw, k_raw = act[:, :dk], act[:, dk : 2 * dk]
        q = (q_raw * lax.rsqrt(jnp.sum(q_raw * q_raw, -1, keepdims=True) + EPS_UNIT)).astype(BF)
        key = (k_raw * lax.rsqrt(jnp.sum(k_raw * k_raw, -1, keepdims=True) + EPS_UNIT)).astype(BF)
        q_scr[rows, :] = q
        k_scr[rows, :] = key
        out = o_ref[rows, :]
        inv = lax.rsqrt(jnp.mean(out * out, -1, keepdims=True) + EPS_HEAD)
        ohat = out * inv
        d_act2 = dact_ref[n].astype(F32)
        ghead = ghead + jnp.sum(d_act2 * ohat, 0, keepdims=True)
        lean = d_act2 * head_gain
        d_out = inv * (lean - ohat * jnp.mean(lean * ohat, -1, keepdims=True))
        do_scr[rows, :] = d_out
        g_scr[rows, :] = mm1(att_ref[n], d_out, TN)
    ghead_ref[...] = jnp.broadcast_to(ghead, ghead_ref.shape)
    for n in range(n_seq):
        rows = pl.ds(n * size, size)
        col, keep, tail, whole = marks[n]
        add[n] = mm1(q_scr[rows, :], (scale * keep) * do_scr[rows, :], TN) - mm1(w_ref[n], keep * g_scr[rows, :], TN)
    grad = jnp.zeros((dk, dk), F32)
    for n in range(n_seq - 1, -1, -1):
        x_scr[n] = grad
        if n > 0:
            grad = marks[n][3] * grad - mm(p_ref[n], grad, TN) + add[n]
    gconv = [jnp.zeros((1, 3 * dk), F32) for _ in range(taps)]
    for n in range(n_seq - 1, -1, -1):
        rows = pl.ds(n * size, size)
        col, keep, tail, whole = marks[n]
        here, there, strict, incl = chunk_masks(n, size, col, table)
        rate = rates_ref[rows, :]
        key, q = k_scr[rows, :], q_scr[rows, :]
        key_f, q_f = key.astype(F32), q.astype(F32)
        pre = pre_scr[rows, :]
        sig = jax.nn.sigmoid(pre)
        act = pre * sig
        value = act[:, 2 * dk :].astype(BF).astype(F32)
        grad, state, u = x_scr[n], s_ref[n], u_ref[n]
        d_out = do_scr[rows, :]
        d_u = g_scr[rows, :] + tail * mm1(key, grad)
        d_r = mm1(inv_ref[n], d_u, TN)
        d_att = jnp.where(incl, mm1(d_out, u, NT), 0.0)
        d_low = jnp.where(strict, -mm1(d_r, u, NT), 0.0)
        d_q = keep * mm1(d_out, state, NT) + mm1(d_att, key)
        d_kb = mm1(d_low, key) - keep * mm1(d_r, state, NT)
        d_k = (
            scale * mm1(d_att, q, TN)
            + mm1(d_low, rate * key_f, TN)
            + tail * mm1(u, grad, NT)
            + rate * d_kb
        )
        d_v = rate * d_r
        d_rate = jnp.sum(d_r * value + d_kb * key_f, -1, keepdims=True)
        d_q = d_q * scale
        q_raw, k_raw = act[:, :dk], act[:, dk : 2 * dk]
        q_inv = lax.rsqrt(jnp.sum(q_raw * q_raw, -1, keepdims=True) + EPS_UNIT)
        k_inv = lax.rsqrt(jnp.sum(k_raw * k_raw, -1, keepdims=True) + EPS_UNIT)
        q_unit, k_unit = q_raw * q_inv, k_raw * k_inv
        d_q = q_inv * (d_q - q_unit * jnp.sum(d_q * q_unit, -1, keepdims=True))
        d_k = k_inv * (d_k - k_unit * jnp.sum(d_k * k_unit, -1, keepdims=True))
        d_act = jnp.concatenate([d_q, d_k, d_v], 1)
        d_pre = d_act * sig * (1.0 + pre * (1.0 - sig))
        dpre[rows, :] = d_pre
        depth = (n * size + lax.broadcasted_iota(jnp.int32, (size, 1), 0)).astype(F32) - col
        d_proj = conv[0:1, :] * d_pre
        gconv[0] = gconv[0] + jnp.sum(d_pre * pad[pl.ds(RIM + n * size, size), :], 0, keepdims=True)
        for tap in range(1, taps):
            match = table[2][tap - 1][:, n : n + 1]
            d_proj = d_proj + conv[tap : tap + 1, :] * dpre[pl.ds(n * size + tap, size), :] * match
            reach = (depth >= float(tap)).astype(F32)
            gconv[tap] = gconv[tap] + jnp.sum(
                d_pre * reach * pad[pl.ds(RIM - tap + n * size, size), :], 0, keepdims=True
            )
        d_proj = d_proj.astype(BF)
        dproj_ref[rows, :] = d_proj
        one_rate = rate[:, 0:1]
        d_logit = (d_rate * one_rate * (1.0 - one_rate)).astype(BF).astype(F32)
        logit_scr[rows, :] = jnp.broadcast_to(d_logit, (size, dk))
        dlog_ref[pl.ds(n, 1), :] = jnp.broadcast_to(d_logit, (size, dk)).T[0:1]
    for n in range(0, n_seq, 2):
        rows = pl.ds(n * size, 2 * size)
        d_act1 = dot_low(dproj_ref[rows, :], weight_ref[...], NT) + logit_scr[rows, 0:1] * beta_row
        part_ref[rows, :] = d_act1.astype(BF)
    gconv_ref[...] = jnp.zeros_like(gconv_ref)
    for tap in range(taps):
        gconv_ref[tap : tap + 1, :] = gconv[tap]


def lead_kernel(place_ref, qkv_ref, conv_ref, gains_ref, head_ref, beta_ref, out_ref, rows):
    place, row = place_ref[0], place_ref[1]
    heads, dk = out_ref.shape[0], out_ref.shape[2]
    part = dk // 4
    from_row = pl.ds(pl.multiple_of(row * part, part), part)
    per = head_ref.shape[1]
    down = lax.broadcasted_iota(jnp.int32, (dk, dk), 0)
    along = lax.broadcasted_iota(jnp.int32, (dk, dk), 1)
    spot = (along == down + place * per)[0:per].astype(BF)
    rows[...] = jnp.zeros_like(rows)
    taps = conv_ref.shape[0]
    for kind in range(3):
        rows[kind * 16 : kind * 16 + taps, :] = conv_ref[:, kind * dk : (kind + 1) * dk].astype(F32)
    rows[4:6, :] = gains_ref[...].astype(F32)
    rows[6:7, :] = dot_low(jnp.broadcast_to(head_ref[...], (16, per)), spot)[0:1]
    rows[8:16, :] = beta_ref[...].astype(F32)
    small = rows[...].astype(BF)
    for h in range(heads):
        for kind in range(3):
            block = qkv_ref[from_row, pl.ds((kind * heads + h) * dk, dk)]
            out_ref[h, kind * part : (kind + 1) * part, :] = block
        out_ref[h, 3 * part : 3 * part + 48, :] = small


SLOT = 96


def columns_kernel(place_ref, gu_ref, down_ref, own_ref, other_ref, rows_ref, wide_own, wide_other):
    side, row = lax.rem(place_ref[0], 2), place_ref[1]
    size, lanes = gu_ref.shape[0], own_ref.shape[1]
    hidden = down_ref.shape[0]
    part, wide = hidden // 4, wide_own.shape[1] // 2
    for ref in (wide_own, wide_other):
        for kind in range(2):
            ref[:, kind * wide + wide - 128 : (kind + 1) * wide] = jnp.zeros((size, 128), F32)

    def take(x, r):
        for ref, block in ((wide_own, x), (wide_other, 1 - x)):
            for kind in range(2):
                for z in range(4):
                    at = (kind * 8 + z * 2 + block) * hidden + r * part
                    to = kind * wide + z * part
                    ref[:, to : to + part] = gu_ref[:, at : at + part].astype(F32)
        for j in range(down_ref.shape[1] // lanes):
            block = down_ref[r * part : (r + 1) * part, j * lanes : (j + 1) * lanes].astype(F32)
            block = jnp.concatenate([block, jnp.zeros((SLOT - part, lanes), F32)], 0)
            rows_ref[j * SLOT : (j + 1) * SLOT, :] = block.astype(BF)

    for x in range(2):
        for r in range(4):
            pl.when((side == x) & (row == r))(functools.partial(take, x, r))
    for ref, out in ((wide_own, own_ref), (wide_other, other_ref)):
        for j in range(2 * wide // lanes):
            out[j * size : (j + 1) * size, :] = ref[:, j * lanes : (j + 1) * lanes].astype(BF)


def mid_kernel(place_ref, act2_ref, own_ref, y_ref, cores_ref, x_ref, gains_ref, resid_ref, act3_ref, weight_ref):
    row = place_ref[1]
    heads, size, dk = act2_ref.shape
    part = dk // 4
    for m in range(4):
        ref = (own_ref, cores_ref.at[0], y_ref, cores_ref.at[1])[m]
        for s in range(heads):
            at = pl.multiple_of((s * 4 + (row ^ m)) * part, part)
            weight_ref[pl.ds(at, part), :] = ref[s]
    act2 = jnp.concatenate([act2_ref[h] for h in range(heads)], 1)
    resid = x_ref[...].astype(F32) + dot_low(act2, weight_ref[...])
    resid_ref[...] = resid
    inv = lax.rsqrt(jnp.mean(resid * resid, -1, keepdims=True) + EPS_NORM)
    act3_ref[...] = ((resid * inv) * gains_ref[1:2, :]).astype(BF)


GROUP_BITS = (0, 2, 4, 6, 1, 3, 5, 7)


def store_part(bits, block, own_ref, next_ref):
    @pl.when((bits & 1) == 0)
    def _():
        own_ref[bits >> 1] = block

    @pl.when((bits & 1) == 1)
    def _():
        next_ref[bits >> 1] = block


def mixed_kernel(place_ref, act4_ref, down_ref, own_ref, next_ref):
    me = lax.rem(place_ref[0], 2) * 4 + place_ref[1]
    size = own_ref.shape[1]
    for i in range(4):
        parts = dot_low(act4_ref[pl.ds(i * 2 * size, 2 * size), :], down_ref[...]).astype(BF)
        for half in range(2):
            store_part(me ^ (2 * i + half), parts[half * size : (half + 1) * size], own_ref, next_ref)


def feed_kernel(hidden, place_ref, *refs):
    act3_refs, core_ref, cot_refs, cot_core_ref, packs_ref = refs[0:5], refs[5], refs[6:10], refs[10], refs[11]
    own_ref, next_ref, act4_ref, dgu_ref, act3_ref, cot_ref, down_ref, gu, down32 = refs[12:]
    place, row = place_ref[0], place_ref[1]
    side = lax.rem(place, 2)
    me = side * 4 + row
    size, width = act3_refs[0].shape
    wide = act4_ref.shape[1]
    lanes = packs_ref.shape[2]
    slot, part = 96, hidden // 4
    gu_rows = gu.shape[0] // 4
    n_cols = gu.shape[1] // lanes
    down32[hidden:wide, :] = jnp.zeros((wide - hidden, width), F32)

    for src in range(4):
        for i in range(2):
            shard = src * 2 + (side if i == 0 else 1 - side)
            rows = pl.ds(pl.multiple_of(shard * size, size), size)
            for j in range(n_cols):
                from_rows = pl.ds((i * n_cols + j) * size, size)
                gu[rows, j * lanes : (j + 1) * lanes] = packs_ref[src, from_rows, :]
        for j in range(width // lanes):
            block = packs_ref[src, pl.ds(n_cols * gu_rows + j * slot, slot), :].astype(F32)
            down32[src * part : (src + 1) * part, j * lanes : (j + 1) * lanes] = block[0:part]
    down_ref[...] = down32[...].astype(BF)
    for i, bits in enumerate(GROUP_BITS):
        at = pl.multiple_of((me ^ bits) * size, size)
        if i == 3:
            block = jnp.concatenate([act3_refs[3][...], act3_refs[4][...]], 0)
        else:
            block = act3_refs[i][...] if i < 3 else core_ref[i - 4]
        act3_ref[pl.ds(at, size), :] = block
        cot_ref[pl.ds(at, size), :] = cot_refs[i][...] if i < 4 else cot_core_ref[i - 4]
    for i in range(4):
        rows = pl.ds(i * 2 * size, 2 * size)
        act3 = act3_ref[rows, :]
        cot = cot_ref[rows, :]
        gate_up = dot_low(act3, gu[...])
        gate, up = gate_up[:, :wide], gate_up[:, wide:]
        sig = jax.nn.sigmoid(gate)
        silu = gate * sig
        act4_ref[rows, :] = (silu * up).astype(BF)
        d_act4 = dot_low(cot, down_ref[...], NT)
        d_gate = d_act4 * up * sig * (1.0 + gate * (1.0 - sig))
        d_gu = jnp.concatenate([d_gate, d_act4 * silu], 1).astype(BF)
        dgu_ref[rows, :] = d_gu
        parts = dot_low(d_gu, gu[...], NT).astype(BF)
        for half in range(2):
            store_part(me ^ (2 * i + half), parts[half * size : (half + 1) * size], own_ref, next_ref)


def grads_kernel(hidden, place_ref, act3_ref, cot_ref, act4_ref, dgu_ref, out_ref, down32):
    side = lax.rem(place_ref[0], 2)
    lanes = out_ref.shape[2]
    slot, part = 96, hidden // 4
    gu_rows = act3_ref.shape[1] // 4
    n_cols = dgu_ref.shape[1] // lanes
    down32[...] = dot_low(act4_ref[...], cot_ref[...], TN)
    for k in range(4):
        at = k * gu_rows
        grad = dot_low(act3_ref[:, at : at + gu_rows], dgu_ref[...], TN).astype(BF)
        size = gu_rows // 2
        for parity in range(2):
            first = jnp.where(side == parity, 0, n_cols * size)
            for j in range(n_cols):
                rows = pl.ds(pl.multiple_of(first + j * size, size), size)
                out_ref[k, rows, :] = grad[parity * size : (parity + 1) * size, j * lanes : (j + 1) * lanes]
        rows = pl.ds(k * part, part)
        for j in range(cot_ref.shape[1] // lanes):
            block = down32[rows, j * lanes : (j + 1) * lanes]
            block = jnp.concatenate([block, jnp.zeros((slot - part, lanes), F32)], 0)
            out_ref[k, pl.ds(n_cols * gu_rows + j * slot, slot), :] = block.astype(BF)


def out_grad_kernel(place_ref, act2_ref, low_ref, same_ref, other_ref, full):
    row = place_ref[1]
    heads, _, dk = act2_ref.shape
    part = dk // 4
    for h in range(heads):
        full[h * dk : (h + 1) * dk, :] = dot_low(act2_ref[h], low_ref[...], TN)
    for m in range(4):
        ref = same_ref if m % 2 == 0 else other_ref
        for h in range(heads):
            at = pl.multiple_of(h * dk + (row ^ m) * part, part)
            ref[m // 2, h] = full[pl.ds(at, part), :].astype(BF)


def qkv_grad_kernel(place_ref, act1_ref, dproj_ref, dlog_ref, gconv_ref, ghead_ref, same_ref, other_ref, full, rows):
    row = place_ref[1]
    shards, total, cols = same_ref.shape[1:]
    dk = cols // 3
    part = total - 16
    for h in range(shards):
        lanes = pl.ds(h * dk, dk)
        full[h * dk : (h + 1) * dk, :] = dot_low(act1_ref[:, lanes], dproj_ref[...], TN)
    g_beta = None
    dlog = dlog_ref[...].astype(BF)
    for n in range(dlog.shape[0]):
        one = jnp.broadcast_to(dlog[n : n + 1], (16, dk))
        term = dot_low(one, act1_ref[n * dk : (n + 1) * dk, :])[0:1]
        g_beta = term if g_beta is None else g_beta + term
    rows[...] = jnp.zeros_like(rows)
    for s in range(shards):
        rows[s, 0:4, :] = gconv_ref[0:4, :]
        rows[s, 4:5, 0:dk] = g_beta[:, s * dk : (s + 1) * dk]
        rows[s, 4:5, dk : 2 * dk] = ghead_ref[0:1, :]
    for m in range(4):
        ref = same_ref if m % 2 == 0 else other_ref
        for s in range(shards):
            at = pl.multiple_of(s * dk + (row ^ m) * part, part)
            ref[m // 2, s, 0:part, :] = full[pl.ds(at, part), :].astype(BF)
            ref[m // 2, s, pl.ds(part, 16), :] = rows[s].astype(BF)


def turn_kernel(heads, own_ref, core_ref, x_ref, y_ref, top_ref, bottom_ref, resid_ref, cot_ref, gains_ref, weight_ref, dresid_ref, low_ref, dact2_ref):
    resid = resid_ref[...]
    inv = lax.rsqrt(jnp.mean(resid * resid, -1, keepdims=True) + EPS_NORM)
    rhat = resid * inv
    d_act3 = own_ref[0].astype(F32) + core_ref[0].astype(F32)
    d_act3 = d_act3 + jnp.concatenate([x_ref[0], y_ref[0]], 0).astype(F32)
    d_act3 = d_act3 + jnp.concatenate([top_ref[...], bottom_ref[...]], 0).astype(F32)
    lean = d_act3 * gains_ref[1:2, :]
    d_resid = cot_ref[...].astype(F32) + inv * (lean - rhat * jnp.mean(lean * rhat, -1, keepdims=True))
    dresid_ref[...] = d_resid
    low = d_resid.astype(BF)
    low_ref[...] = low
    d_act2 = dot_low(low, weight_ref[...], NT).astype(BF)
    dk = d_act2.shape[1] // heads
    for h in range(heads):
        dact2_ref[h] = d_act2[:, h * dk : (h + 1) * dk]


def last_kernel(part_ref, x_ref, gains_ref, dresid_ref, out_ref):
    d_act1 = part_ref[...].astype(F32)
    rows = x_ref[...].astype(F32)
    inv = lax.rsqrt(jnp.mean(rows * rows, -1, keepdims=True) + EPS_NORM)
    xhat = rows * inv
    lean = d_act1 * gains_ref[0:1, :]
    out = dresid_ref[...] + inv * (lean - xhat * jnp.mean(lean * xhat, -1, keepdims=True))
    out_ref[...] = out.astype(BF)


def row_sums(v):
    total = jnp.sum(v, 1, keepdims=True)
    return jnp.broadcast_to(total, (v.shape[0], 128)).T[0:1]


def lay_feed_kernel(place_ref, *refs):
    own_ref, y_ref, cores_ref = refs[0:3]
    packs = (own_ref, cores_ref.at[0], y_ref, cores_ref.at[1])
    weight_ref, gain_ref, gu_out, down_out, gain_out, held = refs[3:]
    side, row = lax.rem(place_ref[0], 2), place_ref[1]
    size, hidden = gain_out.shape[1], down_out.shape[0]
    lanes, slot, part = packs[0].shape[1], 96, hidden // 4
    wide = held.shape[3] // 2
    n_cols = held.shape[3] // lanes
    for m in range(4):
        for own in range(2):
            block = side if own == 0 else 1 - side
            for j in range(n_cols):
                rows = pl.ds((own * n_cols + j) * size, size)
                held[row ^ m, block, :, j * lanes : (j + 1) * lanes] = packs[m][rows, :]
        at = pl.multiple_of((row ^ m) * part, 8)
        for j in range(down_out.shape[1] // lanes):
            block = packs[m][pl.ds(2 * n_cols * size + j * slot, slot), :].astype(F32)
            down_out[pl.ds(at, part), j * lanes : (j + 1) * lanes] = block[0:part]
    total = None
    for kind in range(2):
        for m in range(4):
            for x in range(2):
                for z in range(4):
                    at = kind * wide + z * part
                    piece = held[m, x, :, at : at + part].astype(F32)
                    to = (kind * 8 + z * 2 + x) * hidden + m * part
                    gu_out[:, to : to + part] = piece
    for at in range(0, gu_out.shape[1], lanes):
        term = gu_out[:, at : at + lanes] * weight_ref[:, at : at + lanes].astype(F32)
        total = term if total is None else total + term
    gain_out[...] = row_sums(total) / gain_ref[1:2, :].astype(F32)


def lay_mix_kernel(place_ref, *refs):
    qkv_refs = (refs[0], refs[2].at[0], refs[1], refs[2].at[1])
    out_refs = (refs[3], refs[5].at[0], refs[4], refs[5].at[1])
    weight_ref, beta_ref, gain_ref, second_ref, qkv_out, out_out, gain_out, conv_out, beta_out, head_out = refs[6:]
    place, row = place_ref[0], place_ref[1]
    heads, total, cols = qkv_refs[0].shape
    dk = cols // 3
    part = total - 16
    for m in range(4):
        rows = pl.ds(pl.multiple_of((row ^ m) * part, 8), part)
        out_out[rows, :] = out_refs[m][...].astype(F32)
        for h in range(heads):
            for kind in range(3):
                lanes = pl.ds((kind * heads + h) * dk, dk)
                block = qkv_refs[m][h, 0:part, kind * dk : (kind + 1) * dk]
                qkv_out[rows, lanes] = block.astype(F32)
    sums = jnp.sum(qkv_out[...] * weight_ref[...].astype(F32), 1, keepdims=True)
    ref = qkv_refs[0]
    small = [ref[h, pl.ds(part, 16), :].astype(F32) for h in range(heads)]
    beta_rows = jnp.concatenate([v[4:5, 0:dk] for v in small], 0)
    beta_out[...] = beta_rows
    head = small[0][4:5, dk : 2 * dk]
    for v in small[1:]:
        head = head + v[4:5, dk : 2 * dk]
    per = head_out.shape[1]
    spot = lax.broadcasted_iota(jnp.int32, (dk, per), 0) == (
        lax.broadcasted_iota(jnp.int32, (dk, per), 1) + place * per
    )
    head_out[...] = mm(jnp.broadcast_to(head, (8, dk)), spot.astype(BF))[0:1]
    for i in range(3):
        block = place * 3 + i
        kind = block // heads
        source = block - kind * heads
        lanes = pl.ds(pl.multiple_of(kind * dk, dk), dk)
        conv_out[:, i * dk : (i + 1) * dk] = ref[source, pl.ds(part, 16), lanes].astype(F32)[0 : conv_out.shape[0]]
    weight_rows = beta_ref[...].astype(F32)
    gain = jnp.broadcast_to(sums, (sums.shape[0], 128)).T[0:1]
    gain = gain + jnp.sum(beta_rows * weight_rows, 0, keepdims=True)
    gain_out[0:1, :] = gain / gain_ref[0:1, :].astype(F32)
    gain_out[1:2, :] = second_ref[...]


def local_call(kernel, outs, args, scratch=(), smem=0, us=1, mib=56, name=None):
    space = [pl.BlockSpec(memory_space=pltpu.SMEM)] * smem
    space += [pl.BlockSpec(memory_space=pltpu.VMEM)] * (len(args) - smem)
    return pl.pallas_call(
        kernel,
        out_shape=tuple(outs),
        in_specs=space,
        out_specs=tuple(pl.BlockSpec(memory_space=pltpu.VMEM) for _ in outs),
        scratch_shapes=list(scratch),
        compiler_params=pltpu.CompilerParams(vmem_limit_bytes=mib * 2**20),
        cost_estimate=pl.CostEstimate(flops=us * 10**9, bytes_accessed=1024, transcendentals=0),
        name=name,
    )(*args)


def head_plan(
    block_input,
    cotangent,
    doc_starts,
    qkv_weight,
    beta_weight,
    conv_weight,
    norm_gains,
    head_gain,
    out_weight,
    gate_up_weight,
    down_weight,
):
    x, cot = block_input[0], cotangent[0]
    starts = doc_starts[0]
    size, width = x.shape
    n_seq, n_row = lax.axis_size("seq"), lax.axis_size("row")
    place, row = lax.axis_index("seq"), lax.axis_index("row")
    half = n_seq // 2
    z, side = place // 2, place % 2
    total = n_seq * size
    where_at = jnp.stack([place, row])
    taps = conv_weight.shape[0]
    hidden = down_weight.shape[0]
    wide = -(-hidden // 128) * 128
    shape = jax.ShapeDtypeStruct

    def flip(v):
        return lax.ppermute(v, "seq", [(s, s ^ 1) for s in range(n_seq)])

    def roll(v, k):
        return lax.ppermute(v, "seq", [(s, (s // 2 + k) % half * 2 + s % 2) for s in range(n_seq)])

    def core(v):
        return lax.ppermute(v, "row", [(r, r ^ 1) for r in range(n_row)])

    def across(v):
        return lax.ppermute(v, "row", [(r, r ^ 2) for r in range(n_row)])

    def group_gather(v):
        y, s = across(v), flip(v)
        part = v.shape[0] // 2
        top, bottom = flip(y[:part]), across(s[part:])
        four = jnp.stack([v, y, s, jnp.concatenate([top, bottom], 0)])
        return [v, y, s, top, bottom, core(four)]

    def row_sum(same, other):
        mine = same.astype(F32) + core(other).astype(F32)
        return mine[0], mine[1].astype(BF)

    def row_relative(v):
        y = across(v)
        return [v, core(v), y, core(y)]

    def stage(*values):
        return lax.optimization_barrier(values)

    def line(v, step, t):
        ends = range(t - 1, half - 1) if step > 0 else range(1, half - t + 1)
        return lax.ppermute(
            v, "seq", [(2 * a + j, 2 * (a + step) + j) for a in ends for j in range(2)]
        )

    part_rows = size // n_row
    dk = width // n_seq
    lead_rows = 3 * part_rows + 48
    mid_row = size // 2
    row_top = lax.all_gather(x[:mid_row], "seq", tiled=True)
    far = {k: roll(x[mid_row:], k) for k in (2, 1, 3)}
    near = flip(x[mid_row:])
    (payload,) = local_call(
        lead_kernel,
        [shape((n_seq, lead_rows, dk), BF)],
        [where_at, qkv_weight, conv_weight, norm_gains, head_gain.reshape(1, -1), beta_weight.T],
        scratch=[pltpu.VMEM((48, dk), F32)],
        smem=1,
        us=2,
        name="lead",
    )

    rows3 = shape((3 * size, 256), BF)
    pack_rows = 6 * size + 4 * SLOT
    own_cols, other_cols, down_rows = local_call(
        columns_kernel,
        [rows3, rows3, shape((4 * SLOT, 256), BF)],
        [where_at, gate_up_weight, down_weight],
        scratch=[pltpu.VMEM((size, 2 * wide), F32)] * 2,
        smem=1,
        us=2,
        name="columns",
    )
    pack = jnp.concatenate([own_cols, flip(other_cols), down_rows], 0)
    got = lax.all_to_all(payload, "seq", 0, 0)
    got_y = across(got)
    got_cores = core(jnp.stack([got, got_y]))
    out_part = lax.dynamic_slice_in_dim(out_weight, row * part_rows, part_rows, 0)
    out_part = jnp.broadcast_to(out_part[None], (n_seq, part_rows, width))
    groups_z = [[2 * a + j for a in range(half)] for j in range(2)]
    packs = lax.all_gather(pack, "seq", axis_index_groups=groups_z)
    out_part, _, near, far[1], far[2], far[3] = stage(out_part, pack, near, far[1], far[2], far[3])
    out_part = lax.all_to_all(out_part, "seq", 0, 0)
    row_low = [x[mid_row:], near]
    for k in range(1, half):
        row_low += [far[k], flip(far[k])]
    row_top, got, got_y, got_cores, out_part, cot, _, *row_low = stage(
        row_top, got, got_y, got_cores, out_part, cot, pack, *row_low
    )
    cot_y, cot_x = across(cot), flip(cot)
    out_y = across(out_part)
    square = shape((n_seq, size, dk), F32)
    (
        w_head,
        act1,
        proj,
        rates,
        outs,
        act2,
        inverse,
        w_mat,
        att,
        p_mat,
        u_mat,
        states,
        conv,
        gains,
        beta,
        head,
    ) = local_call(
        functools.partial(front_kernel, taps),
        [
            shape((width, 3 * dk), BF),
            shape((total, width), BF),
            shape((total, 3 * dk), BF),
            shape((total, dk), F32),
            shape((total, dk), F32),
            shape((n_seq, size, dk), BF),
            square,
            square,
            square,
            square,
            square,
            square,
            shape((8, 3 * dk), F32),
            shape((8, width), F32),
            shape((8, width), BF),
            shape((8, dk), F32),
        ],
        [where_at, starts, row_top, *row_low, got, got_y, got_cores],
        scratch=[
            pltpu.VMEM((RIM + total, 3 * dk), F32),
            pltpu.VMEM((n_seq, size, size), F32),
            pltpu.VMEM((n_seq, size, size), F32),
            pltpu.VMEM((total, dk), BF),
            pltpu.VMEM((total, dk), BF),
            pltpu.VMEM((total, dk), BF),
            pltpu.VMEM((total // 2, width), BF),
            pltpu.VMEM((n_seq, dk, dk), F32),
        ],
        smem=2,
        us=4,
        name="front",
    )
    act2, cot_y, cot_x, out_y = stage(act2, cot_y, cot_x, out_y)
    act2 = lax.all_to_all(act2, "seq", 0, 0)
    cot_four = [cot, cot_y, cot_x, flip(cot_y)]
    out_cores = core(jnp.stack([out_part, out_y]))
    act2, out_cores, cot_four[3] = stage(act2, out_cores, cot_four[3])
    cot_all = [*cot_four, core(jnp.stack(cot_four))]
    resid, act3, w_out = local_call(
        mid_kernel,
        [shape((size, width), F32), shape((size, width), BF), shape((width, width), BF)],
        [where_at, act2, out_part, out_y, out_cores, x, gains],
        smem=1,
        us=1,
        mib=24,
        name="mid",
    )
    four = shape((4, size, width), BF)
    d_own, d_next, act4, d_gu, act3_all, cot_all, w_down = local_call(
        functools.partial(feed_kernel, hidden),
        [
            four,
            four,
            shape((total, wide), BF),
            shape((total, 2 * wide), BF),
            shape((total, width), BF),
            shape((total, width), BF),
            shape((wide, width), BF),
        ],
        [where_at, *group_gather(act3), *cot_all, packs],
        scratch=[pltpu.VMEM((width, 2 * wide), BF), pltpu.VMEM((wide, width), F32)],
        smem=1,
        us=3,
        mib=24,
        name="feed",
    )
    d_got = core(d_next)
    (grads,) = local_call(
        functools.partial(grads_kernel, hidden),
        [shape((half, pack_rows, 256), BF)],
        [where_at, act3_all, cot_all, act4, d_gu],
        scratch=[pltpu.VMEM((wide, width), F32)],
        smem=1,
        us=3,
        mib=24,
        name="grads",
    )
    d_got, d_own, act4, grads = stage(d_got, d_own, act4, grads)
    grads = lax.psum_scatter(grads, "seq", scatter_dimension=0, axis_index_groups=groups_z)
    top, low = slice(0, mid_row), slice(mid_row, size)

    def core_sum(i, part):
        return d_own[i, part].astype(F32) + d_got[i, part].astype(F32)

    d_x = flip(jnp.stack([core_sum(2, top), core_sum(3, top)]).astype(BF))
    d_y = across(jnp.stack([core_sum(1, low), core_sum(3, low)]).astype(BF))
    mixed_own, mixed_next = local_call(
        mixed_kernel, [four, four], [where_at, act4, w_down], smem=1, us=5, name="mixed"
    )
    d_x, d_y, mixed_own, mixed_next = stage(d_x, d_y, mixed_own, mixed_next)
    d_top = across((core_sum(1, top) + d_x[1].astype(F32)).astype(BF))
    d_bottom = flip((core_sum(2, low) + d_y[1].astype(F32)).astype(BF))
    d_resid, d_low, d_act2 = local_call(
        functools.partial(turn_kernel, n_seq),
        [shape((size, width), F32), shape((size, width), BF), shape((n_seq, size, dk), BF)],
        [d_own, d_got, d_x, d_y, d_top, d_bottom, resid, cot, gains, w_out],
        us=1,
        mib=24,
        name="turn",
    )
    d_act2 = lax.all_to_all(d_act2, "seq", 0, 0)
    out_shape = shape((2, n_seq, part_rows, width), BF)
    out_same, out_other = local_call(
        out_grad_kernel,
        [out_shape, out_shape],
        [where_at, act2, d_low],
        scratch=[pltpu.VMEM((width, width), F32)],
        smem=1,
        us=3,
        name="out_grad",
    )
    d_act2, out_same, out_other, mixed_own, mixed_next = stage(d_act2, out_same, out_other, mixed_own, mixed_next)
    mixed_got = core(mixed_next)
    out_got = core(out_other)
    d_proj, parts, d_log, g_conv, g_head = local_call(
        functools.partial(back_kernel, taps),
        [
            shape((total, 3 * dk), BF),
            shape((total, width), BF),
            shape((n_seq, size), F32),
            shape((8, 3 * dk), F32),
            shape((8, dk), F32),
        ],
        [
            where_at,
            starts,
            d_act2,
            outs,
            head,
            conv,
            proj,
            rates,
            inverse,
            w_mat,
            att,
            p_mat,
            u_mat,
            states,
            w_head,
            beta,
        ],
        scratch=[
            pltpu.VMEM((total, dk), F32),
            pltpu.VMEM((RIM + total, 3 * dk), F32),
            pltpu.VMEM((total, 3 * dk), F32),
            pltpu.VMEM((RIM + total, 3 * dk), F32),
            pltpu.VMEM((total, dk), F32),
            pltpu.VMEM((total, dk), F32),
            pltpu.VMEM((n_seq, dk, dk), F32),
            pltpu.VMEM((n_seq, dk, dk), F32),
            pltpu.VMEM((total, dk), BF),
            pltpu.VMEM((total, dk), BF),
        ],
        smem=2,
        us=14,
        name="back",
    )
    d_proj, parts, d_log, g_conv, g_head, out_got, mixed_got, grads = stage(
        d_proj, parts, d_log, g_conv, g_head, out_got, mixed_got, grads
    )
    mixed_both = [mixed_own[i].astype(F32) + mixed_got[i].astype(F32) for i in range(4)]
    mixed_x = flip(jnp.stack([mixed_both[2], mixed_both[3]]).astype(BF))
    d_act1 = lax.psum_scatter(parts, "seq", scatter_dimension=0, tiled=True)
    out_mine = out_same[0].astype(F32) + out_got[0].astype(F32)
    out_y = across((out_same[1].astype(F32) + out_got[1].astype(F32)).astype(BF))
    out_piece = lax.all_to_all((out_mine + out_y.astype(F32)).astype(BF), "seq", 0, 0)
    out_piece = out_piece.astype(F32).sum(0).astype(BF)
    out_y = across(out_piece)
    out_cores = core(jnp.stack([out_piece, out_y]))
    mixed_y = across((mixed_both[1] + mixed_x[1].astype(F32)).astype(BF))
    mixed = (resid + mixed_both[0] + mixed_x[0].astype(F32) + mixed_y.astype(F32)).astype(BF)
    gu_rows = 3 * size
    gu_other = flip(grads[gu_rows : 2 * gu_rows])
    feed_part = jnp.concatenate([grads[:gu_rows], gu_other, grads[2 * gu_rows :]], 0)
    feed_y = across(feed_part)
    feed_cores = core(jnp.stack([feed_part, feed_y]))
    cut_shape = shape((2, n_seq, part_rows + 16, 3 * dk), BF)
    qkv_same, qkv_other = local_call(
        qkv_grad_kernel,
        [cut_shape, cut_shape],
        [where_at, act1, d_proj, d_log, g_conv, g_head],
        scratch=[pltpu.VMEM((width, 3 * dk), F32), pltpu.VMEM((n_seq, 16, 3 * dk), F32)],
        smem=1,
        us=5,
        name="qkv_grad",
    )
    qkv_got = core(qkv_other)
    qkv_mine = qkv_same[0].astype(F32) + qkv_got[0].astype(F32)
    qkv_y = across((qkv_same[1].astype(F32) + qkv_got[1].astype(F32)).astype(BF))
    qkv_piece = lax.all_to_all((qkv_mine + qkv_y.astype(F32)).astype(BF), "seq", 0, 0)
    qkv_y = across(qkv_piece)
    qkv_cores = core(jnp.stack([qkv_piece, qkv_y]))
    (input_gradient,) = local_call(
        last_kernel,
        [shape((size, width), BF)],
        [d_act1, x, gains, d_resid],
        us=3,
        mib=56,
        name="last",
    )
    red_gu, red_down, second_gain = local_call(
        lay_feed_kernel,
        [
            shape((size, 2 * n_seq * hidden), F32),
            shape((hidden, width), F32),
            shape((1, size), F32),
        ],
        [where_at, feed_part, feed_y, feed_cores, gate_up_weight, norm_gains],
        scratch=[pltpu.VMEM((n_row, 2, size, 2 * wide), BF)],
        smem=1,
        us=0,
        mib=56,
        name="lay_feed",
    )
    red_qkv, red_out, red_gains, red_conv, red_beta, red_head = local_call(
        lay_mix_kernel,
        [
            shape((size, 3 * width), F32),
            shape((size, width), F32),
            shape((2, size), F32),
            shape((taps, 3 * dk), F32),
            shape((n_seq, dk), F32),
            shape((1, head_gain.shape[0]), F32),
        ],
        [where_at, qkv_piece, qkv_y, qkv_cores, out_piece, out_y, out_cores, qkv_weight, beta_weight.T, norm_gains, second_gain],
        smem=1,
        us=3,
        mib=56,
        name="lay_mix",
    )
    red_beta = red_beta.T
    red_head = red_head[0]
    return (
        mixed[None],
        input_gradient[None],
        red_qkv,
        red_beta,
        red_conv,
        red_gains,
        red_head,
        red_out,
        red_gu,
        red_down,
    )


def plan(block_input, *rest):
    seq, row = lax.axis_size("seq"), lax.axis_size("row")
    if seq == H and row * 2 == H and block_input.shape[1] == DK:
        return head_plan(block_input, *rest)
    return on_device(block_input, *rest)


def solution(mesh):
    in_specs = (
        P("row", "seq", None),
        P("row", "seq", None),
        P("row", None),
        P("seq", None),
        P("seq", None),
        P(None, "seq"),
        P(None, "seq"),
        P("seq"),
        P("seq", None),
        P("seq", None),
        P("seq", None),
    )
    out_specs = (
        P("row", "seq", None),
        P("row", "seq", None),
        P("seq", None),
        P("seq", None),
        P(None, "seq"),
        P(None, "seq"),
        P("seq"),
        P("seq", None),
        P("seq", None),
        P("seq", None),
    )
    return jax.shard_map(
        plan, mesh=mesh, in_specs=in_specs, out_specs=out_specs, check_vma=False
    )
```
